32 devices in a mesh: dp: 4 (over z), fsdp: 8 (over y, x, core).
Axes of the slice: x: 2, y: 2, z: 4, core: 2. Of those that a mesh axis runs over, the one named last changes fastest.
Arguments:
- hidden_in: bfloat16 [4096, 2048], P(('dp', 'fsdp')), may hold values from -6 to 6
- lengths: int32 [4], replicated, may hold values from 256 to 1024, as said below
- routes: int32 [4096, 8], P(('dp', 'fsdp')), may hold values from 0 to 15, all different within a row; in each aligned block of 128 rows (0 to 127, 128 to 255, ...) at most 80 rows name the same one
- attn_gain: bfloat16 [2048], P(('dp', 'fsdp')), may hold values from 0.25 to 1.75
- query_gain: bfloat16 [2048], P(('dp', 'fsdp')), may hold values from 0.25 to 1.75
- key_gain: bfloat16 [2048], P(('dp', 'fsdp')), may hold values from 0.25 to 1.75
- ffn_gain: bfloat16 [2048], P(('dp', 'fsdp')), may hold values from 0.25 to 1.75
- qkv_weight: bfloat16 [2048, 6144], P(('dp', 'fsdp')), may hold values from -0.125 to 0.125
- out_weight: bfloat16 [2048, 2048], P(('dp', 'fsdp')), may hold values from -1 to 1
- router_weight: bfloat16 [2048, 16], P(('dp', 'fsdp')), may hold values from -0.0625 to 0.0625
- expert_in: bfloat16 [2048, 16, 2048], P(('dp', 'fsdp')), may hold values from -0.125 to 0.125
- expert_out: bfloat16 [1024, 16, 2048], P(('dp', 'fsdp')), may hold values from -1.5 to 1.5
- cotangent: bfloat16 [4096, 2048], P(('dp', 'fsdp')), may hold values from -6 to 6
Outputs:
- block_out: bfloat16 [4096, 2048], P(('dp', 'fsdp'))
- hidden_grad: float32 [4096, 2048], P(('dp', 'fsdp'))
- attn_gain_grad: float32 [2048], P(('dp', 'fsdp'))
- query_gain_grad: float32 [2048], P(('dp', 'fsdp'))
- key_gain_grad: float32 [2048], P(('dp', 'fsdp'))
- ffn_gain_grad: float32 [2048], P(('dp', 'fsdp'))
- qkv_weight_grad: float32 [2048, 6144], P(('dp', 'fsdp'))
- out_weight_grad: float32 [2048, 2048], P(('dp', 'fsdp'))
- router_weight_grad: float32 [2048, 16], P(('dp', 'fsdp'))
- expert_in_grad: float32 [2048, 16, 2048], P(('dp', 'fsdp'))
- expert_out_grad: float32 [1024, 16, 2048], P(('dp', 'fsdp'))
- stats: float32 [3], replicated
The draws below stay inside these ranges and needn't reach their ends.
Inputs may be any that keep to these rules, and one draw needn't show every extreme that they name: `lengths`: one sequence, chosen by the seed, has all 1024 slots valid and another has 256. `routes`: each token names 8 different experts; among the 128 tokens of one device no expert is named more than 80 times, a bound that some block reaches.
All inputs are finite; a program needn't handle non-finite values.
Results may differ from the reference program's by a relative error of at most 0.02.
Values may be sent and summed in bfloat16 or wider, within the bound.
A program may use at most 320 MiB of HBM per device.

```python
import math
import jax
import jax.numpy as jnp
import numpy as np
from jax import lax

D = 2048
HEADS = 16
HEAD_DIM = 128
FF = 1024
EXPERTS = 16
TOPK = 8
TOK_DEV = 128
CAP = 80
SEQ = 1024
SEQS = 4
TOKENS = 4096


def draw_lengths(key, part):
    key = jax.random.fold_in(key, 11)
    key_base, key_full, key_short = jax.random.split(key, 3)
    drawn_lengths = jax.random.randint(key_base, (SEQS,), SEQ // 4, SEQ + 1)
    full_index = jax.random.randint(key_full, (), 0, SEQS)
    short_index = (full_index + jax.random.randint(key_short, (), 1, SEQS)) % SEQS
    seq_index = jnp.arange(SEQS)
    drawn_lengths = jnp.where(seq_index == full_index, SEQ, drawn_lengths)
    return jnp.where(seq_index == short_index, SEQ // 4, drawn_lengths).astype(jnp.int32)


def strengthened(entries, own_key, source, target, blocks, factor):
    owner, partner = [(jnp.arange(entries.shape[position]) // (entries.shape[position] // blocks)).reshape([-1 if axis == position else 1 for axis in range(entries.ndim)]) for position in (source, target)]
    chosen = jax.random.permutation(own_key, blocks)[partner]
    strong = (owner == chosen) | (owner == (partner + blocks // 2) % blocks)
    return jnp.where(strong, factor * entries, entries)


def level_of(rng, extent, cuts, least, high):
    def one(dim, parts):
        draws = jax.random.uniform(jax.random.fold_in(jax.random.fold_in(rng, 6), dim), (parts,), jnp.float32, least / len(cuts), high / len(cuts))
        return jnp.repeat(jnp.exp(draws), extent[dim] // parts).reshape((-1,) + (1,) * (len(extent) - dim - 1))

    level = one(*cuts[0])
    for cut in cuts[1:]:
        level = level * one(*cut)
    return level


def routed_block(key, own, number, rows, amount, top, reach, slope):
    ranking = jax.random.permutation(key, amount)
    packed, common = portions_of(amount, rows * top, reach, slope, True), portions_of(amount, rows * top, reach, slope, False)
    places = jnp.arange(amount)

    def named(sizes, rotation):
        used = int((sizes > 0).sum())
        fixed = max(1, used // 4)
        moved = fixed + (places - fixed + rotation * (used - fixed)) % max(1, amount - fixed)
        return jnp.zeros((amount,), jnp.int32).at[ranking[jnp.where(places < fixed, places, moved)]].set(jnp.asarray(sizes, jnp.int32))

    sizes = jnp.where(number % 4 == 0, named(packed, number // 4), named(common, number - number // 4 - 1))
    mixed = jax.random.permutation(jax.random.fold_in(own, 3), amount)
    donor, sink = mixed[0:amount // 2 * 2:2], mixed[1:amount // 2 * 2:2]
    margin = jnp.minimum(sizes[donor] - 1, reach - sizes[sink]) // 2
    margin = jnp.where((donor == ranking[0]) | (sink == ranking[0]) | (sizes[sink] == 0), 0, jnp.maximum(margin, 0))
    moved = jax.random.randint(jax.random.fold_in(own, 4), (amount // 2,), 0, 1 << 20) % (margin + 1)
    sizes = sizes.at[donor].add(-moved).at[sink].add(moved)
    items = jnp.searchsorted(jnp.cumsum(sizes), jnp.arange(rows * top), side="right").astype(jnp.int32)
    listing = items.reshape(top, rows).T
    listing = listing[jax.random.permutation(jax.random.fold_in(own, 1), rows)]
    rotation = jax.random.randint(jax.random.fold_in(own, 2), (rows, 1), 0, top)
    return jnp.take_along_axis(listing, (jnp.arange(top)[None, :] + rotation) % top, axis=1)


def portions_of(amount, total, bound, skew, full):
    portions = [(1 << 20) // math.isqrt(grade ** skew) + 1 for grade in range(1, amount + 1)]
    largest = bound if full else min(bound, max(-(-total // amount), total * portions[0] // sum(portions)))
    least = 1 if total - largest >= amount - 1 else 0
    counts, surplus = [largest] + [least] * (amount - 1), total - largest - least * (amount - 1)
    while surplus > 0:
        movable = [i for i in range(1, amount) if counts[i] < largest] or [i for i in range(1, amount) if counts[i] < bound]
        pool, remaining = sum([portions[i] for i in movable]), surplus
        for i in movable:
            addition = min(bound - counts[i], max(1, remaining * portions[i] // pool), surplus)
            counts[i] = counts[i] + addition
            surplus = surplus - addition
    return np.array(counts)


def normal_values(own_key, dims, spread, limit, cuts=(), kind=jnp.bfloat16):
    values = jax.random.normal(own_key, dims, jnp.float32) * spread
    if len(cuts) > 0:
        values = level_of(own_key, dims, cuts, -0.22, 0.18) * values
    return jnp.clip(values, min=-limit, max=limit).astype(kind)


def noise_with(own_key, dims, scale, reach, cuts, heavy, kind=jnp.bfloat16):
    values = scale * jax.random.normal(own_key, dims, jnp.float32)
    if cuts:
        values = values * level_of(own_key, dims, cuts, -0.22, 0.18)
    return jnp.clip(strengthened(values, jax.random.fold_in(own_key, 3), *heavy), -reach, reach).astype(kind)


def setup_inputs(seed: int = 0) -> dict:
    streams_of = jax.random.split(jax.random.key(seed), 14)
    hidden_in = normal_values(streams_of[0], (TOKENS, D), 1.0, 6.0, ((0, 32),))
    lengths = draw_lengths(jax.random.fold_in(streams_of[13], 71), 0)
    routes_keys = jax.random.split(jax.random.fold_in(streams_of[2], 1), TOKENS // TOK_DEV)
    routes_turns = jax.random.permutation(jax.random.fold_in(streams_of[2], 3), TOKENS // TOK_DEV)
    routes = jax.vmap(lambda own, number: routed_block(jax.random.fold_in(streams_of[2], 2), own, number, TOK_DEV, EXPERTS, TOPK, CAP, 0))(routes_keys, routes_turns).reshape((TOKENS, TOPK))
    attn_gain = jnp.clip(1.0 + 0.15 * jax.random.normal(streams_of[3], (D,), jnp.float32), 0.25, 1.75).astype(jnp.bfloat16)
    query_gain = jnp.clip(1.0 + 0.15 * jax.random.normal(streams_of[4], (D,), jnp.float32), 0.25, 1.75).astype(jnp.bfloat16)
    key_gain = jnp.clip(1.0 + 0.15 * jax.random.normal(streams_of[5], (D,), jnp.float32), 0.25, 1.75).astype(jnp.bfloat16)
    ffn_gain = jnp.clip(1.0 + 0.15 * jax.random.normal(streams_of[6], (D,), jnp.float32), 0.25, 1.75).astype(jnp.bfloat16)
    qkv_weight = normal_values(streams_of[7], (D, 3 * D), D ** -0.5, 0.125, ((0, 32),))
    out_weight = normal_values(streams_of[8], (D, D), (D // 64) ** -0.5, 1.0, ((0, 32),))
    router_weight = normal_values(streams_of[9], (D, EXPERTS), (4 * D) ** -0.5, 0.0625, ((0, 32),))
    expert_in = normal_values(streams_of[10], (D, EXPERTS, 2 * FF), D ** -0.5, 0.125, ((0, 32),))
    expert_out = normal_values(streams_of[11], (FF, EXPERTS, D), (FF // 64) ** -0.5, 1.5, ((0, 32),))
    cotangent = noise_with(streams_of[12], (TOKENS, D), 1.0, 6.0, ((0, 32),), (0, 1, 32, 2.75))
    return {"hidden_in": hidden_in, "lengths": lengths, "routes": routes, "attn_gain": attn_gain, "query_gain": query_gain, "key_gain": key_gain, "ffn_gain": ffn_gain, "qkv_weight": qkv_weight, "out_weight": out_weight, "router_weight": router_weight, "expert_in": expert_in, "expert_out": expert_out, "cotangent": cotangent}


EPS = 1e-05
HIGH = lax.Precision.HIGHEST

@jax.custom_vjp
def low(v):
    return lax.optimization_barrier(v.astype(jnp.bfloat16)).astype(jnp.float32)

@jax.custom_vjp
def low_back(v):
    return v

def low_keep(v):
    return (low(v), None)

def low_pass(kept, grad):
    return (grad,)

def back_keep(v):
    return (v, None)

def back_low(kept, grad):
    return (low(grad),)
low.defvjp(low_keep, low_pass)
low_back.defvjp(back_keep, back_low)

def rms_scale(values_in):
    return lax.rsqrt(lax.optimization_barrier(jnp.mean(values_in * values_in, axis=-1, keepdims=True)) + EPS)

def rotate(values_in, cosine, sine):
    half_width = values_in.shape[-1] // 2
    first_half = values_in[..., :half_width]
    second_half = values_in[..., half_width:]
    return jnp.concatenate([first_half * cosine - second_half * sine, second_half * cosine + first_half * sine], axis=-1)

def attend(query, keys, values, lengths):
    block_size = min(512, SEQ)
    block_count = SEQ // block_size
    key_pos = jnp.arange(SEQ, dtype=jnp.int32)
    key_live = key_pos[None, :] < lengths[:, None]
    scaling = HEAD_DIM ** (-0.5)

    def one_block(block_index):
        start = block_index * block_size
        query_rows = lax.dynamic_slice_in_dim(query, start, block_size, 1)
        scores = jnp.einsum('sqhd,skhd->shqk', query_rows, keys, precision=HIGH) * scaling
        scores = low_back(scores)
        query_pos = start + jnp.arange(block_size, dtype=jnp.int32)
        allowed = (key_pos[None, :] <= query_pos[:, None])[None, None] & key_live[:, None, None, :]
        masked = jnp.where(allowed, scores, -1e+30)
        row_max = lax.optimization_barrier(jnp.max(masked, axis=-1, keepdims=True))
        weights = jnp.where(allowed, jnp.exp(masked - row_max), 0.0)
        probs = weights / lax.optimization_barrier(jnp.sum(weights, axis=-1, keepdims=True))
        return jnp.einsum('shqk,skhd->sqhd', low(probs), values, precision=HIGH)
    blocks = lax.map(jax.checkpoint(one_block), jnp.arange(block_count, dtype=jnp.int32))
    return jnp.moveaxis(blocks, 0, 1).reshape(SEQS, SEQ, HEADS, HEAD_DIM)

def forward(hidden, gain_attn, gain_query, gain_key, gain_ffn, weight_qkv, weight_out, weight_router, weight_in, weight_expert, lengths, routes):
    normed = low(hidden * rms_scale(hidden) * gain_attn)
    qkv_mixed = low_back(jnp.dot(normed, weight_qkv, precision=HIGH))
    query_raw = qkv_mixed[:, :D]
    key_raw = qkv_mixed[:, D:2 * D]
    value_raw = qkv_mixed[:, 2 * D:]
    query_norm = query_raw * rms_scale(query_raw) * gain_query
    key_norm = key_raw * rms_scale(key_raw) * gain_key
    positions = jnp.arange(SEQ, dtype=jnp.float32)
    frequency = jnp.power(10000.0, -jnp.arange(HEAD_DIM // 2, dtype=jnp.float32) * 2.0 / HEAD_DIM)
    angles = positions[:, None] * frequency[None, :]
    cosine = jnp.cos(angles)[None, :, None, :]
    sine = jnp.sin(angles)[None, :, None, :]
    shape4 = (SEQS, SEQ, HEADS, HEAD_DIM)
    query = low(rotate(query_norm.reshape(shape4), cosine, sine))
    keys = low(rotate(key_norm.reshape(shape4), cosine, sine))
    values = low(value_raw.reshape(shape4))
    attended = attend(query, keys, values, lengths).reshape(TOKENS, D)
    attended = low(low_back(attended))
    branch = jnp.dot(attended, weight_out, precision=HIGH)
    middle = hidden + branch
    normed2 = low(middle * rms_scale(middle) * gain_ffn)
    logits = low_back(jnp.dot(normed2, weight_router, precision=HIGH))
    router_probs = jax.nn.softmax(logits, axis=-1)
    chosen = lax.optimization_barrier(jnp.sum((routes[:, :, None] == jnp.arange(EXPERTS, dtype=jnp.int32)[None, None, :]).astype(jnp.float32), axis=1))
    mixing = router_probs * chosen

    def expert_step(running, pieces):
        inner_weight, outer_weight, expert_mix = pieces
        gate_up = low_back(jnp.dot(normed2, inner_weight, precision=HIGH))
        activation = low(jax.nn.silu(gate_up[:, :FF]) * gate_up[:, FF:])
        result = low_back(jnp.dot(activation, outer_weight, precision=HIGH))
        return (running + expert_mix[:, None] * result, None)
    expert_sum, unused = lax.scan(jax.checkpoint(expert_step), jnp.zeros((TOKENS, D), jnp.float32), (jnp.moveaxis(weight_in, 1, 0), jnp.moveaxis(weight_expert, 1, 0), mixing.T))
    return (middle + expert_sum, branch, expert_sum)

def reference(hidden_in, lengths, routes, attn_gain, query_gain, key_gain, ffn_gain, qkv_weight, out_weight, router_weight, expert_in, expert_out, cotangent):
    floats = tuple((argument.astype(jnp.float32) for argument in (hidden_in, attn_gain, query_gain, key_gain, ffn_gain, qkv_weight, out_weight, router_weight, expert_in, expert_out)))
    live_mask = (jnp.arange(SEQ, dtype=jnp.int32)[None, :] < lengths[:, None]).astype(jnp.float32).reshape(TOKENS)

    def run(hidden, gain_attn, gain_query, gain_key, gain_ffn, weight_qkv, weight_out, weight_router, weight_in, weight_expert):
        return forward(hidden, gain_attn, gain_query, gain_key, gain_ffn, weight_qkv, weight_out, weight_router, weight_in, weight_expert, lengths, routes)
    outputs, pullback = jax.vjp(run, *floats)
    block_total, branch, expert_sum = outputs
    grad_total = cotangent.astype(jnp.float32) * live_mask[:, None]
    grads = pullback((grad_total, jnp.zeros_like(branch), jnp.zeros_like(expert_sum)))
    valid_cells = jnp.sum(lengths).astype(jnp.float32) * D

    def root_mean(values_in):
        return jnp.sqrt(jnp.sum(live_mask[:, None] * values_in * values_in) / valid_cells)
    stats = jnp.stack([root_mean(block_total), root_mean(branch), root_mean(expert_sum)])
    return (block_total.astype(jnp.bfloat16), grads[0], grads[1], grads[2], grads[3], grads[4], grads[5], grads[6], grads[7], grads[8], grads[9], stats)
```

```python
import functools

import jax
import jax.numpy as jnp
from jax import lax
from jax.experimental import pallas as pl
from jax.experimental.pallas import tpu as pltpu
from jax.sharding import PartitionSpec as P

HEADS = 16
HEAD_DIM = 128
EPS = 1e-05
BOTH = ("dp", "fsdp")
MESH_ID = pl.DeviceIdType.MESH
F32 = jnp.float32
BF16 = jnp.bfloat16


def rms_scale(values_in):
    return lax.rsqrt(jnp.mean(values_in * values_in, axis=-1, keepdims=True) + EPS)


def norm_back(grad_in, unit_rows, scaling):
    return scaling * (grad_in - unit_rows * jnp.mean(grad_in * unit_rows, axis=-1, keepdims=True))


def rotate(values_in, cosine, sine, direction):
    half_width = values_in.shape[-1] // 2
    first_half = values_in[..., :half_width]
    second_half = values_in[..., half_width:]
    return jnp.concatenate(
        [
            first_half * cosine - direction * second_half * sine,
            second_half * cosine + direction * first_half * sine,
        ],
        axis=-1,
    )


def place(axes, fsdp, index):
    if axes == BOTH:
        return {"dp": index // fsdp, "fsdp": lax.rem(index, fsdp)}
    return {axes[0]: index}


def exchange_kernel(axes, n, fsdp, spread, x, o, send, recv, own):
    if axes == BOTH:
        me = lax.axis_index("dp") * fsdp + lax.axis_index("fsdp")
    else:
        me = lax.axis_index(axes[0])
    barrier = pltpu.get_barrier_semaphore()
    for k in range(1, n):
        peer = place(axes, fsdp, lax.rem(me + k, n))
        pl.semaphore_signal(barrier, inc=1, device_id=peer, device_id_type=MESH_ID)
    pl.semaphore_wait(barrier, n - 1)
    local = pltpu.make_async_copy(x.at[me] if spread else x, o.at[me], own)
    local.start()
    copies = []
    for k in range(1, n):
        target = lax.rem(me + k, n)
        copy = pltpu.make_async_remote_copy(
            x.at[target] if spread else x,
            o.at[me],
            send.at[k],
            recv.at[k],
            device_id=place(axes, fsdp, target),
            device_id_type=MESH_ID,
        )
        copy.start()
        copies.append(copy)
    local.wait()
    for copy in copies:
        copy.wait()


def exchange(x, axes, ident, spread):
    fsdp = lax.axis_size("fsdp")
    n = lax.axis_size(axes)
    shape = x.shape if spread else (n,) + x.shape
    return pl.pallas_call(
        functools.partial(exchange_kernel, axes, n, fsdp, spread),
        out_shape=jax.ShapeDtypeStruct(shape, x.dtype),
        in_specs=[pl.BlockSpec(memory_space=pl.ANY)],
        out_specs=pl.BlockSpec(memory_space=pl.ANY),
        scratch_shapes=[
            pltpu.SemaphoreType.DMA((n,)),
            pltpu.SemaphoreType.DMA((n,)),
            pltpu.SemaphoreType.DMA,
        ],
        compiler_params=pltpu.CompilerParams(collective_id=ident, has_side_effects=True),
    )(x)


def tiles_of(x, rows):
    flat = x.reshape(-1)
    return jnp.pad(flat, (0, rows * 128 - flat.shape[0])).reshape(rows, 128)


def plane_sum(x, ident):
    rows = -(-x.size // 1024) * 8
    got = exchange(tiles_of(x, rows), ("fsdp",), ident, False)
    return jnp.sum(got, axis=0).reshape(-1)[: x.size].reshape(x.shape)


def dot(a, b, dims):
    return lax.dot_general(a, b, (dims, ((), ())), preferred_element_type=F32)


def body(
    hidden_in,
    lengths,
    routes,
    attn_gain,
    query_gain,
    key_gain,
    ffn_gain,
    qkv_weight,
    out_weight,
    router_weight,
    expert_in,
    expert_out,
    cotangent,
):
    rows, width = hidden_in.shape
    dp = lax.axis_size("dp")
    fsdp = lax.axis_size("fsdp")
    n = dp * fsdp
    experts = router_weight.shape[1]
    seq = rows * fsdp
    tokens = rows * n
    own_rows = width // n
    heads_here = HEADS // fsdp
    cols = heads_here * HEAD_DIM
    experts_here = experts // fsdp
    ff = expert_out.shape[0] * n
    ff_here = ff // dp
    inner = experts_here * ff_here
    z = lax.axis_index("dp")
    f = lax.axis_index("fsdp")
    valid = lengths[z]
    scaling = HEAD_DIM ** (-0.5)

    small = jnp.concatenate(
        [attn_gain, query_gain, key_gain, ffn_gain, router_weight.reshape(-1)]
    )
    small_rows = -(-small.size // 2048) * 16
    small = exchange(tiles_of(small, small_rows), BOTH, 0, False).reshape(n, -1)
    gains = small[:, : 4 * own_rows].reshape(n, 4, own_rows).transpose(1, 0, 2)
    gains = gains.reshape(4, width).astype(F32)
    router_full = small[:, 4 * own_rows : 4 * own_rows + own_rows * experts]
    router_full = router_full.reshape(width, experts)
    gain_attn, gain_query, gain_key, gain_ffn = gains[0], gains[1], gains[2], gains[3]

    attn_weight = jnp.concatenate(
        [
            qkv_weight.reshape(own_rows, 3, fsdp, cols),
            out_weight.reshape(own_rows, 1, fsdp, cols),
        ],
        axis=1,
    )
    attn_weight = attn_weight.transpose(2, 0, 1, 3).reshape(fsdp, own_rows, 4 * cols)
    attn_weight = lax.all_to_all(attn_weight, "fsdp", 0, 0, tiled=True)
    attn_weight = lax.all_gather(
        attn_weight.reshape(fsdp * own_rows, 4 * cols), "dp", axis=0, tiled=True
    )
    qkv_here = attn_weight[:, : 3 * cols]
    out_here = attn_weight[:, 3 * cols :]

    inner_weight = expert_in.reshape(own_rows, fsdp, experts_here, 2, dp, ff_here)
    inner_weight = inner_weight.transpose(4, 1, 0, 3, 2, 5).reshape(n, own_rows, 2 * inner)
    inner_weight = lax.all_to_all(inner_weight, BOTH, 0, 0, tiled=True).reshape(width, 2 * inner)
    outer_weight = expert_out.reshape(-1, fsdp, experts_here, width).transpose(1, 2, 0, 3)
    outer_weight = lax.all_to_all(outer_weight, "fsdp", 0, 0, tiled=True)
    outer_weight = outer_weight.transpose(1, 0, 2, 3).reshape(inner, width)

    hidden_all = lax.all_gather(hidden_in, "fsdp", axis=0, tiled=True).astype(F32)
    normed_all = (hidden_all * rms_scale(hidden_all) * gain_attn).astype(BF16)
    mixed = dot(normed_all, qkv_here, ((1,), (0,)))
    raw = mixed[:, : 2 * cols].reshape(seq, 2, cols)
    squares = plane_sum(jnp.sum(raw * raw, axis=-1), 1)
    qk_scale = lax.rsqrt(squares / width + EPS)[:, :, None]
    qk_unit = raw * qk_scale
    here = f * cols
    qk_gain = jnp.stack(
        [
            lax.dynamic_slice(gain_query, (here,), (cols,)),
            lax.dynamic_slice(gain_key, (here,), (cols,)),
        ]
    )
    pos = jnp.arange(seq, dtype=jnp.int32)
    frequency = jnp.power(10000.0, -jnp.arange(HEAD_DIM // 2, dtype=F32) * 2.0 / HEAD_DIM)
    angles = pos.astype(F32)[:, None] * frequency[None, :]
    cosine = jnp.cos(angles)[:, None, None, :]
    sine = jnp.sin(angles)[:, None, None, :]
    shape4 = (seq, 2, heads_here, HEAD_DIM)
    turned = rotate((qk_unit * qk_gain).reshape(shape4), cosine, sine, 1.0).astype(BF16)
    query = turned[:, 0]
    key = turned[:, 1]
    value = mixed[:, 2 * cols :].astype(BF16).reshape(seq, heads_here, HEAD_DIM)
    allowed = ((pos[None, :] <= pos[:, None]) & (pos[None, :] < valid))[None]
    scores = jnp.einsum("qhd,khd->hqk", query, key, preferred_element_type=F32) * scaling
    masked = jnp.where(allowed, scores, -1e30)
    weights = jnp.where(allowed, jnp.exp(masked - jnp.max(masked, axis=-1, keepdims=True)), 0.0)
    probs = weights / jnp.sum(weights, axis=-1, keepdims=True)
    probs_low = probs.astype(BF16)
    attended = jnp.einsum("hqk,khd->qhd", probs_low, value, preferred_element_type=F32)
    attended = attended.reshape(seq, cols).astype(BF16)
    attended_all = lax.all_gather(attended, "fsdp", axis=0, tiled=False)
    branch = jnp.einsum(
        "fsc,fcn->sn", attended_all, out_here.reshape(fsdp, cols, cols), preferred_element_type=F32
    )
    branch = exchange(branch.astype(BF16).reshape(fsdp, rows, cols), ("fsdp",), 2, True)
    branch = branch.transpose(1, 0, 2).reshape(rows, width).astype(F32)

    hidden = hidden_in.astype(F32)
    scale1 = rms_scale(hidden)
    unit1 = hidden * scale1
    middle = hidden + branch
    scale2 = rms_scale(middle)
    unit2 = middle * scale2
    normed2 = (unit2 * gain_ffn).astype(BF16)
    logits = dot(normed2, router_full, ((1,), (0,)))
    router_probs = jax.nn.softmax(logits, axis=-1)
    chosen = jnp.sum(
        (routes[:, :, None] == jnp.arange(experts, dtype=jnp.int32)[None, None, :]).astype(F32),
        axis=1,
    )
    live_mask = (f * rows + jnp.arange(rows, dtype=jnp.int32) < valid).astype(F32)[:, None]
    grad_total = cotangent.astype(F32) * live_mask

    grad_all = lax.all_gather(grad_total.astype(BF16), BOTH, axis=0, tiled=True)
    rows_all = lax.all_gather(normed2, BOTH, axis=0, tiled=True)
    gates = (router_probs * chosen).reshape(rows, fsdp, experts_here).transpose(1, 2, 0)
    gates = jnp.broadcast_to(gates[None], (dp, fsdp, experts_here, rows))
    gates = gates.reshape(n, experts_here, rows)
    gates = jnp.pad(gates, ((0, 0), (0, 8 - experts_here), (0, 0)))
    gates = exchange(gates, BOTH, 3, True)[:, :experts_here]
    gates = gates.transpose(0, 2, 1).reshape(tokens, experts_here, 1)
    gate_up = dot(rows_all, inner_weight, ((1,), (0,)))
    gate = gate_up[:, :inner]
    up = gate_up[:, inner:]
    sigmoid = jax.nn.sigmoid(gate)
    silu = gate * sigmoid
    activation = (silu * up).astype(BF16).astype(F32)
    grad_act = dot(grad_all, outer_weight, ((1,), (1,)))
    grad_gates = jnp.sum(
        (activation * grad_act).reshape(tokens, experts_here, ff_here), axis=-1
    )
    by_part = (tokens, experts_here, ff_here)
    activation = (activation.reshape(by_part) * gates).reshape(tokens, inner).astype(BF16)
    grad_act = (grad_act.reshape(by_part) * gates).reshape(tokens, inner)
    grad_gate_up = jnp.concatenate(
        [grad_act * up * sigmoid * (1.0 + gate * (1.0 - sigmoid)), grad_act * silu], axis=1
    ).astype(BF16)
    expert_sum = dot(activation, outer_weight, ((1,), (0,))).astype(BF16)
    expert_sum = lax.psum_scatter(expert_sum, BOTH, scatter_dimension=0, tiled=True).astype(F32)
    if tokens > 8192:
        grad_gate_up, expert_sum = lax.optimization_barrier((grad_gate_up, expert_sum))
    grad_rows = dot(grad_gate_up, inner_weight, ((1,), (1,))).astype(BF16)
    grad_rows = lax.psum_scatter(grad_rows, BOTH, scatter_dimension=0, tiled=True).astype(F32)
    inner_grad = dot(rows_all, grad_gate_up, ((0,), (0,))).astype(BF16)
    outer_grad = dot(activation, grad_all, ((0,), (0,))).astype(BF16)
    grad_gates = grad_gates.reshape(n, rows, experts_here).transpose(0, 2, 1)
    grad_gates = jnp.pad(grad_gates, ((0, 0), (0, 8 - experts_here), (0, 0)))
    grad_gates = exchange(grad_gates, BOTH, 4, True)[:, :experts_here]
    grad_gates = jnp.sum(grad_gates.reshape(dp, fsdp, experts_here, rows), axis=0)
    grad_router_probs = grad_gates.reshape(experts, rows).transpose(1, 0) * chosen

    inner_grad = lax.all_to_all(inner_grad.reshape(n, own_rows, 2 * inner), BOTH, 0, 0, tiled=True)
    inner_grad = inner_grad.reshape(dp, fsdp, own_rows, 2, experts_here, ff_here)
    inner_grad = inner_grad.transpose(2, 1, 4, 3, 0, 5).reshape(own_rows, experts, 2 * ff)
    outer_grad = outer_grad.reshape(experts_here, fsdp, -1, width).transpose(1, 0, 2, 3)
    outer_grad = lax.all_to_all(outer_grad, "fsdp", 0, 0, tiled=True)
    outer_grad = outer_grad.transpose(2, 0, 1, 3).reshape(-1, experts, width)

    block_total = middle + expert_sum
    squares = jnp.stack(
        [
            jnp.sum(live_mask * block_total * block_total),
            jnp.sum(live_mask * branch * branch),
            jnp.sum(live_mask * expert_sum * expert_sum),
        ]
    )

    grad_logits = router_probs * (
        grad_router_probs - jnp.sum(router_probs * grad_router_probs, axis=-1, keepdims=True)
    )
    grad_logits = grad_logits.astype(BF16)
    router_term = dot(normed2, grad_logits, ((0,), (0,)))
    grad_normed2 = grad_rows + dot(grad_logits, router_full, ((1,), (1,)))
    ffn_term = jnp.sum(grad_normed2 * unit2, axis=0)
    grad_middle = grad_total + norm_back(grad_normed2 * gain_ffn, unit2, scale2)

    grad_cols = grad_middle.astype(BF16).reshape(rows, fsdp, cols).transpose(1, 0, 2)
    grad_cols = exchange(grad_cols, ("fsdp",), 5, True).reshape(seq, cols)
    out_grad = jnp.einsum("fsc,sn->fcn", attended_all, grad_cols, preferred_element_type=F32)
    grad_attended = jnp.einsum(
        "sn,fcn->fsc", grad_cols, out_here.reshape(fsdp, cols, cols), preferred_element_type=F32
    )
    grad_attended = lax.psum_scatter(
        grad_attended.astype(BF16).reshape(fsdp * seq, cols), "fsdp", scatter_dimension=0, tiled=True
    )
    grad_attended = grad_attended.reshape(seq, heads_here, HEAD_DIM)
    grad_probs = jnp.einsum("qhd,khd->hqk", grad_attended, value, preferred_element_type=F32)
    grad_scores = probs * (grad_probs - jnp.sum(probs * grad_probs, axis=-1, keepdims=True))
    grad_scores = grad_scores.astype(BF16)
    grad_query = jnp.einsum("hqk,khd->qhd", grad_scores, key, preferred_element_type=F32)
    grad_key = jnp.einsum("hqk,qhd->khd", grad_scores, query, preferred_element_type=F32)
    grad_value = jnp.einsum("hqk,qhd->khd", probs_low, grad_attended, preferred_element_type=F32)
    grad_qk = rotate(jnp.stack([grad_query, grad_key], axis=1) * scaling, cosine, sine, -1.0)
    grad_qk = grad_qk.reshape(seq, 2, cols)
    qk_term = jnp.sum(grad_qk * qk_unit, axis=0)
    grad_qk = grad_qk * qk_gain
    inner_means = plane_sum(jnp.sum(grad_qk * qk_unit, axis=-1), 6)[:, :, None] / width
    grad_qk = qk_scale * (grad_qk - qk_unit * inner_means)
    grad_qkv = jnp.concatenate(
        [grad_qk.reshape(seq, 2 * cols), grad_value.reshape(seq, cols)], axis=1
    ).astype(BF16)
    qkv_grad = dot(normed_all, grad_qkv, ((0,), (0,)))
    grad_normed = dot(grad_qkv, qkv_here, ((1,), (1,))).astype(BF16)
    grad_normed = lax.psum_scatter(grad_normed, "fsdp", scatter_dimension=0, tiled=True).astype(F32)
    attn_term = jnp.sum(grad_normed * unit1, axis=0)
    hidden_grad = grad_middle + norm_back(grad_normed * gain_attn, unit1, scale1)

    attn_grad = jnp.concatenate([qkv_grad, out_grad.reshape(width, cols)], axis=1).astype(BF16)
    attn_grad = lax.psum_scatter(attn_grad, "dp", scatter_dimension=0, tiled=True)
    attn_grad = attn_grad.reshape(fsdp, own_rows, 4 * cols)
    attn_grad = lax.all_to_all(attn_grad, "fsdp", 0, 0, tiled=True)
    attn_grad = attn_grad.reshape(fsdp, own_rows, 4, cols).transpose(1, 2, 0, 3).astype(F32)
    attn_grad = attn_grad.reshape(own_rows, 4 * width)

    qk_full = jnp.zeros((2, width), F32)
    qk_full = lax.dynamic_update_slice(qk_full, qk_term, (0, here))
    terms = jnp.concatenate([attn_term[None], qk_full, ffn_term[None]])
    terms = terms.reshape(4, n, own_rows).transpose(1, 0, 2).reshape(n, 4 * own_rows)
    terms = jnp.concatenate(
        [
            terms,
            router_term.reshape(n, own_rows * experts),
            jnp.broadcast_to(squares[None], (n, 3)),
        ],
        axis=1,
    )
    term_size = terms.shape[1]
    term_rows = -(-term_size // 1024) * 8
    terms = jnp.pad(terms, ((0, 0), (0, term_rows * 128 - term_size)))
    terms = exchange(terms.reshape(n, term_rows, 128), BOTH, 7, True)
    terms = jnp.sum(terms, axis=0).reshape(-1)
    gain_grads = terms[: 4 * own_rows].reshape(4, own_rows)
    router_grad = terms[4 * own_rows : 4 * own_rows + own_rows * experts]
    valid_cells = jnp.sum(lengths).astype(F32) * width
    stats = jnp.sqrt(terms[term_size - 3 : term_size] / valid_cells)

    return (
        block_total.astype(BF16),
        hidden_grad,
        gain_grads[0],
        gain_grads[1],
        gain_grads[2],
        gain_grads[3],
        attn_grad[:, : 3 * width],
        attn_grad[:, 3 * width :],
        router_grad.reshape(own_rows, experts),
        inner_grad.astype(F32),
        outer_grad.astype(F32),
        stats,
    )


def solution(mesh):
    one = P(BOTH)
    two = P(BOTH, None)
    three = P(BOTH, None, None)
    in_specs = (two, P(), two, one, one, one, one, two, two, two, three, three, two)
    out_specs = (two, two, one, one, one, one, two, two, two, three, three, P())
    return jax.shard_map(body, mesh=mesh, in_specs=in_specs, out_specs=out_specs, check_vma=False)
```

```python
import functools

import jax
import jax.numpy as jnp
from jax import lax
from jax.experimental import pallas as pl
from jax.experimental.pallas import tpu as pltpu
from jax.sharding import PartitionSpec as P

HEADS = 16
HEAD_DIM = 128
EPS = 1e-05
BOTH = ("dp", "fsdp")
MESH_ID = pl.DeviceIdType.MESH
F32 = jnp.float32
BF16 = jnp.bfloat16


def rms_scale(values_in):
    return lax.rsqrt(jnp.mean(values_in * values_in, axis=-1, keepdims=True) + EPS)


def norm_back(grad_in, unit_rows, scaling):
    return scaling * (grad_in - unit_rows * jnp.mean(grad_in * unit_rows, axis=-1, keepdims=True))


def rotate(values_in, cosine, sine, direction):
    half_width = values_in.shape[-1] // 2
    first_half = values_in[..., :half_width]
    second_half = values_in[..., half_width:]
    return jnp.concatenate(
        [
            first_half * cosine - direction * second_half * sine,
            second_half * cosine + direction * first_half * sine,
        ],
        axis=-1,
    )


def place(axes, fsdp, index):
    if axes == BOTH:
        return {"dp": index // fsdp, "fsdp": lax.rem(index, fsdp)}
    return {axes[0]: index}


def exchange_kernel(axes, n, fsdp, spread, x, o, send, recv, own):
    if axes == BOTH:
        me = lax.axis_index("dp") * fsdp + lax.axis_index("fsdp")
    else:
        me = lax.axis_index(axes[0])
    barrier = pltpu.get_barrier_semaphore()
    for k in range(1, n):
        peer = place(axes, fsdp, lax.rem(me + k, n))
        pl.semaphore_signal(barrier, inc=1, device_id=peer, device_id_type=MESH_ID)
    pl.semaphore_wait(barrier, n - 1)
    local = pltpu.make_async_copy(x.at[me] if spread else x, o.at[me], own)
    local.start()
    copies = []
    for k in range(1, n):
        target = lax.rem(me + k, n)
        copy = pltpu.make_async_remote_copy(
            x.at[target] if spread else x,
            o.at[me],
            send.at[k],
            recv.at[k],
            device_id=place(axes, fsdp, target),
            device_id_type=MESH_ID,
        )
        copy.start()
        copies.append(copy)
    local.wait()
    for copy in copies:
        copy.wait()


def exchange(x, axes, ident, spread):
    fsdp = lax.axis_size("fsdp")
    n = lax.axis_size(axes)
    shape = x.shape if spread else (n,) + x.shape
    return pl.pallas_call(
        functools.partial(exchange_kernel, axes, n, fsdp, spread),
        out_shape=jax.ShapeDtypeStruct(shape, x.dtype),
        in_specs=[pl.BlockSpec(memory_space=pl.ANY)],
        out_specs=pl.BlockSpec(memory_space=pl.ANY),
        scratch_shapes=[
            pltpu.SemaphoreType.DMA((n,)),
            pltpu.SemaphoreType.DMA((n,)),
            pltpu.SemaphoreType.DMA,
        ],
        compiler_params=pltpu.CompilerParams(collective_id=ident, has_side_effects=True),
    )(x)


def tiles_of(x, rows):
    flat = x.reshape(-1)
    return jnp.pad(flat, (0, rows * 128 - flat.shape[0])).reshape(rows, 128)


def plane_sum(x, ident):
    rows = -(-x.size // 1024) * 8
    got = exchange(tiles_of(x, rows), ("fsdp",), ident, False)
    return jnp.sum(got, axis=0).reshape(-1)[: x.size].reshape(x.shape)


def dot(a, b, dims):
    return lax.dot_general(a, b, (dims, ((), ())), preferred_element_type=F32)


def expert_kernel(
    dp,
    x_in,
    c_all,
    gates,
    inner_in,
    outer_in,
    sums,
    gate_out,
    inner_out,
    outer_out,
    gathered,
    far,
    xv,
    cv,
    wi,
    wo,
    gi,
    go,
    ggu,
    act,
    gv,
    part,
    held,
    core_in,
    half_in,
    full_in,
    local,
    z_send,
    z_recv,
    a_send,
    a_recv,
    b_send,
    b_recv,
    k_send,
    k_recv,
    c_send,
    c_recv,
    s1_send,
    s1_recv,
    s2_send,
    s2_recv,
    o_send,
    o_recv,
    credit,
):
    rows, width = x_in.shape
    half = rows // 2
    z = lax.axis_index("dp")
    f = lax.axis_index("fsdp")
    core = lax.rem(f, 2)
    chip = f // 2
    xbit = lax.rem(chip, 2)
    ybit = chip // 2
    chip_x = ybit * 2 + (1 - xbit)
    chip_y = (1 - ybit) * 2 + xbit
    chip_d = (1 - ybit) * 2 + (1 - xbit)
    fx = chip_x * 2 + core
    fy = chip_y * 2 + core
    fd = chip_d * 2 + core
    fc = chip * 2 + (1 - core)
    to_x = {"fsdp": fx}
    to_y = {"fsdp": fy}
    to_c = {"fsdp": fc}
    upper = pl.ds(0, half)
    lower = pl.ds(half, half)

    def remote(src, dst, send, recv, device):
        return pltpu.make_async_remote_copy(
            src, dst, send, recv, device_id=device, device_id_type=MESH_ID
        )

    def plane_at(s):
        return lax.rem(z + 1 + s, dp)

    def far_copy(i):
        return remote(
            x_in,
            gathered.at[z, f],
            z_send.at[i],
            z_recv.at[i],
            {"dp": lax.rem(z + dp - i, dp)},
        )

    def gather_one(s):
        block = gathered.at[plane_at(s), f]
        return (
            remote(block.at[upper], block.at[upper], a_send.at[s, 0], a_recv.at[s, 0], to_x),
            remote(block.at[lower], block.at[lower], a_send.at[s, 1], a_recv.at[s, 1], to_y),
        )

    def gather_two(s):
        p = plane_at(s)
        copies = []
        for i, (owner, piece, device) in enumerate(
            ((f, upper, to_y), (fx, upper, to_y), (f, lower, to_x), (fy, lower, to_x))
        ):
            ref = gathered.at[p, owner, piece]
            copies.append(remote(ref, ref, b_send.at[s, i], b_recv.at[s, i], device))
        return copies

    def gather_core(s):
        p = plane_at(s)
        copies = []
        for i, owner in enumerate((f, fx, fy, fd)):
            ref = gathered.at[p, owner]
            copies.append(remote(ref, ref, k_send.at[s, i], k_recv.at[s, i], to_c))
        return copies

    def block_rows(owner):
        return pl.ds(pl.multiple_of(owner * rows, rows), rows)

    def core_copy(k, j):
        return remote(
            part.at[k, block_rows(j * 2 + 1 - core)],
            core_in.at[k, j],
            c_send.at[k, j],
            c_recv.at[k, j],
            to_c,
        )

    def half_copies(k):
        return (
            remote(
                held.at[k, chip_d, upper], half_in.at[k, 0], s1_send.at[k, 0], s1_recv.at[k, 0], to_x
            ),
            remote(
                held.at[k, chip_d, lower], half_in.at[k, 1], s1_send.at[k, 1], s1_recv.at[k, 1], to_y
            ),
        )

    def full_copies(k):
        return (
            remote(held.at[k, chip_x], full_in.at[k, 0], s2_send.at[k, 0], s2_recv.at[k, 0], to_x),
            remote(held.at[k, chip_y], full_in.at[k, 1], s2_send.at[k, 1], s2_recv.at[k, 1], to_y),
        )

    def out_copy(s, k):
        return remote(
            held.at[k, chip], far.at[k, z], o_send.at[s, k], o_recv.at[s, k], {"dp": plane_at(s)}
        )

    def add_core():
        for k in range(2):
            for j in range(4):
                core_copy(k, j).wait()
            def one(j, carry):
                held[k, j] = (
                    part[k, block_rows(j * 2 + core)].astype(F32) + core_in[k, j].astype(F32)
                ).astype(BF16)
                return carry
            lax.fori_loop(0, 4, one, 0)
        pl.semaphore_signal(credit, inc=1, device_id=to_c, device_id_type=MESH_ID)

    def start_half():
        for k in range(2):
            for copy in half_copies(k):
                copy.start()

    def pass_full():
        for k in range(2):
            for copy in half_copies(k):
                copy.wait()
            held[k, chip_y, upper] = (
                held[k, chip_y, upper].astype(F32) + half_in[k, 0].astype(F32)
            ).astype(BF16)
            held[k, chip_x, lower] = (
                held[k, chip_x, lower].astype(F32) + half_in[k, 1].astype(F32)
            ).astype(BF16)
            for copy in full_copies(k):
                copy.start()

    def total_here(k):
        for copy in full_copies(k):
            copy.wait()
        return held[k, chip].astype(F32) + full_in[k, 0].astype(F32) + full_in[k, 1].astype(F32)

    barrier = pltpu.get_barrier_semaphore()
    for device in (to_x, to_y, to_c):
        pl.semaphore_signal(barrier, inc=1, device_id=device, device_id_type=MESH_ID)
    for i in range(1, dp):
        pl.semaphore_signal(
            barrier, inc=1, device_id={"dp": lax.rem(z + i, dp)}, device_id_type=MESH_ID
        )
    pl.semaphore_wait(barrier, 3 + dp - 1)

    for i in range(1, dp):
        far_copy(i).start()
    loads = [pltpu.make_async_copy(x_in, gathered.at[z, f], local.at[0])]
    for q in range(4):
        loads.append(pltpu.make_async_copy(inner_in.at[:, q], wi.at[q], local.at[1 + q]))
    for e in range(2):
        loads.append(pltpu.make_async_copy(outer_in.at[:, e], wo.at[e], local.at[5 + e]))
    for load in loads:
        load.start()
    gi[...] = jnp.zeros_like(gi)
    go[...] = jnp.zeros_like(go)
    for load in loads:
        load.wait()

    def begin_gather(s):
        @pl.when(s < dp - 1)
        def _():
            far_copy(s + 1).wait_recv()

        for copy in gather_one(s):
            copy.start()

    def middle_gather(s):
        for copy in gather_one(s):
            copy.wait_recv()
        for copy in gather_two(s):
            copy.start()

    def end_gather(s):
        for copy in gather_two(s):
            copy.wait_recv()
        for copy in gather_core(s):
            copy.start()

    begin_gather(0)
    middle_gather(0)
    begin_gather(1)
    end_gather(0)

    inner_rows = wi.shape[1] * wi.shape[2]
    ff_here = wo.shape[1] * wo.shape[2]
    tile = xv.shape[0] // 2

    def tile_step(t):
        r = pl.ds(pl.multiple_of(t * tile, tile), tile)
        x = xv[r, :]
        c = cv[r, :]
        for e in range(2):
            gate = dot(x, wi[e].reshape(inner_rows, ff_here), ((1,), (0,)))
            up = dot(x, wi[2 + e].reshape(inner_rows, ff_here), ((1,), (0,)))
            back = dot(c, wo[e].reshape(ff_here, width), ((1,), (1,)))
            sigmoid = 1.0 / (1.0 + jnp.exp(-gate))
            silu = gate * sigmoid
            active = (silu * up).astype(BF16).astype(F32)
            weight = gv[r, e : e + 1]
            gv[r, 8 + e : 9 + e] = jnp.sum(active * back, axis=-1, keepdims=True)
            act[e, r, :] = (weight * active).astype(BF16)
            back = weight * back
            ggu[e, r, :] = (back * up * sigmoid * (1.0 + gate * (1.0 - sigmoid))).astype(BF16)
            ggu[2 + e, r, :] = (back * silu).astype(BF16)
        step = 512
        for i in range(width // step):
            col = pl.ds(i * step, step)
            blocks = pl.ds(i * step // wi.shape[2], step // wi.shape[2])
            total = dot(act[0, r, :], wo[0, :, :, col].reshape(ff_here, step), ((1,), (0,)))
            total += dot(act[1, r, :], wo[1, :, :, col].reshape(ff_here, step), ((1,), (0,)))
            part[0, r, col] = total.astype(BF16)
            total = dot(ggu[0, r, :], wi[0, blocks].reshape(step, ff_here), ((1,), (1,)))
            for q in range(1, 4):
                total += dot(ggu[q, r, :], wi[q, blocks].reshape(step, ff_here), ((1,), (1,)))
            part[1, r, col] = total.astype(BF16)

    def weight_step():
        def inner_part(i, carry):
            col = pl.ds(pl.multiple_of(i * 256, 256), 256)
            xt = xv[:, col]
            for q in range(4):
                gi[q, col, :] += dot(xt, ggu[q], ((0,), (0,)))
            return carry

        lax.fori_loop(0, width // 256, inner_part, 0)

        def outer_part(i, carry):
            col = pl.ds(pl.multiple_of(i * 512, 512), 512)
            ct = cv[:, col]
            for e in range(2):
                go[e, :, col] += dot(act[e], ct, ((0,), (0,)))
            return carry

        lax.fori_loop(0, width // 512, outer_part, 0)

    def chunk(s, carry):
        p = plane_at(s)
        c_load = pltpu.make_async_copy(c_all.at[p], cv, local.at[1])
        g_load = pltpu.make_async_copy(gates.at[p], gv, local.at[2])
        c_load.start()
        g_load.start()
        for copy in gather_core(s):
            copy.wait_recv()
        for j in range(8):
            pltpu.make_async_copy(
                gathered.at[p, j], xv.at[pl.ds(j * rows, rows)], local.at[3 + j]
            ).start()
        c_load.wait()
        g_load.wait()
        for j in range(8):
            pltpu.make_async_copy(
                gathered.at[p, j], xv.at[pl.ds(j * rows, rows)], local.at[3 + j]
            ).wait()
        tile_step(0)

        @pl.when(s > 0)
        def _():
            pass_full()

        @pl.when(s < dp - 1)
        def _():
            middle_gather(s + 1)

        @pl.when(s < dp - 2)
        def _():
            begin_gather(s + 2)

        tile_step(1)
        g_store = pltpu.make_async_copy(gv, gate_out.at[p], local.at[2])
        g_store.start()

        @pl.when(s > 0)
        def _():
            pl.semaphore_wait(credit, 1)

        for k in range(2):
            for j in range(4):
                core_copy(k, j).start()
        weight_step()

        @pl.when(s > 0)
        def _():
            for k in range(2):
                held[k, chip] = total_here(k).astype(BF16)
                out_copy(s - 1, k).start()
            for k in range(2):
                out_copy(s - 1, k).wait_send()

        add_core()
        start_half()

        @pl.when(s < dp - 1)
        def _():
            end_gather(s + 1)

        g_store.wait()
        return carry

    lax.fori_loop(0, dp, chunk, 0)

    pass_full()
    for q in range(4):
        wi[q] = gi[q].astype(BF16).reshape(wi.shape[1:])
    for e in range(2):
        wo[e] = go[e].astype(BF16).reshape(wo.shape[1:])
    stores = []
    for q in range(4):
        stores.append(pltpu.make_async_copy(wi.at[q], inner_out.at[:, q], local.at[q]))
    for e in range(2):
        stores.append(pltpu.make_async_copy(wo.at[e], outer_out.at[:, e], local.at[4 + e]))
    for store in stores:
        store.start()
    pl.semaphore_wait(credit, 1)
    for i in range(1, dp):
        for k in range(2):
            remote(
                held.at[k, chip],
                far.at[k, lax.rem(z + dp - i, dp)],
                o_send.at[i - 1, k],
                o_recv.at[i - 1, k],
                to_x,
            ).wait_recv()
    fetch = []
    for i in range(1, dp):
        for k in range(2):
            fetch.append(
                pltpu.make_async_copy(
                    far.at[k, lax.rem(z + i, dp)], core_in.at[k, i], local.at[6 + (i - 1) * 2 + k]
                )
            )
    for copy in fetch:
        copy.start()
    for copy in fetch:
        copy.wait()
    for k in range(2):
        total = total_here(k)
        for i in range(1, dp):
            total += core_in[k, i].astype(F32)
        sums[k] = total
    for store in stores:
        store.wait()
    for i in range(1, dp):
        far_copy(i).wait_send()

    def settle(s, carry):
        for copy in (*gather_one(s), *gather_two(s), *gather_core(s)):
            copy.wait_send()
        return carry

    lax.fori_loop(0, dp, settle, 0)


def expert_pass(x_in, c_all, gates, inner_in, outer_in, ident):
    dp = lax.axis_size("dp")
    fsdp = lax.axis_size("fsdp")
    rows, width = x_in.shape
    n, four, own_rows, ff_here = inner_in.shape
    _, two, out_rows, _ = outer_in.shape
    chunk = fsdp * rows
    shape = jax.ShapeDtypeStruct
    dma = pltpu.SemaphoreType.DMA
    anywhere = pl.BlockSpec(memory_space=pl.ANY)
    got = pl.pallas_call(
        functools.partial(expert_kernel, dp),
        out_shape=(
            shape((2, rows, width), F32),
            shape((dp, chunk, 128), F32),
            shape(inner_in.shape, BF16),
            shape(outer_in.shape, BF16),
            shape((dp, fsdp, rows, width), BF16),
            shape((2, dp, rows, width), BF16),
        ),
        in_specs=[anywhere] * 5,
        out_specs=(pl.BlockSpec(memory_space=pltpu.VMEM),) + (anywhere,) * 5,
        scratch_shapes=[
            pltpu.VMEM((chunk, width), BF16),
            pltpu.VMEM((chunk, width), BF16),
            pltpu.VMEM((four, n, own_rows, ff_here), BF16),
            pltpu.VMEM((two, fsdp, out_rows, width), BF16),
            pltpu.VMEM((four, width, ff_here), F32),
            pltpu.VMEM((two, ff_here, width), F32),
            pltpu.VMEM((four, chunk, ff_here), BF16),
            pltpu.VMEM((two, chunk, ff_here), BF16),
            pltpu.VMEM((chunk, 128), F32),
            pltpu.VMEM((2, chunk, width), BF16),
            pltpu.VMEM((2, 4, rows, width), BF16),
            pltpu.VMEM((2, 4, rows, width), BF16),
            pltpu.VMEM((2, 2, rows // 2, width), BF16),
            pltpu.VMEM((2, 2, rows, width), BF16),
            dma((12 + 2 * dp,)),
            dma((dp,)),
            dma((dp,)),
            dma((dp, 2)),
            dma((dp, 2)),
            dma((dp, 4)),
            dma((dp, 4)),
            dma((dp, 4)),
            dma((dp, 4)),
            dma((2, 4)),
            dma((2, 4)),
            dma((2, 2)),
            dma((2, 2)),
            dma((2, 2)),
            dma((2, 2)),
            dma((dp, 2)),
            dma((dp, 2)),
            pltpu.SemaphoreType.REGULAR,
        ],
        compiler_params=pltpu.CompilerParams(
            collective_id=ident, has_side_effects=True, vmem_limit_bytes=63 * 1024 * 1024
        ),
    )(x_in, c_all, gates, inner_in, outer_in)
    return got[:4]


def expert_pass_dense(normed2, grad_all, gates, inner_weight, outer_weight):
    n, parts, own_rows, ff_here = inner_weight.shape
    experts_here = parts // 2
    inner = experts_here * ff_here
    width = n * own_rows
    tokens = grad_all.shape[0]
    gates = gates[:, :, None]
    rows_all = lax.all_gather(normed2, BOTH, axis=0, tiled=True)
    inner_block = inner_weight.transpose(0, 2, 1, 3).reshape(width, 2 * inner)
    outer_shape = outer_weight.shape
    outer_block = outer_weight.transpose(1, 0, 2, 3).reshape(inner, width)
    gate_up = dot(rows_all, inner_block, ((1,), (0,)))
    gate = gate_up[:, :inner]
    up = gate_up[:, inner:]
    sigmoid = jax.nn.sigmoid(gate)
    silu = gate * sigmoid
    activation = (silu * up).astype(BF16).astype(F32)
    grad_act = dot(grad_all, outer_block, ((1,), (1,)))
    grad_gates = jnp.sum(
        (activation * grad_act).reshape(tokens, experts_here, ff_here), axis=-1
    )
    by_part = (tokens, experts_here, ff_here)
    activation = (activation.reshape(by_part) * gates).reshape(tokens, inner).astype(BF16)
    grad_act = (grad_act.reshape(by_part) * gates).reshape(tokens, inner)
    grad_gate_up = jnp.concatenate(
        [grad_act * up * sigmoid * (1.0 + gate * (1.0 - sigmoid)), grad_act * silu], axis=1
    ).astype(BF16)
    expert_sum = dot(activation, outer_block, ((1,), (0,))).astype(BF16)
    expert_sum = lax.psum_scatter(expert_sum, BOTH, scatter_dimension=0, tiled=True).astype(F32)
    if tokens > 8192:
        grad_gate_up, expert_sum = lax.optimization_barrier((grad_gate_up, expert_sum))
    grad_rows = dot(grad_gate_up, inner_block, ((1,), (1,))).astype(BF16)
    grad_rows = lax.psum_scatter(grad_rows, BOTH, scatter_dimension=0, tiled=True).astype(F32)
    inner_grad = dot(rows_all, grad_gate_up, ((0,), (0,))).astype(BF16)
    outer_grad = dot(activation, grad_all, ((0,), (0,))).astype(BF16)
    inner_grad = inner_grad.reshape(n, own_rows, parts, ff_here).transpose(0, 2, 1, 3)
    outer_grad = outer_grad.reshape(experts_here, outer_shape[0], outer_shape[2], width)
    return expert_sum, grad_rows, grad_gates, inner_grad, outer_grad.transpose(1, 0, 2, 3)


def body(
    hidden_in,
    lengths,
    routes,
    attn_gain,
    query_gain,
    key_gain,
    ffn_gain,
    qkv_weight,
    out_weight,
    router_weight,
    expert_in,
    expert_out,
    cotangent,
):
    rows, width = hidden_in.shape
    dp = lax.axis_size("dp")
    fsdp = lax.axis_size("fsdp")
    n = dp * fsdp
    experts = router_weight.shape[1]
    seq = rows * fsdp
    tokens = rows * n
    own_rows = width // n
    heads_here = HEADS // fsdp
    cols = heads_here * HEAD_DIM
    experts_here = experts // fsdp
    ff = expert_out.shape[0] * n
    ff_here = ff // dp
    z = lax.axis_index("dp")
    f = lax.axis_index("fsdp")
    valid = lengths[z]
    scaling = HEAD_DIM ** (-0.5)

    small = jnp.concatenate(
        [attn_gain, query_gain, key_gain, ffn_gain, router_weight.reshape(-1)]
    )
    small_rows = -(-small.size // 2048) * 16
    small = exchange(tiles_of(small, small_rows), BOTH, 0, False).reshape(n, -1)
    gains = small[:, : 4 * own_rows].reshape(n, 4, own_rows).transpose(1, 0, 2)
    gains = gains.reshape(4, width).astype(F32)
    router_full = small[:, 4 * own_rows : 4 * own_rows + own_rows * experts]
    router_full = router_full.reshape(width, experts)
    gain_attn, gain_query, gain_key, gain_ffn = gains[0], gains[1], gains[2], gains[3]

    attn_weight = jnp.concatenate(
        [
            qkv_weight.reshape(own_rows, 3, fsdp, cols),
            out_weight.reshape(own_rows, 1, fsdp, cols),
        ],
        axis=1,
    )
    attn_weight = attn_weight.transpose(2, 0, 1, 3).reshape(fsdp, own_rows, 4 * cols)
    attn_weight = lax.all_to_all(attn_weight, "fsdp", 0, 0, tiled=True)
    attn_weight = lax.all_gather(
        attn_weight.reshape(fsdp * own_rows, 4 * cols), "dp", axis=0, tiled=True
    )
    qkv_here = attn_weight[:, : 3 * cols]
    out_here = attn_weight[:, 3 * cols :]

    fused = fsdp == 8
    inner_weight = expert_in.reshape(own_rows, fsdp, experts_here, 2, dp, ff_here)
    inner_weight = inner_weight.transpose(4, 1, 3, 2, 0, 5)
    inner_weight = inner_weight.reshape(n, 2 * experts_here, own_rows, ff_here)
    inner_weight = lax.all_to_all(inner_weight, BOTH, 0, 0, tiled=True)
    outer_weight = expert_out.reshape(-1, fsdp, experts_here, width).transpose(1, 2, 0, 3)
    outer_weight = lax.all_to_all(outer_weight, "fsdp", 0, 0, tiled=True)

    hidden_all = lax.all_gather(hidden_in, "fsdp", axis=0, tiled=True).astype(F32)
    normed_all = (hidden_all * rms_scale(hidden_all) * gain_attn).astype(BF16)
    mixed = dot(normed_all, qkv_here, ((1,), (0,)))
    raw = mixed[:, : 2 * cols].reshape(seq, 2, cols)
    squares = plane_sum(jnp.sum(raw * raw, axis=-1), 1)
    qk_scale = lax.rsqrt(squares / width + EPS)[:, :, None]
    qk_unit = raw * qk_scale
    here = f * cols
    qk_gain = jnp.stack(
        [
            lax.dynamic_slice(gain_query, (here,), (cols,)),
            lax.dynamic_slice(gain_key, (here,), (cols,)),
        ]
    )
    pos = jnp.arange(seq, dtype=jnp.int32)
    frequency = jnp.power(10000.0, -jnp.arange(HEAD_DIM // 2, dtype=F32) * 2.0 / HEAD_DIM)
    angles = pos.astype(F32)[:, None] * frequency[None, :]
    cosine = jnp.cos(angles)[:, None, None, :]
    sine = jnp.sin(angles)[:, None, None, :]
    shape4 = (seq, 2, heads_here, HEAD_DIM)
    turned = rotate((qk_unit * qk_gain).reshape(shape4), cosine, sine, 1.0).astype(BF16)
    query = turned[:, 0]
    key = turned[:, 1]
    value = mixed[:, 2 * cols :].astype(BF16).reshape(seq, heads_here, HEAD_DIM)
    allowed = ((pos[None, :] <= pos[:, None]) & (pos[None, :] < valid))[None]
    scores = jnp.einsum("qhd,khd->hqk", query, key, preferred_element_type=F32) * scaling
    masked = jnp.where(allowed, scores, -1e30)
    weights = jnp.where(allowed, jnp.exp(masked - jnp.max(masked, axis=-1, keepdims=True)), 0.0)
    probs = weights / jnp.sum(weights, axis=-1, keepdims=True)
    probs_low = probs.astype(BF16)
    attended = jnp.einsum("hqk,khd->qhd", probs_low, value, preferred_element_type=F32)
    attended = attended.reshape(seq, cols).astype(BF16)
    attended_all = lax.all_gather(attended, "fsdp", axis=0, tiled=False)
    branch = jnp.einsum(
        "fsc,fcn->sn", attended_all, out_here.reshape(fsdp, cols, cols), preferred_element_type=F32
    )
    branch = exchange(branch.astype(BF16).reshape(fsdp, rows, cols), ("fsdp",), 2, True)
    branch = branch.transpose(1, 0, 2).reshape(rows, width).astype(F32)

    hidden = hidden_in.astype(F32)
    scale1 = rms_scale(hidden)
    unit1 = hidden * scale1
    middle = hidden + branch
    scale2 = rms_scale(middle)
    unit2 = middle * scale2
    normed2 = (unit2 * gain_ffn).astype(BF16)
    logits = dot(normed2, router_full, ((1,), (0,)))
    router_probs = jax.nn.softmax(logits, axis=-1)
    chosen = jnp.sum(
        (routes[:, :, None] == jnp.arange(experts, dtype=jnp.int32)[None, None, :]).astype(F32),
        axis=1,
    )
    live_mask = (f * rows + jnp.arange(rows, dtype=jnp.int32) < valid).astype(F32)[:, None]
    grad_total = cotangent.astype(F32) * live_mask

    grad_all = lax.all_gather(grad_total.astype(BF16), BOTH, axis=0, tiled=True)
    gates = (router_probs * chosen).reshape(rows, fsdp, experts_here).transpose(1, 2, 0)
    gates = jnp.broadcast_to(gates[None], (dp, fsdp, experts_here, rows))
    gates = gates.reshape(n, experts_here, rows)
    gates = jnp.pad(gates, ((0, 0), (0, 8 - experts_here), (0, 0)))
    gates = exchange(gates, BOTH, 3, True)[:, :experts_here]
    gates = gates.transpose(0, 2, 1).reshape(tokens, experts_here)
    if fused:
        gates = jnp.pad(gates, ((0, 0), (0, 128 - experts_here))).reshape(dp, seq, 128)
        sums, grad_gates, inner_grad, outer_grad = expert_pass(
            normed2, grad_all.reshape(dp, seq, width), gates, inner_weight, outer_weight, 8
        )
        expert_sum = sums[0]
        grad_rows = sums[1]
        grad_gates = grad_gates.reshape(tokens, 128)[:, 8 : 8 + experts_here]
    else:
        expert_sum, grad_rows, grad_gates, inner_grad, outer_grad = expert_pass_dense(
            normed2, grad_all, gates, inner_weight, outer_weight
        )
    grad_gates = grad_gates.reshape(n, rows, experts_here).transpose(0, 2, 1)
    grad_gates = jnp.pad(grad_gates, ((0, 0), (0, 8 - experts_here), (0, 0)))
    grad_gates = exchange(grad_gates, BOTH, 4, True)[:, :experts_here]
    grad_gates = jnp.sum(grad_gates.reshape(dp, fsdp, experts_here, rows), axis=0)
    grad_router_probs = grad_gates.reshape(experts, rows).transpose(1, 0) * chosen

    inner_grad = lax.all_to_all(inner_grad, BOTH, 0, 0, tiled=True)
    inner_grad = inner_grad.reshape(dp, fsdp, 2, experts_here, own_rows, ff_here)
    inner_grad = inner_grad.transpose(4, 1, 3, 2, 0, 5).reshape(own_rows, experts, 2 * ff)
    outer_grad = lax.all_to_all(outer_grad, "fsdp", 0, 0, tiled=True)
    outer_grad = outer_grad.transpose(2, 0, 1, 3).reshape(-1, experts, width)

    block_total = middle + expert_sum
    squares = jnp.stack(
        [
            jnp.sum(live_mask * block_total * block_total),
            jnp.sum(live_mask * branch * branch),
            jnp.sum(live_mask * expert_sum * expert_sum),
        ]
    )

    grad_logits = router_probs * (
        grad_router_probs - jnp.sum(router_probs * grad_router_probs, axis=-1, keepdims=True)
    )
    grad_logits = grad_logits.astype(BF16)
    router_term = dot(normed2, grad_logits, ((0,), (0,)))
    grad_normed2 = grad_rows + dot(grad_logits, router_full, ((1,), (1,)))
    ffn_term = jnp.sum(grad_normed2 * unit2, axis=0)
    grad_middle = grad_total + norm_back(grad_normed2 * gain_ffn, unit2, scale2)

    grad_cols = grad_middle.astype(BF16).reshape(rows, fsdp, cols).transpose(1, 0, 2)
    grad_cols = exchange(grad_cols, ("fsdp",), 5, True).reshape(seq, cols)
    out_grad = jnp.einsum("fsc,sn->fcn", attended_all, grad_cols, preferred_element_type=F32)
    grad_attended = jnp.einsum(
        "sn,fcn->fsc", grad_cols, out_here.reshape(fsdp, cols, cols), preferred_element_type=F32
    )
    grad_attended = lax.psum_scatter(
        grad_attended.astype(BF16).reshape(fsdp * seq, cols), "fsdp", scatter_dimension=0, tiled=True
    )
    grad_attended = grad_attended.reshape(seq, heads_here, HEAD_DIM)
    grad_probs = jnp.einsum("qhd,khd->hqk", grad_attended, value, preferred_element_type=F32)
    grad_scores = probs * (grad_probs - jnp.sum(probs * grad_probs, axis=-1, keepdims=True))
    grad_scores = grad_scores.astype(BF16)
    grad_query = jnp.einsum("hqk,khd->qhd", grad_scores, key, preferred_element_type=F32)
    grad_key = jnp.einsum("hqk,qhd->khd", grad_scores, query, preferred_element_type=F32)
    grad_value = jnp.einsum("hqk,qhd->khd", probs_low, grad_attended, preferred_element_type=F32)
    grad_qk = rotate(jnp.stack([grad_query, grad_key], axis=1) * scaling, cosine, sine, -1.0)
    grad_qk = grad_qk.reshape(seq, 2, cols)
    qk_term = jnp.sum(grad_qk * qk_unit, axis=0)
    grad_qk = grad_qk * qk_gain
    inner_means = plane_sum(jnp.sum(grad_qk * qk_unit, axis=-1), 6)[:, :, None] / width
    grad_qk = qk_scale * (grad_qk - qk_unit * inner_means)
    grad_qkv = jnp.concatenate(
        [grad_qk.reshape(seq, 2 * cols), grad_value.reshape(seq, cols)], axis=1
    ).astype(BF16)
    qkv_grad = dot(normed_all, grad_qkv, ((0,), (0,)))
    grad_normed = dot(grad_qkv, qkv_here, ((1,), (1,))).astype(BF16)
    grad_normed = lax.psum_scatter(grad_normed, "fsdp", scatter_dimension=0, tiled=True).astype(F32)
    attn_term = jnp.sum(grad_normed * unit1, axis=0)
    hidden_grad = grad_middle + norm_back(grad_normed * gain_attn, unit1, scale1)

    attn_grad = jnp.concatenate([qkv_grad, out_grad.reshape(width, cols)], axis=1).astype(BF16)
    attn_grad = lax.psum_scatter(attn_grad, "dp", scatter_dimension=0, tiled=True)
    attn_grad = attn_grad.reshape(fsdp, own_rows, 4 * cols)
    attn_grad = lax.all_to_all(attn_grad, "fsdp", 0, 0, tiled=True)
    attn_grad = attn_grad.reshape(fsdp, own_rows, 4, cols).transpose(1, 2, 0, 3).astype(F32)
    attn_grad = attn_grad.reshape(own_rows, 4 * width)

    qk_full = jnp.zeros((2, width), F32)
    qk_full = lax.dynamic_update_slice(qk_full, qk_term, (0, here))
    terms = jnp.concatenate([attn_term[None], qk_full, ffn_term[None]])
    terms = terms.reshape(4, n, own_rows).transpose(1, 0, 2).reshape(n, 4 * own_rows)
    terms = jnp.concatenate(
        [
            terms,
            router_term.reshape(n, own_rows * experts),
            jnp.broadcast_to(squares[None], (n, 3)),
        ],
        axis=1,
    )
    term_size = terms.shape[1]
    term_rows = -(-term_size // 1024) * 8
    terms = jnp.pad(terms, ((0, 0), (0, term_rows * 128 - term_size)))
    terms = exchange(terms.reshape(n, term_rows, 128), BOTH, 7, True)
    terms = jnp.sum(terms, axis=0).reshape(-1)
    gain_grads = terms[: 4 * own_rows].reshape(4, own_rows)
    router_grad = terms[4 * own_rows : 4 * own_rows + own_rows * experts]
    valid_cells = jnp.sum(lengths).astype(F32) * width
    stats = jnp.sqrt(terms[term_size - 3 : term_size] / valid_cells)

    return (
        block_total.astype(BF16),
        hidden_grad,
        gain_grads[0],
        gain_grads[1],
        gain_grads[2],
        gain_grads[3],
        attn_grad[:, : 3 * width],
        attn_grad[:, 3 * width :],
        router_grad.reshape(own_rows, experts),
        inner_grad.astype(F32),
        outer_grad.astype(F32),
        stats,
    )


def solution(mesh):
    one = P(BOTH)
    two = P(BOTH, None)
    three = P(BOTH, None, None)
    in_specs = (two, P(), two, one, one, one, one, two, two, two, three, three, two)
    out_specs = (two, two, one, one, one, one, two, two, two, three, three, P())
    return jax.shard_map(body, mesh=mesh, in_specs=in_specs, out_specs=out_specs, check_vma=False)
```

```python
import functools

import jax
import jax.numpy as jnp
from jax import lax
from jax.experimental import pallas as pl
from jax.experimental.pallas import tpu as pltpu
from jax.sharding import PartitionSpec as P

HEADS = 16
HEAD_DIM = 128
EPS = 1e-05
BOTH = ("dp", "fsdp")
MESH_ID = pl.DeviceIdType.MESH
F32 = jnp.float32
BF16 = jnp.bfloat16


def rms_scale(values_in):
    return lax.rsqrt(jnp.mean(values_in * values_in, axis=-1, keepdims=True) + EPS)


def norm_back(grad_in, unit_rows, scaling):
    return scaling * (grad_in - unit_rows * jnp.mean(grad_in * unit_rows, axis=-1, keepdims=True))


def rotate(values_in, cosine, sine, direction):
    half_width = values_in.shape[-1] // 2
    first_half = values_in[..., :half_width]
    second_half = values_in[..., half_width:]
    return jnp.concatenate(
        [
            first_half * cosine - direction * second_half * sine,
            second_half * cosine + direction * first_half * sine,
        ],
        axis=-1,
    )


def place(axes, fsdp, index):
    if axes == BOTH:
        return {"dp": index // fsdp, "fsdp": lax.rem(index, fsdp)}
    return {axes[0]: index}


def exchange_kernel(axes, n, fsdp, spread, x, o, send, recv, own):
    if axes == BOTH:
        me = lax.axis_index("dp") * fsdp + lax.axis_index("fsdp")
    else:
        me = lax.axis_index(axes[0])
    barrier = pltpu.get_barrier_semaphore()
    for k in range(1, n):
        peer = place(axes, fsdp, lax.rem(me + k, n))
        pl.semaphore_signal(barrier, inc=1, device_id=peer, device_id_type=MESH_ID)
    pl.semaphore_wait(barrier, n - 1)
    local = pltpu.make_async_copy(x.at[me] if spread else x, o.at[me], own)
    local.start()
    copies = []
    for k in range(1, n):
        target = lax.rem(me + k, n)
        copy = pltpu.make_async_remote_copy(
            x.at[target] if spread else x,
            o.at[me],
            send.at[k],
            recv.at[k],
            device_id=place(axes, fsdp, target),
            device_id_type=MESH_ID,
        )
        copy.start()
        copies.append(copy)
    local.wait()
    for copy in copies:
        copy.wait()


def exchange(x, axes, ident, spread):
    fsdp = lax.axis_size("fsdp")
    n = lax.axis_size(axes)
    shape = x.shape if spread else (n,) + x.shape
    return pl.pallas_call(
        functools.partial(exchange_kernel, axes, n, fsdp, spread),
        out_shape=jax.ShapeDtypeStruct(shape, x.dtype),
        in_specs=[pl.BlockSpec(memory_space=pl.ANY)],
        out_specs=pl.BlockSpec(memory_space=pl.ANY),
        scratch_shapes=[
            pltpu.SemaphoreType.DMA((n,)),
            pltpu.SemaphoreType.DMA((n,)),
            pltpu.SemaphoreType.DMA,
        ],
        compiler_params=pltpu.CompilerParams(collective_id=ident, has_side_effects=True),
    )(x)


def tiles_of(x, rows):
    flat = x.reshape(-1)
    return jnp.pad(flat, (0, rows * 128 - flat.shape[0])).reshape(rows, 128)


def plane_sum(x, ident):
    rows = -(-x.size // 1024) * 8
    got = exchange(tiles_of(x, rows), ("fsdp",), ident, False)
    return jnp.sum(got, axis=0).reshape(-1)[: x.size].reshape(x.shape)


def dot(a, b, dims):
    return lax.dot_general(a, b, (dims, ((), ())), preferred_element_type=F32)


HIGH = lax.Precision.HIGHEST


def remote(src, dst, send, recv, device):
    return pltpu.make_async_remote_copy(
        src, dst, send, recv, device_id=device, device_id_type=MESH_ID
    )


def greet_all(n, fsdp, me):
    barrier = pltpu.get_barrier_semaphore()
    for k in range(1, n):
        peer = place(BOTH, fsdp, lax.rem(me + k, n))
        pl.semaphore_signal(barrier, inc=1, device_id=peer, device_id_type=MESH_ID)
    pl.semaphore_wait(barrier, n - 1)


class Plane:
    def __init__(self, f):
        self.f = f
        self.core = lax.rem(f, 2)
        self.chip = f // 2
        xbit = lax.rem(self.chip, 2)
        ybit = self.chip // 2
        self.chip_x = ybit * 2 + (1 - xbit)
        self.chip_y = (1 - ybit) * 2 + xbit
        self.chip_d = (1 - ybit) * 2 + (1 - xbit)
        self.fx = self.chip_x * 2 + self.core
        self.fy = self.chip_y * 2 + self.core
        self.fd = self.chip_d * 2 + self.core
        self.to_x = {"fsdp": self.fx}
        self.to_y = {"fsdp": self.fy}
        self.to_c = {"fsdp": self.chip * 2 + 1 - self.core}


class PlaneSum:
    def __init__(self, plane, part, held, core_in, half_in, full_in, send, recv):
        self.plane = plane
        self.part = part
        self.held = held
        self.core_in = core_in
        self.half_in = half_in
        self.full_in = full_in
        self.send = send
        self.recv = recv
        half = held.shape[1] // 2
        self.upper = pl.ds(0, half)
        self.lower = pl.ds(half, half)

    def core_copy(self, j):
        owner = j * 2 + 1 - self.plane.core
        return remote(
            self.part.at[owner],
            self.core_in.at[j],
            self.send.at[j],
            self.recv.at[j],
            self.plane.to_c,
        )

    def half_copies(self):
        block = self.held.at[self.plane.chip_d]
        send, recv, half_in = self.send, self.recv, self.half_in
        return (
            remote(block.at[self.upper], half_in.at[0], send.at[4], recv.at[4], self.plane.to_x),
            remote(block.at[self.lower], half_in.at[1], send.at[5], recv.at[5], self.plane.to_y),
        )

    def full_copies(self):
        held, full_in, send, recv = self.held, self.full_in, self.send, self.recv
        plane = self.plane
        return (
            remote(held.at[plane.chip_x], full_in.at[0], send.at[6], recv.at[6], plane.to_x),
            remote(held.at[plane.chip_y], full_in.at[1], send.at[7], recv.at[7], plane.to_y),
        )

    def start(self):
        for j in range(4):
            self.core_copy(j).start()

    def add_core(self):
        for j in range(4):
            self.core_copy(j).wait()

        def one(j, carry):
            own = self.part[j * 2 + self.plane.core].astype(F32)
            self.held[j] = (own + self.core_in[j].astype(F32)).astype(BF16)
            return carry

        lax.fori_loop(0, 4, one, 0)
        for copy in self.half_copies():
            copy.start()

    def pass_on(self):
        for copy in self.half_copies():
            copy.wait()
        held, half_in = self.held, self.half_in
        for chip, piece, i in (
            (self.plane.chip_y, self.upper, 0),
            (self.plane.chip_x, self.lower, 1),
        ):
            total = held[chip, piece].astype(F32) + half_in[i].astype(F32)
            held[chip, piece] = total.astype(BF16)
        for copy in self.full_copies():
            copy.start()

    def total(self):
        for copy in self.full_copies():
            copy.wait()
        total = self.held[self.plane.chip].astype(F32)
        return total + self.full_in[0].astype(F32) + self.full_in[1].astype(F32)


class PlaneGather:
    def __init__(self, plane, block, rows, send, recv):
        self.plane = plane
        self.block = block
        self.send = send
        self.recv = recv
        self.upper = pl.ds(0, rows // 2)
        self.lower = pl.ds(rows // 2, rows // 2)

    def same(self, ref, i, device):
        return remote(ref, ref, self.send(i), self.recv(i), device)

    def first(self):
        own = self.block(self.plane.f)
        return (
            self.same(own.at[self.upper], 0, self.plane.to_x),
            self.same(own.at[self.lower], 1, self.plane.to_y),
        )

    def second(self):
        plane = self.plane
        return (
            self.same(self.block(plane.f).at[self.upper], 2, plane.to_y),
            self.same(self.block(plane.fx).at[self.upper], 3, plane.to_y),
            self.same(self.block(plane.f).at[self.lower], 4, plane.to_x),
            self.same(self.block(plane.fy).at[self.lower], 5, plane.to_x),
        )

    def third(self):
        plane = self.plane
        owners = (plane.f, plane.fx, plane.fy, plane.fd)
        return [self.same(self.block(o), 6 + i, plane.to_c) for i, o in enumerate(owners)]

    def start(self):
        for copy in self.first():
            copy.start()

    def middle(self):
        for copy in self.first():
            copy.wait_recv()
        for copy in self.second():
            copy.start()

    def finish(self):
        for copy in self.second():
            copy.wait_recv()
        for copy in self.third():
            copy.start()

    def wait(self):
        for copy in self.third():
            copy.wait_recv()

    def settle(self):
        for copy in (*self.first(), *self.second(), *self.third()):
            copy.wait_send()


def attention_kernel(
    dp,
    fsdp,
    hidden,
    cot,
    weight_in,
    inner_in,
    outer_in,
    gain_attn,
    gain,
    turn,
    live,
    branch,
    qkv,
    unit,
    scale,
    normed,
    weight,
    attended,
    c_all,
    inner_out,
    outer_out,
    hid_v,
    normed_v,
    w_v,
    raw,
    stat,
    stat_in,
    att_v,
    cols_v,
    rows_v,
    local,
    w_send,
    w_recv,
    right_send,
    right_recv,
    left_send,
    left_recv,
    h_send,
    h_recv,
    t_send,
    t_recv,
    a_send,
    a_recv,
    b_send,
    b_recv,
    c_send,
    c_recv,
    z_send,
    z_recv,
    in_send,
    in_recv,
    out_send,
    out_recv,
):
    n = dp * fsdp
    z = lax.axis_index("dp")
    f = lax.axis_index("fsdp")
    me = z * fsdp + f
    plane = Plane(f)
    rows, width = hidden.shape
    seq, cols = cols_v.shape
    own_rows = weight_in.shape[1]
    slab = fsdp * own_rows
    scaling = HEAD_DIM ** (-0.5)
    greet_all(n, fsdp, me)

    def weight_rows(index):
        return pl.ds(pl.multiple_of(index * own_rows, own_rows), own_rows)

    def weight_copy(k):
        target = lax.rem(f + k, fsdp)
        return remote(
            weight_in.at[target],
            w_v.at[weight_rows(me)],
            w_send.at[k],
            w_recv.at[k],
            {"fsdp": target},
        )

    def slab_copy(p, near, far, send, recv):
        ref = w_v.at[pl.ds(pl.multiple_of(p * slab, slab), slab)]
        return remote(ref, ref, send.at[near], recv.at[near], {"dp": far})

    def inner_copy(k):
        target = lax.rem(me + k, n)
        return remote(
            inner_in.at[target],
            inner_out.at[me],
            in_send.at[k],
            in_recv.at[k],
            place(BOTH, fsdp, target),
        )

    def outer_copy(k):
        target = lax.rem(f + k, fsdp)
        return remote(
            outer_in.at[target], outer_out.at[f], out_send.at[k], out_recv.at[k], {"fsdp": target}
        )

    def cot_copy(i):
        return remote(
            cot,
            c_all.at[z, f],
            z_send.at[i],
            z_recv.at[i],
            {"dp": lax.rem(z + dp - i, dp)},
        )

    hidden_gather = PlaneGather(
        plane, lambda o: hid_v.at[o], rows, lambda i: h_send.at[i], lambda i: h_recv.at[i]
    )
    attended_gather = PlaneGather(
        plane, lambda o: att_v.at[o], seq, lambda i: a_send.at[i], lambda i: a_recv.at[i]
    )
    cot_gather = [
        PlaneGather(
            plane,
            lambda o, s=s: c_all.at[lax.rem(z + 1 + s, dp), o],
            rows,
            lambda i, s=s: c_send.at[s, i],
            lambda i, s=s: c_recv.at[s, i],
        )
        for s in range(dp)
    ]

    keeps = [
        pltpu.make_async_copy(hidden, hid_v.at[f], local.at[0]),
        pltpu.make_async_copy(weight_in.at[f], w_v.at[weight_rows(me)], local.at[1]),
        pltpu.make_async_copy(cot, c_all.at[z, f], local.at[2]),
        pltpu.make_async_copy(inner_in.at[me], inner_out.at[me], local.at[3]),
        pltpu.make_async_copy(outer_in.at[f], outer_out.at[f], local.at[4]),
    ]
    for copy in keeps:
        copy.start()
    for k in range(1, fsdp):
        weight_copy(k).start()
    keeps[0].wait()
    hidden_gather.start()
    keeps[1].wait()
    for k in range(1, fsdp):
        weight_copy(k).wait_recv()

    @pl.when(z < dp - 1)
    def _():
        slab_copy(z, 1, z + 1, right_send, right_recv).start()

    @pl.when(z > 0)
    def _():
        slab_copy(z, 1, z - 1, left_send, left_recv).start()

    hidden_gather.middle()
    keeps[2].wait()
    cot_gather[dp - 1].start()
    hidden_gather.finish()
    for k in range(1, fsdp):
        outer_copy(k).start()
    hidden_gather.wait()

    def norm_rows(i, carry):
        values = hid_v[i].astype(F32)
        values = values * lax.rsqrt(jnp.mean(values * values, axis=-1, keepdims=True) + EPS)
        r = pl.ds(pl.multiple_of(i * rows, rows), rows)
        normed_v[r, :] = (values * gain_attn[0:1, :]).astype(BF16)
        return carry

    lax.fori_loop(0, fsdp, norm_rows, 0)
    normed_store = pltpu.make_async_copy(normed_v, normed, local.at[0])
    normed_store.start()

    for d in range(1, dp):

        @pl.when(z >= d)
        def _(d=d):
            slab_copy(z - d, d, 0, right_send, right_recv).wait_recv()

            @pl.when(z < dp - 1)
            def _():
                slab_copy(z - d, d + 1, z + 1, right_send, right_recv).start()

        @pl.when(z + d < dp)
        def _(d=d):
            slab_copy(z + d, d, 0, left_send, left_recv).wait_recv()

            @pl.when(z > 0)
            def _():
                slab_copy(z + d, d + 1, z - 1, left_send, left_recv).start()

        if d == 1:
            cot_gather[dp - 1].middle()
        if d == 2:
            cot_gather[dp - 1].finish()

    for i in range(1, dp):
        cot_copy(i).start()
    for k in range(1, n):
        inner_copy(k).start()
    weight_store = pltpu.make_async_copy(w_v, weight, local.at[1])
    weight_store.start()

    tile = 256

    def project(i, carry):
        r = pl.ds(pl.multiple_of(i * tile, tile), tile)
        for j in range(3):
            col = pl.ds(j * cols, cols)
            value = dot(normed_v[r, :], w_v[:, col], ((1,), (0,)))
            if j < 2:
                raw[r, col] = value
            else:
                qkv[2, r, :] = value.astype(BF16)
        return carry

    lax.fori_loop(0, seq // tile, project, 0)
    row = lax.broadcasted_iota(jnp.int32, (8, 2 * cols), 0)
    lane_of = lax.broadcasted_iota(jnp.int32, (8, 2 * cols), 1)
    chooser = jnp.where(lane_of // cols == row, 1.0, 0.0).astype(F32)
    stat[...] = lax.dot_general(
        chooser,
        raw[...] * raw[...],
        (((1,), (1,)), ((), ())),
        precision=HIGH,
        preferred_element_type=F32,
    )

    def stat_copy(k):
        return remote(
            stat, stat_in.at[f], t_send.at[k], t_recv.at[k], {"fsdp": lax.rem(f + k, fsdp)}
        )

    for k in range(1, fsdp):
        stat_copy(k).start()
    stat_in[f] = stat[...]
    for k in range(1, fsdp):
        stat_copy(k).wait_recv()
    sums = stat_in[0]
    for i in range(1, fsdp):
        sums = sums + stat_in[i]
    corner = jnp.where(
        lax.broadcasted_iota(jnp.int32, (8, 128), 0) == lax.broadcasted_iota(jnp.int32, (8, 128), 1),
        1.0 / width,
        0.0,
    ).astype(F32)
    means = lax.dot_general(
        sums, corner, (((0,), (0,)), ((), ())), precision=HIGH, preferred_element_type=F32
    )
    scale[...] = lax.rsqrt(means + EPS)
    for i in range(2):
        wide = pl.ds(i * cols, cols)
        unit[:, wide] = raw[:, wide] * scale[:, i : i + 1]
        for h in range(cols // HEAD_DIM):
            lane = pl.ds(i * cols + h * HEAD_DIM, HEAD_DIM)
            values = unit[:, lane] * gain[0:1, lane]
            values = values * turn[0] - pltpu.roll(values, HEAD_DIM // 2, 1) * turn[1]
            qkv[i, :, pl.ds(h * HEAD_DIM, HEAD_DIM)] = values.astype(BF16)

    def head(h, carry):
        lane = pl.ds(pl.multiple_of(h * HEAD_DIM, HEAD_DIM), HEAD_DIM)
        for t in range(seq // tile):
            r = pl.ds(t * tile, tile)
            extent = (t + 1) * tile
            upto = pl.ds(0, extent)
            scores = dot(qkv[0, r, lane], qkv[1, upto, lane], ((1,), (1,))) * scaling
            q_pos = t * tile + lax.broadcasted_iota(jnp.int32, (tile, extent), 0)
            k_pos = lax.broadcasted_iota(jnp.int32, (tile, extent), 1)
            allowed = (k_pos <= q_pos) & (live[0:1, 0:extent] > 0.0)
            masked = jnp.where(allowed, scores, -1e30)
            weights = jnp.exp(masked - jnp.max(masked, axis=-1, keepdims=True))
            weights = jnp.where(allowed, weights, 0.0)
            probs = weights / jnp.sum(weights, axis=-1, keepdims=True)
            att_v[f, r, lane] = dot(
                probs.astype(BF16), qkv[2, upto, lane], ((1,), (0,))
            ).astype(BF16)
        return carry

    lax.fori_loop(0, cols // HEAD_DIM, head, 0)
    attended_gather.start()
    for s in range(dp - 1):
        cot_copy(s + 1).wait_recv()
        cot_gather[s].start()
        if s == 0:
            attended_gather.middle()
    cot_gather[0].middle()
    attended_gather.finish()
    for s in range(1, dp - 1):
        cot_gather[s].middle()
    attended_gather.wait()
    attended_store = pltpu.make_async_copy(att_v, attended, local.at[2])
    attended_store.start()

    out_cols = pl.ds(3 * cols, cols)

    def project_out(i, carry):
        r = pl.ds(pl.multiple_of(i * tile, tile), tile)
        total = dot(att_v[0, r, :], w_v[pl.ds(0, cols), out_cols], ((1,), (0,)))
        for j in range(1, fsdp):
            total += dot(att_v[j, r, :], w_v[pl.ds(j * cols, cols), out_cols], ((1,), (0,)))
        cols_v[r, :] = total.astype(BF16)
        return carry

    lax.fori_loop(0, seq // tile, project_out, 0)

    def branch_copy(k):
        target = lax.rem(f + k, fsdp)
        return remote(
            cols_v.at[pl.ds(pl.multiple_of(target * rows, rows), rows)],
            rows_v.at[f],
            b_send.at[k],
            b_recv.at[k],
            {"fsdp": target},
        )

    for k in range(1, fsdp):
        branch_copy(k).start()
    rows_v[f] = cols_v[pl.ds(pl.multiple_of(f * rows, rows), rows), :]
    for s in range(dp - 1):
        cot_gather[s].finish()
    for k in range(1, fsdp):
        branch_copy(k).wait()
    for i in range(fsdp):
        branch[:, pl.ds(i * cols, cols)] = rows_v[i]

    for s in range(dp):
        cot_gather[s].wait()
        cot_gather[s].settle()
    hidden_gather.settle()
    attended_gather.settle()
    for i in range(1, dp):
        cot_copy(i).wait_send()

    @pl.when(z < dp - 1)
    def _():
        slab_copy(z, 1, z + 1, right_send, right_recv).wait_send()

    @pl.when(z > 0)
    def _():
        slab_copy(z, 1, z - 1, left_send, left_recv).wait_send()

    for d in range(1, dp):

        @pl.when((z >= d) & (z < dp - 1))
        def _(d=d):
            slab_copy(z - d, d + 1, z + 1, right_send, right_recv).wait_send()

        @pl.when((z + d < dp) & (z > 0))
        def _(d=d):
            slab_copy(z + d, d + 1, z - 1, left_send, left_recv).wait_send()

    for k in range(1, fsdp):
        weight_copy(k).wait_send()
        stat_copy(k).wait_send()
        outer_copy(k).wait()
    for k in range(1, n):
        inner_copy(k).wait()
    for copy in keeps[3:]:
        copy.wait()
    normed_store.wait()
    weight_store.wait()
    attended_store.wait()


def attention_forward(
    hidden, cot, weight_in, inner_in, outer_in, gain_attn, gain, turn, live, ident
):
    dp = lax.axis_size("dp")
    fsdp = lax.axis_size("fsdp")
    n = dp * fsdp
    rows, width = hidden.shape
    seq = rows * fsdp
    cols = width // fsdp
    shape = jax.ShapeDtypeStruct
    dma = pltpu.SemaphoreType.DMA
    vmem = pltpu.VMEM
    anywhere = pl.BlockSpec(memory_space=pl.ANY)
    inside = pl.BlockSpec(memory_space=pltpu.VMEM)
    pairs = [fsdp, dp + 1, dp + 1, 10, fsdp, 10, fsdp]
    sems = []
    for size in pairs:
        sems += [dma((size,)), dma((size,))]
    sems += [dma((dp, 10)), dma((dp, 10))]
    for size in (dp, n, fsdp):
        sems += [dma((size,)), dma((size,))]
    return pl.pallas_call(
        functools.partial(attention_kernel, dp, fsdp),
        out_shape=(
            shape((rows, width), BF16),
            shape((3, seq, cols), BF16),
            shape((seq, 2 * cols), F32),
            shape((seq, 128), F32),
            shape((seq, width), BF16),
            shape((width, 4 * cols), BF16),
            shape((fsdp, seq, cols), BF16),
            shape((dp, fsdp, rows, width), BF16),
            shape(inner_in.shape, BF16),
            shape(outer_in.shape, BF16),
        ),
        in_specs=[anywhere] * 5 + [inside] * 4,
        out_specs=(inside,) * 4 + (anywhere,) * 6,
        scratch_shapes=[
            vmem((fsdp, rows, width), BF16),
            vmem((seq, width), BF16),
            vmem((width, 4 * cols), BF16),
            vmem((seq, 2 * cols), F32),
            vmem((8, seq), F32),
            vmem((fsdp, 8, seq), F32),
            vmem((fsdp, seq, cols), BF16),
            vmem((seq, cols), BF16),
            vmem((fsdp, rows, cols), BF16),
            dma((5,)),
            *sems,
        ],
        compiler_params=pltpu.CompilerParams(
            collective_id=ident, has_side_effects=True, vmem_limit_bytes=63 * 1024 * 1024
        ),
    )(hidden, cot, weight_in, inner_in, outer_in, gain_attn, gain, turn, live)


def attention_back_kernel(
    dp,
    fsdp,
    grad_rows,
    attended,
    weight,
    normed,
    qkv,
    unit,
    scale,
    gain,
    turn,
    live,
    inner_in,
    outer_in,
    grad_normed,
    terms,
    owned,
    inner_out,
    outer_out,
    att_v,
    w_v,
    normed_v,
    gcols,
    part1,
    held1,
    core1,
    half1,
    full1,
    part2,
    held2,
    core2,
    half2,
    full2,
    gatt,
    gq,
    gk,
    gval,
    gqk,
    gqkv,
    stat,
    stat_in,
    wgrad,
    z_in,
    wsum,
    local,
    in_send,
    in_recv,
    out_send,
    out_recv,
    g_send,
    g_recv,
    s1_send,
    s1_recv,
    s2_send,
    s2_recv,
    t_send,
    t_recv,
    zo_send,
    zo_recv,
    zq_send,
    zq_recv,
    w_send,
    w_recv,
):
    n = dp * fsdp
    z = lax.axis_index("dp")
    f = lax.axis_index("fsdp")
    me = z * fsdp + f
    plane = Plane(f)
    rows, width = grad_rows.shape
    seq, cols = gcols.shape
    own_rows = inner_in.shape[2]
    slab = fsdp * own_rows
    scaling = HEAD_DIM ** (-0.5)
    greet_all(n, fsdp, me)

    loads = [
        pltpu.make_async_copy(attended, att_v, local.at[0]),
        pltpu.make_async_copy(weight, w_v, local.at[1]),
        pltpu.make_async_copy(normed, normed_v, local.at[2]),
        pltpu.make_async_copy(
            grad_rows.at[:, pl.ds(pl.multiple_of(f * cols, cols), cols)],
            gcols.at[pl.ds(pl.multiple_of(f * rows, rows), rows)],
            local.at[3],
        ),
    ]
    keeps = [
        pltpu.make_async_copy(inner_in.at[me], inner_out.at[me], local.at[4]),
        pltpu.make_async_copy(outer_in.at[f], outer_out.at[f], local.at[5]),
    ]
    for copy in loads:
        copy.start()

    def cols_copy(k):
        target = lax.rem(f + k, fsdp)
        return remote(
            grad_rows.at[:, pl.ds(pl.multiple_of(target * cols, cols), cols)],
            gcols.at[pl.ds(pl.multiple_of(f * rows, rows), rows)],
            g_send.at[k],
            g_recv.at[k],
            {"fsdp": target},
        )

    def inner_copy(k):
        target = lax.rem(me + k, n)
        return remote(
            inner_in.at[target],
            inner_out.at[me],
            in_send.at[k],
            in_recv.at[k],
            place(BOTH, fsdp, target),
        )

    def outer_copy(k):
        target = lax.rem(f + k, fsdp)
        return remote(
            outer_in.at[target], outer_out.at[f], out_send.at[k], out_recv.at[k], {"fsdp": target}
        )

    def slab_rows(p):
        return pl.ds(pl.multiple_of(p * slab, slab), slab)

    def far_copy(i, col, send, recv):
        p = lax.rem(z + i, dp)
        return remote(
            wgrad.at[slab_rows(p), col], z_in.at[i, :, col], send.at[i], recv.at[i], {"dp": p}
        )

    qkv_cols = pl.ds(0, 3 * cols)
    out_cols = pl.ds(3 * cols, cols)

    for k in range(1, fsdp):
        cols_copy(k).start()
    for k in range(1, n):
        inner_copy(k).start()
    for k in range(1, fsdp):
        outer_copy(k).start()
    for copy in keeps:
        copy.start()
    for copy in loads:
        copy.wait()
    for k in range(1, fsdp):
        cols_copy(k).wait_recv()

    def attended_back(i, carry):
        block = pl.ds(pl.multiple_of(i * cols, cols), cols)
        part1[i] = dot(gcols[...], w_v[block, out_cols], ((1,), (1,))).astype(BF16)
        return carry

    lax.fori_loop(0, fsdp, attended_back, 0)
    sum1 = PlaneSum(plane, part1, held1, core1, half1, full1, s1_send, s1_recv)
    sum1.start()

    def out_grads(i, carry):
        block = pl.ds(pl.multiple_of(i * cols, cols), cols)
        wgrad[block, out_cols] = dot(att_v[i], gcols[...], ((0,), (0,))).astype(BF16)
        return carry

    lax.fori_loop(0, fsdp // 2, out_grads, 0)
    sum1.add_core()
    lax.fori_loop(fsdp // 2, fsdp, out_grads, 0)
    for i in range(1, dp):
        far_copy(i, out_cols, zo_send, zo_recv).start()
    sum1.pass_on()
    gk[...] = jnp.zeros_like(gk)
    gval[...] = jnp.zeros_like(gval)
    gatt[...] = sum1.total().astype(BF16)

    tile = 256

    def head(h, carry):
        lane = pl.ds(pl.multiple_of(h * HEAD_DIM, HEAD_DIM), HEAD_DIM)
        for t in range(seq // tile):
            r = pl.ds(t * tile, tile)
            extent = (t + 1) * tile
            upto = pl.ds(0, extent)
            query = qkv[0, r, lane]
            key = qkv[1, upto, lane]
            value = qkv[2, upto, lane]
            grad = gatt[r, lane]
            scores = dot(query, key, ((1,), (1,))) * scaling
            q_pos = t * tile + lax.broadcasted_iota(jnp.int32, (tile, extent), 0)
            k_pos = lax.broadcasted_iota(jnp.int32, (tile, extent), 1)
            allowed = (k_pos <= q_pos) & (live[0:1, 0:extent] > 0.0)
            masked = jnp.where(allowed, scores, -1e30)
            weights = jnp.exp(masked - jnp.max(masked, axis=-1, keepdims=True))
            weights = jnp.where(allowed, weights, 0.0)
            probs = weights / jnp.sum(weights, axis=-1, keepdims=True)
            grad_probs = dot(grad, value, ((1,), (1,)))
            mean = jnp.sum(probs * grad_probs, axis=-1, keepdims=True)
            grad_scores = (probs * (grad_probs - mean)).astype(BF16)
            gq[r, lane] = dot(grad_scores, key, ((1,), (0,)))
            gk[upto, lane] += dot(grad_scores, query, ((0,), (0,)))
            gval[upto, lane] += dot(probs.astype(BF16), grad, ((0,), (0,)))
        return carry

    lax.fori_loop(0, cols // HEAD_DIM, head, 0)

    heads_here = cols // HEAD_DIM
    for i, source in enumerate((gq, gk)):
        for h in range(heads_here):
            lane = pl.ds(h * HEAD_DIM, HEAD_DIM)
            wide = pl.ds(i * cols + h * HEAD_DIM, HEAD_DIM)
            grad = source[:, lane] * scaling
            grad = grad * turn[0] + pltpu.roll(grad, HEAD_DIM // 2, 1) * turn[1]
            terms[:, wide] = jnp.broadcast_to(
                jnp.sum(grad * unit[:, wide], axis=0, keepdims=True), (8, HEAD_DIM)
            )
            gqk[:, wide] = grad * gain[0:1, wide]
    row = lax.broadcasted_iota(jnp.int32, (8, 2 * cols), 0)
    lane_of = lax.broadcasted_iota(jnp.int32, (8, 2 * cols), 1)
    chooser = jnp.where(lane_of // cols == row, 1.0, 0.0).astype(F32)
    stat[...] = lax.dot_general(
        chooser,
        gqk[...] * unit[...],
        (((1,), (1,)), ((), ())),
        precision=HIGH,
        preferred_element_type=F32,
    )

    def stat_copy(k):
        return remote(
            stat, stat_in.at[f], t_send.at[k], t_recv.at[k], {"fsdp": lax.rem(f + k, fsdp)}
        )

    for k in range(1, fsdp):
        stat_copy(k).start()
    stat_in[f] = stat[...]
    gqkv[:, pl.ds(2 * cols, cols)] = gval[...].astype(BF16)
    for k in range(1, fsdp):
        stat_copy(k).wait_recv()
    sums = stat_in[0]
    for i in range(1, fsdp):
        sums = sums + stat_in[i]
    corner = jnp.where(
        lax.broadcasted_iota(jnp.int32, (8, 128), 0) == lax.broadcasted_iota(jnp.int32, (8, 128), 1),
        1.0 / width,
        0.0,
    ).astype(F32)
    means = lax.dot_general(
        sums, corner, (((0,), (0,)), ((), ())), precision=HIGH, preferred_element_type=F32
    )
    for i in range(2):
        wide = pl.ds(i * cols, cols)
        grad = scale[:, i : i + 1] * (gqk[:, wide] - unit[:, wide] * means[:, i : i + 1])
        gqkv[:, wide] = grad.astype(BF16)

    step = 512

    def normed_back(i, carry):
        r = pl.ds(pl.multiple_of(i * rows, rows), rows)
        for c in range(width // step):
            col = pl.ds(c * step, step)
            part2[i, :, col] = dot(gqkv[r, :], w_v[col, qkv_cols], ((1,), (1,))).astype(BF16)
        return carry

    lax.fori_loop(0, fsdp, normed_back, 0)
    sum2 = PlaneSum(plane, part2, held2, core2, half2, full2, s2_send, s2_recv)
    sum2.start()

    def qkv_grads(p):
        for i in range(2):
            block = pl.ds(pl.multiple_of(p * slab + i * (slab // 2), slab // 2), slab // 2)
            wgrad[block, qkv_cols] = dot(normed_v[:, block], gqkv[...], ((0,), (0,))).astype(BF16)

    for i in range(1, dp):
        qkv_grads(lax.rem(z + i, dp))
        far_copy(i, qkv_cols, zq_send, zq_recv).start()
        if i == 1:
            sum2.add_core()
        if i == 2:
            sum2.pass_on()
    qkv_grads(z)
    grad_normed[...] = sum2.total()

    for i in range(1, dp):
        far_copy(i, out_cols, zo_send, zo_recv).wait()
    for i in range(1, dp):
        far_copy(i, qkv_cols, zq_send, zq_recv).wait()
    total = wgrad[slab_rows(z), :].astype(F32)
    for i in range(1, dp):
        total += z_in[i].astype(F32)
    wsum[...] = total.astype(BF16).reshape(wsum.shape)

    def owner_copy(k):
        target = lax.rem(f + k, fsdp)
        return remote(
            wsum.at[target], owned.at[f], w_send.at[k], w_recv.at[k], {"fsdp": target}
        )

    for k in range(1, fsdp):
        owner_copy(k).start()
    owned[f] = wsum[f]
    for k in range(1, fsdp):
        owner_copy(k).wait()
    for k in range(1, fsdp):
        cols_copy(k).wait_send()
        stat_copy(k).wait_send()
        outer_copy(k).wait()
    for k in range(1, n):
        inner_copy(k).wait()
    for copy in keeps:
        copy.wait()


def attention_back(
    grad_rows, attended, weight, normed, qkv, unit, scale, gain, turn, live, inner_in, outer_in, ident
):
    dp = lax.axis_size("dp")
    fsdp = lax.axis_size("fsdp")
    n = dp * fsdp
    rows, width = grad_rows.shape
    seq = rows * fsdp
    cols = width // fsdp
    own_rows = width // n
    shape = jax.ShapeDtypeStruct
    dma = pltpu.SemaphoreType.DMA
    vmem = pltpu.VMEM
    anywhere = pl.BlockSpec(memory_space=pl.ANY)
    inside = pl.BlockSpec(memory_space=pltpu.VMEM)
    return pl.pallas_call(
        functools.partial(attention_back_kernel, dp, fsdp),
        out_shape=(
            shape((rows, width), F32),
            shape((8, 2 * cols), F32),
            shape((fsdp, own_rows, 4 * cols), BF16),
            shape(inner_in.shape, BF16),
            shape(outer_in.shape, BF16),
        ),
        in_specs=[anywhere] * 4 + [inside] * 6 + [anywhere] * 2,
        out_specs=(inside, inside, inside, anywhere, anywhere),
        scratch_shapes=[
            vmem((fsdp, seq, cols), BF16),
            vmem((width, 4 * cols), BF16),
            vmem((seq, width), BF16),
            vmem((seq, cols), BF16),
            vmem((fsdp, seq, cols), BF16),
            vmem((4, seq, cols), BF16),
            vmem((4, seq, cols), BF16),
            vmem((2, seq // 2, cols), BF16),
            vmem((2, seq, cols), BF16),
            vmem((fsdp, rows, width), BF16),
            vmem((4, rows, width), BF16),
            vmem((4, rows, width), BF16),
            vmem((2, rows // 2, width), BF16),
            vmem((2, rows, width), BF16),
            vmem((seq, cols), BF16),
            vmem((seq, cols), F32),
            vmem((seq, cols), F32),
            vmem((seq, cols), F32),
            vmem((seq, 2 * cols), F32),
            vmem((seq, 3 * cols), BF16),
            vmem((8, seq), F32),
            vmem((fsdp, 8, seq), F32),
            vmem((width, 4 * cols), BF16),
            vmem((dp, fsdp * own_rows, 4 * cols), BF16),
            vmem((fsdp, own_rows, 4 * cols), BF16),
            dma((6,)),
            dma((n,)),
            dma((n,)),
            dma((fsdp,)),
            dma((fsdp,)),
            dma((fsdp,)),
            dma((fsdp,)),
            dma((8,)),
            dma((8,)),
            dma((8,)),
            dma((8,)),
            dma((fsdp,)),
            dma((fsdp,)),
            dma((dp,)),
            dma((dp,)),
            dma((dp,)),
            dma((dp,)),
            dma((fsdp,)),
            dma((fsdp,)),
        ],
        compiler_params=pltpu.CompilerParams(
            collective_id=ident, has_side_effects=True, vmem_limit_bytes=63 * 1024 * 1024
        ),
    )(grad_rows, attended, weight, normed, qkv, unit, scale, gain, turn, live, inner_in, outer_in)


def expert_kernel(
    dp,
    x_in,
    c_all,
    gates,
    inner_in,
    outer_in,
    sums,
    gate_out,
    inner_out,
    outer_out,
    gathered,
    far,
    xv,
    cv,
    wi,
    wo,
    gi,
    go,
    ggu,
    act,
    gv,
    part,
    held,
    core_in,
    half_in,
    full_in,
    local,
    z_send,
    z_recv,
    a_send,
    a_recv,
    b_send,
    b_recv,
    k_send,
    k_recv,
    c_send,
    c_recv,
    s1_send,
    s1_recv,
    s2_send,
    s2_recv,
    o_send,
    o_recv,
    credit,
):
    rows, width = x_in.shape
    half = rows // 2
    z = lax.axis_index("dp")
    f = lax.axis_index("fsdp")
    core = lax.rem(f, 2)
    chip = f // 2
    xbit = lax.rem(chip, 2)
    ybit = chip // 2
    chip_x = ybit * 2 + (1 - xbit)
    chip_y = (1 - ybit) * 2 + xbit
    chip_d = (1 - ybit) * 2 + (1 - xbit)
    fx = chip_x * 2 + core
    fy = chip_y * 2 + core
    fd = chip_d * 2 + core
    fc = chip * 2 + (1 - core)
    to_x = {"fsdp": fx}
    to_y = {"fsdp": fy}
    to_c = {"fsdp": fc}
    upper = pl.ds(0, half)
    lower = pl.ds(half, half)

    def remote(src, dst, send, recv, device):
        return pltpu.make_async_remote_copy(
            src, dst, send, recv, device_id=device, device_id_type=MESH_ID
        )

    def plane_at(s):
        return lax.rem(z + 1 + s, dp)

    def far_copy(i):
        return remote(
            x_in,
            gathered.at[z, f],
            z_send.at[i],
            z_recv.at[i],
            {"dp": lax.rem(z + dp - i, dp)},
        )

    def gather_one(s):
        block = gathered.at[plane_at(s), f]
        return (
            remote(block.at[upper], block.at[upper], a_send.at[s, 0], a_recv.at[s, 0], to_x),
            remote(block.at[lower], block.at[lower], a_send.at[s, 1], a_recv.at[s, 1], to_y),
        )

    def gather_two(s):
        p = plane_at(s)
        copies = []
        for i, (owner, piece, device) in enumerate(
            ((f, upper, to_y), (fx, upper, to_y), (f, lower, to_x), (fy, lower, to_x))
        ):
            ref = gathered.at[p, owner, piece]
            copies.append(remote(ref, ref, b_send.at[s, i], b_recv.at[s, i], device))
        return copies

    def gather_core(s):
        p = plane_at(s)
        copies = []
        for i, owner in enumerate((f, fx, fy, fd)):
            ref = gathered.at[p, owner]
            copies.append(remote(ref, ref, k_send.at[s, i], k_recv.at[s, i], to_c))
        return copies

    def block_rows(owner):
        return pl.ds(pl.multiple_of(owner * rows, rows), rows)

    def core_copy(k, j):
        return remote(
            part.at[k, block_rows(j * 2 + 1 - core)],
            core_in.at[k, j],
            c_send.at[k, j],
            c_recv.at[k, j],
            to_c,
        )

    def half_copies(k):
        return (
            remote(
                held.at[k, chip_d, upper], half_in.at[k, 0], s1_send.at[k, 0], s1_recv.at[k, 0], to_x
            ),
            remote(
                held.at[k, chip_d, lower], half_in.at[k, 1], s1_send.at[k, 1], s1_recv.at[k, 1], to_y
            ),
        )

    def full_copies(k):
        return (
            remote(held.at[k, chip_x], full_in.at[k, 0], s2_send.at[k, 0], s2_recv.at[k, 0], to_x),
            remote(held.at[k, chip_y], full_in.at[k, 1], s2_send.at[k, 1], s2_recv.at[k, 1], to_y),
        )

    def out_copy(s, k):
        return remote(
            held.at[k, chip], far.at[k, z], o_send.at[s, k], o_recv.at[s, k], {"dp": plane_at(s)}
        )

    def add_core():
        for k in range(2):
            for j in range(4):
                core_copy(k, j).wait()
            def one(j, carry):
                held[k, j] = (
                    part[k, block_rows(j * 2 + core)].astype(F32) + core_in[k, j].astype(F32)
                ).astype(BF16)
                return carry
            lax.fori_loop(0, 4, one, 0)
        pl.semaphore_signal(credit, inc=1, device_id=to_c, device_id_type=MESH_ID)

    def start_half():
        for k in range(2):
            for copy in half_copies(k):
                copy.start()

    def pass_full():
        for k in range(2):
            for copy in half_copies(k):
                copy.wait()
            held[k, chip_y, upper] = (
                held[k, chip_y, upper].astype(F32) + half_in[k, 0].astype(F32)
            ).astype(BF16)
            held[k, chip_x, lower] = (
                held[k, chip_x, lower].astype(F32) + half_in[k, 1].astype(F32)
            ).astype(BF16)
            for copy in full_copies(k):
                copy.start()

    def total_here(k):
        for copy in full_copies(k):
            copy.wait()
        return held[k, chip].astype(F32) + full_in[k, 0].astype(F32) + full_in[k, 1].astype(F32)

    barrier = pltpu.get_barrier_semaphore()
    for device in (to_x, to_y, to_c):
        pl.semaphore_signal(barrier, inc=1, device_id=device, device_id_type=MESH_ID)
    for i in range(1, dp):
        pl.semaphore_signal(
            barrier, inc=1, device_id={"dp": lax.rem(z + i, dp)}, device_id_type=MESH_ID
        )
    pl.semaphore_wait(barrier, 3 + dp - 1)

    for i in range(1, dp):
        far_copy(i).start()
    loads = [pltpu.make_async_copy(x_in, gathered.at[z, f], local.at[0])]
    for q in range(4):
        loads.append(pltpu.make_async_copy(inner_in.at[:, q], wi.at[q], local.at[1 + q]))
    for e in range(2):
        loads.append(pltpu.make_async_copy(outer_in.at[:, e], wo.at[e], local.at[5 + e]))
    for load in loads:
        load.start()
    gi[...] = jnp.zeros_like(gi)
    go[...] = jnp.zeros_like(go)
    for load in loads:
        load.wait()

    def begin_gather(s):
        @pl.when(s < dp - 1)
        def _():
            far_copy(s + 1).wait_recv()

        for copy in gather_one(s):
            copy.start()

    def middle_gather(s):
        for copy in gather_one(s):
            copy.wait_recv()
        for copy in gather_two(s):
            copy.start()

    def end_gather(s):
        for copy in gather_two(s):
            copy.wait_recv()
        for copy in gather_core(s):
            copy.start()

    begin_gather(0)
    middle_gather(0)
    begin_gather(1)
    end_gather(0)

    inner_rows = wi.shape[1] * wi.shape[2]
    ff_here = wo.shape[1] * wo.shape[2]
    tile = xv.shape[0] // 2

    def tile_step(t):
        r = pl.ds(pl.multiple_of(t * tile, tile), tile)
        x = xv[r, :]
        c = cv[r, :]
        for e in range(2):
            gate = dot(x, wi[e].reshape(inner_rows, ff_here), ((1,), (0,)))
            up = dot(x, wi[2 + e].reshape(inner_rows, ff_here), ((1,), (0,)))
            back = dot(c, wo[e].reshape(ff_here, width), ((1,), (1,)))
            sigmoid = 1.0 / (1.0 + jnp.exp(-gate))
            silu = gate * sigmoid
            active = (silu * up).astype(BF16).astype(F32)
            weight = gv[r, e : e + 1]
            gv[r, 8 + e : 9 + e] = jnp.sum(active * back, axis=-1, keepdims=True)
            act[e, r, :] = (weight * active).astype(BF16)
            back = weight * back
            ggu[e, r, :] = (back * up * sigmoid * (1.0 + gate * (1.0 - sigmoid))).astype(BF16)
            ggu[2 + e, r, :] = (back * silu).astype(BF16)
        step = 512
        for i in range(width // step):
            col = pl.ds(i * step, step)
            blocks = pl.ds(i * step // wi.shape[2], step // wi.shape[2])
            total = dot(act[0, r, :], wo[0, :, :, col].reshape(ff_here, step), ((1,), (0,)))
            total += dot(act[1, r, :], wo[1, :, :, col].reshape(ff_here, step), ((1,), (0,)))
            part[0, r, col] = total.astype(BF16)
            total = dot(ggu[0, r, :], wi[0, blocks].reshape(step, ff_here), ((1,), (1,)))
            for q in range(1, 4):
                total += dot(ggu[q, r, :], wi[q, blocks].reshape(step, ff_here), ((1,), (1,)))
            part[1, r, col] = total.astype(BF16)

    def weight_step():
        def inner_part(i, carry):
            col = pl.ds(pl.multiple_of(i * 256, 256), 256)
            xt = xv[:, col]
            for q in range(4):
                gi[q, col, :] += dot(xt, ggu[q], ((0,), (0,)))
            return carry

        lax.fori_loop(0, width // 256, inner_part, 0)

        def outer_part(i, carry):
            col = pl.ds(pl.multiple_of(i * 512, 512), 512)
            ct = cv[:, col]
            for e in range(2):
                go[e, :, col] += dot(act[e], ct, ((0,), (0,)))
            return carry

        lax.fori_loop(0, width // 512, outer_part, 0)

    def chunk(s, carry):
        p = plane_at(s)
        c_load = pltpu.make_async_copy(c_all.at[p], cv, local.at[1])
        g_load = pltpu.make_async_copy(gates.at[p], gv, local.at[2])
        c_load.start()
        g_load.start()
        for copy in gather_core(s):
            copy.wait_recv()
        for j in range(8):
            pltpu.make_async_copy(
                gathered.at[p, j], xv.at[pl.ds(j * rows, rows)], local.at[3 + j]
            ).start()
        c_load.wait()
        g_load.wait()
        for j in range(8):
            pltpu.make_async_copy(
                gathered.at[p, j], xv.at[pl.ds(j * rows, rows)], local.at[3 + j]
            ).wait()
        tile_step(0)

        @pl.when(s > 0)
        def _():
            pass_full()

        @pl.when(s < dp - 1)
        def _():
            middle_gather(s + 1)

        @pl.when(s < dp - 2)
        def _():
            begin_gather(s + 2)

        tile_step(1)
        g_store = pltpu.make_async_copy(gv, gate_out.at[p], local.at[2])
        g_store.start()

        @pl.when(s > 0)
        def _():
            pl.semaphore_wait(credit, 1)

        for k in range(2):
            for j in range(4):
                core_copy(k, j).start()
        weight_step()

        @pl.when(s > 0)
        def _():
            for k in range(2):
                held[k, chip] = total_here(k).astype(BF16)
                out_copy(s - 1, k).start()
            for k in range(2):
                out_copy(s - 1, k).wait_send()

        add_core()
        start_half()

        @pl.when(s < dp - 1)
        def _():
            end_gather(s + 1)

        g_store.wait()
        return carry

    lax.fori_loop(0, dp, chunk, 0)

    pass_full()
    for q in range(4):
        wi[q] = gi[q].astype(BF16).reshape(wi.shape[1:])
    for e in range(2):
        wo[e] = go[e].astype(BF16).reshape(wo.shape[1:])
    stores = []
    for q in range(4):
        stores.append(pltpu.make_async_copy(wi.at[q], inner_out.at[:, q], local.at[q]))
    for e in range(2):
        stores.append(pltpu.make_async_copy(wo.at[e], outer_out.at[:, e], local.at[4 + e]))
    for store in stores:
        store.start()
    pl.semaphore_wait(credit, 1)
    for i in range(1, dp):
        for k in range(2):
            remote(
                held.at[k, chip],
                far.at[k, lax.rem(z + dp - i, dp)],
                o_send.at[i - 1, k],
                o_recv.at[i - 1, k],
                to_x,
            ).wait_recv()
    fetch = []
    for i in range(1, dp):
        for k in range(2):
            fetch.append(
                pltpu.make_async_copy(
                    far.at[k, lax.rem(z + i, dp)], core_in.at[k, i], local.at[6 + (i - 1) * 2 + k]
                )
            )
    for copy in fetch:
        copy.start()
    for copy in fetch:
        copy.wait()
    for k in range(2):
        total = total_here(k)
        for i in range(1, dp):
            total += core_in[k, i].astype(F32)
        sums[k] = total
    for store in stores:
        store.wait()
    for i in range(1, dp):
        far_copy(i).wait_send()

    def settle(s, carry):
        for copy in (*gather_one(s), *gather_two(s), *gather_core(s)):
            copy.wait_send()
        return carry

    lax.fori_loop(0, dp, settle, 0)


def expert_pass(x_in, c_all, gates, inner_in, outer_in, ident):
    dp = lax.axis_size("dp")
    fsdp = lax.axis_size("fsdp")
    rows, width = x_in.shape
    n, four, own_rows, ff_here = inner_in.shape
    _, two, out_rows, _ = outer_in.shape
    chunk = fsdp * rows
    shape = jax.ShapeDtypeStruct
    dma = pltpu.SemaphoreType.DMA
    anywhere = pl.BlockSpec(memory_space=pl.ANY)
    got = pl.pallas_call(
        functools.partial(expert_kernel, dp),
        out_shape=(
            shape((2, rows, width), F32),
            shape((dp, chunk, 128), F32),
            shape(inner_in.shape, BF16),
            shape(outer_in.shape, BF16),
            shape((dp, fsdp, rows, width), BF16),
            shape((2, dp, rows, width), BF16),
        ),
        in_specs=[anywhere] * 5,
        out_specs=(pl.BlockSpec(memory_space=pltpu.VMEM),) + (anywhere,) * 5,
        scratch_shapes=[
            pltpu.VMEM((chunk, width), BF16),
            pltpu.VMEM((chunk, width), BF16),
            pltpu.VMEM((four, n, own_rows, ff_here), BF16),
            pltpu.VMEM((two, fsdp, out_rows, width), BF16),
            pltpu.VMEM((four, width, ff_here), F32),
            pltpu.VMEM((two, ff_here, width), F32),
            pltpu.VMEM((four, chunk, ff_here), BF16),
            pltpu.VMEM((two, chunk, ff_here), BF16),
            pltpu.VMEM((chunk, 128), F32),
            pltpu.VMEM((2, chunk, width), BF16),
            pltpu.VMEM((2, 4, rows, width), BF16),
            pltpu.VMEM((2, 4, rows, width), BF16),
            pltpu.VMEM((2, 2, rows // 2, width), BF16),
            pltpu.VMEM((2, 2, rows, width), BF16),
            dma((12 + 2 * dp,)),
            dma((dp,)),
            dma((dp,)),
            dma((dp, 2)),
            dma((dp, 2)),
            dma((dp, 4)),
            dma((dp, 4)),
            dma((dp, 4)),
            dma((dp, 4)),
            dma((2, 4)),
            dma((2, 4)),
            dma((2, 2)),
            dma((2, 2)),
            dma((2, 2)),
            dma((2, 2)),
            dma((dp, 2)),
            dma((dp, 2)),
            pltpu.SemaphoreType.REGULAR,
        ],
        compiler_params=pltpu.CompilerParams(
            collective_id=ident, has_side_effects=True, vmem_limit_bytes=63 * 1024 * 1024
        ),
    )(x_in, c_all, gates, inner_in, outer_in)
    return got[:4]


def expert_pass_dense(normed2, grad_all, gates, inner_weight, outer_weight):
    n, parts, own_rows, ff_here = inner_weight.shape
    experts_here = parts // 2
    inner = experts_here * ff_here
    width = n * own_rows
    tokens = grad_all.shape[0]
    gates = gates[:, :, None]
    rows_all = lax.all_gather(normed2, BOTH, axis=0, tiled=True)
    inner_block = inner_weight.transpose(0, 2, 1, 3).reshape(width, 2 * inner)
    outer_shape = outer_weight.shape
    outer_block = outer_weight.transpose(1, 0, 2, 3).reshape(inner, width)
    gate_up = dot(rows_all, inner_block, ((1,), (0,)))
    gate = gate_up[:, :inner]
    up = gate_up[:, inner:]
    sigmoid = jax.nn.sigmoid(gate)
    silu = gate * sigmoid
    activation = (silu * up).astype(BF16).astype(F32)
    grad_act = dot(grad_all, outer_block, ((1,), (1,)))
    grad_gates = jnp.sum(
        (activation * grad_act).reshape(tokens, experts_here, ff_here), axis=-1
    )
    by_part = (tokens, experts_here, ff_here)
    activation = (activation.reshape(by_part) * gates).reshape(tokens, inner).astype(BF16)
    grad_act = (grad_act.reshape(by_part) * gates).reshape(tokens, inner)
    grad_gate_up = jnp.concatenate(
        [grad_act * up * sigmoid * (1.0 + gate * (1.0 - sigmoid)), grad_act * silu], axis=1
    ).astype(BF16)
    expert_sum = dot(activation, outer_block, ((1,), (0,))).astype(BF16)
    expert_sum = lax.psum_scatter(expert_sum, BOTH, scatter_dimension=0, tiled=True).astype(F32)
    if tokens > 8192:
        grad_gate_up, expert_sum = lax.optimization_barrier((grad_gate_up, expert_sum))
    grad_rows = dot(grad_gate_up, inner_block, ((1,), (1,))).astype(BF16)
    grad_rows = lax.psum_scatter(grad_rows, BOTH, scatter_dimension=0, tiled=True).astype(F32)
    inner_grad = dot(rows_all, grad_gate_up, ((0,), (0,))).astype(BF16)
    outer_grad = dot(activation, grad_all, ((0,), (0,))).astype(BF16)
    inner_grad = inner_grad.reshape(n, own_rows, parts, ff_here).transpose(0, 2, 1, 3)
    outer_grad = outer_grad.reshape(experts_here, outer_shape[0], outer_shape[2], width)
    return expert_sum, grad_rows, grad_gates, inner_grad, outer_grad.transpose(1, 0, 2, 3)


def body(
    hidden_in,
    lengths,
    routes,
    attn_gain,
    query_gain,
    key_gain,
    ffn_gain,
    qkv_weight,
    out_weight,
    router_weight,
    expert_in,
    expert_out,
    cotangent,
):
    rows, width = hidden_in.shape
    dp = lax.axis_size("dp")
    fsdp = lax.axis_size("fsdp")
    fused = fsdp == 8
    n = dp * fsdp
    experts = router_weight.shape[1]
    seq = rows * fsdp
    tokens = rows * n
    own_rows = width // n
    heads_here = HEADS // fsdp
    cols = heads_here * HEAD_DIM
    experts_here = experts // fsdp
    ff = expert_out.shape[0] * n
    ff_here = ff // dp
    z = lax.axis_index("dp")
    f = lax.axis_index("fsdp")
    valid = lengths[z]
    scaling = HEAD_DIM ** (-0.5)

    small = jnp.concatenate(
        [attn_gain, query_gain, key_gain, ffn_gain, router_weight.reshape(-1)]
    )
    small_rows = -(-small.size // 2048) * 16
    small = exchange(tiles_of(small, small_rows), BOTH, 0, False).reshape(n, -1)
    gains = small[:, : 4 * own_rows].reshape(n, 4, own_rows).transpose(1, 0, 2)
    gains = gains.reshape(4, width).astype(F32)
    router_full = small[:, 4 * own_rows : 4 * own_rows + own_rows * experts]
    router_full = router_full.reshape(width, experts)
    gain_attn, gain_query, gain_key, gain_ffn = gains[0], gains[1], gains[2], gains[3]

    attn_weight = jnp.concatenate(
        [
            qkv_weight.reshape(own_rows, 3, fsdp, cols),
            out_weight.reshape(own_rows, 1, fsdp, cols),
        ],
        axis=1,
    )
    attn_weight = attn_weight.transpose(2, 0, 1, 3).reshape(fsdp, own_rows, 4 * cols)
    inner_weight = expert_in.reshape(own_rows, fsdp, experts_here, 2, dp, ff_here)
    inner_weight = inner_weight.transpose(4, 1, 3, 2, 0, 5)
    inner_weight = inner_weight.reshape(n, 2 * experts_here, own_rows, ff_here)
    outer_weight = expert_out.reshape(-1, fsdp, experts_here, width).transpose(1, 2, 0, 3)
    live_mask = (f * rows + jnp.arange(rows, dtype=jnp.int32) < valid).astype(F32)[:, None]
    grad_total = cotangent.astype(F32) * live_mask

    here = f * cols
    qk_gain = jnp.stack(
        [
            lax.dynamic_slice(gain_query, (here,), (cols,)),
            lax.dynamic_slice(gain_key, (here,), (cols,)),
        ]
    )
    pos = jnp.arange(seq, dtype=jnp.int32)
    frequency = jnp.power(10000.0, -jnp.arange(HEAD_DIM // 2, dtype=F32) * 2.0 / HEAD_DIM)
    angles = pos.astype(F32)[:, None] * frequency[None, :]
    cosine = jnp.cos(angles)[:, None, None, :]
    sine = jnp.sin(angles)[:, None, None, :]

    if fused:
        gain_wide = jnp.broadcast_to(qk_gain.reshape(1, 2 * cols), (8, 2 * cols))
        turn = jnp.stack(
            [
                jnp.concatenate([cosine, cosine], axis=-1).reshape(seq, HEAD_DIM),
                jnp.concatenate([sine, -sine], axis=-1).reshape(seq, HEAD_DIM),
            ]
        )
        live_keys = jnp.broadcast_to((pos < valid).astype(F32)[None], (8, seq))
        (
            branch,
            qkv,
            qk_unit,
            qk_scale,
            normed_all,
            attn_weight,
            attended_all,
            grad_all,
            inner_weight,
            outer_weight,
        ) = attention_forward(
            hidden_in,
            grad_total.astype(BF16),
            attn_weight,
            inner_weight,
            outer_weight,
            jnp.broadcast_to(gain_attn[None], (8, width)),
            gain_wide,
            turn,
            live_keys,
            10,
        )
        branch = branch.astype(F32)
    else:
        attn_weight = lax.all_to_all(attn_weight, "fsdp", 0, 0, tiled=True)
        attn_weight = lax.all_gather(
            attn_weight.reshape(fsdp * own_rows, 4 * cols), "dp", axis=0, tiled=True
        )
        qkv_here = attn_weight[:, : 3 * cols]
        out_here = attn_weight[:, 3 * cols :]
        inner_weight = lax.all_to_all(inner_weight, BOTH, 0, 0, tiled=True)
        outer_weight = lax.all_to_all(outer_weight, "fsdp", 0, 0, tiled=True)
        hidden_all = lax.all_gather(hidden_in, "fsdp", axis=0, tiled=True).astype(F32)
        normed_all = (hidden_all * rms_scale(hidden_all) * gain_attn).astype(BF16)
        mixed = dot(normed_all, qkv_here, ((1,), (0,)))
        raw = mixed[:, : 2 * cols].reshape(seq, 2, cols)
        squares = plane_sum(jnp.sum(raw * raw, axis=-1), 1)
        qk_scale = lax.rsqrt(squares / width + EPS)[:, :, None]
        qk_unit = raw * qk_scale
        shape4 = (seq, 2, heads_here, HEAD_DIM)
        turned = rotate((qk_unit * qk_gain).reshape(shape4), cosine, sine, 1.0).astype(BF16)
        query = turned[:, 0]
        key = turned[:, 1]
        value = mixed[:, 2 * cols :].astype(BF16).reshape(seq, heads_here, HEAD_DIM)
        allowed = ((pos[None, :] <= pos[:, None]) & (pos[None, :] < valid))[None]
        scores = jnp.einsum("qhd,khd->hqk", query, key, preferred_element_type=F32) * scaling
        masked = jnp.where(allowed, scores, -1e30)
        weights = jnp.exp(masked - jnp.max(masked, axis=-1, keepdims=True))
        weights = jnp.where(allowed, weights, 0.0)
        probs = weights / jnp.sum(weights, axis=-1, keepdims=True)
        probs_low = probs.astype(BF16)
        attended = jnp.einsum("hqk,khd->qhd", probs_low, value, preferred_element_type=F32)
        attended = attended.reshape(seq, cols).astype(BF16)
        attended_all = lax.all_gather(attended, "fsdp", axis=0, tiled=False)
        branch = jnp.einsum(
            "fsc,fcn->sn",
            attended_all,
            out_here.reshape(fsdp, cols, cols),
            preferred_element_type=F32,
        )
        branch = exchange(branch.astype(BF16).reshape(fsdp, rows, cols), ("fsdp",), 2, True)
        branch = branch.transpose(1, 0, 2).reshape(rows, width).astype(F32)
        grad_all = lax.all_gather(grad_total.astype(BF16), BOTH, axis=0, tiled=True)

    hidden = hidden_in.astype(F32)
    scale1 = rms_scale(hidden)
    unit1 = hidden * scale1
    middle = hidden + branch
    scale2 = rms_scale(middle)
    unit2 = middle * scale2
    normed2 = (unit2 * gain_ffn).astype(BF16)
    logits = dot(normed2, router_full, ((1,), (0,)))
    router_probs = jax.nn.softmax(logits, axis=-1)
    chosen = jnp.sum(
        (routes[:, :, None] == jnp.arange(experts, dtype=jnp.int32)[None, None, :]).astype(F32),
        axis=1,
    )

    gates = (router_probs * chosen).reshape(rows, fsdp, experts_here).transpose(1, 2, 0)
    gates = jnp.broadcast_to(gates[None], (dp, fsdp, experts_here, rows))
    gates = gates.reshape(n, experts_here, rows)
    gates = jnp.pad(gates, ((0, 0), (0, 8 - experts_here), (0, 0)))
    gates = exchange(gates, BOTH, 3, True)[:, :experts_here]
    gates = gates.transpose(0, 2, 1).reshape(tokens, experts_here)
    if fused:
        gates = jnp.pad(gates, ((0, 0), (0, 128 - experts_here))).reshape(dp, seq, 128)
        sums, grad_gates, inner_grad, outer_grad = expert_pass(
            normed2, grad_all.reshape(dp, seq, width), gates, inner_weight, outer_weight, 8
        )
        expert_sum = sums[0]
        grad_rows = sums[1]
        grad_gates = grad_gates.reshape(tokens, 128)[:, 8 : 8 + experts_here]
    else:
        expert_sum, grad_rows, grad_gates, inner_grad, outer_grad = expert_pass_dense(
            normed2, grad_all, gates, inner_weight, outer_weight
        )
    grad_gates = grad_gates.reshape(n, rows, experts_here).transpose(0, 2, 1)
    grad_gates = jnp.pad(grad_gates, ((0, 0), (0, 8 - experts_here), (0, 0)))
    grad_gates = exchange(grad_gates, BOTH, 4, True)[:, :experts_here]
    grad_gates = jnp.sum(grad_gates.reshape(dp, fsdp, experts_here, rows), axis=0)
    grad_router_probs = grad_gates.reshape(experts, rows).transpose(1, 0) * chosen

    block_total = middle + expert_sum
    squares = jnp.stack(
        [
            jnp.sum(live_mask * block_total * block_total),
            jnp.sum(live_mask * branch * branch),
            jnp.sum(live_mask * expert_sum * expert_sum),
        ]
    )

    grad_logits = router_probs * (
        grad_router_probs - jnp.sum(router_probs * grad_router_probs, axis=-1, keepdims=True)
    )
    grad_logits = grad_logits.astype(BF16)
    router_term = dot(normed2, grad_logits, ((0,), (0,)))
    grad_normed2 = grad_rows + dot(grad_logits, router_full, ((1,), (1,)))
    ffn_term = jnp.sum(grad_normed2 * unit2, axis=0)
    grad_middle = grad_total + norm_back(grad_normed2 * gain_ffn, unit2, scale2)

    if fused:
        grad_normed, qk_term, attn_grad, inner_grad, outer_grad = attention_back(
            grad_middle.astype(BF16),
            attended_all,
            attn_weight,
            normed_all,
            qkv,
            qk_unit,
            qk_scale,
            gain_wide,
            turn,
            live_keys,
            inner_grad,
            outer_grad,
            9,
        )
        qk_term = qk_term[0].reshape(2, cols)
    else:
        grad_cols = grad_middle.astype(BF16).reshape(rows, fsdp, cols).transpose(1, 0, 2)
        grad_cols = exchange(grad_cols, ("fsdp",), 5, True).reshape(seq, cols)
        out_grad = jnp.einsum("fsc,sn->fcn", attended_all, grad_cols, preferred_element_type=F32)
        grad_attended = jnp.einsum(
            "sn,fcn->fsc", grad_cols, out_here.reshape(fsdp, cols, cols), preferred_element_type=F32
        )
        grad_attended = lax.psum_scatter(
            grad_attended.astype(BF16).reshape(fsdp * seq, cols), "fsdp", scatter_dimension=0, tiled=True
        )
        grad_attended = grad_attended.reshape(seq, heads_here, HEAD_DIM)
        grad_probs = jnp.einsum("qhd,khd->hqk", grad_attended, value, preferred_element_type=F32)
        grad_scores = probs * (grad_probs - jnp.sum(probs * grad_probs, axis=-1, keepdims=True))
        grad_scores = grad_scores.astype(BF16)
        grad_query = jnp.einsum("hqk,khd->qhd", grad_scores, key, preferred_element_type=F32)
        grad_key = jnp.einsum("hqk,qhd->khd", grad_scores, query, preferred_element_type=F32)
        grad_value = jnp.einsum("hqk,qhd->khd", probs_low, grad_attended, preferred_element_type=F32)
        grad_qk = rotate(jnp.stack([grad_query, grad_key], axis=1) * scaling, cosine, sine, -1.0)
        grad_qk = grad_qk.reshape(seq, 2, cols)
        qk_term = jnp.sum(grad_qk * qk_unit, axis=0)
        grad_qk = grad_qk * qk_gain
        inner_means = plane_sum(jnp.sum(grad_qk * qk_unit, axis=-1), 6)[:, :, None] / width
        grad_qk = qk_scale * (grad_qk - qk_unit * inner_means)
        grad_qkv = jnp.concatenate(
            [grad_qk.reshape(seq, 2 * cols), grad_value.reshape(seq, cols)], axis=1
        ).astype(BF16)
        qkv_grad = dot(normed_all, grad_qkv, ((0,), (0,)))
        grad_normed = dot(grad_qkv, qkv_here, ((1,), (1,))).astype(BF16)
        grad_normed = lax.psum_scatter(grad_normed, "fsdp", scatter_dimension=0, tiled=True).astype(F32)
        attn_grad = jnp.concatenate([qkv_grad, out_grad.reshape(width, cols)], axis=1).astype(BF16)
        attn_grad = lax.psum_scatter(attn_grad, "dp", scatter_dimension=0, tiled=True)
        attn_grad = attn_grad.reshape(fsdp, own_rows, 4 * cols)
        attn_grad = lax.all_to_all(attn_grad, "fsdp", 0, 0, tiled=True)
        inner_grad = lax.all_to_all(inner_grad, BOTH, 0, 0, tiled=True)
        outer_grad = lax.all_to_all(outer_grad, "fsdp", 0, 0, tiled=True)
    inner_grad = inner_grad.reshape(dp, fsdp, 2, experts_here, own_rows, ff_here)
    inner_grad = inner_grad.transpose(4, 1, 3, 2, 0, 5).reshape(own_rows, experts, 2 * ff)
    outer_grad = outer_grad.transpose(2, 0, 1, 3).reshape(-1, experts, width)
    attn_grad = attn_grad.reshape(fsdp, own_rows, 4, cols).transpose(1, 2, 0, 3).astype(F32)
    attn_grad = attn_grad.reshape(own_rows, 4 * width)
    attn_term = jnp.sum(grad_normed * unit1, axis=0)
    hidden_grad = grad_middle + norm_back(grad_normed * gain_attn, unit1, scale1)

    qk_full = jnp.zeros((2, width), F32)
    qk_full = lax.dynamic_update_slice(qk_full, qk_term, (0, here))
    terms = jnp.concatenate([attn_term[None], qk_full, ffn_term[None]])
    terms = terms.reshape(4, n, own_rows).transpose(1, 0, 2).reshape(n, 4 * own_rows)
    terms = jnp.concatenate(
        [
            terms,
            router_term.reshape(n, own_rows * experts),
            jnp.broadcast_to(squares[None], (n, 3)),
        ],
        axis=1,
    )
    term_size = terms.shape[1]
    term_rows = -(-term_size // 1024) * 8
    terms = jnp.pad(terms, ((0, 0), (0, term_rows * 128 - term_size)))
    terms = exchange(terms.reshape(n, term_rows, 128), BOTH, 7, True)
    terms = jnp.sum(terms, axis=0).reshape(-1)
    gain_grads = terms[: 4 * own_rows].reshape(4, own_rows)
    router_grad = terms[4 * own_rows : 4 * own_rows + own_rows * experts]
    valid_cells = jnp.sum(lengths).astype(F32) * width
    stats = jnp.sqrt(terms[term_size - 3 : term_size] / valid_cells)

    return (
        block_total.astype(BF16),
        hidden_grad,
        gain_grads[0],
        gain_grads[1],
        gain_grads[2],
        gain_grads[3],
        attn_grad[:, : 3 * width],
        attn_grad[:, 3 * width :],
        router_grad.reshape(own_rows, experts),
        inner_grad.astype(F32),
        outer_grad.astype(F32),
        stats,
    )


def solution(mesh):
    one = P(BOTH)
    two = P(BOTH, None)
    three = P(BOTH, None, None)
    in_specs = (two, P(), two, one, one, one, one, two, two, two, three, three, two)
    out_specs = (two, two, one, one, one, one, two, two, two, three, three, P())
    return jax.shard_map(body, mesh=mesh, in_specs=in_specs, out_specs=out_specs, check_vma=False)
```

```python
import functools

import jax
import jax.numpy as jnp
from jax import lax
from jax.experimental import pallas as pl
from jax.experimental.pallas import tpu as pltpu
from jax.sharding import PartitionSpec as P

HEADS = 16
HEAD_DIM = 128
EPS = 1e-05
BOTH = ("dp", "fsdp")
MESH_ID = pl.DeviceIdType.MESH
F32 = jnp.float32
BF16 = jnp.bfloat16


def rms_scale(values_in):
    return lax.rsqrt(jnp.mean(values_in * values_in, axis=-1, keepdims=True) + EPS)


def norm_back(grad_in, unit_rows, scaling):
    return scaling * (grad_in - unit_rows * jnp.mean(grad_in * unit_rows, axis=-1, keepdims=True))


def rotate(values_in, cosine, sine, direction):
    half_width = values_in.shape[-1] // 2
    first_half = values_in[..., :half_width]
    second_half = values_in[..., half_width:]
    return jnp.concatenate(
        [
            first_half * cosine - direction * second_half * sine,
            second_half * cosine + direction * first_half * sine,
        ],
        axis=-1,
    )


def place(axes, fsdp, index):
    if axes == BOTH:
        return {"dp": index // fsdp, "fsdp": lax.rem(index, fsdp)}
    return {axes[0]: index}


def exchange_kernel(axes, n, fsdp, spread, x, o, send, recv, own):
    if axes == BOTH:
        me = lax.axis_index("dp") * fsdp + lax.axis_index("fsdp")
    else:
        me = lax.axis_index(axes[0])
    barrier = pltpu.get_barrier_semaphore()
    for k in range(1, n):
        peer = place(axes, fsdp, lax.rem(me + k, n))
        pl.semaphore_signal(barrier, inc=1, device_id=peer, device_id_type=MESH_ID)
    pl.semaphore_wait(barrier, n - 1)
    local = pltpu.make_async_copy(x.at[me] if spread else x, o.at[me], own)
    local.start()
    copies = []
    for k in range(1, n):
        target = lax.rem(me + k, n)
        copy = pltpu.make_async_remote_copy(
            x.at[target] if spread else x,
            o.at[me],
            send.at[k],
            recv.at[k],
            device_id=place(axes, fsdp, target),
            device_id_type=MESH_ID,
        )
        copy.start()
        copies.append(copy)
    local.wait()
    for copy in copies:
        copy.wait()


def exchange(x, axes, ident, spread):
    fsdp = lax.axis_size("fsdp")
    n = lax.axis_size(axes)
    shape = x.shape if spread else (n,) + x.shape
    return pl.pallas_call(
        functools.partial(exchange_kernel, axes, n, fsdp, spread),
        out_shape=jax.ShapeDtypeStruct(shape, x.dtype),
        in_specs=[pl.BlockSpec(memory_space=pl.ANY)],
        out_specs=pl.BlockSpec(memory_space=pl.ANY),
        scratch_shapes=[
            pltpu.SemaphoreType.DMA((n,)),
            pltpu.SemaphoreType.DMA((n,)),
            pltpu.SemaphoreType.DMA,
        ],
        compiler_params=pltpu.CompilerParams(collective_id=ident, has_side_effects=True),
    )(x)


def tiles_of(x, rows):
    flat = x.reshape(-1)
    return jnp.pad(flat, (0, rows * 128 - flat.shape[0])).reshape(rows, 128)


def plane_sum(x, ident):
    rows = -(-x.size // 1024) * 8
    got = exchange(tiles_of(x, rows), ("fsdp",), ident, False)
    return jnp.sum(got, axis=0).reshape(-1)[: x.size].reshape(x.shape)


def dot(a, b, dims):
    return lax.dot_general(a, b, (dims, ((), ())), preferred_element_type=F32)


HIGH = lax.Precision.HIGHEST


def remote(src, dst, send, recv, device):
    return pltpu.make_async_remote_copy(
        src, dst, send, recv, device_id=device, device_id_type=MESH_ID
    )


def greet_all(n, fsdp, me):
    barrier = pltpu.get_barrier_semaphore()
    for k in range(1, n):
        peer = place(BOTH, fsdp, lax.rem(me + k, n))
        pl.semaphore_signal(barrier, inc=1, device_id=peer, device_id_type=MESH_ID)
    pl.semaphore_wait(barrier, n - 1)


def reorder(get, put, outer, inner):
    total = outer * inner
    tile = 256
    step = 512

    def one(i, carry):
        row = i * tile + lax.broadcasted_iota(jnp.int32, (tile, total), 0)
        col = lax.broadcasted_iota(jnp.int32, (tile, total), 1)
        pick = jnp.where(lax.rem(row, outer) * inner + row // outer == col, 1.0, 0.0).astype(BF16)
        for c in range(2048 // step):
            lanes = pl.ds(c * step, step)
            put(i, tile, lanes, dot(pick, get(lanes), ((1,), (0,))).astype(BF16))
        return carry

    lax.fori_loop(0, total // tile, one, 0)


def corner_of(rows, shift, value):
    row = lax.broadcasted_iota(jnp.int32, (rows, 128), 0)
    lane = lax.broadcasted_iota(jnp.int32, (rows, 128), 1)
    return jnp.where(lane == row + shift, value, 0.0).astype(F32)


def exact_dot(a, b, dims):
    return lax.dot_general(
        a, b, (dims, ((), ())), precision=HIGH, preferred_element_type=F32
    )


class Plane:
    def __init__(self, f):
        self.f = f
        self.core = lax.rem(f, 2)
        self.chip = f // 2
        xbit = lax.rem(self.chip, 2)
        ybit = self.chip // 2
        self.chip_x = ybit * 2 + (1 - xbit)
        self.chip_y = (1 - ybit) * 2 + xbit
        self.chip_d = (1 - ybit) * 2 + (1 - xbit)
        self.fx = self.chip_x * 2 + self.core
        self.fy = self.chip_y * 2 + self.core
        self.fd = self.chip_d * 2 + self.core
        self.to_x = {"fsdp": self.fx}
        self.to_y = {"fsdp": self.fy}
        self.to_c = {"fsdp": self.chip * 2 + 1 - self.core}


class PlaneSum:
    def __init__(self, plane, part, held, core_in, half_in, full_in, send, recv):
        self.plane = plane
        self.part = part
        self.held = held
        self.core_in = core_in
        self.half_in = half_in
        self.full_in = full_in
        self.send = send
        self.recv = recv
        half = held.shape[1] // 2
        self.upper = pl.ds(0, half)
        self.lower = pl.ds(half, half)

    def core_copy(self, j):
        owner = j * 2 + 1 - self.plane.core
        return remote(
            self.part.at[owner],
            self.core_in.at[j],
            self.send.at[j],
            self.recv.at[j],
            self.plane.to_c,
        )

    def half_copies(self):
        block = self.held.at[self.plane.chip_d]
        send, recv, half_in = self.send, self.recv, self.half_in
        return (
            remote(block.at[self.upper], half_in.at[0], send.at[4], recv.at[4], self.plane.to_x),
            remote(block.at[self.lower], half_in.at[1], send.at[5], recv.at[5], self.plane.to_y),
        )

    def full_copies(self):
        held, full_in, send, recv = self.held, self.full_in, self.send, self.recv
        plane = self.plane
        return (
            remote(held.at[plane.chip_x], full_in.at[0], send.at[6], recv.at[6], plane.to_x),
            remote(held.at[plane.chip_y], full_in.at[1], send.at[7], recv.at[7], plane.to_y),
        )

    def start(self):
        for j in range(4):
            self.core_copy(j).start()

    def add_core(self):
        for j in range(4):
            self.core_copy(j).wait()

        def one(j, carry):
            own = self.part[j * 2 + self.plane.core].astype(F32)
            self.held[j] = (own + self.core_in[j].astype(F32)).astype(BF16)
            return carry

        lax.fori_loop(0, 4, one, 0)
        for copy in self.half_copies():
            copy.start()

    def pass_on(self):
        for copy in self.half_copies():
            copy.wait()
        held, half_in = self.held, self.half_in
        for chip, piece, i in (
            (self.plane.chip_y, self.upper, 0),
            (self.plane.chip_x, self.lower, 1),
        ):
            total = held[chip, piece].astype(F32) + half_in[i].astype(F32)
            held[chip, piece] = total.astype(BF16)
        for copy in self.full_copies():
            copy.start()

    def total(self):
        for copy in self.full_copies():
            copy.wait()
        total = self.held[self.plane.chip].astype(F32)
        return total + self.full_in[0].astype(F32) + self.full_in[1].astype(F32)


class PlaneGather:
    def __init__(self, plane, block, rows, send, recv):
        self.plane = plane
        self.block = block
        self.send = send
        self.recv = recv
        self.upper = pl.ds(0, rows // 2)
        self.lower = pl.ds(rows // 2, rows // 2)

    def same(self, ref, i, device):
        return remote(ref, ref, self.send(i), self.recv(i), device)

    def first(self):
        own = self.block(self.plane.f)
        return (
            self.same(own.at[self.upper], 0, self.plane.to_x),
            self.same(own.at[self.lower], 1, self.plane.to_y),
        )

    def second(self):
        plane = self.plane
        return (
            self.same(self.block(plane.f).at[self.upper], 2, plane.to_y),
            self.same(self.block(plane.fx).at[self.upper], 3, plane.to_y),
            self.same(self.block(plane.f).at[self.lower], 4, plane.to_x),
            self.same(self.block(plane.fy).at[self.lower], 5, plane.to_x),
        )

    def third(self):
        plane = self.plane
        owners = (plane.f, plane.fx, plane.fy, plane.fd)
        return [self.same(self.block(o), 6 + i, plane.to_c) for i, o in enumerate(owners)]

    def start(self):
        for copy in self.first():
            copy.start()

    def middle(self):
        for copy in self.first():
            copy.wait_recv()
        for copy in self.second():
            copy.start()

    def finish(self):
        for copy in self.second():
            copy.wait_recv()
        for copy in self.third():
            copy.start()

    def wait(self):
        for copy in self.third():
            copy.wait_recv()

    def settle(self):
        for copy in (*self.first(), *self.second(), *self.third()):
            copy.wait_send()


def attention_kernel(
    dp,
    fsdp,
    hidden,
    cot,
    weight_in,
    inner_in,
    outer_in,
    gain_attn,
    gain,
    turn,
    live,
    branch,
    qkv,
    unit,
    scale,
    normed,
    weight,
    attended,
    c_all,
    inner_out,
    outer_out,
    hid_v,
    normed_v,
    w_v,
    raw,
    stat,
    stat_in,
    att_v,
    cols_v,
    rows_v,
    inner_raw,
    inner_v,
    outer_raw,
    outer_v,
    local,
    w_send,
    w_recv,
    right_send,
    right_recv,
    left_send,
    left_recv,
    h_send,
    h_recv,
    t_send,
    t_recv,
    a_send,
    a_recv,
    b_send,
    b_recv,
    c_send,
    c_recv,
    z_send,
    z_recv,
    in_send,
    in_recv,
    out_send,
    out_recv,
):
    n = dp * fsdp
    z = lax.axis_index("dp")
    f = lax.axis_index("fsdp")
    me = z * fsdp + f
    plane = Plane(f)
    rows, width = hidden.shape
    seq, cols = cols_v.shape
    own_rows = weight_in.shape[1]
    slab = fsdp * own_rows
    scaling = HEAD_DIM ** (-0.5)
    greet_all(n, fsdp, me)

    def weight_rows(index):
        return pl.ds(pl.multiple_of(index * own_rows, own_rows), own_rows)

    def weight_copy(k):
        target = lax.rem(f + k, fsdp)
        return remote(
            weight_in.at[target],
            w_v.at[weight_rows(me)],
            w_send.at[k],
            w_recv.at[k],
            {"fsdp": target},
        )

    def slab_copy(p, near, far, send, recv):
        ref = w_v.at[pl.ds(pl.multiple_of(p * slab, slab), slab)]
        return remote(ref, ref, send.at[near], recv.at[near], {"dp": far})

    experts = inner_v.shape[0]
    here = experts // fsdp
    ff = width // 2
    part = ff // dp

    def inner_block(target, half):
        lanes = pl.ds(pl.multiple_of(half * ff + target // fsdp * part, part), part)
        owned = pl.ds(lax.rem(target, fsdp) * here, here)
        return inner_v.at[owned, :, lanes], inner_out.at[me, pl.ds(half * here, here)]

    def inner_copies(k):
        target = lax.rem(me + k, n)
        return [
            remote(
                *inner_block(target, half),
                in_send.at[k, half],
                in_recv.at[k, half],
                place(BOTH, fsdp, target),
            )
            for half in range(2)
        ]

    def outer_block(target):
        return outer_v.at[pl.ds(target * here, here)]

    def outer_copy(k):
        target = lax.rem(f + k, fsdp)
        return remote(
            outer_block(target), outer_out.at[f], out_send.at[k], out_recv.at[k], {"fsdp": target}
        )

    def cot_copy(i):
        return remote(
            cot,
            c_all.at[z, f],
            z_send.at[i],
            z_recv.at[i],
            {"dp": lax.rem(z + dp - i, dp)},
        )

    hidden_gather = PlaneGather(
        plane, lambda o: hid_v.at[o], rows, lambda i: h_send.at[i], lambda i: h_recv.at[i]
    )
    attended_gather = PlaneGather(
        plane, lambda o: att_v.at[o], seq, lambda i: a_send.at[i], lambda i: a_recv.at[i]
    )
    cot_gather = [
        PlaneGather(
            plane,
            lambda o, s=s: c_all.at[lax.rem(z + 1 + s, dp), o],
            rows,
            lambda i, s=s: c_send.at[s, i],
            lambda i, s=s: c_recv.at[s, i],
        )
        for s in range(dp)
    ]

    keeps = [
        pltpu.make_async_copy(hidden, hid_v.at[f], local.at[0]),
        pltpu.make_async_copy(weight_in.at[f], w_v.at[weight_rows(me)], local.at[1]),
        pltpu.make_async_copy(cot, c_all.at[z, f], local.at[2]),
        pltpu.make_async_copy(outer_in, outer_raw, local.at[3]),
        pltpu.make_async_copy(inner_in, inner_raw, local.at[4]),
    ]
    for copy in keeps:
        copy.start()
    for k in range(1, fsdp):
        weight_copy(k).start()
    keeps[0].wait()
    hidden_gather.start()
    keeps[1].wait()
    for k in range(1, fsdp):
        weight_copy(k).wait_recv()

    @pl.when(z < dp - 1)
    def _():
        slab_copy(z, 1, z + 1, right_send, right_recv).start()

    @pl.when(z > 0)
    def _():
        slab_copy(z, 1, z - 1, left_send, left_recv).start()

    hidden_gather.middle()
    keeps[2].wait()
    cot_gather[dp - 1].start()

    keeps[3].wait()
    outer_rows = outer_v.shape[1]

    def put_outer(i, tile, lanes, value):
        block = tile // outer_rows
        outer_v[pl.ds(i * block, block), :, lanes] = value.reshape(block, outer_rows, -1)

    reorder(lambda lanes: outer_raw[:, lanes], put_outer, outer_rows, experts)
    hidden_gather.finish()
    for k in range(1, fsdp):
        outer_copy(k).start()
    keeps[4].wait()

    def put_inner(i, tile, lanes, value):
        block = tile // own_rows
        inner_v[pl.ds(i * block, block), :, lanes] = value.reshape(block, own_rows, -1)

    reorder(lambda lanes: inner_raw[:, lanes], put_inner, own_rows, experts)
    owns = [
        pltpu.make_async_copy(outer_block(f), outer_out.at[f], local.at[3]),
        pltpu.make_async_copy(*inner_block(me, 0), local.at[4]),
        pltpu.make_async_copy(*inner_block(me, 1), local.at[5]),
    ]
    for copy in owns:
        copy.start()
    hidden_gather.wait()

    def norm_rows(i, carry):
        values = hid_v[i].astype(F32)
        values = values * lax.rsqrt(jnp.mean(values * values, axis=-1, keepdims=True) + EPS)
        r = pl.ds(pl.multiple_of(i * rows, rows), rows)
        normed_v[r, :] = (values * gain_attn[0:1, :]).astype(BF16)
        return carry

    lax.fori_loop(0, fsdp, norm_rows, 0)
    normed_store = pltpu.make_async_copy(normed_v, normed, local.at[0])
    normed_store.start()

    for d in range(1, dp):

        @pl.when(z >= d)
        def _(d=d):
            slab_copy(z - d, d, 0, right_send, right_recv).wait_recv()

            @pl.when(z < dp - 1)
            def _():
                slab_copy(z - d, d + 1, z + 1, right_send, right_recv).start()

        @pl.when(z + d < dp)
        def _(d=d):
            slab_copy(z + d, d, 0, left_send, left_recv).wait_recv()

            @pl.when(z > 0)
            def _():
                slab_copy(z + d, d + 1, z - 1, left_send, left_recv).start()

        if d == 1:
            cot_gather[dp - 1].middle()
        if d == 2:
            cot_gather[dp - 1].finish()

    for i in range(1, dp):
        cot_copy(i).start()
    for k in range(1, n):
        for copy in inner_copies(k):
            copy.start()
    weight_store = pltpu.make_async_copy(w_v, weight, local.at[1])
    weight_store.start()

    tile = 256

    def project(i, carry):
        r = pl.ds(pl.multiple_of(i * tile, tile), tile)
        for j in range(3):
            col = pl.ds(j * cols, cols)
            value = dot(normed_v[r, :], w_v[:, col], ((1,), (0,)))
            if j < 2:
                raw[r, col] = value
            else:
                qkv[2, r, :] = value.astype(BF16)
        return carry

    lax.fori_loop(0, seq // tile, project, 0)
    row = lax.broadcasted_iota(jnp.int32, (8, 2 * cols), 0)
    lane_of = lax.broadcasted_iota(jnp.int32, (8, 2 * cols), 1)
    chooser = jnp.where(lane_of // cols == row, 1.0, 0.0).astype(F32)
    stat[...] = lax.dot_general(
        chooser,
        raw[...] * raw[...],
        (((1,), (1,)), ((), ())),
        precision=HIGH,
        preferred_element_type=F32,
    )

    def stat_copy(k):
        return remote(
            stat, stat_in.at[f], t_send.at[k], t_recv.at[k], {"fsdp": lax.rem(f + k, fsdp)}
        )

    for k in range(1, fsdp):
        stat_copy(k).start()
    stat_in[f] = stat[...]
    for k in range(1, fsdp):
        stat_copy(k).wait_recv()
    sums = stat_in[0]
    for i in range(1, fsdp):
        sums = sums + stat_in[i]
    corner = jnp.where(
        lax.broadcasted_iota(jnp.int32, (8, 128), 0) == lax.broadcasted_iota(jnp.int32, (8, 128), 1),
        1.0 / width,
        0.0,
    ).astype(F32)
    means = lax.dot_general(
        sums, corner, (((0,), (0,)), ((), ())), precision=HIGH, preferred_element_type=F32
    )
    scale[...] = lax.rsqrt(means + EPS)
    for i in range(2):
        wide = pl.ds(i * cols, cols)
        unit[:, wide] = raw[:, wide] * scale[:, i : i + 1]
        for h in range(cols // HEAD_DIM):
            lane = pl.ds(i * cols + h * HEAD_DIM, HEAD_DIM)
            values = unit[:, lane] * gain[0:1, lane]
            values = values * turn[0] - pltpu.roll(values, HEAD_DIM // 2, 1) * turn[1]
            qkv[i, :, pl.ds(h * HEAD_DIM, HEAD_DIM)] = values.astype(BF16)

    def head(h, carry):
        lane = pl.ds(pl.multiple_of(h * HEAD_DIM, HEAD_DIM), HEAD_DIM)
        for t in range(seq // tile):
            r = pl.ds(t * tile, tile)
            extent = (t + 1) * tile
            upto = pl.ds(0, extent)
            scores = dot(qkv[0, r, lane], qkv[1, upto, lane], ((1,), (1,))) * scaling
            q_pos = t * tile + lax.broadcasted_iota(jnp.int32, (tile, extent), 0)
            k_pos = lax.broadcasted_iota(jnp.int32, (tile, extent), 1)
            allowed = (k_pos <= q_pos) & (live[0:1, 0:extent] > 0.0)
            masked = jnp.where(allowed, scores, -1e30)
            weights = jnp.exp(masked - jnp.max(masked, axis=-1, keepdims=True))
            weights = jnp.where(allowed, weights, 0.0)
            probs = weights / jnp.sum(weights, axis=-1, keepdims=True)
            att_v[f, r, lane] = dot(
                probs.astype(BF16), qkv[2, upto, lane], ((1,), (0,))
            ).astype(BF16)
        return carry

    lax.fori_loop(0, cols // HEAD_DIM, head, 0)
    attended_gather.start()
    for s in range(dp - 1):
        cot_copy(s + 1).wait_recv()
        cot_gather[s].start()
        if s == 0:
            attended_gather.middle()
    cot_gather[0].middle()
    attended_gather.finish()
    for s in range(1, dp - 1):
        cot_gather[s].middle()
    attended_gather.wait()
    attended_store = pltpu.make_async_copy(att_v, attended, local.at[2])
    attended_store.start()

    out_cols = pl.ds(3 * cols, cols)

    def project_out(i, carry):
        r = pl.ds(pl.multiple_of(i * tile, tile), tile)
        total = dot(att_v[0, r, :], w_v[pl.ds(0, cols), out_cols], ((1,), (0,)))
        for j in range(1, fsdp):
            total += dot(att_v[j, r, :], w_v[pl.ds(j * cols, cols), out_cols], ((1,), (0,)))
        cols_v[r, :] = total.astype(BF16)
        return carry

    lax.fori_loop(0, seq // tile, project_out, 0)

    def branch_copy(k):
        target = lax.rem(f + k, fsdp)
        return remote(
            cols_v.at[pl.ds(pl.multiple_of(target * rows, rows), rows)],
            rows_v.at[f],
            b_send.at[k],
            b_recv.at[k],
            {"fsdp": target},
        )

    for k in range(1, fsdp):
        branch_copy(k).start()
    rows_v[f] = cols_v[pl.ds(pl.multiple_of(f * rows, rows), rows), :]
    for s in range(dp - 1):
        cot_gather[s].finish()
    for k in range(1, fsdp):
        branch_copy(k).wait()
    for i in range(fsdp):
        branch[:, pl.ds(i * cols, cols)] = rows_v[i]

    for s in range(dp):
        cot_gather[s].wait()
        cot_gather[s].settle()
    hidden_gather.settle()
    attended_gather.settle()
    for i in range(1, dp):
        cot_copy(i).wait_send()

    @pl.when(z < dp - 1)
    def _():
        slab_copy(z, 1, z + 1, right_send, right_recv).wait_send()

    @pl.when(z > 0)
    def _():
        slab_copy(z, 1, z - 1, left_send, left_recv).wait_send()

    for d in range(1, dp):

        @pl.when((z >= d) & (z < dp - 1))
        def _(d=d):
            slab_copy(z - d, d + 1, z + 1, right_send, right_recv).wait_send()

        @pl.when((z + d < dp) & (z > 0))
        def _(d=d):
            slab_copy(z + d, d + 1, z - 1, left_send, left_recv).wait_send()

    for k in range(1, fsdp):
        weight_copy(k).wait_send()
        stat_copy(k).wait_send()
        outer_copy(k).wait()
    for k in range(1, n):
        for copy in inner_copies(k):
            copy.wait()
    for copy in owns:
        copy.wait()
    normed_store.wait()
    weight_store.wait()
    attended_store.wait()


def attention_forward(
    hidden, cot, weight_in, inner_in, outer_in, gain_attn, gain, turn, live, ident
):
    dp = lax.axis_size("dp")
    fsdp = lax.axis_size("fsdp")
    n = dp * fsdp
    rows, width = hidden.shape
    seq = rows * fsdp
    cols = width // fsdp
    shape = jax.ShapeDtypeStruct
    dma = pltpu.SemaphoreType.DMA
    vmem = pltpu.VMEM
    anywhere = pl.BlockSpec(memory_space=pl.ANY)
    inside = pl.BlockSpec(memory_space=pltpu.VMEM)
    pairs = [fsdp, dp + 1, dp + 1, 10, fsdp, 10, fsdp]
    sems = []
    for size in pairs:
        sems += [dma((size,)), dma((size,))]
    sems += [dma((dp, 10)), dma((dp, 10)), dma((dp,)), dma((dp,))]
    sems += [dma((n, 2)), dma((n, 2)), dma((fsdp,)), dma((fsdp,))]
    experts = inner_in.shape[1]
    out_rows = outer_in.shape[0]
    here = experts // fsdp
    return pl.pallas_call(
        functools.partial(attention_kernel, dp, fsdp),
        out_shape=(
            shape((rows, width), BF16),
            shape((3, seq, cols), BF16),
            shape((seq, 2 * cols), F32),
            shape((seq, 128), F32),
            shape((seq, width), BF16),
            shape((width, 4 * cols), BF16),
            shape((fsdp, seq, cols), BF16),
            shape((dp, fsdp, rows, width), BF16),
            shape((n, 2 * here, width // n, width // 2 // dp), BF16),
            shape((fsdp, here, out_rows, width), BF16),
        ),
        in_specs=[anywhere] * 5 + [inside] * 4,
        out_specs=(inside,) * 4 + (anywhere,) * 6,
        scratch_shapes=[
            vmem((fsdp, rows, width), BF16),
            vmem((seq, width), BF16),
            vmem((width, 4 * cols), BF16),
            vmem((seq, 2 * cols), F32),
            vmem((8, seq), F32),
            vmem((fsdp, 8, seq), F32),
            vmem((fsdp, seq, cols), BF16),
            vmem((seq, cols), BF16),
            vmem((fsdp, rows, cols), BF16),
            vmem((width // n * experts, width), BF16),
            vmem((experts, width // n, width), BF16),
            vmem((out_rows * experts, width), BF16),
            vmem((experts, out_rows, width), BF16),
            dma((6,)),
            *sems,
        ],
        compiler_params=pltpu.CompilerParams(
            collective_id=ident, has_side_effects=True, vmem_limit_bytes=63 * 1024 * 1024
        ),
    )(
        hidden,
        cot,
        weight_in,
        inner_in.reshape(-1, width),
        outer_in.reshape(-1, width),
        gain_attn,
        gain,
        turn,
        live,
    )


def attention_back_kernel(
    dp,
    fsdp,
    grad_rows,
    attended,
    weight,
    normed,
    qkv,
    unit,
    scale,
    gain,
    turn,
    live,
    grad_middle,
    hidden,
    gain_attn,
    terms,
    inner_in,
    outer_in,
    hidden_grad,
    terms_out,
    owned,
    inner_owned,
    outer_owned,
    inner_out,
    outer_out,
    att_v,
    w_v,
    normed_v,
    gcols,
    part1,
    held1,
    core1,
    half1,
    full1,
    part2,
    held2,
    core2,
    half2,
    full2,
    gatt,
    gq,
    gk,
    gval,
    gqk,
    gqkv,
    stat,
    stat_in,
    wgrad,
    z_in,
    wsum,
    term_v,
    term_in,
    local,
    v_send,
    v_recv,
    in_send,
    in_recv,
    out_send,
    out_recv,
    g_send,
    g_recv,
    s1_send,
    s1_recv,
    s2_send,
    s2_recv,
    t_send,
    t_recv,
    zo_send,
    zo_recv,
    zq_send,
    zq_recv,
    w_send,
    w_recv,
):
    n = dp * fsdp
    z = lax.axis_index("dp")
    f = lax.axis_index("fsdp")
    me = z * fsdp + f
    plane = Plane(f)
    rows, width = grad_rows.shape
    seq, cols = gcols.shape
    own_rows = width // n
    slab = fsdp * own_rows
    scaling = HEAD_DIM ** (-0.5)
    greet_all(n, fsdp, me)
    ff = width // 2
    ff_here = ff // dp

    def inner_place(half):
        lanes = pl.ds(pl.multiple_of(half * ff + z * ff_here, ff_here), ff_here)
        return inner_out.at[f, :, lanes]

    pair = outer_in.shape[1]
    outer_place = outer_out.at[f // 2, pl.ds(pl.multiple_of(lax.rem(f, 2) * pair, pair), pair)]

    loads = [
        pltpu.make_async_copy(attended, att_v, local.at[0]),
        pltpu.make_async_copy(weight, w_v, local.at[1]),
        pltpu.make_async_copy(normed, normed_v, local.at[2]),
        pltpu.make_async_copy(
            grad_rows.at[:, pl.ds(pl.multiple_of(f * cols, cols), cols)],
            gcols.at[pl.ds(pl.multiple_of(f * rows, rows), rows)],
            local.at[3],
        ),
    ]
    keeps = [
        pltpu.make_async_copy(inner_in.at[me, 0], inner_place(0), local.at[4]),
        pltpu.make_async_copy(inner_in.at[me, 1], inner_place(1), local.at[5]),
        pltpu.make_async_copy(outer_in.at[f], outer_place, local.at[6]),
    ]
    for copy in loads:
        copy.start()

    def cols_copy(k):
        target = lax.rem(f + k, fsdp)
        return remote(
            grad_rows.at[:, pl.ds(pl.multiple_of(target * cols, cols), cols)],
            gcols.at[pl.ds(pl.multiple_of(f * rows, rows), rows)],
            g_send.at[k],
            g_recv.at[k],
            {"fsdp": target},
        )

    def inner_copies(k):
        target = lax.rem(me + k, n)
        return [
            remote(
                inner_in.at[target, half],
                inner_place(half),
                in_send.at[k, half],
                in_recv.at[k, half],
                place(BOTH, fsdp, target),
            )
            for half in range(2)
        ]

    def outer_copy(k):
        target = lax.rem(f + k, fsdp)
        return remote(
            outer_in.at[target], outer_place, out_send.at[k], out_recv.at[k], {"fsdp": target}
        )

    def slab_rows(p):
        return pl.ds(pl.multiple_of(p * slab, slab), slab)

    def far_copy(i, col, send, recv):
        p = lax.rem(z + i, dp)
        return remote(
            wgrad.at[slab_rows(p), col], z_in.at[i, :, col], send.at[i], recv.at[i], {"dp": p}
        )

    qkv_cols = pl.ds(0, 3 * cols)
    out_cols = pl.ds(3 * cols, cols)

    for k in range(1, fsdp):
        cols_copy(k).start()
    for k in range(1, n):
        for copy in inner_copies(k):
            copy.start()
    for k in range(1, fsdp):
        outer_copy(k).start()
    for copy in keeps:
        copy.start()
    term_v[...] = terms[...]
    for copy in loads:
        copy.wait()
    for k in range(1, fsdp):
        cols_copy(k).wait_recv()

    def attended_back(i, carry):
        block = pl.ds(pl.multiple_of(i * cols, cols), cols)
        part1[i] = dot(gcols[...], w_v[block, out_cols], ((1,), (1,))).astype(BF16)
        return carry

    lax.fori_loop(0, fsdp, attended_back, 0)
    sum1 = PlaneSum(plane, part1, held1, core1, half1, full1, s1_send, s1_recv)
    sum1.start()

    def out_grads(i, carry):
        block = pl.ds(pl.multiple_of(i * cols, cols), cols)
        wgrad[block, out_cols] = dot(att_v[i], gcols[...], ((0,), (0,))).astype(BF16)
        return carry

    lax.fori_loop(0, fsdp // 2, out_grads, 0)
    sum1.add_core()
    lax.fori_loop(fsdp // 2, fsdp, out_grads, 0)
    for i in range(1, dp):
        far_copy(i, out_cols, zo_send, zo_recv).start()
    sum1.pass_on()
    gk[...] = jnp.zeros_like(gk)
    gval[...] = jnp.zeros_like(gval)
    gatt[...] = sum1.total().astype(BF16)

    tile = 256

    def head(h, carry):
        lane = pl.ds(pl.multiple_of(h * HEAD_DIM, HEAD_DIM), HEAD_DIM)
        for t in range(seq // tile):
            r = pl.ds(t * tile, tile)
            extent = (t + 1) * tile
            upto = pl.ds(0, extent)
            query = qkv[0, r, lane]
            key = qkv[1, upto, lane]
            value = qkv[2, upto, lane]
            grad = gatt[r, lane]
            scores = dot(query, key, ((1,), (1,))) * scaling
            q_pos = t * tile + lax.broadcasted_iota(jnp.int32, (tile, extent), 0)
            k_pos = lax.broadcasted_iota(jnp.int32, (tile, extent), 1)
            allowed = (k_pos <= q_pos) & (live[0:1, 0:extent] > 0.0)
            masked = jnp.where(allowed, scores, -1e30)
            weights = jnp.exp(masked - jnp.max(masked, axis=-1, keepdims=True))
            weights = jnp.where(allowed, weights, 0.0)
            probs = weights / jnp.sum(weights, axis=-1, keepdims=True)
            grad_probs = dot(grad, value, ((1,), (1,)))
            mean = jnp.sum(probs * grad_probs, axis=-1, keepdims=True)
            grad_scores = (probs * (grad_probs - mean)).astype(BF16)
            gq[r, lane] = dot(grad_scores, key, ((1,), (0,)))
            gk[upto, lane] += dot(grad_scores, query, ((0,), (0,)))
            gval[upto, lane] += dot(probs.astype(BF16), grad, ((0,), (0,)))
        return carry

    lax.fori_loop(0, cols // HEAD_DIM, head, 0)

    heads_here = cols // HEAD_DIM
    for i, source in enumerate((gq, gk)):
        for h in range(heads_here):
            lane = pl.ds(h * HEAD_DIM, HEAD_DIM)
            wide = pl.ds(i * cols + h * HEAD_DIM, HEAD_DIM)
            grad = source[:, lane] * scaling
            grad = grad * turn[0] + pltpu.roll(grad, HEAD_DIM // 2, 1) * turn[1]
            place_lanes = pl.ds(pl.multiple_of(f * cols + h * HEAD_DIM, HEAD_DIM), HEAD_DIM)
            term_v[1 + i : 2 + i, place_lanes] = jnp.sum(
                grad * unit[:, wide], axis=0, keepdims=True
            )
            gqk[:, wide] = grad * gain[0:1, wide]
    row = lax.broadcasted_iota(jnp.int32, (8, 2 * cols), 0)
    lane_of = lax.broadcasted_iota(jnp.int32, (8, 2 * cols), 1)
    chooser = jnp.where(lane_of // cols == row, 1.0, 0.0).astype(F32)
    stat[...] = lax.dot_general(
        chooser,
        gqk[...] * unit[...],
        (((1,), (1,)), ((), ())),
        precision=HIGH,
        preferred_element_type=F32,
    )

    def stat_copy(k):
        return remote(
            stat, stat_in.at[f], t_send.at[k], t_recv.at[k], {"fsdp": lax.rem(f + k, fsdp)}
        )

    for k in range(1, fsdp):
        stat_copy(k).start()
    stat_in[f] = stat[...]
    gqkv[:, pl.ds(2 * cols, cols)] = gval[...].astype(BF16)
    for k in range(1, fsdp):
        stat_copy(k).wait_recv()
    sums = stat_in[0]
    for i in range(1, fsdp):
        sums = sums + stat_in[i]
    corner = jnp.where(
        lax.broadcasted_iota(jnp.int32, (8, 128), 0) == lax.broadcasted_iota(jnp.int32, (8, 128), 1),
        1.0 / width,
        0.0,
    ).astype(F32)
    means = lax.dot_general(
        sums, corner, (((0,), (0,)), ((), ())), precision=HIGH, preferred_element_type=F32
    )
    for i in range(2):
        wide = pl.ds(i * cols, cols)
        grad = scale[:, i : i + 1] * (gqk[:, wide] - unit[:, wide] * means[:, i : i + 1])
        gqkv[:, wide] = grad.astype(BF16)

    step = 512

    def normed_back(i, carry):
        r = pl.ds(pl.multiple_of(i * rows, rows), rows)
        for c in range(width // step):
            col = pl.ds(c * step, step)
            part2[i, :, col] = dot(gqkv[r, :], w_v[col, qkv_cols], ((1,), (1,))).astype(BF16)
        return carry

    lax.fori_loop(0, fsdp, normed_back, 0)
    sum2 = PlaneSum(plane, part2, held2, core2, half2, full2, s2_send, s2_recv)
    sum2.start()

    def qkv_grads(p):
        for i in range(2):
            block = pl.ds(pl.multiple_of(p * slab + i * (slab // 2), slab // 2), slab // 2)
            wgrad[block, qkv_cols] = dot(normed_v[:, block], gqkv[...], ((0,), (0,))).astype(BF16)

    for i in range(1, dp):
        qkv_grads(lax.rem(z + i, dp))
        far_copy(i, qkv_cols, zq_send, zq_recv).start()
        if i == 1:
            sum2.add_core()
        if i == 2:
            sum2.pass_on()
    qkv_grads(z)

    grad = sum2.total()
    values = hidden[...].astype(F32)
    scale1 = lax.rsqrt(jnp.mean(values * values, axis=-1, keepdims=True) + EPS)
    values = values * scale1
    term_v[0:1, :] = jnp.sum(grad * values, axis=0, keepdims=True)
    grad = grad * gain_attn[0:1, :]
    grad = scale1 * (grad - values * jnp.mean(grad * values, axis=-1, keepdims=True))
    hidden_grad[...] = grad_middle[...] + grad

    def term_copy(k):
        target = lax.rem(me + k, n)
        lanes = pl.ds(pl.multiple_of(target // 2 * 128, 128), 128)
        return remote(
            term_v.at[:, lanes],
            term_in.at[me],
            v_send.at[k],
            v_recv.at[k],
            place(BOTH, fsdp, target),
        )

    for k in range(1, n):
        term_copy(k).start()
    term_in[me] = term_v[:, pl.ds(pl.multiple_of(me // 2 * 128, 128), 128)]

    for copy in keeps:
        copy.wait()
    for k in range(1, fsdp):
        outer_copy(k).wait()
    outer_load = pltpu.make_async_copy(outer_out, core2, local.at[0])
    outer_load.start()
    for k in range(1, n):
        for copy in inner_copies(k):
            copy.wait()
    inner_load = pltpu.make_async_copy(inner_out, part2, local.at[1])
    inner_load.start()
    experts = fsdp * (inner_in.shape[2] // own_rows)
    outer_load.wait()
    outer_rows = core2.shape[0] * core2.shape[1]
    inner_rows = part2.shape[0] * part2.shape[1]

    def put_outer(i, tile, lanes, value):
        block = tile // rows
        held2[pl.ds(i * block, block), :, lanes] = value.reshape(block, rows, -1)

    reorder(
        lambda lanes: core2[:, :, lanes].reshape(outer_rows, -1),
        put_outer,
        experts,
        outer_rows // experts,
    )
    inner_load.wait()

    def put_inner(i, tile, lanes, value):
        normed_v[pl.ds(pl.multiple_of(i * tile, tile), tile), lanes] = value

    reorder(
        lambda lanes: part2[:, :, lanes].reshape(inner_rows, -1),
        put_inner,
        experts,
        inner_rows // experts,
    )
    stores = [
        pltpu.make_async_copy(held2, outer_owned, local.at[0]),
        pltpu.make_async_copy(normed_v, inner_owned, local.at[1]),
    ]
    for store in stores:
        store.start()

    for i in range(1, dp):
        far_copy(i, out_cols, zo_send, zo_recv).wait()
    for i in range(1, dp):
        far_copy(i, qkv_cols, zq_send, zq_recv).wait()
    total = wgrad[slab_rows(z), :].astype(F32)
    for i in range(1, dp):
        total += z_in[i].astype(F32)
    wsum[...] = total.astype(BF16).reshape(wsum.shape)

    def owner_copy(k):
        target = lax.rem(f + k, fsdp)
        return remote(
            wsum.at[target], owned.at[f], w_send.at[k], w_recv.at[k], {"fsdp": target}
        )

    for k in range(1, fsdp):
        owner_copy(k).start()
    owned[f] = wsum[f]
    for k in range(1, fsdp):
        owner_copy(k).wait()
    for k in range(1, fsdp):
        cols_copy(k).wait_send()
        stat_copy(k).wait_send()
    for k in range(1, n):
        term_copy(k).wait()
    total = term_in[0]
    for i in range(1, n):
        total += term_in[i]
    terms_out[...] = total
    for store in stores:
        store.wait()


def attention_back(
    grad_rows,
    attended,
    weight,
    normed,
    qkv,
    unit,
    scale,
    gain,
    turn,
    live,
    grad_middle,
    hidden,
    gain_attn,
    terms,
    inner_in,
    outer_in,
    ident,
):
    dp = lax.axis_size("dp")
    fsdp = lax.axis_size("fsdp")
    n = dp * fsdp
    rows, width = grad_rows.shape
    seq = rows * fsdp
    cols = width // fsdp
    own_rows = width // n
    shape = jax.ShapeDtypeStruct
    dma = pltpu.SemaphoreType.DMA
    vmem = pltpu.VMEM
    anywhere = pl.BlockSpec(memory_space=pl.ANY)
    inside = pl.BlockSpec(memory_space=pltpu.VMEM)
    return pl.pallas_call(
        functools.partial(attention_back_kernel, dp, fsdp),
        out_shape=(
            shape((rows, width), F32),
            shape((terms.shape[0], 128), F32),
            shape((fsdp, own_rows, 4 * cols), BF16),
            shape((seq, width), BF16),
            shape((4, rows, width), BF16),
            shape((fsdp, rows, width), BF16),
            shape((4, rows, width), BF16),
        ),
        in_specs=[anywhere] * 4 + [inside] * 10 + [anywhere] * 2,
        out_specs=(inside,) * 3 + (anywhere,) * 4,
        scratch_shapes=[
            vmem((fsdp, seq, cols), BF16),
            vmem((width, 4 * cols), BF16),
            vmem((seq, width), BF16),
            vmem((seq, cols), BF16),
            vmem((fsdp, seq, cols), BF16),
            vmem((4, seq, cols), BF16),
            vmem((4, seq, cols), BF16),
            vmem((2, seq // 2, cols), BF16),
            vmem((2, seq, cols), BF16),
            vmem((fsdp, rows, width), BF16),
            vmem((4, rows, width), BF16),
            vmem((4, rows, width), BF16),
            vmem((2, rows // 2, width), BF16),
            vmem((2, rows, width), BF16),
            vmem((seq, cols), BF16),
            vmem((seq, cols), F32),
            vmem((seq, cols), F32),
            vmem((seq, cols), F32),
            vmem((seq, 2 * cols), F32),
            vmem((seq, 3 * cols), BF16),
            vmem((8, seq), F32),
            vmem((fsdp, 8, seq), F32),
            vmem((width, 4 * cols), BF16),
            vmem((dp, fsdp * own_rows, 4 * cols), BF16),
            vmem((fsdp, own_rows, 4 * cols), BF16),
            vmem(terms.shape, F32),
            vmem((n, terms.shape[0], 128), F32),
            dma((7,)),
            dma((n,)),
            dma((n,)),
            dma((n, 2)),
            dma((n, 2)),
            dma((fsdp,)),
            dma((fsdp,)),
            dma((fsdp,)),
            dma((fsdp,)),
            dma((8,)),
            dma((8,)),
            dma((8,)),
            dma((8,)),
            dma((fsdp,)),
            dma((fsdp,)),
            dma((dp,)),
            dma((dp,)),
            dma((dp,)),
            dma((dp,)),
            dma((fsdp,)),
            dma((fsdp,)),
        ],
        compiler_params=pltpu.CompilerParams(
            collective_id=ident, has_side_effects=True, vmem_limit_bytes=63 * 1024 * 1024
        ),
    )(
        grad_rows,
        attended,
        weight,
        normed,
        qkv,
        unit,
        scale,
        gain,
        turn,
        live,
        grad_middle,
        hidden,
        gain_attn,
        terms,
        inner_in,
        outer_in,
    )


def expert_kernel(
    dp,
    fsdp,
    x_in,
    c_all,
    gates,
    inner_in,
    outer_in,
    sums,
    gate_sum,
    inner_out,
    outer_out,
    gathered,
    far,
    xv,
    cv,
    wi,
    wo,
    gi,
    go,
    ggu,
    act,
    gv,
    part,
    held,
    core_in,
    half_in,
    full_in,
    gates_in,
    grads_out,
    grads_in,
    local,
    g_send,
    g_recv,
    gg_send,
    gg_recv,
    z_send,
    z_recv,
    a_send,
    a_recv,
    b_send,
    b_recv,
    k_send,
    k_recv,
    c_send,
    c_recv,
    s1_send,
    s1_recv,
    s2_send,
    s2_recv,
    o_send,
    o_recv,
    credit,
):
    rows, width = x_in.shape
    half = rows // 2
    z = lax.axis_index("dp")
    f = lax.axis_index("fsdp")
    core = lax.rem(f, 2)
    chip = f // 2
    xbit = lax.rem(chip, 2)
    ybit = chip // 2
    chip_x = ybit * 2 + (1 - xbit)
    chip_y = (1 - ybit) * 2 + xbit
    chip_d = (1 - ybit) * 2 + (1 - xbit)
    fx = chip_x * 2 + core
    fy = chip_y * 2 + core
    fd = chip_d * 2 + core
    fc = chip * 2 + (1 - core)
    to_x = {"fsdp": fx}
    to_y = {"fsdp": fy}
    to_c = {"fsdp": fc}
    upper = pl.ds(0, half)
    lower = pl.ds(half, half)

    def remote(src, dst, send, recv, device):
        return pltpu.make_async_remote_copy(
            src, dst, send, recv, device_id=device, device_id_type=MESH_ID
        )

    def plane_at(s):
        return lax.rem(z + 1 + s, dp)

    def far_copy(i):
        return remote(
            x_in,
            gathered.at[z, f],
            z_send.at[i],
            z_recv.at[i],
            {"dp": lax.rem(z + dp - i, dp)},
        )

    def gather_one(s):
        block = gathered.at[plane_at(s), f]
        return (
            remote(block.at[upper], block.at[upper], a_send.at[s, 0], a_recv.at[s, 0], to_x),
            remote(block.at[lower], block.at[lower], a_send.at[s, 1], a_recv.at[s, 1], to_y),
        )

    def gather_two(s):
        p = plane_at(s)
        copies = []
        for i, (owner, piece, device) in enumerate(
            ((f, upper, to_y), (fx, upper, to_y), (f, lower, to_x), (fy, lower, to_x))
        ):
            ref = gathered.at[p, owner, piece]
            copies.append(remote(ref, ref, b_send.at[s, i], b_recv.at[s, i], device))
        return copies

    def gather_core(s):
        p = plane_at(s)
        copies = []
        for i, owner in enumerate((f, fx, fy, fd)):
            ref = gathered.at[p, owner]
            copies.append(remote(ref, ref, k_send.at[s, i], k_recv.at[s, i], to_c))
        return copies

    def block_rows(owner):
        return pl.ds(pl.multiple_of(owner * rows, rows), rows)

    def core_copy(k, j):
        return remote(
            part.at[k, block_rows(j * 2 + 1 - core)],
            core_in.at[k, j],
            c_send.at[k, j],
            c_recv.at[k, j],
            to_c,
        )

    def half_copies(k):
        return (
            remote(
                held.at[k, chip_d, upper], half_in.at[k, 0], s1_send.at[k, 0], s1_recv.at[k, 0], to_x
            ),
            remote(
                held.at[k, chip_d, lower], half_in.at[k, 1], s1_send.at[k, 1], s1_recv.at[k, 1], to_y
            ),
        )

    def full_copies(k):
        return (
            remote(held.at[k, chip_x], full_in.at[k, 0], s2_send.at[k, 0], s2_recv.at[k, 0], to_x),
            remote(held.at[k, chip_y], full_in.at[k, 1], s2_send.at[k, 1], s2_recv.at[k, 1], to_y),
        )

    def out_copy(s, k):
        return remote(
            held.at[k, chip], far.at[k, z], o_send.at[s, k], o_recv.at[s, k], {"dp": plane_at(s)}
        )

    def add_core():
        for k in range(2):
            for j in range(4):
                core_copy(k, j).wait()
            def one(j, carry):
                held[k, j] = (
                    part[k, block_rows(j * 2 + core)].astype(F32) + core_in[k, j].astype(F32)
                ).astype(BF16)
                return carry
            lax.fori_loop(0, 4, one, 0)
        pl.semaphore_signal(credit, inc=1, device_id=to_c, device_id_type=MESH_ID)

    def start_half():
        for k in range(2):
            for copy in half_copies(k):
                copy.start()

    def pass_full():
        for k in range(2):
            for copy in half_copies(k):
                copy.wait()
            held[k, chip_y, upper] = (
                held[k, chip_y, upper].astype(F32) + half_in[k, 0].astype(F32)
            ).astype(BF16)
            held[k, chip_x, lower] = (
                held[k, chip_x, lower].astype(F32) + half_in[k, 1].astype(F32)
            ).astype(BF16)
            for copy in full_copies(k):
                copy.start()

    def total_here(k):
        for copy in full_copies(k):
            copy.wait()
        return held[k, chip].astype(F32) + full_in[k, 0].astype(F32) + full_in[k, 1].astype(F32)

    n = dp * fsdp
    me = z * fsdp + f
    greet_all(n, fsdp, me)

    def gate_copy(k):
        target = lax.rem(me + k, n)
        return remote(
            gates.at[target],
            gates_in.at[me],
            g_send.at[k],
            g_recv.at[k],
            place(BOTH, fsdp, target),
        )

    def gate_grad_copy(k):
        target = lax.rem(me + k, n)
        return remote(
            grads_out.at[target],
            grads_in.at[me],
            gg_send.at[k],
            gg_recv.at[k],
            place(BOTH, fsdp, target),
        )

    far_copy(1).start()
    for k in range(1, n):
        gate_copy(k).start()
    loads = [pltpu.make_async_copy(x_in, gathered.at[z, f], local.at[0])]
    for q in range(4):
        loads.append(pltpu.make_async_copy(inner_in.at[:, q], wi.at[q], local.at[1 + q]))
    for e in range(2):
        loads.append(pltpu.make_async_copy(outer_in.at[:, e], wo.at[e], local.at[5 + e]))
    loads.append(pltpu.make_async_copy(gates.at[me], gates_in.at[me], local.at[7]))
    for load in loads:
        load.start()
    gi[...] = jnp.zeros_like(gi)
    go[...] = jnp.zeros_like(go)
    for load in loads:
        load.wait()

    def begin_gather(s):
        @pl.when(s < dp - 1)
        def _():
            far_copy(s + 1).wait_recv()

        for copy in gather_one(s):
            copy.start()

    def middle_gather(s):
        for copy in gather_one(s):
            copy.wait_recv()
        for copy in gather_two(s):
            copy.start()

    def end_gather(s):
        for copy in gather_two(s):
            copy.wait_recv()
        for copy in gather_core(s):
            copy.start()

    begin_gather(0)
    for i in range(2, dp):
        far_copy(i).start()
    middle_gather(0)
    end_gather(0)
    for k in range(1, n):
        gate_copy(k).wait()

    inner_rows = wi.shape[1] * wi.shape[2]
    ff_here = wo.shape[1] * wo.shape[2]
    tile = xv.shape[0] // 2

    def tile_step(t):
        r = pl.ds(pl.multiple_of(t * tile, tile), tile)
        x = xv[r, :]
        c = cv[r, :]
        for e in range(2):
            gate = dot(x, wi[e].reshape(inner_rows, ff_here), ((1,), (0,)))
            up = dot(x, wi[2 + e].reshape(inner_rows, ff_here), ((1,), (0,)))
            back = dot(c, wo[e].reshape(ff_here, width), ((1,), (1,)))
            sigmoid = 1.0 / (1.0 + jnp.exp(-gate))
            silu = gate * sigmoid
            active = (silu * up).astype(BF16).astype(F32)
            weight = gv[r, e : e + 1]
            gv[r, 8 + e : 9 + e] = jnp.sum(active * back, axis=-1, keepdims=True)
            act[e, r, :] = (weight * active).astype(BF16)
            back = weight * back
            ggu[e, r, :] = (back * up * sigmoid * (1.0 + gate * (1.0 - sigmoid))).astype(BF16)
            ggu[2 + e, r, :] = (back * silu).astype(BF16)
        step = 512
        for i in range(width // step):
            col = pl.ds(i * step, step)
            blocks = pl.ds(i * step // wi.shape[2], step // wi.shape[2])
            total = dot(act[0, r, :], wo[0, :, :, col].reshape(ff_here, step), ((1,), (0,)))
            total += dot(act[1, r, :], wo[1, :, :, col].reshape(ff_here, step), ((1,), (0,)))
            part[0, r, col] = total.astype(BF16)
            total = dot(ggu[0, r, :], wi[0, blocks].reshape(step, ff_here), ((1,), (1,)))
            for q in range(1, 4):
                total += dot(ggu[q, r, :], wi[q, blocks].reshape(step, ff_here), ((1,), (1,)))
            part[1, r, col] = total.astype(BF16)

    def weight_step():
        def inner_part(i, carry):
            col = pl.ds(pl.multiple_of(i * 256, 256), 256)
            xt = xv[:, col]
            for q in range(4):
                gi[q, col, :] += dot(xt, ggu[q], ((0,), (0,)))
            return carry

        lax.fori_loop(0, width // 256, inner_part, 0)

        def outer_part(i, carry):
            col = pl.ds(pl.multiple_of(i * 512, 512), 512)
            ct = cv[:, col]
            for e in range(2):
                go[e, :, col] += dot(act[e], ct, ((0,), (0,)))
            return carry

        lax.fori_loop(0, width // 512, outer_part, 0)

    def chunk(s, carry):
        p = plane_at(s)
        c_load = pltpu.make_async_copy(c_all.at[p], cv, local.at[1])
        c_load.start()

        def to_columns(j, carry):
            r = pl.ds(pl.multiple_of(j * rows, rows), rows)
            gv[r, :] = exact_dot(gates_in[p * fsdp + j], corner_of(8, 0, 1.0), ((0,), (0,)))
            return carry

        lax.fori_loop(0, fsdp, to_columns, 0)
        for copy in gather_core(s):
            copy.wait_recv()
        for j in range(8):
            pltpu.make_async_copy(
                gathered.at[p, j], xv.at[pl.ds(j * rows, rows)], local.at[3 + j]
            ).start()
        c_load.wait()
        for j in range(8):
            pltpu.make_async_copy(
                gathered.at[p, j], xv.at[pl.ds(j * rows, rows)], local.at[3 + j]
            ).wait()
        @pl.when(s < dp - 1)
        def _():
            begin_gather(s + 1)

        tile_step(0)

        @pl.when(s > 0)
        def _():
            pass_full()

        @pl.when(s < dp - 1)
        def _():
            middle_gather(s + 1)

        tile_step(1)

        @pl.when(s > 0)
        def _():
            pl.semaphore_wait(credit, 1)

        for k in range(2):
            for j in range(4):
                core_copy(k, j).start()
        def to_rows(j, carry):
            r = pl.ds(pl.multiple_of(j * rows, rows), rows)
            grads_out[p * fsdp + j] = exact_dot(corner_of(8, 8, 1.0), gv[r, :], ((1,), (1,)))
            return carry

        lax.fori_loop(0, fsdp, to_rows, 0)
        weight_step()

        @pl.when(s > 0)
        def _():
            for k in range(2):
                held[k, chip] = total_here(k).astype(BF16)
                out_copy(s - 1, k).start()
            for k in range(2):
                out_copy(s - 1, k).wait_send()

        add_core()
        start_half()

        @pl.when(s < dp - 1)
        def _():
            end_gather(s + 1)

        return carry

    lax.fori_loop(0, dp, chunk, 0)

    pass_full()
    for k in range(1, n):
        gate_grad_copy(k).start()
    grads_in[me] = grads_out[me]
    for q in range(4):
        wi[q] = gi[q].astype(BF16).reshape(wi.shape[1:])
    for e in range(2):
        wo[e] = go[e].astype(BF16).reshape(wo.shape[1:])
    stores = []
    for q in range(4):
        stores.append(pltpu.make_async_copy(wi.at[q], inner_out.at[:, q], local.at[q]))
    for e in range(2):
        stores.append(pltpu.make_async_copy(wo.at[e], outer_out.at[:, e], local.at[4 + e]))
    for store in stores:
        store.start()
    pl.semaphore_wait(credit, 1)
    for i in range(1, dp):
        for k in range(2):
            remote(
                held.at[k, chip],
                far.at[k, lax.rem(z + dp - i, dp)],
                o_send.at[i - 1, k],
                o_recv.at[i - 1, k],
                to_x,
            ).wait_recv()
    fetch = []
    for i in range(1, dp):
        for k in range(2):
            fetch.append(
                pltpu.make_async_copy(
                    far.at[k, lax.rem(z + i, dp)], core_in.at[k, i], local.at[6 + (i - 1) * 2 + k]
                )
            )
    for copy in fetch:
        copy.start()
    for copy in fetch:
        copy.wait()
    for k in range(2):
        total = total_here(k)
        for i in range(1, dp):
            total += core_in[k, i].astype(F32)
        sums[k] = total
    for k in range(1, n):
        gate_grad_copy(k).wait()
    for j in range(fsdp):
        total = grads_in[j]
        for i in range(1, dp):
            total += grads_in[i * fsdp + j]
        gate_sum[j] = total
    for store in stores:
        store.wait()
    for i in range(1, dp):
        far_copy(i).wait_send()

    def settle(s, carry):
        for copy in (*gather_one(s), *gather_two(s), *gather_core(s)):
            copy.wait_send()
        return carry

    lax.fori_loop(0, dp, settle, 0)


def expert_pass(x_in, c_all, gates, inner_in, outer_in, ident):
    dp = lax.axis_size("dp")
    fsdp = lax.axis_size("fsdp")
    rows, width = x_in.shape
    n, four, own_rows, ff_here = inner_in.shape
    _, two, out_rows, _ = outer_in.shape
    chunk = fsdp * rows
    shape = jax.ShapeDtypeStruct
    dma = pltpu.SemaphoreType.DMA
    anywhere = pl.BlockSpec(memory_space=pl.ANY)
    got = pl.pallas_call(
        functools.partial(expert_kernel, dp, fsdp),
        out_shape=(
            shape((2, rows, width), F32),
            shape((fsdp, 8, 128), F32),
            shape(inner_in.shape, BF16),
            shape(outer_in.shape, BF16),
            shape((dp, fsdp, rows, width), BF16),
            shape((2, dp, rows, width), BF16),
        ),
        in_specs=[anywhere] * 5,
        out_specs=(pl.BlockSpec(memory_space=pltpu.VMEM),) * 2 + (anywhere,) * 4,
        scratch_shapes=[
            pltpu.VMEM((chunk, width), BF16),
            pltpu.VMEM((chunk, width), BF16),
            pltpu.VMEM((four, n, own_rows, ff_here), BF16),
            pltpu.VMEM((two, fsdp, out_rows, width), BF16),
            pltpu.VMEM((four, width, ff_here), F32),
            pltpu.VMEM((two, ff_here, width), F32),
            pltpu.VMEM((four, chunk, ff_here), BF16),
            pltpu.VMEM((two, chunk, ff_here), BF16),
            pltpu.VMEM((chunk, 128), F32),
            pltpu.VMEM((2, chunk, width), BF16),
            pltpu.VMEM((2, 4, rows, width), BF16),
            pltpu.VMEM((2, 4, rows, width), BF16),
            pltpu.VMEM((2, 2, rows // 2, width), BF16),
            pltpu.VMEM((2, 2, rows, width), BF16),
            pltpu.VMEM((n, 8, 128), F32),
            pltpu.VMEM((n, 8, 128), F32),
            pltpu.VMEM((n, 8, 128), F32),
            dma((12 + 2 * dp,)),
            dma((n,)),
            dma((n,)),
            dma((n,)),
            dma((n,)),
            dma((dp,)),
            dma((dp,)),
            dma((dp, 2)),
            dma((dp, 2)),
            dma((dp, 4)),
            dma((dp, 4)),
            dma((dp, 4)),
            dma((dp, 4)),
            dma((2, 4)),
            dma((2, 4)),
            dma((2, 2)),
            dma((2, 2)),
            dma((2, 2)),
            dma((2, 2)),
            dma((dp, 2)),
            dma((dp, 2)),
            pltpu.SemaphoreType.REGULAR,
        ],
        compiler_params=pltpu.CompilerParams(
            collective_id=ident, has_side_effects=True, vmem_limit_bytes=63 * 1024 * 1024
        ),
    )(x_in, c_all, gates, inner_in, outer_in)
    return got[:4]


def expert_pass_dense(normed2, grad_all, gates, inner_weight, outer_weight):
    n, parts, own_rows, ff_here = inner_weight.shape
    experts_here = parts // 2
    inner = experts_here * ff_here
    width = n * own_rows
    tokens = grad_all.shape[0]
    gates = gates[:, :, None]
    rows_all = lax.all_gather(normed2, BOTH, axis=0, tiled=True)
    inner_block = inner_weight.transpose(0, 2, 1, 3).reshape(width, 2 * inner)
    outer_shape = outer_weight.shape
    outer_block = outer_weight.transpose(1, 0, 2, 3).reshape(inner, width)
    gate_up = dot(rows_all, inner_block, ((1,), (0,)))
    gate = gate_up[:, :inner]
    up = gate_up[:, inner:]
    sigmoid = jax.nn.sigmoid(gate)
    silu = gate * sigmoid
    activation = (silu * up).astype(BF16).astype(F32)
    grad_act = dot(grad_all, outer_block, ((1,), (1,)))
    grad_gates = jnp.sum(
        (activation * grad_act).reshape(tokens, experts_here, ff_here), axis=-1
    )
    by_part = (tokens, experts_here, ff_here)
    activation = (activation.reshape(by_part) * gates).reshape(tokens, inner).astype(BF16)
    grad_act = (grad_act.reshape(by_part) * gates).reshape(tokens, inner)
    grad_gate_up = jnp.concatenate(
        [grad_act * up * sigmoid * (1.0 + gate * (1.0 - sigmoid)), grad_act * silu], axis=1
    ).astype(BF16)
    expert_sum = dot(activation, outer_block, ((1,), (0,))).astype(BF16)
    expert_sum = lax.psum_scatter(expert_sum, BOTH, scatter_dimension=0, tiled=True).astype(F32)
    if tokens > 8192:
        grad_gate_up, expert_sum = lax.optimization_barrier((grad_gate_up, expert_sum))
    grad_rows = dot(grad_gate_up, inner_block, ((1,), (1,))).astype(BF16)
    grad_rows = lax.psum_scatter(grad_rows, BOTH, scatter_dimension=0, tiled=True).astype(F32)
    inner_grad = dot(rows_all, grad_gate_up, ((0,), (0,))).astype(BF16)
    outer_grad = dot(activation, grad_all, ((0,), (0,))).astype(BF16)
    inner_grad = inner_grad.reshape(n, own_rows, parts, ff_here).transpose(0, 2, 1, 3)
    outer_grad = outer_grad.reshape(experts_here, outer_shape[0], outer_shape[2], width)
    return expert_sum, grad_rows, grad_gates, inner_grad, outer_grad.transpose(1, 0, 2, 3)


def body(
    hidden_in,
    lengths,
    routes,
    attn_gain,
    query_gain,
    key_gain,
    ffn_gain,
    qkv_weight,
    out_weight,
    router_weight,
    expert_in,
    expert_out,
    cotangent,
):
    rows, width = hidden_in.shape
    dp = lax.axis_size("dp")
    fsdp = lax.axis_size("fsdp")
    fused = fsdp == 8
    n = dp * fsdp
    experts = router_weight.shape[1]
    seq = rows * fsdp
    tokens = rows * n
    own_rows = width // n
    heads_here = HEADS // fsdp
    cols = heads_here * HEAD_DIM
    experts_here = experts // fsdp
    ff = expert_out.shape[0] * n
    ff_here = ff // dp
    z = lax.axis_index("dp")
    f = lax.axis_index("fsdp")
    valid = lengths[z]
    scaling = HEAD_DIM ** (-0.5)

    small = jnp.concatenate(
        [attn_gain, query_gain, key_gain, ffn_gain, router_weight.reshape(-1)]
    )
    small_rows = -(-small.size // 2048) * 16
    small = exchange(tiles_of(small, small_rows), BOTH, 0, False).reshape(n, -1)
    gains = small[:, : 4 * own_rows].reshape(n, 4, own_rows).transpose(1, 0, 2)
    gains = gains.reshape(4, width).astype(F32)
    router_full = small[:, 4 * own_rows : 4 * own_rows + own_rows * experts]
    router_full = router_full.reshape(width, experts)
    gain_attn, gain_query, gain_key, gain_ffn = gains[0], gains[1], gains[2], gains[3]

    attn_weight = jnp.concatenate(
        [
            qkv_weight.reshape(own_rows, 3, fsdp, cols),
            out_weight.reshape(own_rows, 1, fsdp, cols),
        ],
        axis=1,
    )
    attn_weight = attn_weight.transpose(2, 0, 1, 3).reshape(fsdp, own_rows, 4 * cols)
    live_mask = (f * rows + jnp.arange(rows, dtype=jnp.int32) < valid).astype(F32)[:, None]
    grad_total = cotangent.astype(F32) * live_mask

    here = f * cols
    qk_gain = jnp.stack(
        [
            lax.dynamic_slice(gain_query, (here,), (cols,)),
            lax.dynamic_slice(gain_key, (here,), (cols,)),
        ]
    )
    pos = jnp.arange(seq, dtype=jnp.int32)
    frequency = jnp.power(10000.0, -jnp.arange(HEAD_DIM // 2, dtype=F32) * 2.0 / HEAD_DIM)
    angles = pos.astype(F32)[:, None] * frequency[None, :]
    cosine = jnp.cos(angles)[:, None, None, :]
    sine = jnp.sin(angles)[:, None, None, :]

    if fused:
        gain_wide = jnp.broadcast_to(qk_gain.reshape(1, 2 * cols), (8, 2 * cols))
        turn = jnp.stack(
            [
                jnp.concatenate([cosine, cosine], axis=-1).reshape(seq, HEAD_DIM),
                jnp.concatenate([sine, -sine], axis=-1).reshape(seq, HEAD_DIM),
            ]
        )
        live_keys = jnp.broadcast_to((pos < valid).astype(F32)[None], (8, seq))
        (
            branch,
            qkv,
            qk_unit,
            qk_scale,
            normed_all,
            attn_weight,
            attended_all,
            grad_all,
            inner_weight,
            outer_weight,
        ) = attention_forward(
            hidden_in,
            grad_total.astype(BF16),
            attn_weight,
            expert_in,
            expert_out,
            jnp.broadcast_to(gain_attn[None], (8, width)),
            gain_wide,
            turn,
            live_keys,
            10,
        )
        branch = branch.astype(F32)
    else:
        attn_weight = lax.all_to_all(attn_weight, "fsdp", 0, 0, tiled=True)
        attn_weight = lax.all_gather(
            attn_weight.reshape(fsdp * own_rows, 4 * cols), "dp", axis=0, tiled=True
        )
        qkv_here = attn_weight[:, : 3 * cols]
        out_here = attn_weight[:, 3 * cols :]
        inner_weight = expert_in.reshape(own_rows, fsdp, experts_here, 2, dp, ff_here)
        inner_weight = inner_weight.transpose(4, 1, 3, 2, 0, 5)
        inner_weight = inner_weight.reshape(n, 2 * experts_here, own_rows, ff_here)
        outer_weight = expert_out.reshape(-1, fsdp, experts_here, width).transpose(1, 2, 0, 3)
        inner_weight = lax.all_to_all(inner_weight, BOTH, 0, 0, tiled=True)
        outer_weight = lax.all_to_all(outer_weight, "fsdp", 0, 0, tiled=True)
        hidden_all = lax.all_gather(hidden_in, "fsdp", axis=0, tiled=True).astype(F32)
        normed_all = (hidden_all * rms_scale(hidden_all) * gain_attn).astype(BF16)
        mixed = dot(normed_all, qkv_here, ((1,), (0,)))
        raw = mixed[:, : 2 * cols].reshape(seq, 2, cols)
        squares = plane_sum(jnp.sum(raw * raw, axis=-1), 1)
        qk_scale = lax.rsqrt(squares / width + EPS)[:, :, None]
        qk_unit = raw * qk_scale
        shape4 = (seq, 2, heads_here, HEAD_DIM)
        turned = rotate((qk_unit * qk_gain).reshape(shape4), cosine, sine, 1.0).astype(BF16)
        query = turned[:, 0]
        key = turned[:, 1]
        value = mixed[:, 2 * cols :].astype(BF16).reshape(seq, heads_here, HEAD_DIM)
        allowed = ((pos[None, :] <= pos[:, None]) & (pos[None, :] < valid))[None]
        scores = jnp.einsum("qhd,khd->hqk", query, key, preferred_element_type=F32) * scaling
        masked = jnp.where(allowed, scores, -1e30)
        weights = jnp.exp(masked - jnp.max(masked, axis=-1, keepdims=True))
        weights = jnp.where(allowed, weights, 0.0)
        probs = weights / jnp.sum(weights, axis=-1, keepdims=True)
        probs_low = probs.astype(BF16)
        attended = jnp.einsum("hqk,khd->qhd", probs_low, value, preferred_element_type=F32)
        attended = attended.reshape(seq, cols).astype(BF16)
        attended_all = lax.all_gather(attended, "fsdp", axis=0, tiled=False)
        branch = jnp.einsum(
            "fsc,fcn->sn",
            attended_all,
            out_here.reshape(fsdp, cols, cols),
            preferred_element_type=F32,
        )
        branch = exchange(branch.astype(BF16).reshape(fsdp, rows, cols), ("fsdp",), 2, True)
        branch = branch.transpose(1, 0, 2).reshape(rows, width).astype(F32)
        grad_all = lax.all_gather(grad_total.astype(BF16), BOTH, axis=0, tiled=True)

    hidden = hidden_in.astype(F32)
    scale1 = rms_scale(hidden)
    unit1 = hidden * scale1
    middle = hidden + branch
    scale2 = rms_scale(middle)
    unit2 = middle * scale2
    normed2 = (unit2 * gain_ffn).astype(BF16)
    logits = dot(normed2, router_full, ((1,), (0,)))
    router_probs = jax.nn.softmax(logits, axis=-1)
    chosen = jnp.sum(
        (routes[:, :, None] == jnp.arange(experts, dtype=jnp.int32)[None, None, :]).astype(F32),
        axis=1,
    )

    gates = (router_probs * chosen).reshape(rows, fsdp, experts_here).transpose(1, 2, 0)
    gates = jnp.broadcast_to(gates[None], (dp, fsdp, experts_here, rows))
    gates = gates.reshape(n, experts_here, rows)
    gates = jnp.pad(gates, ((0, 0), (0, 8 - experts_here), (0, 0)))
    if fused:
        sums, grad_gates, inner_grad, outer_grad = expert_pass(
            normed2, grad_all.reshape(dp, seq, width), gates, inner_weight, outer_weight, 8
        )
        expert_sum = sums[0]
        grad_rows = sums[1]
        grad_gates = grad_gates[:, :experts_here]
    else:
        gates = exchange(gates, BOTH, 3, True)[:, :experts_here]
        gates = gates.transpose(0, 2, 1).reshape(tokens, experts_here)
        expert_sum, grad_rows, grad_gates, inner_grad, outer_grad = expert_pass_dense(
            normed2, grad_all, gates, inner_weight, outer_weight
        )
        grad_gates = grad_gates.reshape(n, rows, experts_here).transpose(0, 2, 1)
        grad_gates = jnp.pad(grad_gates, ((0, 0), (0, 8 - experts_here), (0, 0)))
        grad_gates = exchange(grad_gates, BOTH, 4, True)[:, :experts_here]
        grad_gates = jnp.sum(grad_gates.reshape(dp, fsdp, experts_here, rows), axis=0)
    grad_router_probs = grad_gates.reshape(experts, rows).transpose(1, 0) * chosen

    block_total = middle + expert_sum
    squares = jnp.stack(
        [
            jnp.sum(live_mask * block_total * block_total),
            jnp.sum(live_mask * branch * branch),
            jnp.sum(live_mask * expert_sum * expert_sum),
        ]
    )

    grad_logits = router_probs * (
        grad_router_probs - jnp.sum(router_probs * grad_router_probs, axis=-1, keepdims=True)
    )
    grad_logits = grad_logits.astype(BF16)
    grad_normed2 = grad_rows + dot(grad_logits, router_full, ((1,), (1,)))
    ffn_term = jnp.sum(grad_normed2 * unit2, axis=0)
    grad_middle = grad_total + norm_back(grad_normed2 * gain_ffn, unit2, scale2)

    if fused:
        terms = jnp.concatenate(
            [
                jnp.zeros((3, width), F32),
                ffn_term[None],
                jnp.broadcast_to(squares[:, None], (3, width)),
                jnp.zeros((1, width), F32),
                dot(grad_logits, normed2, ((0,), (0,))),
            ]
        )
        hidden_grad, terms, attn_grad, inner_grad, outer_grad, _, _ = attention_back(
            grad_middle.astype(BF16),
            attended_all,
            attn_weight,
            normed_all,
            qkv,
            qk_unit,
            qk_scale,
            gain_wide,
            turn,
            live_keys,
            grad_middle,
            hidden_in,
            jnp.broadcast_to(gain_attn[None], (8, width)),
            terms,
            inner_grad.reshape(n, 2, experts_here * own_rows, ff_here),
            outer_grad.reshape(fsdp, -1, width),
            9,
        )
        inner_grad = inner_grad.reshape(own_rows, experts, 2 * ff)
        outer_grad = outer_grad.reshape(-1, experts, width)
        terms = lax.dynamic_slice(terms, (0, lax.rem(f, 2) * own_rows), (terms.shape[0], own_rows))
        gain_grads = terms[:4]
        router_grad = terms[8:].transpose(1, 0)
        square_sums = terms[4:7, 0]
    else:
        grad_cols = grad_middle.astype(BF16).reshape(rows, fsdp, cols).transpose(1, 0, 2)
        grad_cols = exchange(grad_cols, ("fsdp",), 5, True).reshape(seq, cols)
        out_grad = jnp.einsum("fsc,sn->fcn", attended_all, grad_cols, preferred_element_type=F32)
        grad_attended = jnp.einsum(
            "sn,fcn->fsc", grad_cols, out_here.reshape(fsdp, cols, cols), preferred_element_type=F32
        )
        grad_attended = lax.psum_scatter(
            grad_attended.astype(BF16).reshape(fsdp * seq, cols), "fsdp", scatter_dimension=0, tiled=True
        )
        grad_attended = grad_attended.reshape(seq, heads_here, HEAD_DIM)
        grad_probs = jnp.einsum("qhd,khd->hqk", grad_attended, value, preferred_element_type=F32)
        grad_scores = probs * (grad_probs - jnp.sum(probs * grad_probs, axis=-1, keepdims=True))
        grad_scores = grad_scores.astype(BF16)
        grad_query = jnp.einsum("hqk,khd->qhd", grad_scores, key, preferred_element_type=F32)
        grad_key = jnp.einsum("hqk,qhd->khd", grad_scores, query, preferred_element_type=F32)
        grad_value = jnp.einsum("hqk,qhd->khd", probs_low, grad_attended, preferred_element_type=F32)
        grad_qk = rotate(jnp.stack([grad_query, grad_key], axis=1) * scaling, cosine, sine, -1.0)
        grad_qk = grad_qk.reshape(seq, 2, cols)
        qk_term = jnp.sum(grad_qk * qk_unit, axis=0)
        grad_qk = grad_qk * qk_gain
        inner_means = plane_sum(jnp.sum(grad_qk * qk_unit, axis=-1), 6)[:, :, None] / width
        grad_qk = qk_scale * (grad_qk - qk_unit * inner_means)
        grad_qkv = jnp.concatenate(
            [grad_qk.reshape(seq, 2 * cols), grad_value.reshape(seq, cols)], axis=1
        ).astype(BF16)
        qkv_grad = dot(normed_all, grad_qkv, ((0,), (0,)))
        grad_normed = dot(grad_qkv, qkv_here, ((1,), (1,))).astype(BF16)
        grad_normed = lax.psum_scatter(grad_normed, "fsdp", scatter_dimension=0, tiled=True).astype(F32)
        attn_grad = jnp.concatenate([qkv_grad, out_grad.reshape(width, cols)], axis=1).astype(BF16)
        attn_grad = lax.psum_scatter(attn_grad, "dp", scatter_dimension=0, tiled=True)
        attn_grad = attn_grad.reshape(fsdp, own_rows, 4 * cols)
        attn_grad = lax.all_to_all(attn_grad, "fsdp", 0, 0, tiled=True)
        inner_grad = lax.all_to_all(inner_grad, BOTH, 0, 0, tiled=True)
        outer_grad = lax.all_to_all(outer_grad, "fsdp", 0, 0, tiled=True)
        inner_grad = inner_grad.reshape(dp, fsdp, 2, experts_here, own_rows, ff_here)
        inner_grad = inner_grad.transpose(4, 1, 3, 2, 0, 5).reshape(own_rows, experts, 2 * ff)
        outer_grad = outer_grad.transpose(2, 0, 1, 3).reshape(-1, experts, width)
        attn_term = jnp.sum(grad_normed * unit1, axis=0)
        hidden_grad = grad_middle + norm_back(grad_normed * gain_attn, unit1, scale1)

        router_term = dot(normed2, grad_logits, ((0,), (0,)))
        qk_full = jnp.zeros((2, width), F32)
        qk_full = lax.dynamic_update_slice(qk_full, qk_term, (0, here))
        terms = jnp.concatenate([attn_term[None], qk_full, ffn_term[None]])
        terms = terms.reshape(4, n, own_rows).transpose(1, 0, 2).reshape(n, 4 * own_rows)
        terms = jnp.concatenate(
            [
                terms,
                router_term.reshape(n, own_rows * experts),
                jnp.broadcast_to(squares[None], (n, 3)),
            ],
            axis=1,
        )
        term_size = terms.shape[1]
        term_rows = -(-term_size // 1024) * 8
        terms = jnp.pad(terms, ((0, 0), (0, term_rows * 128 - term_size)))
        terms = exchange(terms.reshape(n, term_rows, 128), BOTH, 7, True)
        terms = jnp.sum(terms, axis=0).reshape(-1)
        gain_grads = terms[: 4 * own_rows].reshape(4, own_rows)
        router_grad = terms[4 * own_rows : 4 * own_rows + own_rows * experts]
        router_grad = router_grad.reshape(own_rows, experts)
        square_sums = terms[term_size - 3 : term_size]
    attn_grad = attn_grad.reshape(fsdp, own_rows, 4, cols).transpose(1, 2, 0, 3).astype(F32)
    attn_grad = attn_grad.reshape(own_rows, 4 * width)
    valid_cells = jnp.sum(lengths).astype(F32) * width
    stats = jnp.sqrt(square_sums / valid_cells)

    return (
        block_total.astype(BF16),
        hidden_grad,
        gain_grads[0],
        gain_grads[1],
        gain_grads[2],
        gain_grads[3],
        attn_grad[:, : 3 * width],
        attn_grad[:, 3 * width :],
        router_grad,
        inner_grad.astype(F32),
        outer_grad.astype(F32),
        stats,
    )


def solution(mesh):
    one = P(BOTH)
    two = P(BOTH, None)
    three = P(BOTH, None, None)
    in_specs = (two, P(), two, one, one, one, one, two, two, two, three, three, two)
    out_specs = (two, two, one, one, one, one, two, two, two, three, three, P())
    return jax.shard_map(body, mesh=mesh, in_specs=in_specs, out_specs=out_specs, check_vma=False)
```

```python
import functools

import jax
import jax.numpy as jnp
from jax import lax
from jax.experimental import pallas as pl
from jax.experimental.pallas import tpu as pltpu
from jax.sharding import PartitionSpec as P

HEADS = 16
HEAD_DIM = 128
EPS = 1e-05
BOTH = ("dp", "fsdp")
MESH_ID = pl.DeviceIdType.MESH
F32 = jnp.float32
BF16 = jnp.bfloat16


def rms_scale(values_in):
    return lax.rsqrt(jnp.mean(values_in * values_in, axis=-1, keepdims=True) + EPS)


def norm_back(grad_in, unit_rows, scaling):
    return scaling * (grad_in - unit_rows * jnp.mean(grad_in * unit_rows, axis=-1, keepdims=True))


def rotate(values_in, cosine, sine, direction):
    half_width = values_in.shape[-1] // 2
    first_half = values_in[..., :half_width]
    second_half = values_in[..., half_width:]
    return jnp.concatenate(
        [
            first_half * cosine - direction * second_half * sine,
            second_half * cosine + direction * first_half * sine,
        ],
        axis=-1,
    )


def place(axes, fsdp, index):
    if axes == BOTH:
        return {"dp": index // fsdp, "fsdp": lax.rem(index, fsdp)}
    return {axes[0]: index}


def exchange_kernel(axes, n, fsdp, spread, x, o, send, recv, own):
    if axes == BOTH:
        me = lax.axis_index("dp") * fsdp + lax.axis_index("fsdp")
    else:
        me = lax.axis_index(axes[0])
    barrier = pltpu.get_barrier_semaphore()
    for k in range(1, n):
        peer = place(axes, fsdp, lax.rem(me + k, n))
        pl.semaphore_signal(barrier, inc=1, device_id=peer, device_id_type=MESH_ID)
    pl.semaphore_wait(barrier, n - 1)
    local = pltpu.make_async_copy(x.at[me] if spread else x, o.at[me], own)
    local.start()
    copies = []
    for k in range(1, n):
        target = lax.rem(me + k, n)
        copy = pltpu.make_async_remote_copy(
            x.at[target] if spread else x,
            o.at[me],
            send.at[k],
            recv.at[k],
            device_id=place(axes, fsdp, target),
            device_id_type=MESH_ID,
        )
        copy.start()
        copies.append(copy)
    local.wait()
    for copy in copies:
        copy.wait()


def exchange(x, axes, ident, spread):
    fsdp = lax.axis_size("fsdp")
    n = lax.axis_size(axes)
    shape = x.shape if spread else (n,) + x.shape
    return pl.pallas_call(
        functools.partial(exchange_kernel, axes, n, fsdp, spread),
        out_shape=jax.ShapeDtypeStruct(shape, x.dtype),
        in_specs=[pl.BlockSpec(memory_space=pl.ANY)],
        out_specs=pl.BlockSpec(memory_space=pl.ANY),
        scratch_shapes=[
            pltpu.SemaphoreType.DMA((n,)),
            pltpu.SemaphoreType.DMA((n,)),
            pltpu.SemaphoreType.DMA,
        ],
        compiler_params=pltpu.CompilerParams(collective_id=ident, has_side_effects=True),
    )(x)


def tiles_of(x, rows):
    flat = x.reshape(-1)
    return jnp.pad(flat, (0, rows * 128 - flat.shape[0])).reshape(rows, 128)


def plane_sum(x, ident):
    rows = -(-x.size // 1024) * 8
    got = exchange(tiles_of(x, rows), ("fsdp",), ident, False)
    return jnp.sum(got, axis=0).reshape(-1)[: x.size].reshape(x.shape)


def dot(a, b, dims):
    return lax.dot_general(a, b, (dims, ((), ())), preferred_element_type=F32)


HIGH = lax.Precision.HIGHEST


def remote(src, dst, send, recv, device):
    return pltpu.make_async_remote_copy(
        src, dst, send, recv, device_id=device, device_id_type=MESH_ID
    )


def greet_all(n, fsdp, me):
    barrier = pltpu.get_barrier_semaphore()
    for k in range(1, n):
        peer = place(BOTH, fsdp, lax.rem(me + k, n))
        pl.semaphore_signal(barrier, inc=1, device_id=peer, device_id_type=MESH_ID)
    pl.semaphore_wait(barrier, n - 1)


def reorder(get, put, outer, inner):
    total = outer * inner
    tile = 256
    step = 512

    def one(i, carry):
        row = i * tile + lax.broadcasted_iota(jnp.int32, (tile, total), 0)
        col = lax.broadcasted_iota(jnp.int32, (tile, total), 1)
        pick = jnp.where(lax.rem(row, outer) * inner + row // outer == col, 1.0, 0.0).astype(BF16)
        for c in range(2048 // step):
            lanes = pl.ds(c * step, step)
            put(i, tile, lanes, dot(pick, get(lanes), ((1,), (0,))).astype(BF16))
        return carry

    lax.fori_loop(0, total // tile, one, 0)


def corner_of(rows, shift, value):
    row = lax.broadcasted_iota(jnp.int32, (rows, 128), 0)
    lane = lax.broadcasted_iota(jnp.int32, (rows, 128), 1)
    return jnp.where(lane == row + shift, value, 0.0).astype(F32)


def exact_dot(a, b, dims):
    return lax.dot_general(
        a, b, (dims, ((), ())), precision=HIGH, preferred_element_type=F32
    )


class Plane:
    def __init__(self, f):
        self.f = f
        self.core = lax.rem(f, 2)
        self.chip = f // 2
        xbit = lax.rem(self.chip, 2)
        ybit = self.chip // 2
        self.chip_x = ybit * 2 + (1 - xbit)
        self.chip_y = (1 - ybit) * 2 + xbit
        self.chip_d = (1 - ybit) * 2 + (1 - xbit)
        self.fx = self.chip_x * 2 + self.core
        self.fy = self.chip_y * 2 + self.core
        self.fd = self.chip_d * 2 + self.core
        self.to_x = {"fsdp": self.fx}
        self.to_y = {"fsdp": self.fy}
        self.to_c = {"fsdp": self.chip * 2 + 1 - self.core}


class PlaneSum:
    def __init__(self, plane, part, held, core_in, half_in, full_in, send, recv):
        self.plane = plane
        self.part = part
        self.held = held
        self.core_in = core_in
        self.half_in = half_in
        self.full_in = full_in
        self.send = send
        self.recv = recv
        half = held.shape[1] // 2
        self.upper = pl.ds(0, half)
        self.lower = pl.ds(half, half)

    def core_copy(self, j):
        owner = j * 2 + 1 - self.plane.core
        return remote(
            self.part.at[owner],
            self.core_in.at[j],
            self.send.at[j],
            self.recv.at[j],
            self.plane.to_c,
        )

    def half_copies(self):
        block = self.held.at[self.plane.chip_d]
        send, recv, half_in = self.send, self.recv, self.half_in
        return (
            remote(block.at[self.upper], half_in.at[0], send.at[4], recv.at[4], self.plane.to_x),
            remote(block.at[self.lower], half_in.at[1], send.at[5], recv.at[5], self.plane.to_y),
        )

    def full_copies(self):
        held, full_in, send, recv = self.held, self.full_in, self.send, self.recv
        plane = self.plane
        return (
            remote(held.at[plane.chip_x], full_in.at[0], send.at[6], recv.at[6], plane.to_x),
            remote(held.at[plane.chip_y], full_in.at[1], send.at[7], recv.at[7], plane.to_y),
        )

    def start(self):
        for j in range(4):
            self.core_copy(j).start()

    def add_core(self):
        for j in range(4):
            self.core_copy(j).wait()

        def one(j, carry):
            own = self.part[j * 2 + self.plane.core].astype(F32)
            self.held[j] = (own + self.core_in[j].astype(F32)).astype(BF16)
            return carry

        lax.fori_loop(0, 4, one, 0)
        for copy in self.half_copies():
            copy.start()

    def pass_on(self):
        for copy in self.half_copies():
            copy.wait()
        held, half_in = self.held, self.half_in
        for chip, piece, i in (
            (self.plane.chip_y, self.upper, 0),
            (self.plane.chip_x, self.lower, 1),
        ):
            total = held[chip, piece].astype(F32) + half_in[i].astype(F32)
            held[chip, piece] = total.astype(BF16)
        for copy in self.full_copies():
            copy.start()

    def total(self):
        for copy in self.full_copies():
            copy.wait()
        total = self.held[self.plane.chip].astype(F32)
        return total + self.full_in[0].astype(F32) + self.full_in[1].astype(F32)


class PlaneGather:
    def __init__(self, plane, block, rows, send, recv):
        self.plane = plane
        self.block = block
        self.send = send
        self.recv = recv
        self.upper = pl.ds(0, rows // 2)
        self.lower = pl.ds(rows // 2, rows // 2)

    def same(self, ref, i, device):
        return remote(ref, ref, self.send(i), self.recv(i), device)

    def first(self):
        own = self.block(self.plane.f)
        return (
            self.same(own.at[self.upper], 0, self.plane.to_x),
            self.same(own.at[self.lower], 1, self.plane.to_y),
        )

    def second(self):
        plane = self.plane
        return (
            self.same(self.block(plane.f).at[self.upper], 2, plane.to_y),
            self.same(self.block(plane.fx).at[self.upper], 3, plane.to_y),
            self.same(self.block(plane.f).at[self.lower], 4, plane.to_x),
            self.same(self.block(plane.fy).at[self.lower], 5, plane.to_x),
        )

    def third(self):
        plane = self.plane
        owners = (plane.f, plane.fx, plane.fy, plane.fd)
        return [self.same(self.block(o), 6 + i, plane.to_c) for i, o in enumerate(owners)]

    def start(self):
        for copy in self.first():
            copy.start()

    def middle(self):
        for copy in self.first():
            copy.wait_recv()
        for copy in self.second():
            copy.start()

    def finish(self):
        for copy in self.second():
            copy.wait_recv()
        for copy in self.third():
            copy.start()

    def wait(self):
        for copy in self.third():
            copy.wait_recv()

    def settle(self):
        for copy in (*self.first(), *self.second(), *self.third()):
            copy.wait_send()


def attention_kernel(
    dp,
    fsdp,
    hidden,
    cot,
    weight_in,
    inner_in,
    outer_in,
    gain_attn,
    gain,
    turn,
    live,
    branch,
    qkv,
    unit,
    scale,
    normed,
    weight,
    attended,
    c_all,
    inner_out,
    outer_out,
    hid_v,
    normed_v,
    w_v,
    raw,
    stat,
    stat_in,
    att_v,
    cols_v,
    rows_v,
    inner_raw,
    inner_v,
    outer_raw,
    outer_v,
    local,
    w_send,
    w_recv,
    right_send,
    right_recv,
    left_send,
    left_recv,
    h_send,
    h_recv,
    t_send,
    t_recv,
    a_send,
    a_recv,
    b_send,
    b_recv,
    c_send,
    c_recv,
    z_send,
    z_recv,
    in_send,
    in_recv,
    out_send,
    out_recv,
):
    n = dp * fsdp
    z = lax.axis_index("dp")
    f = lax.axis_index("fsdp")
    me = z * fsdp + f
    plane = Plane(f)
    rows, width = hidden.shape
    seq, cols = cols_v.shape
    own_rows = weight_in.shape[1]
    slab = fsdp * own_rows
    scaling = HEAD_DIM ** (-0.5)
    greet_all(n, fsdp, me)

    def weight_rows(index):
        return pl.ds(pl.multiple_of(index * own_rows, own_rows), own_rows)

    def weight_copy(k):
        target = lax.rem(f + k, fsdp)
        return remote(
            weight_in.at[target],
            w_v.at[weight_rows(me)],
            w_send.at[k],
            w_recv.at[k],
            {"fsdp": target},
        )

    qkv_cols = pl.ds(0, 3 * cols)
    out_cols = pl.ds(3 * cols, cols)

    def slab_copy(part, p, near, far, send, recv):
        lanes = (qkv_cols, out_cols)[part]
        ref = w_v.at[pl.ds(pl.multiple_of(p * slab, slab), slab), lanes]
        return remote(ref, ref, send.at[part, near], recv.at[part, near], {"dp": far})

    def slab_start(part):
        @pl.when(z < dp - 1)
        def _():
            slab_copy(part, z, 1, z + 1, right_send, right_recv).start()

        @pl.when(z > 0)
        def _():
            slab_copy(part, z, 1, z - 1, left_send, left_recv).start()

    def slab_pass(part, d):
        @pl.when(z >= d)
        def _():
            slab_copy(part, z - d, d, 0, right_send, right_recv).wait_recv()

            @pl.when(z < dp - 1)
            def _():
                slab_copy(part, z - d, d + 1, z + 1, right_send, right_recv).start()

        @pl.when(z + d < dp)
        def _():
            slab_copy(part, z + d, d, 0, left_send, left_recv).wait_recv()

            @pl.when(z > 0)
            def _():
                slab_copy(part, z + d, d + 1, z - 1, left_send, left_recv).start()

    def slab_settle(part):
        @pl.when(z < dp - 1)
        def _():
            slab_copy(part, z, 1, z + 1, right_send, right_recv).wait_send()

        @pl.when(z > 0)
        def _():
            slab_copy(part, z, 1, z - 1, left_send, left_recv).wait_send()

        for d in range(1, dp):

            @pl.when((z >= d) & (z < dp - 1))
            def _(d=d):
                slab_copy(part, z - d, d + 1, z + 1, right_send, right_recv).wait_send()

            @pl.when((z + d < dp) & (z > 0))
            def _(d=d):
                slab_copy(part, z + d, d + 1, z - 1, left_send, left_recv).wait_send()

    experts = inner_v.shape[0]
    here = experts // fsdp
    ff = width // 2
    part = ff // dp

    def inner_block(target, half):
        lanes = pl.ds(pl.multiple_of(half * ff + target // fsdp * part, part), part)
        owned = pl.ds(lax.rem(target, fsdp) * here, here)
        return inner_v.at[owned, :, lanes], inner_out.at[me, pl.ds(half * here, here)]

    def inner_copies(k):
        target = lax.rem(me + k, n)
        return [
            remote(
                *inner_block(target, half),
                in_send.at[k, half],
                in_recv.at[k, half],
                place(BOTH, fsdp, target),
            )
            for half in range(2)
        ]

    def outer_block(target):
        return outer_v.at[pl.ds(target * here, here)]

    def outer_copy(k):
        target = lax.rem(f + k, fsdp)
        return remote(
            outer_block(target), outer_out.at[f], out_send.at[k], out_recv.at[k], {"fsdp": target}
        )

    def cot_copy(i):
        return remote(
            cot,
            c_all.at[z, f],
            z_send.at[i],
            z_recv.at[i],
            {"dp": lax.rem(z + dp - i, dp)},
        )

    hidden_gather = PlaneGather(
        plane, lambda o: hid_v.at[o], rows, lambda i: h_send.at[i], lambda i: h_recv.at[i]
    )
    attended_gather = PlaneGather(
        plane, lambda o: att_v.at[o], seq, lambda i: a_send.at[i], lambda i: a_recv.at[i]
    )
    cot_gather = [
        PlaneGather(
            plane,
            lambda o, s=s: c_all.at[lax.rem(z + 1 + s, dp), o],
            rows,
            lambda i, s=s: c_send.at[s, i],
            lambda i, s=s: c_recv.at[s, i],
        )
        for s in range(dp)
    ]

    keeps = [
        pltpu.make_async_copy(hidden, hid_v.at[f], local.at[0]),
        pltpu.make_async_copy(weight_in.at[f], w_v.at[weight_rows(me)], local.at[1]),
        pltpu.make_async_copy(cot, c_all.at[z, f], local.at[2]),
        pltpu.make_async_copy(outer_in, outer_raw, local.at[3]),
        pltpu.make_async_copy(inner_in, inner_raw, local.at[4]),
    ]
    for copy in keeps:
        copy.start()
    for k in range(1, fsdp):
        weight_copy(k).start()
    for i in range(1, dp):
        cot_copy(i).start()
    keeps[0].wait()
    hidden_gather.start()
    keeps[1].wait()
    for k in range(1, fsdp):
        weight_copy(k).wait_recv()

    slab_start(0)
    hidden_gather.middle()
    keeps[2].wait()
    cot_gather[dp - 1].start()

    keeps[3].wait()
    outer_rows = outer_v.shape[1]

    def put_outer(i, tile, lanes, value):
        block = tile // outer_rows
        outer_v[pl.ds(i * block, block), :, lanes] = value.reshape(block, outer_rows, -1)

    reorder(lambda lanes: outer_raw[:, lanes], put_outer, outer_rows, experts)
    hidden_gather.finish()
    for k in range(1, fsdp):
        outer_copy(k).start()
    keeps[4].wait()

    def put_inner(i, tile, lanes, value):
        block = tile // own_rows
        inner_v[pl.ds(i * block, block), :, lanes] = value.reshape(block, own_rows, -1)

    reorder(lambda lanes: inner_raw[:, lanes], put_inner, own_rows, experts)
    owns = [
        pltpu.make_async_copy(outer_block(f), outer_out.at[f], local.at[3]),
        pltpu.make_async_copy(*inner_block(me, 0), local.at[4]),
        pltpu.make_async_copy(*inner_block(me, 1), local.at[5]),
    ]
    for copy in owns:
        copy.start()
    hidden_gather.wait()

    def norm_rows(i, carry):
        values = hid_v[i].astype(F32)
        values = values * lax.rsqrt(jnp.mean(values * values, axis=-1, keepdims=True) + EPS)
        r = pl.ds(pl.multiple_of(i * rows, rows), rows)
        normed_v[r, :] = (values * gain_attn[0:1, :]).astype(BF16)
        return carry

    lax.fori_loop(0, fsdp, norm_rows, 0)
    normed_store = pltpu.make_async_copy(normed_v, normed, local.at[0])
    normed_store.start()

    def cot_begin(s):
        cot_copy(s + 1).wait_recv()
        cot_gather[s].start()

    for d in range(1, dp):
        slab_pass(0, d)
        if d == 1:
            cot_gather[dp - 1].middle()
            cot_begin(0)
        elif d == 2:
            cot_gather[dp - 1].finish()
            cot_gather[0].middle()
            cot_begin(1)
    slab_start(1)
    for k in range(1, n):
        for copy in inner_copies(k):
            copy.start()

    tile = 256

    def project(i, carry):
        r = pl.ds(pl.multiple_of(i * tile, tile), tile)
        for j in range(3):
            col = pl.ds(j * cols, cols)
            value = dot(normed_v[r, :], w_v[:, col], ((1,), (0,)))
            if j < 2:
                raw[r, col] = value
            else:
                qkv[2, r, :] = value.astype(BF16)
        return carry

    lax.fori_loop(0, seq // tile, project, 0)
    row = lax.broadcasted_iota(jnp.int32, (8, 2 * cols), 0)
    lane_of = lax.broadcasted_iota(jnp.int32, (8, 2 * cols), 1)
    chooser = jnp.where(lane_of // cols == row, 1.0, 0.0).astype(F32)
    stat[...] = lax.dot_general(
        chooser,
        raw[...] * raw[...],
        (((1,), (1,)), ((), ())),
        precision=HIGH,
        preferred_element_type=F32,
    )

    def stat_copy(k):
        return remote(
            stat, stat_in.at[f], t_send.at[k], t_recv.at[k], {"fsdp": lax.rem(f + k, fsdp)}
        )

    for k in range(1, fsdp):
        stat_copy(k).start()
    stat_in[f] = stat[...]
    cot_gather[0].finish()
    cot_gather[1].middle()
    cot_begin(2)
    for k in range(1, fsdp):
        stat_copy(k).wait_recv()
    sums = stat_in[0]
    for i in range(1, fsdp):
        sums = sums + stat_in[i]
    corner = jnp.where(
        lax.broadcasted_iota(jnp.int32, (8, 128), 0) == lax.broadcasted_iota(jnp.int32, (8, 128), 1),
        1.0 / width,
        0.0,
    ).astype(F32)
    means = lax.dot_general(
        sums, corner, (((0,), (0,)), ((), ())), precision=HIGH, preferred_element_type=F32
    )
    slab_pass(1, 1)
    cot_gather[1].finish()
    cot_gather[2].middle()
    scale[...] = lax.rsqrt(means + EPS)
    for i in range(2):
        wide = pl.ds(i * cols, cols)
        unit[:, wide] = raw[:, wide] * scale[:, i : i + 1]
        for h in range(cols // HEAD_DIM):
            lane = pl.ds(i * cols + h * HEAD_DIM, HEAD_DIM)
            values = unit[:, lane] * gain[0:1, lane]
            values = values * turn[0] - pltpu.roll(values, HEAD_DIM // 2, 1) * turn[1]
            qkv[i, :, pl.ds(h * HEAD_DIM, HEAD_DIM)] = values.astype(BF16)

    def head(h, carry):
        lane = pl.ds(pl.multiple_of(h * HEAD_DIM, HEAD_DIM), HEAD_DIM)
        for t in range(seq // tile):
            r = pl.ds(t * tile, tile)
            extent = (t + 1) * tile
            upto = pl.ds(0, extent)
            scores = dot(qkv[0, r, lane], qkv[1, upto, lane], ((1,), (1,))) * scaling
            q_pos = t * tile + lax.broadcasted_iota(jnp.int32, (tile, extent), 0)
            k_pos = lax.broadcasted_iota(jnp.int32, (tile, extent), 1)
            allowed = (k_pos <= q_pos) & (live[0:1, 0:extent] > 0.0)
            masked = jnp.where(allowed, scores, -1e30)
            weights = jnp.exp(masked - jnp.max(masked, axis=-1, keepdims=True))
            weights = jnp.where(allowed, weights, 0.0)
            probs = weights / jnp.sum(weights, axis=-1, keepdims=True)
            att_v[f, r, lane] = dot(
                probs.astype(BF16), qkv[2, upto, lane], ((1,), (0,))
            ).astype(BF16)
        return carry

    lax.fori_loop(0, cols // HEAD_DIM, head, 0)
    attended_gather.start()
    slab_pass(1, 2)
    attended_gather.middle()
    cot_gather[2].finish()
    slab_pass(1, 3)
    attended_gather.finish()
    attended_gather.wait()
    attended_store = pltpu.make_async_copy(att_v, attended, local.at[2])
    attended_store.start()

    weight_store = pltpu.make_async_copy(w_v, weight, local.at[1])
    weight_store.start()


    def project_out(i, carry):
        r = pl.ds(pl.multiple_of(i * tile, tile), tile)
        total = dot(att_v[0, r, :], w_v[pl.ds(0, cols), out_cols], ((1,), (0,)))
        for j in range(1, fsdp):
            total += dot(att_v[j, r, :], w_v[pl.ds(j * cols, cols), out_cols], ((1,), (0,)))
        cols_v[r, :] = total.astype(BF16)
        return carry

    lax.fori_loop(0, seq // tile, project_out, 0)

    def branch_copy(k):
        target = lax.rem(f + k, fsdp)
        return remote(
            cols_v.at[pl.ds(pl.multiple_of(target * rows, rows), rows)],
            rows_v.at[f],
            b_send.at[k],
            b_recv.at[k],
            {"fsdp": target},
        )

    for k in range(1, fsdp):
        branch_copy(k).start()
    rows_v[f] = cols_v[pl.ds(pl.multiple_of(f * rows, rows), rows), :]
    for k in range(1, fsdp):
        branch_copy(k).wait()
    for i in range(fsdp):
        branch[:, pl.ds(i * cols, cols)] = rows_v[i]

    for s in range(dp):
        cot_gather[s].wait()
        cot_gather[s].settle()
    hidden_gather.settle()
    attended_gather.settle()
    for i in range(1, dp):
        cot_copy(i).wait_send()

    slab_settle(0)
    slab_settle(1)
    for k in range(1, fsdp):
        weight_copy(k).wait_send()
        stat_copy(k).wait_send()
        outer_copy(k).wait()
    for k in range(1, n):
        for copy in inner_copies(k):
            copy.wait()
    for copy in owns:
        copy.wait()
    normed_store.wait()
    weight_store.wait()
    attended_store.wait()


def attention_forward(
    hidden, cot, weight_in, inner_in, outer_in, gain_attn, gain, turn, live, ident
):
    dp = lax.axis_size("dp")
    fsdp = lax.axis_size("fsdp")
    n = dp * fsdp
    rows, width = hidden.shape
    seq = rows * fsdp
    cols = width // fsdp
    shape = jax.ShapeDtypeStruct
    dma = pltpu.SemaphoreType.DMA
    vmem = pltpu.VMEM
    anywhere = pl.BlockSpec(memory_space=pl.ANY)
    inside = pl.BlockSpec(memory_space=pltpu.VMEM)
    sems = [dma((fsdp,)), dma((fsdp,))] + [dma((2, dp + 1))] * 4
    for size in (10, fsdp, 10, fsdp):
        sems += [dma((size,)), dma((size,))]
    sems += [dma((dp, 10)), dma((dp, 10)), dma((dp,)), dma((dp,))]
    sems += [dma((n, 2)), dma((n, 2)), dma((fsdp,)), dma((fsdp,))]
    experts = inner_in.shape[1]
    out_rows = outer_in.shape[0]
    here = experts // fsdp
    return pl.pallas_call(
        functools.partial(attention_kernel, dp, fsdp),
        out_shape=(
            shape((rows, width), BF16),
            shape((3, seq, cols), BF16),
            shape((seq, 2 * cols), F32),
            shape((seq, 128), F32),
            shape((seq, width), BF16),
            shape((width, 4 * cols), BF16),
            shape((fsdp, seq, cols), BF16),
            shape((dp, fsdp, rows, width), BF16),
            shape((n, 2 * here, width // n, width // 2 // dp), BF16),
            shape((fsdp, here, out_rows, width), BF16),
        ),
        in_specs=[anywhere] * 5 + [inside] * 4,
        out_specs=(inside,) * 4 + (anywhere,) * 6,
        scratch_shapes=[
            vmem((fsdp, rows, width), BF16),
            vmem((seq, width), BF16),
            vmem((width, 4 * cols), BF16),
            vmem((seq, 2 * cols), F32),
            vmem((8, seq), F32),
            vmem((fsdp, 8, seq), F32),
            vmem((fsdp, seq, cols), BF16),
            vmem((seq, cols), BF16),
            vmem((fsdp, rows, cols), BF16),
            vmem((width // n * experts, width), BF16),
            vmem((experts, width // n, width), BF16),
            vmem((out_rows * experts, width), BF16),
            vmem((experts, out_rows, width), BF16),
            dma((6,)),
            *sems,
        ],
        compiler_params=pltpu.CompilerParams(
            collective_id=ident, has_side_effects=True, vmem_limit_bytes=63 * 1024 * 1024
        ),
    )(
        hidden,
        cot,
        weight_in,
        inner_in.reshape(-1, width),
        outer_in.reshape(-1, width),
        gain_attn,
        gain,
        turn,
        live,
    )


def attention_back_kernel(
    dp,
    fsdp,
    grad_rows,
    attended,
    weight,
    normed,
    qkv,
    unit,
    scale,
    gain,
    turn,
    live,
    grad_middle,
    hidden,
    gain_attn,
    terms,
    first_in,
    inner_in,
    outer_in,
    hidden_grad,
    terms_out,
    owned,
    inner_owned,
    outer_owned,
    inner_out,
    outer_out,
    att_v,
    w_v,
    normed_v,
    gcols,
    part1,
    held1,
    core1,
    half1,
    full1,
    part2,
    held2,
    core2,
    half2,
    full2,
    gatt,
    gq,
    gk,
    gval,
    gqk,
    gqkv,
    stat,
    stat_in,
    wgrad,
    z_in,
    wsum,
    term_v,
    term_in,
    local,
    v_send,
    v_recv,
    in_send,
    in_recv,
    out_send,
    out_recv,
    g_send,
    g_recv,
    s1_send,
    s1_recv,
    s2_send,
    s2_recv,
    t_send,
    t_recv,
    r_send,
    r_recv,
    l_send,
    l_recv,
    w_send,
    w_recv,
):
    n = dp * fsdp
    z = lax.axis_index("dp")
    f = lax.axis_index("fsdp")
    me = z * fsdp + f
    plane = Plane(f)
    rows, width = grad_rows.shape
    seq, cols = gcols.shape
    own_rows = width // n
    slab = fsdp * own_rows
    scaling = HEAD_DIM ** (-0.5)
    greet_all(n, fsdp, me)
    ff = width // 2
    ff_here = ff // dp

    inner_place = inner_out.at[f, :, pl.ds(pl.multiple_of(z * ff_here, ff_here), ff_here)]

    pair = outer_in.shape[1]
    outer_place = outer_out.at[f // 2, pl.ds(pl.multiple_of(lax.rem(f, 2) * pair, pair), pair)]

    loads = [
        pltpu.make_async_copy(attended, att_v, local.at[0]),
        pltpu.make_async_copy(weight, w_v, local.at[1]),
        pltpu.make_async_copy(normed, normed_v, local.at[2]),
        pltpu.make_async_copy(
            grad_rows.at[:, pl.ds(pl.multiple_of(f * cols, cols), cols)],
            gcols.at[pl.ds(pl.multiple_of(f * rows, rows), rows)],
            local.at[3],
        ),
    ]
    keeps = [
        pltpu.make_async_copy(inner_in.at[me], inner_place, local.at[4]),
        pltpu.make_async_copy(outer_in.at[f], outer_place, local.at[6]),
    ]
    for copy in loads:
        copy.start()

    def cols_copy(k):
        target = lax.rem(f + k, fsdp)
        return remote(
            grad_rows.at[:, pl.ds(pl.multiple_of(target * cols, cols), cols)],
            gcols.at[pl.ds(pl.multiple_of(f * rows, rows), rows)],
            g_send.at[k],
            g_recv.at[k],
            {"fsdp": target},
        )

    def inner_copy(k):
        target = lax.rem(me + k, n)
        return remote(
            inner_in.at[target],
            inner_place,
            in_send.at[k],
            in_recv.at[k],
            place(BOTH, fsdp, target),
        )

    def outer_copy(k):
        target = lax.rem(f + k, fsdp)
        return remote(
            outer_in.at[target], outer_place, out_send.at[k], out_recv.at[k], {"fsdp": target}
        )

    def slab_rows(p):
        return pl.ds(pl.multiple_of(p * slab, slab), slab)

    def right_copy(part, d):
        lanes = (qkv_cols, out_cols)[part]
        return remote(
            wgrad.at[slab_rows(z + d), lanes],
            z_in.at[z + d, :, lanes],
            r_send.at[part, d],
            r_recv.at[part, d - 1],
            {"dp": z + 1},
        )

    def left_copy(part, d):
        lanes = (qkv_cols, out_cols)[part]
        return remote(
            wgrad.at[slab_rows(z - d), lanes],
            z_in.at[dp if d == 1 else z - d, :, lanes],
            l_send.at[part, d],
            l_recv.at[part, d - 1],
            {"dp": z - 1},
        )

    def arrived(part, slot, sem):
        lanes = (qkv_cols, out_cols)[part]
        ref = z_in.at[slot, :, lanes]
        remote(ref, ref, sem, sem, plane.to_x).wait_recv()

    def pass_along(part, d):
        lanes = (qkv_cols, out_cols)[part]

        def add(p):
            block = slab_rows(p)
            wgrad[block, lanes] = (
                wgrad[block, lanes].astype(F32) + z_in[p, :, lanes].astype(F32)
            ).astype(BF16)

        @pl.when(z + d < dp)
        def _():
            @pl.when(z > 0)
            def _():
                arrived(part, z + d, r_recv.at[part, d])
                add(z + d)

            right_copy(part, d).start()

        @pl.when(z >= d)
        def _():
            @pl.when(z < dp - 1)
            def _():
                arrived(part, z - d, l_recv.at[part, d])
                add(z - d)

            left_copy(part, d).start()

    qkv_cols = pl.ds(0, 3 * cols)
    out_cols = pl.ds(3 * cols, cols)

    for k in range(1, fsdp):
        cols_copy(k).start()
    for k in range(1, n):
        inner_copy(k).start()
    for k in range(1, fsdp):
        outer_copy(k).start()
    for copy in keeps:
        copy.start()
    term_v[...] = terms[...]
    for copy in loads:
        copy.wait()
    for k in range(1, fsdp):
        cols_copy(k).wait_recv()

    def attended_back(i, carry):
        block = pl.ds(pl.multiple_of(i * cols, cols), cols)
        part1[i] = dot(gcols[...], w_v[block, out_cols], ((1,), (1,))).astype(BF16)
        return carry

    lax.fori_loop(0, fsdp, attended_back, 0)
    sum1 = PlaneSum(plane, part1, held1, core1, half1, full1, s1_send, s1_recv)
    sum1.start()

    def out_grads(i, carry):
        block = pl.ds(pl.multiple_of(i * cols, cols), cols)
        wgrad[block, out_cols] = dot(att_v[i], gcols[...], ((0,), (0,))).astype(BF16)
        return carry

    lax.fori_loop(0, fsdp // 2, out_grads, 0)
    sum1.add_core()
    lax.fori_loop(fsdp // 2, fsdp, out_grads, 0)
    sum1.pass_on()
    pass_along(1, 3)
    gk[...] = jnp.zeros_like(gk)
    gval[...] = jnp.zeros_like(gval)
    gatt[...] = sum1.total().astype(BF16)

    tile = 256

    def head(h, carry):
        lane = pl.ds(pl.multiple_of(h * HEAD_DIM, HEAD_DIM), HEAD_DIM)
        for t in range(seq // tile):
            r = pl.ds(t * tile, tile)
            extent = (t + 1) * tile
            upto = pl.ds(0, extent)
            query = qkv[0, r, lane]
            key = qkv[1, upto, lane]
            value = qkv[2, upto, lane]
            grad = gatt[r, lane]
            scores = dot(query, key, ((1,), (1,))) * scaling
            q_pos = t * tile + lax.broadcasted_iota(jnp.int32, (tile, extent), 0)
            k_pos = lax.broadcasted_iota(jnp.int32, (tile, extent), 1)
            allowed = (k_pos <= q_pos) & (live[0:1, 0:extent] > 0.0)
            masked = jnp.where(allowed, scores, -1e30)
            weights = jnp.exp(masked - jnp.max(masked, axis=-1, keepdims=True))
            weights = jnp.where(allowed, weights, 0.0)
            probs = weights / jnp.sum(weights, axis=-1, keepdims=True)
            grad_probs = dot(grad, value, ((1,), (1,)))
            mean = jnp.sum(probs * grad_probs, axis=-1, keepdims=True)
            grad_scores = (probs * (grad_probs - mean)).astype(BF16)
            gq[r, lane] = dot(grad_scores, key, ((1,), (0,)))
            gk[upto, lane] += dot(grad_scores, query, ((0,), (0,)))
            gval[upto, lane] += dot(probs.astype(BF16), grad, ((0,), (0,)))
        return carry

    lax.fori_loop(0, cols // HEAD_DIM, head, 0)

    pass_along(1, 2)

    heads_here = cols // HEAD_DIM
    for i, source in enumerate((gq, gk)):
        for h in range(heads_here):
            lane = pl.ds(h * HEAD_DIM, HEAD_DIM)
            wide = pl.ds(i * cols + h * HEAD_DIM, HEAD_DIM)
            grad = source[:, lane] * scaling
            grad = grad * turn[0] + pltpu.roll(grad, HEAD_DIM // 2, 1) * turn[1]
            place_lanes = pl.ds(pl.multiple_of(f * cols + h * HEAD_DIM, HEAD_DIM), HEAD_DIM)
            term_v[1 + i : 2 + i, place_lanes] = jnp.sum(
                grad * unit[:, wide], axis=0, keepdims=True
            )
            gqk[:, wide] = grad * gain[0:1, wide]
    row = lax.broadcasted_iota(jnp.int32, (8, 2 * cols), 0)
    lane_of = lax.broadcasted_iota(jnp.int32, (8, 2 * cols), 1)
    chooser = jnp.where(lane_of // cols == row, 1.0, 0.0).astype(F32)
    stat[...] = lax.dot_general(
        chooser,
        gqk[...] * unit[...],
        (((1,), (1,)), ((), ())),
        precision=HIGH,
        preferred_element_type=F32,
    )

    def stat_copy(k):
        return remote(
            stat, stat_in.at[f], t_send.at[k], t_recv.at[k], {"fsdp": lax.rem(f + k, fsdp)}
        )

    for k in range(1, fsdp):
        stat_copy(k).start()
    stat_in[f] = stat[...]
    gqkv[:, pl.ds(2 * cols, cols)] = gval[...].astype(BF16)
    for k in range(1, fsdp):
        stat_copy(k).wait_recv()
    sums = stat_in[0]
    for i in range(1, fsdp):
        sums = sums + stat_in[i]
    corner = jnp.where(
        lax.broadcasted_iota(jnp.int32, (8, 128), 0) == lax.broadcasted_iota(jnp.int32, (8, 128), 1),
        1.0 / width,
        0.0,
    ).astype(F32)
    means = lax.dot_general(
        sums, corner, (((0,), (0,)), ((), ())), precision=HIGH, preferred_element_type=F32
    )
    for i in range(2):
        wide = pl.ds(i * cols, cols)
        grad = scale[:, i : i + 1] * (gqk[:, wide] - unit[:, wide] * means[:, i : i + 1])
        gqkv[:, wide] = grad.astype(BF16)

    step = 512

    def normed_back(i, carry):
        r = pl.ds(pl.multiple_of(i * rows, rows), rows)
        for c in range(width // step):
            col = pl.ds(c * step, step)
            part2[i, :, col] = dot(gqkv[r, :], w_v[col, qkv_cols], ((1,), (1,))).astype(BF16)
        return carry

    lax.fori_loop(0, fsdp, normed_back, 0)
    sum2 = PlaneSum(plane, part2, held2, core2, half2, full2, s2_send, s2_recv)
    sum2.start()

    def qkv_grads(p):
        for i in range(2):
            block = pl.ds(pl.multiple_of(p * slab + i * (slab // 2), slab // 2), slab // 2)
            wgrad[block, qkv_cols] = dot(normed_v[:, block], gqkv[...], ((0,), (0,))).astype(BF16)

    for p in range(dp):
        qkv_grads(p)
    pass_along(0, 3)
    sum2.add_core()
    pass_along(1, 1)
    pass_along(0, 2)
    sum2.pass_on()

    grad = sum2.total()
    pass_along(0, 1)
    values = hidden[...].astype(F32)
    scale1 = lax.rsqrt(jnp.mean(values * values, axis=-1, keepdims=True) + EPS)
    values = values * scale1
    term_v[0:1, :] = jnp.sum(grad * values, axis=0, keepdims=True)
    grad = grad * gain_attn[0:1, :]
    grad = scale1 * (grad - values * jnp.mean(grad * values, axis=-1, keepdims=True))
    hidden_grad[...] = grad_middle[...] + grad

    def term_copy(k):
        target = lax.rem(me + k, n)
        lanes = pl.ds(pl.multiple_of(target // 2 * 128, 128), 128)
        return remote(
            term_v.at[:, lanes],
            term_in.at[me],
            v_send.at[k],
            v_recv.at[k],
            place(BOTH, fsdp, target),
        )

    for k in range(1, n):
        term_copy(k).start()
    term_in[me] = term_v[:, pl.ds(pl.multiple_of(me // 2 * 128, 128), 128)]

    for copy in keeps:
        copy.wait()
    for k in range(1, fsdp):
        outer_copy(k).wait()
    outer_load = pltpu.make_async_copy(outer_out, core2, local.at[0])
    outer_load.start()
    for k in range(1, n):
        inner_copy(k).wait()
    inner_loads = [
        pltpu.make_async_copy(first_in, part2.at[:, :, pl.ds(0, ff)], local.at[1]),
        pltpu.make_async_copy(inner_out, part2.at[:, :, pl.ds(ff, ff)], local.at[2]),
    ]
    for copy in inner_loads:
        copy.start()
    experts = fsdp * (inner_in.shape[1] // own_rows)
    outer_load.wait()
    outer_rows = core2.shape[0] * core2.shape[1]
    inner_rows = part2.shape[0] * part2.shape[1]

    def put_outer(i, tile, lanes, value):
        block = tile // rows
        held2[pl.ds(i * block, block), :, lanes] = value.reshape(block, rows, -1)

    reorder(
        lambda lanes: core2[:, :, lanes].reshape(outer_rows, -1),
        put_outer,
        experts,
        outer_rows // experts,
    )
    for copy in inner_loads:
        copy.wait()

    def put_inner(i, tile, lanes, value):
        normed_v[pl.ds(pl.multiple_of(i * tile, tile), tile), lanes] = value

    reorder(
        lambda lanes: part2[:, :, lanes].reshape(inner_rows, -1),
        put_inner,
        experts,
        inner_rows // experts,
    )
    stores = [
        pltpu.make_async_copy(held2, outer_owned, local.at[0]),
        pltpu.make_async_copy(normed_v, inner_owned, local.at[1]),
    ]
    for store in stores:
        store.start()

    @pl.when(z > 0)
    def _():
        for part in range(2):
            arrived(part, z, r_recv.at[part, 0])
        total = wgrad[slab_rows(z), :].astype(F32) + z_in[z].astype(F32)
        wgrad[slab_rows(z), :] = total.astype(BF16)

    @pl.when(z < dp - 1)
    def _():
        for part in range(2):
            arrived(part, dp, l_recv.at[part, 0])
        total = wgrad[slab_rows(z), :].astype(F32) + z_in[dp].astype(F32)
        wgrad[slab_rows(z), :] = total.astype(BF16)

    for part in range(2):
        for d in range(1, dp):

            @pl.when(z + d < dp)
            def _(part=part, d=d):
                right_copy(part, d).wait_send()

            @pl.when(z >= d)
            def _(part=part, d=d):
                left_copy(part, d).wait_send()

    total = wgrad[slab_rows(z), :]
    wsum[...] = total.astype(BF16).reshape(wsum.shape)

    def owner_copy(k):
        target = lax.rem(f + k, fsdp)
        return remote(
            wsum.at[target], owned.at[f], w_send.at[k], w_recv.at[k], {"fsdp": target}
        )

    for k in range(1, fsdp):
        owner_copy(k).start()
    owned[f] = wsum[f]
    for k in range(1, fsdp):
        owner_copy(k).wait()
    for k in range(1, fsdp):
        cols_copy(k).wait_send()
        stat_copy(k).wait_send()
    for k in range(1, n):
        term_copy(k).wait()
    total = term_in[0]
    for i in range(1, n):
        total += term_in[i]
    terms_out[...] = total
    for store in stores:
        store.wait()


def attention_back(
    grad_rows,
    attended,
    weight,
    normed,
    qkv,
    unit,
    scale,
    gain,
    turn,
    live,
    grad_middle,
    hidden,
    gain_attn,
    terms,
    first_in,
    inner_in,
    outer_in,
    ident,
):
    dp = lax.axis_size("dp")
    fsdp = lax.axis_size("fsdp")
    n = dp * fsdp
    rows, width = grad_rows.shape
    seq = rows * fsdp
    cols = width // fsdp
    own_rows = width // n
    shape = jax.ShapeDtypeStruct
    dma = pltpu.SemaphoreType.DMA
    vmem = pltpu.VMEM
    anywhere = pl.BlockSpec(memory_space=pl.ANY)
    inside = pl.BlockSpec(memory_space=pltpu.VMEM)
    return pl.pallas_call(
        functools.partial(attention_back_kernel, dp, fsdp),
        out_shape=(
            shape((rows, width), F32),
            shape((terms.shape[0], 128), F32),
            shape((fsdp, own_rows, 4 * cols), BF16),
            shape((seq, width), BF16),
            shape((4, rows, width), BF16),
            shape((fsdp, rows, width // 2), BF16),
            shape((4, rows, width), BF16),
        ),
        in_specs=[anywhere] * 4 + [inside] * 10 + [anywhere] * 3,
        out_specs=(inside,) * 3 + (anywhere,) * 4,
        scratch_shapes=[
            vmem((fsdp, seq, cols), BF16),
            vmem((width, 4 * cols), BF16),
            vmem((seq, width), BF16),
            vmem((seq, cols), BF16),
            vmem((fsdp, seq, cols), BF16),
            vmem((4, seq, cols), BF16),
            vmem((4, seq, cols), BF16),
            vmem((2, seq // 2, cols), BF16),
            vmem((2, seq, cols), BF16),
            vmem((fsdp, rows, width), BF16),
            vmem((4, rows, width), BF16),
            vmem((4, rows, width), BF16),
            vmem((2, rows // 2, width), BF16),
            vmem((2, rows, width), BF16),
            vmem((seq, cols), BF16),
            vmem((seq, cols), F32),
            vmem((seq, cols), F32),
            vmem((seq, cols), F32),
            vmem((seq, 2 * cols), F32),
            vmem((seq, 3 * cols), BF16),
            vmem((8, seq), F32),
            vmem((fsdp, 8, seq), F32),
            vmem((width, 4 * cols), BF16),
            vmem((dp + 1, fsdp * own_rows, 4 * cols), BF16),
            vmem((fsdp, own_rows, 4 * cols), BF16),
            vmem(terms.shape, F32),
            vmem((n, terms.shape[0], 128), F32),
            dma((7,)),
            dma((n,)),
            dma((n,)),
            dma((n,)),
            dma((n,)),
            dma((fsdp,)),
            dma((fsdp,)),
            dma((fsdp,)),
            dma((fsdp,)),
            dma((8,)),
            dma((8,)),
            dma((8,)),
            dma((8,)),
            dma((fsdp,)),
            dma((fsdp,)),
            dma((2, dp)),
            dma((2, dp)),
            dma((2, dp)),
            dma((2, dp)),
            dma((fsdp,)),
            dma((fsdp,)),
        ],
        compiler_params=pltpu.CompilerParams(
            collective_id=ident, has_side_effects=True, vmem_limit_bytes=63 * 1024 * 1024
        ),
    )(
        grad_rows,
        attended,
        weight,
        normed,
        qkv,
        unit,
        scale,
        gain,
        turn,
        live,
        grad_middle,
        hidden,
        gain_attn,
        terms,
        first_in,
        inner_in,
        outer_in,
    )


def expert_kernel(
    dp,
    fsdp,
    x_in,
    c_all,
    gates,
    inner_in,
    outer_in,
    sums,
    gate_sum,
    first_out,
    inner_out,
    outer_out,
    gathered,
    far,
    xv,
    cv,
    wi,
    wo,
    gi,
    go,
    ggu,
    act,
    gv,
    part,
    held,
    core_in,
    half_in,
    full_in,
    leaving,
    gates_in,
    grads_out,
    grads_in,
    local,
    g_send,
    g_recv,
    gg_send,
    gg_recv,
    f_send,
    f_recv,
    z_send,
    z_recv,
    a_send,
    a_recv,
    b_send,
    b_recv,
    k_send,
    k_recv,
    c_send,
    c_recv,
    s1_send,
    s1_recv,
    s2_send,
    s2_recv,
    o_send,
    o_recv,
    credit,
):
    rows, width = x_in.shape
    half = rows // 2
    z = lax.axis_index("dp")
    f = lax.axis_index("fsdp")
    core = lax.rem(f, 2)
    chip = f // 2
    xbit = lax.rem(chip, 2)
    ybit = chip // 2
    chip_x = ybit * 2 + (1 - xbit)
    chip_y = (1 - ybit) * 2 + xbit
    chip_d = (1 - ybit) * 2 + (1 - xbit)
    fx = chip_x * 2 + core
    fy = chip_y * 2 + core
    fd = chip_d * 2 + core
    fc = chip * 2 + (1 - core)
    to_x = {"fsdp": fx}
    to_y = {"fsdp": fy}
    to_c = {"fsdp": fc}
    upper = pl.ds(0, half)
    lower = pl.ds(half, half)

    def remote(src, dst, send, recv, device):
        return pltpu.make_async_remote_copy(
            src, dst, send, recv, device_id=device, device_id_type=MESH_ID
        )

    def plane_at(s):
        return lax.rem(z + 1 + s, dp)

    def far_copy(i):
        return remote(
            x_in,
            gathered.at[z, f],
            z_send.at[i],
            z_recv.at[i],
            {"dp": lax.rem(z + dp - i, dp)},
        )

    def gather_one(s):
        block = gathered.at[plane_at(s), f]
        return (
            remote(block.at[upper], block.at[upper], a_send.at[s, 0], a_recv.at[s, 0], to_x),
            remote(block.at[lower], block.at[lower], a_send.at[s, 1], a_recv.at[s, 1], to_y),
        )

    def gather_two(s):
        p = plane_at(s)
        copies = []
        for i, (owner, piece, device) in enumerate(
            ((f, upper, to_y), (fx, upper, to_y), (f, lower, to_x), (fy, lower, to_x))
        ):
            ref = gathered.at[p, owner, piece]
            copies.append(remote(ref, ref, b_send.at[s, i], b_recv.at[s, i], device))
        return copies

    def gather_core(s):
        p = plane_at(s)
        copies = []
        for i, owner in enumerate((f, fx, fy, fd)):
            ref = gathered.at[p, owner]
            copies.append(remote(ref, ref, k_send.at[s, i], k_recv.at[s, i], to_c))
        return copies

    def block_rows(owner):
        return pl.ds(pl.multiple_of(owner * rows, rows), rows)

    def core_copy(k, j):
        return remote(
            part.at[k, block_rows(j * 2 + 1 - core)],
            core_in.at[k, j],
            c_send.at[k, j],
            c_recv.at[k, j],
            to_c,
        )

    def half_copies(k):
        return (
            remote(
                held.at[k, chip_d, upper], half_in.at[k, 0], s1_send.at[k, 0], s1_recv.at[k, 0], to_x
            ),
            remote(
                held.at[k, chip_d, lower], half_in.at[k, 1], s1_send.at[k, 1], s1_recv.at[k, 1], to_y
            ),
        )

    def full_copies(k):
        return (
            remote(held.at[k, chip_x], full_in.at[k, 0], s2_send.at[k, 0], s2_recv.at[k, 0], to_x),
            remote(held.at[k, chip_y], full_in.at[k, 1], s2_send.at[k, 1], s2_recv.at[k, 1], to_y),
        )

    def out_copy(s, k):
        return remote(
            leaving.at[lax.rem(s, 2), k],
            far.at[k, z],
            o_send.at[s, k],
            o_recv.at[s, k],
            {"dp": plane_at(s)},
        )

    def add_core():
        def add_block(k, j):
            core_copy(k, j).wait()
            held[k, j] = (
                part[k, block_rows(j * 2 + core)].astype(F32) + core_in[k, j].astype(F32)
            ).astype(BF16)

        for k in range(2):
            add_block(k, chip_d)
            for copy in half_copies(k):
                copy.start()
        for k in range(2):
            for j in (chip_x, chip_y, chip):
                add_block(k, j)
        pl.semaphore_signal(credit, inc=1, device_id=to_c, device_id_type=MESH_ID)

    def pass_full():
        for k in range(2):
            for copy in half_copies(k):
                copy.wait()
            held[k, chip_y, upper] = (
                held[k, chip_y, upper].astype(F32) + half_in[k, 0].astype(F32)
            ).astype(BF16)
            held[k, chip_x, lower] = (
                held[k, chip_x, lower].astype(F32) + half_in[k, 1].astype(F32)
            ).astype(BF16)
            for copy in full_copies(k):
                copy.start()

    def total_here(k):
        for copy in full_copies(k):
            copy.wait()
        return held[k, chip].astype(F32) + full_in[k, 0].astype(F32) + full_in[k, 1].astype(F32)

    n = dp * fsdp
    me = z * fsdp + f
    greet_all(n, fsdp, me)

    def gate_copy(k):
        target = lax.rem(me + k, n)
        return remote(
            gates.at[target],
            gates_in.at[me],
            g_send.at[k],
            g_recv.at[k],
            place(BOTH, fsdp, target),
        )

    def gate_grad_copy(k):
        target = lax.rem(me + k, n)
        return remote(
            grads_out.at[target],
            grads_in.at[me],
            gg_send.at[k],
            gg_recv.at[k],
            place(BOTH, fsdp, target),
        )

    own_rows = wi.shape[2]
    first_lanes = pl.ds(pl.multiple_of(z * wi.shape[3], wi.shape[3]), wi.shape[3])

    def first_ref(e):
        return first_out.at[f, pl.ds(e * own_rows, own_rows), first_lanes]

    def first_copy(k, e):
        target = lax.rem(me + k, n)
        return remote(
            wi.at[e, target],
            first_ref(e),
            f_send.at[k, e],
            f_recv.at[k, e],
            place(BOTH, fsdp, target),
        )

    far_copy(1).start()
    for k in range(1, n):
        gate_copy(k).start()
    loads = [pltpu.make_async_copy(x_in, gathered.at[z, f], local.at[0])]
    for q in range(4):
        loads.append(pltpu.make_async_copy(inner_in.at[:, q], wi.at[q], local.at[1 + q]))
    for e in range(2):
        loads.append(pltpu.make_async_copy(outer_in.at[:, e], wo.at[e], local.at[5 + e]))
    loads.append(pltpu.make_async_copy(gates.at[me], gates_in.at[me], local.at[7]))
    for load in loads:
        load.start()
    gi[...] = jnp.zeros_like(gi)
    go[...] = jnp.zeros_like(go)
    for load in loads:
        load.wait()

    def begin_gather(s):
        @pl.when(s < dp - 1)
        def _():
            far_copy(s + 1).wait_recv()

        for copy in gather_one(s):
            copy.start()

    def middle_gather(s):
        for copy in gather_one(s):
            copy.wait_recv()
        for copy in gather_two(s):
            copy.start()

    def end_gather(s):
        for copy in gather_two(s):
            copy.wait_recv()
        for copy in gather_core(s):
            copy.start()

    begin_gather(0)
    for i in range(2, dp):
        far_copy(i).start()
    middle_gather(0)
    end_gather(0)
    begin_gather(1)
    for k in range(1, n):
        gate_copy(k).wait()

    inner_rows = wi.shape[1] * wi.shape[2]
    ff_here = wo.shape[1] * wo.shape[2]
    tile = xv.shape[0] // 2

    def tile_step(t):
        r = pl.ds(pl.multiple_of(t * tile, tile), tile)
        x = xv[r, :]
        c = cv[r, :]
        for e in range(2):
            gate = dot(x, wi[e].reshape(inner_rows, ff_here), ((1,), (0,)))
            up = dot(x, wi[2 + e].reshape(inner_rows, ff_here), ((1,), (0,)))
            back = dot(c, wo[e].reshape(ff_here, width), ((1,), (1,)))
            sigmoid = 1.0 / (1.0 + jnp.exp(-gate))
            silu = gate * sigmoid
            active = (silu * up).astype(BF16).astype(F32)
            weight = gv[r, e : e + 1]
            gv[r, 8 + e : 9 + e] = jnp.sum(active * back, axis=-1, keepdims=True)
            act[e, r, :] = (weight * active).astype(BF16)
            back = weight * back
            ggu[e, r, :] = (back * up * sigmoid * (1.0 + gate * (1.0 - sigmoid))).astype(BF16)
            ggu[2 + e, r, :] = (back * silu).astype(BF16)
        step = 512
        for i in range(width // step):
            col = pl.ds(i * step, step)
            blocks = pl.ds(i * step // wi.shape[2], step // wi.shape[2])
            total = dot(act[0, r, :], wo[0, :, :, col].reshape(ff_here, step), ((1,), (0,)))
            total += dot(act[1, r, :], wo[1, :, :, col].reshape(ff_here, step), ((1,), (0,)))
            part[0, r, col] = total.astype(BF16)
            total = dot(ggu[0, r, :], wi[0, blocks].reshape(step, ff_here), ((1,), (1,)))
            for q in range(1, 4):
                total += dot(ggu[q, r, :], wi[q, blocks].reshape(step, ff_here), ((1,), (1,)))
            part[1, r, col] = total.astype(BF16)

    def weight_step():
        def inner_part(i, carry):
            col = pl.ds(pl.multiple_of(i * 256, 256), 256)
            xt = xv[:, col]
            for q in range(4):
                gi[q, col, :] += dot(xt, ggu[q], ((0,), (0,)))
            return carry

        lax.fori_loop(0, width // 256, inner_part, 0)

        def outer_part(i, carry):
            col = pl.ds(pl.multiple_of(i * 512, 512), 512)
            ct = cv[:, col]
            for e in range(2):
                go[e, :, col] += dot(act[e], ct, ((0,), (0,)))
            return carry

        lax.fori_loop(0, width // 512, outer_part, 0)

    def chunk(s, carry):
        p = plane_at(s)
        c_load = pltpu.make_async_copy(c_all.at[p], cv, local.at[1])
        c_load.start()

        def to_columns(j, carry):
            r = pl.ds(pl.multiple_of(j * rows, rows), rows)
            gv[r, :] = exact_dot(gates_in[p * fsdp + j], corner_of(8, 0, 1.0), ((0,), (0,)))
            return carry

        lax.fori_loop(0, fsdp, to_columns, 0)
        for copy in gather_core(s):
            copy.wait_recv()
        for j in range(8):
            pltpu.make_async_copy(
                gathered.at[p, j], xv.at[pl.ds(j * rows, rows)], local.at[3 + j]
            ).start()
        c_load.wait()
        for j in range(8):
            pltpu.make_async_copy(
                gathered.at[p, j], xv.at[pl.ds(j * rows, rows)], local.at[3 + j]
            ).wait()
        @pl.when(s < dp - 1)
        def _():
            middle_gather(s + 1)

        tile_step(0)

        @pl.when(s > 0)
        def _():
            pass_full()

        @pl.when(s < dp - 2)
        def _():
            begin_gather(s + 2)

        tile_step(1)

        @pl.when(s > 0)
        def _():
            pl.semaphore_wait(credit, 1)

        for k in range(2):
            for j in range(4):
                core_copy(k, j).start()
        def to_rows(j, carry):
            r = pl.ds(pl.multiple_of(j * rows, rows), rows)
            grads_out[p * fsdp + j] = exact_dot(corner_of(8, 8, 1.0), gv[r, :], ((1,), (1,)))
            return carry

        lax.fori_loop(0, fsdp, to_rows, 0)
        weight_step()

        @pl.when(s > 0)
        def _():
            @pl.when(s > 2)
            def _():
                for k in range(2):
                    out_copy(s - 3, k).wait_send()

            for k in range(2):
                leaving[lax.rem(s - 1, 2), k] = total_here(k).astype(BF16)
                out_copy(s - 1, k).start()

        add_core()

        @pl.when(s < dp - 1)
        def _():
            end_gather(s + 1)

        @pl.when(s == dp - 1)
        def _():
            for e in range(2):
                wi[e] = gi[e].astype(BF16).reshape(wi.shape[1:])
            for k in range(1, n):
                for e in range(2):
                    first_copy(k, e).start()

        return carry

    lax.fori_loop(0, dp, chunk, 0)

    pass_full()
    for k in range(1, n):
        gate_grad_copy(k).start()
    grads_in[me] = grads_out[me]
    for q in range(2, 4):
        wi[q] = gi[q].astype(BF16).reshape(wi.shape[1:])
    for e in range(2):
        wo[e] = go[e].astype(BF16).reshape(wo.shape[1:])
    stores = []
    for e in range(2):
        stores.append(pltpu.make_async_copy(wi.at[e, me], first_ref(e), local.at[e]))
        stores.append(pltpu.make_async_copy(wi.at[2 + e], inner_out.at[:, e], local.at[2 + e]))
    for e in range(2):
        stores.append(pltpu.make_async_copy(wo.at[e], outer_out.at[:, e], local.at[4 + e]))
    for store in stores:
        store.start()
    pl.semaphore_wait(credit, 1)
    for i in range(1, dp):
        for k in range(2):
            if i > dp - 3:
                out_copy(i - 1, k).wait_send()
            remote(
                held.at[k, chip],
                far.at[k, lax.rem(z + dp - i, dp)],
                o_send.at[i - 1, k],
                o_recv.at[i - 1, k],
                to_x,
            ).wait_recv()
    fetch = []
    for i in range(1, dp):
        for k in range(2):
            fetch.append(
                pltpu.make_async_copy(
                    far.at[k, lax.rem(z + i, dp)], core_in.at[k, i], local.at[6 + (i - 1) * 2 + k]
                )
            )
    for copy in fetch:
        copy.start()
    for copy in fetch:
        copy.wait()
    for k in range(2):
        total = total_here(k)
        for i in range(1, dp):
            total += core_in[k, i].astype(F32)
        sums[k] = total
    for k in range(1, n):
        gate_grad_copy(k).wait()
        for e in range(2):
            first_copy(k, e).wait()
    for j in range(fsdp):
        total = grads_in[j]
        for i in range(1, dp):
            total += grads_in[i * fsdp + j]
        gate_sum[j] = total
    for store in stores:
        store.wait()
    for i in range(1, dp):
        far_copy(i).wait_send()

    def settle(s, carry):
        for copy in (*gather_one(s), *gather_two(s), *gather_core(s)):
            copy.wait_send()
        return carry

    lax.fori_loop(0, dp, settle, 0)


def expert_pass(x_in, c_all, gates, inner_in, outer_in, ident):
    dp = lax.axis_size("dp")
    fsdp = lax.axis_size("fsdp")
    rows, width = x_in.shape
    n, four, own_rows, ff_here = inner_in.shape
    _, two, out_rows, _ = outer_in.shape
    chunk = fsdp * rows
    shape = jax.ShapeDtypeStruct
    dma = pltpu.SemaphoreType.DMA
    anywhere = pl.BlockSpec(memory_space=pl.ANY)
    got = pl.pallas_call(
        functools.partial(expert_kernel, dp, fsdp),
        out_shape=(
            shape((2, rows, width), F32),
            shape((fsdp, 8, 128), F32),
            shape((fsdp, 2 * own_rows, dp * ff_here), BF16),
            shape((n, 2, own_rows, ff_here), BF16),
            shape(outer_in.shape, BF16),
            shape((dp, fsdp, rows, width), BF16),
            shape((2, dp, rows, width), BF16),
        ),
        in_specs=[anywhere] * 5,
        out_specs=(pl.BlockSpec(memory_space=pltpu.VMEM),) * 2 + (anywhere,) * 5,
        scratch_shapes=[
            pltpu.VMEM((chunk, width), BF16),
            pltpu.VMEM((chunk, width), BF16),
            pltpu.VMEM((four, n, own_rows, ff_here), BF16),
            pltpu.VMEM((two, fsdp, out_rows, width), BF16),
            pltpu.VMEM((four, width, ff_here), F32),
            pltpu.VMEM((two, ff_here, width), F32),
            pltpu.VMEM((four, chunk, ff_here), BF16),
            pltpu.VMEM((two, chunk, ff_here), BF16),
            pltpu.VMEM((chunk, 128), F32),
            pltpu.VMEM((2, chunk, width), BF16),
            pltpu.VMEM((2, 4, rows, width), BF16),
            pltpu.VMEM((2, 4, rows, width), BF16),
            pltpu.VMEM((2, 2, rows // 2, width), BF16),
            pltpu.VMEM((2, 2, rows, width), BF16),
            pltpu.VMEM((2, 2, rows, width), BF16),
            pltpu.VMEM((n, 8, 128), F32),
            pltpu.VMEM((n, 8, 128), F32),
            pltpu.VMEM((n, 8, 128), F32),
            dma((12 + 2 * dp,)),
            dma((n,)),
            dma((n,)),
            dma((n,)),
            dma((n,)),
            dma((n, 2)),
            dma((n, 2)),
            dma((dp,)),
            dma((dp,)),
            dma((dp, 2)),
            dma((dp, 2)),
            dma((dp, 4)),
            dma((dp, 4)),
            dma((dp, 4)),
            dma((dp, 4)),
            dma((2, 4)),
            dma((2, 4)),
            dma((2, 2)),
            dma((2, 2)),
            dma((2, 2)),
            dma((2, 2)),
            dma((dp, 2)),
            dma((dp, 2)),
            pltpu.SemaphoreType.REGULAR,
        ],
        compiler_params=pltpu.CompilerParams(
            collective_id=ident, has_side_effects=True, vmem_limit_bytes=63 * 1024 * 1024
        ),
    )(x_in, c_all, gates, inner_in, outer_in)
    return got[:5]


def expert_pass_dense(normed2, grad_all, gates, inner_weight, outer_weight):
    n, parts, own_rows, ff_here = inner_weight.shape
    experts_here = parts // 2
    inner = experts_here * ff_here
    width = n * own_rows
    tokens = grad_all.shape[0]
    gates = gates[:, :, None]
    rows_all = lax.all_gather(normed2, BOTH, axis=0, tiled=True)
    inner_block = inner_weight.transpose(0, 2, 1, 3).reshape(width, 2 * inner)
    outer_shape = outer_weight.shape
    outer_block = outer_weight.transpose(1, 0, 2, 3).reshape(inner, width)
    gate_up = dot(rows_all, inner_block, ((1,), (0,)))
    gate = gate_up[:, :inner]
    up = gate_up[:, inner:]
    sigmoid = jax.nn.sigmoid(gate)
    silu = gate * sigmoid
    activation = (silu * up).astype(BF16).astype(F32)
    grad_act = dot(grad_all, outer_block, ((1,), (1,)))
    grad_gates = jnp.sum(
        (activation * grad_act).reshape(tokens, experts_here, ff_here), axis=-1
    )
    by_part = (tokens, experts_here, ff_here)
    activation = (activation.reshape(by_part) * gates).reshape(tokens, inner).astype(BF16)
    grad_act = (grad_act.reshape(by_part) * gates).reshape(tokens, inner)
    grad_gate_up = jnp.concatenate(
        [grad_act * up * sigmoid * (1.0 + gate * (1.0 - sigmoid)), grad_act * silu], axis=1
    ).astype(BF16)
    expert_sum = dot(activation, outer_block, ((1,), (0,))).astype(BF16)
    expert_sum = lax.psum_scatter(expert_sum, BOTH, scatter_dimension=0, tiled=True).astype(F32)
    if tokens > 8192:
        grad_gate_up, expert_sum = lax.optimization_barrier((grad_gate_up, expert_sum))
    grad_rows = dot(grad_gate_up, inner_block, ((1,), (1,))).astype(BF16)
    grad_rows = lax.psum_scatter(grad_rows, BOTH, scatter_dimension=0, tiled=True).astype(F32)
    inner_grad = dot(rows_all, grad_gate_up, ((0,), (0,))).astype(BF16)
    outer_grad = dot(activation, grad_all, ((0,), (0,))).astype(BF16)
    inner_grad = inner_grad.reshape(n, own_rows, parts, ff_here).transpose(0, 2, 1, 3)
    outer_grad = outer_grad.reshape(experts_here, outer_shape[0], outer_shape[2], width)
    return expert_sum, grad_rows, grad_gates, inner_grad, outer_grad.transpose(1, 0, 2, 3)


def body(
    hidden_in,
    lengths,
    routes,
    attn_gain,
    query_gain,
    key_gain,
    ffn_gain,
    qkv_weight,
    out_weight,
    router_weight,
    expert_in,
    expert_out,
    cotangent,
):
    rows, width = hidden_in.shape
    dp = lax.axis_size("dp")
    fsdp = lax.axis_size("fsdp")
    fused = fsdp == 8
    n = dp * fsdp
    experts = router_weight.shape[1]
    seq = rows * fsdp
    tokens = rows * n
    own_rows = width // n
    heads_here = HEADS // fsdp
    cols = heads_here * HEAD_DIM
    experts_here = experts // fsdp
    ff = expert_out.shape[0] * n
    ff_here = ff // dp
    z = lax.axis_index("dp")
    f = lax.axis_index("fsdp")
    valid = lengths[z]
    scaling = HEAD_DIM ** (-0.5)

    small = jnp.concatenate(
        [attn_gain, query_gain, key_gain, ffn_gain, router_weight.reshape(-1)]
    )
    small_rows = -(-small.size // 2048) * 16
    small = exchange(tiles_of(small, small_rows), BOTH, 0, False).reshape(n, -1)
    gains = small[:, : 4 * own_rows].reshape(n, 4, own_rows).transpose(1, 0, 2)
    gains = gains.reshape(4, width).astype(F32)
    router_full = small[:, 4 * own_rows : 4 * own_rows + own_rows * experts]
    router_full = router_full.reshape(width, experts)
    gain_attn, gain_query, gain_key, gain_ffn = gains[0], gains[1], gains[2], gains[3]

    attn_weight = jnp.concatenate(
        [
            qkv_weight.reshape(own_rows, 3, fsdp, cols),
            out_weight.reshape(own_rows, 1, fsdp, cols),
        ],
        axis=1,
    )
    attn_weight = attn_weight.transpose(2, 0, 1, 3).reshape(fsdp, own_rows, 4 * cols)
    live_mask = (f * rows + jnp.arange(rows, dtype=jnp.int32) < valid).astype(F32)[:, None]
    grad_total = cotangent.astype(F32) * live_mask

    here = f * cols
    qk_gain = jnp.stack(
        [
            lax.dynamic_slice(gain_query, (here,), (cols,)),
            lax.dynamic_slice(gain_key, (here,), (cols,)),
        ]
    )
    pos = jnp.arange(seq, dtype=jnp.int32)
    frequency = jnp.power(10000.0, -jnp.arange(HEAD_DIM // 2, dtype=F32) * 2.0 / HEAD_DIM)
    angles = pos.astype(F32)[:, None] * frequency[None, :]
    cosine = jnp.cos(angles)[:, None, None, :]
    sine = jnp.sin(angles)[:, None, None, :]

    if fused:
        gain_wide = jnp.broadcast_to(qk_gain.reshape(1, 2 * cols), (8, 2 * cols))
        turn = jnp.stack(
            [
                jnp.concatenate([cosine, cosine], axis=-1).reshape(seq, HEAD_DIM),
                jnp.concatenate([sine, -sine], axis=-1).reshape(seq, HEAD_DIM),
            ]
        )
        live_keys = jnp.broadcast_to((pos < valid).astype(F32)[None], (8, seq))
        (
            branch,
            qkv,
            qk_unit,
            qk_scale,
            normed_all,
            attn_weight,
            attended_all,
            grad_all,
            inner_weight,
            outer_weight,
        ) = attention_forward(
            hidden_in,
            grad_total.astype(BF16),
            attn_weight,
            expert_in,
            expert_out,
            jnp.broadcast_to(gain_attn[None], (8, width)),
            gain_wide,
            turn,
            live_keys,
            10,
        )
        branch = branch.astype(F32)
    else:
        attn_weight = lax.all_to_all(attn_weight, "fsdp", 0, 0, tiled=True)
        attn_weight = lax.all_gather(
            attn_weight.reshape(fsdp * own_rows, 4 * cols), "dp", axis=0, tiled=True
        )
        qkv_here = attn_weight[:, : 3 * cols]
        out_here = attn_weight[:, 3 * cols :]
        inner_weight = expert_in.reshape(own_rows, fsdp, experts_here, 2, dp, ff_here)
        inner_weight = inner_weight.transpose(4, 1, 3, 2, 0, 5)
        inner_weight = inner_weight.reshape(n, 2 * experts_here, own_rows, ff_here)
        outer_weight = expert_out.reshape(-1, fsdp, experts_here, width).transpose(1, 2, 0, 3)
        inner_weight = lax.all_to_all(inner_weight, BOTH, 0, 0, tiled=True)
        outer_weight = lax.all_to_all(outer_weight, "fsdp", 0, 0, tiled=True)
        hidden_all = lax.all_gather(hidden_in, "fsdp", axis=0, tiled=True).astype(F32)
        normed_all = (hidden_all * rms_scale(hidden_all) * gain_attn).astype(BF16)
        mixed = dot(normed_all, qkv_here, ((1,), (0,)))
        raw = mixed[:, : 2 * cols].reshape(seq, 2, cols)
        squares = plane_sum(jnp.sum(raw * raw, axis=-1), 1)
        qk_scale = lax.rsqrt(squares / width + EPS)[:, :, None]
        qk_unit = raw * qk_scale
        shape4 = (seq, 2, heads_here, HEAD_DIM)
        turned = rotate((qk_unit * qk_gain).reshape(shape4), cosine, sine, 1.0).astype(BF16)
        query = turned[:, 0]
        key = turned[:, 1]
        value = mixed[:, 2 * cols :].astype(BF16).reshape(seq, heads_here, HEAD_DIM)
        allowed = ((pos[None, :] <= pos[:, None]) & (pos[None, :] < valid))[None]
        scores = jnp.einsum("qhd,khd->hqk", query, key, preferred_element_type=F32) * scaling
        masked = jnp.where(allowed, scores, -1e30)
        weights = jnp.exp(masked - jnp.max(masked, axis=-1, keepdims=True))
        weights = jnp.where(allowed, weights, 0.0)
        probs = weights / jnp.sum(weights, axis=-1, keepdims=True)
        probs_low = probs.astype(BF16)
        attended = jnp.einsum("hqk,khd->qhd", probs_low, value, preferred_element_type=F32)
        attended = attended.reshape(seq, cols).astype(BF16)
        attended_all = lax.all_gather(attended, "fsdp", axis=0, tiled=False)
        branch = jnp.einsum(
            "fsc,fcn->sn",
            attended_all,
            out_here.reshape(fsdp, cols, cols),
            preferred_element_type=F32,
        )
        branch = exchange(branch.astype(BF16).reshape(fsdp, rows, cols), ("fsdp",), 2, True)
        branch = branch.transpose(1, 0, 2).reshape(rows, width).astype(F32)
        grad_all = lax.all_gather(grad_total.astype(BF16), BOTH, axis=0, tiled=True)

    hidden = hidden_in.astype(F32)
    scale1 = rms_scale(hidden)
    unit1 = hidden * scale1
    middle = hidden + branch
    scale2 = rms_scale(middle)
    unit2 = middle * scale2
    normed2 = (unit2 * gain_ffn).astype(BF16)
    logits = dot(normed2, router_full, ((1,), (0,)))
    router_probs = jax.nn.softmax(logits, axis=-1)
    chosen = jnp.sum(
        (routes[:, :, None] == jnp.arange(experts, dtype=jnp.int32)[None, None, :]).astype(F32),
        axis=1,
    )

    gates = (router_probs * chosen).reshape(rows, fsdp, experts_here).transpose(1, 2, 0)
    gates = jnp.broadcast_to(gates[None], (dp, fsdp, experts_here, rows))
    gates = gates.reshape(n, experts_here, rows)
    gates = jnp.pad(gates, ((0, 0), (0, 8 - experts_here), (0, 0)))
    if fused:
        sums, grad_gates, first_grad, inner_grad, outer_grad = expert_pass(
            normed2, grad_all.reshape(dp, seq, width), gates, inner_weight, outer_weight, 8
        )
        expert_sum = sums[0]
        grad_rows = sums[1]
        grad_gates = grad_gates[:, :experts_here]
    else:
        gates = exchange(gates, BOTH, 3, True)[:, :experts_here]
        gates = gates.transpose(0, 2, 1).reshape(tokens, experts_here)
        expert_sum, grad_rows, grad_gates, inner_grad, outer_grad = expert_pass_dense(
            normed2, grad_all, gates, inner_weight, outer_weight
        )
        grad_gates = grad_gates.reshape(n, rows, experts_here).transpose(0, 2, 1)
        grad_gates = jnp.pad(grad_gates, ((0, 0), (0, 8 - experts_here), (0, 0)))
        grad_gates = exchange(grad_gates, BOTH, 4, True)[:, :experts_here]
        grad_gates = jnp.sum(grad_gates.reshape(dp, fsdp, experts_here, rows), axis=0)
    grad_router_probs = grad_gates.reshape(experts, rows).transpose(1, 0) * chosen

    block_total = middle + expert_sum
    squares = jnp.stack(
        [
            jnp.sum(live_mask * block_total * block_total),
            jnp.sum(live_mask * branch * branch),
            jnp.sum(live_mask * expert_sum * expert_sum),
        ]
    )

    grad_logits = router_probs * (
        grad_router_probs - jnp.sum(router_probs * grad_router_probs, axis=-1, keepdims=True)
    )
    grad_logits = grad_logits.astype(BF16)
    grad_normed2 = grad_rows + dot(grad_logits, router_full, ((1,), (1,)))
    ffn_term = jnp.sum(grad_normed2 * unit2, axis=0)
    grad_middle = grad_total + norm_back(grad_normed2 * gain_ffn, unit2, scale2)

    if fused:
        terms = jnp.concatenate(
            [
                jnp.zeros((3, width), F32),
                ffn_term[None],
                jnp.broadcast_to(squares[:, None], (3, width)),
                jnp.zeros((1, width), F32),
                dot(grad_logits, normed2, ((0,), (0,))),
            ]
        )
        hidden_grad, terms, attn_grad, inner_grad, outer_grad, _, _ = attention_back(
            grad_middle.astype(BF16),
            attended_all,
            attn_weight,
            normed_all,
            qkv,
            qk_unit,
            qk_scale,
            gain_wide,
            turn,
            live_keys,
            grad_middle,
            hidden_in,
            jnp.broadcast_to(gain_attn[None], (8, width)),
            terms,
            first_grad,
            inner_grad.reshape(n, experts_here * own_rows, ff_here),
            outer_grad.reshape(fsdp, -1, width),
            9,
        )
        inner_grad = inner_grad.reshape(own_rows, experts, 2 * ff)
        outer_grad = outer_grad.reshape(-1, experts, width)
        terms = lax.dynamic_slice(terms, (0, lax.rem(f, 2) * own_rows), (terms.shape[0], own_rows))
        gain_grads = terms[:4]
        router_grad = terms[8:].transpose(1, 0)
        square_sums = terms[4:7, 0]
    else:
        grad_cols = grad_middle.astype(BF16).reshape(rows, fsdp, cols).transpose(1, 0, 2)
        grad_cols = exchange(grad_cols, ("fsdp",), 5, True).reshape(seq, cols)
        out_grad = jnp.einsum("fsc,sn->fcn", attended_all, grad_cols, preferred_element_type=F32)
        grad_attended = jnp.einsum(
            "sn,fcn->fsc", grad_cols, out_here.reshape(fsdp, cols, cols), preferred_element_type=F32
        )
        grad_attended = lax.psum_scatter(
            grad_attended.astype(BF16).reshape(fsdp * seq, cols), "fsdp", scatter_dimension=0, tiled=True
        )
        grad_attended = grad_attended.reshape(seq, heads_here, HEAD_DIM)
        grad_probs = jnp.einsum("qhd,khd->hqk", grad_attended, value, preferred_element_type=F32)
        grad_scores = probs * (grad_probs - jnp.sum(probs * grad_probs, axis=-1, keepdims=True))
        grad_scores = grad_scores.astype(BF16)
        grad_query = jnp.einsum("hqk,khd->qhd", grad_scores, key, preferred_element_type=F32)
        grad_key = jnp.einsum("hqk,qhd->khd", grad_scores, query, preferred_element_type=F32)
        grad_value = jnp.einsum("hqk,qhd->khd", probs_low, grad_attended, preferred_element_type=F32)
        grad_qk = rotate(jnp.stack([grad_query, grad_key], axis=1) * scaling, cosine, sine, -1.0)
        grad_qk = grad_qk.reshape(seq, 2, cols)
        qk_term = jnp.sum(grad_qk * qk_unit, axis=0)
        grad_qk = grad_qk * qk_gain
        inner_means = plane_sum(jnp.sum(grad_qk * qk_unit, axis=-1), 6)[:, :, None] / width
        grad_qk = qk_scale * (grad_qk - qk_unit * inner_means)
        grad_qkv = jnp.concatenate(
            [grad_qk.reshape(seq, 2 * cols), grad_value.reshape(seq, cols)], axis=1
        ).astype(BF16)
        qkv_grad = dot(normed_all, grad_qkv, ((0,), (0,)))
        grad_normed = dot(grad_qkv, qkv_here, ((1,), (1,))).astype(BF16)
        grad_normed = lax.psum_scatter(grad_normed, "fsdp", scatter_dimension=0, tiled=True).astype(F32)
        attn_grad = jnp.concatenate([qkv_grad, out_grad.reshape(width, cols)], axis=1).astype(BF16)
        attn_grad = lax.psum_scatter(attn_grad, "dp", scatter_dimension=0, tiled=True)
        attn_grad = attn_grad.reshape(fsdp, own_rows, 4 * cols)
        attn_grad = lax.all_to_all(attn_grad, "fsdp", 0, 0, tiled=True)
        inner_grad = lax.all_to_all(inner_grad, BOTH, 0, 0, tiled=True)
        outer_grad = lax.all_to_all(outer_grad, "fsdp", 0, 0, tiled=True)
        inner_grad = inner_grad.reshape(dp, fsdp, 2, experts_here, own_rows, ff_here)
        inner_grad = inner_grad.transpose(4, 1, 3, 2, 0, 5).reshape(own_rows, experts, 2 * ff)
        outer_grad = outer_grad.transpose(2, 0, 1, 3).reshape(-1, experts, width)
        attn_term = jnp.sum(grad_normed * unit1, axis=0)
        hidden_grad = grad_middle + norm_back(grad_normed * gain_attn, unit1, scale1)

        router_term = dot(normed2, grad_logits, ((0,), (0,)))
        qk_full = jnp.zeros((2, width), F32)
        qk_full = lax.dynamic_update_slice(qk_full, qk_term, (0, here))
        terms = jnp.concatenate([attn_term[None], qk_full, ffn_term[None]])
        terms = terms.reshape(4, n, own_rows).transpose(1, 0, 2).reshape(n, 4 * own_rows)
        terms = jnp.concatenate(
            [
                terms,
                router_term.reshape(n, own_rows * experts),
                jnp.broadcast_to(squares[None], (n, 3)),
            ],
            axis=1,
        )
        term_size = terms.shape[1]
        term_rows = -(-term_size // 1024) * 8
        terms = jnp.pad(terms, ((0, 0), (0, term_rows * 128 - term_size)))
        terms = exchange(terms.reshape(n, term_rows, 128), BOTH, 7, True)
        terms = jnp.sum(terms, axis=0).reshape(-1)
        gain_grads = terms[: 4 * own_rows].reshape(4, own_rows)
        router_grad = terms[4 * own_rows : 4 * own_rows + own_rows * experts]
        router_grad = router_grad.reshape(own_rows, experts)
        square_sums = terms[term_size - 3 : term_size]
    attn_grad = attn_grad.reshape(fsdp, own_rows, 4, cols).transpose(1, 2, 0, 3).astype(F32)
    attn_grad = attn_grad.reshape(own_rows, 4 * width)
    valid_cells = jnp.sum(lengths).astype(F32) * width
    stats = jnp.sqrt(square_sums / valid_cells)

    return (
        block_total.astype(BF16),
        hidden_grad,
        gain_grads[0],
        gain_grads[1],
        gain_grads[2],
        gain_grads[3],
        attn_grad[:, : 3 * width],
        attn_grad[:, 3 * width :],
        router_grad,
        inner_grad.astype(F32),
        outer_grad.astype(F32),
        stats,
    )


def solution(mesh):
    one = P(BOTH)
    two = P(BOTH, None)
    three = P(BOTH, None, None)
    in_specs = (two, P(), two, one, one, one, one, two, two, two, three, three, two)
    out_specs = (two, two, one, one, one, one, two, two, two, three, three, P())
    return jax.shard_map(body, mesh=mesh, in_specs=in_specs, out_specs=out_specs, check_vma=False)
```

```python
import functools

import jax
import jax.numpy as jnp
from jax import lax
from jax.experimental import pallas as pl
from jax.experimental.pallas import tpu as pltpu
from jax.sharding import PartitionSpec as P

HEADS = 16
HEAD_DIM = 128
EPS = 1e-05
BOTH = ("dp", "fsdp")
MESH_ID = pl.DeviceIdType.MESH
F32 = jnp.float32
BF16 = jnp.bfloat16


def rms_scale(values_in):
    return lax.rsqrt(jnp.mean(values_in * values_in, axis=-1, keepdims=True) + EPS)


def norm_back(grad_in, unit_rows, scaling):
    return scaling * (grad_in - unit_rows * jnp.mean(grad_in * unit_rows, axis=-1, keepdims=True))


def rotate(values_in, cosine, sine, direction):
    half_width = values_in.shape[-1] // 2
    first_half = values_in[..., :half_width]
    second_half = values_in[..., half_width:]
    return jnp.concatenate(
        [
            first_half * cosine - direction * second_half * sine,
            second_half * cosine + direction * first_half * sine,
        ],
        axis=-1,
    )


def place(axes, fsdp, index):
    if axes == BOTH:
        return {"dp": index // fsdp, "fsdp": lax.rem(index, fsdp)}
    return {axes[0]: index}


def exchange_kernel(axes, n, fsdp, spread, x, o, send, recv, own):
    if axes == BOTH:
        me = lax.axis_index("dp") * fsdp + lax.axis_index("fsdp")
    else:
        me = lax.axis_index(axes[0])
    barrier = pltpu.get_barrier_semaphore()
    for k in range(1, n):
        peer = place(axes, fsdp, lax.rem(me + k, n))
        pl.semaphore_signal(barrier, inc=1, device_id=peer, device_id_type=MESH_ID)
    pl.semaphore_wait(barrier, n - 1)
    local = pltpu.make_async_copy(x.at[me] if spread else x, o.at[me], own)
    local.start()
    copies = []
    for k in range(1, n):
        target = lax.rem(me + k, n)
        copy = pltpu.make_async_remote_copy(
            x.at[target] if spread else x,
            o.at[me],
            send.at[k],
            recv.at[k],
            device_id=place(axes, fsdp, target),
            device_id_type=MESH_ID,
        )
        copy.start()
        copies.append(copy)
    local.wait()
    for copy in copies:
        copy.wait()


def exchange(x, axes, ident, spread):
    fsdp = lax.axis_size("fsdp")
    n = lax.axis_size(axes)
    shape = x.shape if spread else (n,) + x.shape
    return pl.pallas_call(
        functools.partial(exchange_kernel, axes, n, fsdp, spread),
        out_shape=jax.ShapeDtypeStruct(shape, x.dtype),
        in_specs=[pl.BlockSpec(memory_space=pl.ANY)],
        out_specs=pl.BlockSpec(memory_space=pl.ANY),
        scratch_shapes=[
            pltpu.SemaphoreType.DMA((n,)),
            pltpu.SemaphoreType.DMA((n,)),
            pltpu.SemaphoreType.DMA,
        ],
        compiler_params=pltpu.CompilerParams(collective_id=ident, has_side_effects=True),
    )(x)


def tiles_of(x, rows):
    flat = x.reshape(-1)
    return jnp.pad(flat, (0, rows * 128 - flat.shape[0])).reshape(rows, 128)


def plane_sum(x, ident):
    rows = -(-x.size // 1024) * 8
    got = exchange(tiles_of(x, rows), ("fsdp",), ident, False)
    return jnp.sum(got, axis=0).reshape(-1)[: x.size].reshape(x.shape)


def dot(a, b, dims):
    return lax.dot_general(a, b, (dims, ((), ())), preferred_element_type=F32)


HIGH = lax.Precision.HIGHEST


def remote(src, dst, send, recv, device):
    return pltpu.make_async_remote_copy(
        src, dst, send, recv, device_id=device, device_id_type=MESH_ID
    )


def spread(z, f, dp, fsdp, k):
    step = k % dp
    step = (step + 1) // 2 if step % 2 else dp - step // 2
    return lax.rem(z + step, dp) * fsdp + lax.rem(f + k // dp, fsdp)


def greet_all(n, fsdp, me):
    barrier = pltpu.get_barrier_semaphore()
    for k in range(1, n):
        peer = place(BOTH, fsdp, lax.rem(me + k, n))
        pl.semaphore_signal(barrier, inc=1, device_id=peer, device_id_type=MESH_ID)
    pl.semaphore_wait(barrier, n - 1)


def reorder(get, put, outer, inner):
    total = outer * inner
    tile = 256
    step = 512

    def one(i, carry):
        row = i * tile + lax.broadcasted_iota(jnp.int32, (tile, total), 0)
        col = lax.broadcasted_iota(jnp.int32, (tile, total), 1)
        pick = jnp.where(lax.rem(row, outer) * inner + row // outer == col, 1.0, 0.0).astype(BF16)
        for c in range(2048 // step):
            lanes = pl.ds(c * step, step)
            put(i, tile, lanes, dot(pick, get(lanes), ((1,), (0,))).astype(BF16))
        return carry

    lax.fori_loop(0, total // tile, one, 0)


def corner_of(rows, shift, value):
    row = lax.broadcasted_iota(jnp.int32, (rows, 128), 0)
    lane = lax.broadcasted_iota(jnp.int32, (rows, 128), 1)
    return jnp.where(lane == row + shift, value, 0.0).astype(F32)


def exact_dot(a, b, dims):
    return lax.dot_general(
        a, b, (dims, ((), ())), precision=HIGH, preferred_element_type=F32
    )


class Plane:
    def __init__(self, f):
        self.f = f
        self.core = lax.rem(f, 2)
        self.chip = f // 2
        xbit = lax.rem(self.chip, 2)
        ybit = self.chip // 2
        self.chip_x = ybit * 2 + (1 - xbit)
        self.chip_y = (1 - ybit) * 2 + xbit
        self.chip_d = (1 - ybit) * 2 + (1 - xbit)
        self.fx = self.chip_x * 2 + self.core
        self.fy = self.chip_y * 2 + self.core
        self.fd = self.chip_d * 2 + self.core
        self.to_x = {"fsdp": self.fx}
        self.to_y = {"fsdp": self.fy}
        self.to_c = {"fsdp": self.chip * 2 + 1 - self.core}


class PlaneSum:
    def __init__(self, plane, part, held, core_in, half_in, full_in, send, recv):
        self.plane = plane
        self.part = part
        self.held = held
        self.core_in = core_in
        self.half_in = half_in
        self.full_in = full_in
        self.send = send
        self.recv = recv
        half = held.shape[1] // 2
        self.upper = pl.ds(0, half)
        self.lower = pl.ds(half, half)

    def core_copy(self, j):
        owner = j * 2 + 1 - self.plane.core
        return remote(
            self.part.at[owner],
            self.core_in.at[j],
            self.send.at[j],
            self.recv.at[j],
            self.plane.to_c,
        )

    def half_copies(self):
        block = self.held.at[self.plane.chip_d]
        send, recv, half_in = self.send, self.recv, self.half_in
        return (
            remote(block.at[self.upper], half_in.at[0], send.at[4], recv.at[4], self.plane.to_x),
            remote(block.at[self.lower], half_in.at[1], send.at[5], recv.at[5], self.plane.to_y),
        )

    def full_copies(self):
        held, full_in, send, recv = self.held, self.full_in, self.send, self.recv
        plane = self.plane
        return (
            remote(held.at[plane.chip_x], full_in.at[0], send.at[6], recv.at[6], plane.to_x),
            remote(held.at[plane.chip_y], full_in.at[1], send.at[7], recv.at[7], plane.to_y),
        )

    def start(self):
        for j in range(4):
            self.core_copy(j).start()

    def add_core(self):
        for j in range(4):
            self.core_copy(j).wait()

        def one(j, carry):
            own = self.part[j * 2 + self.plane.core].astype(F32)
            self.held[j] = (own + self.core_in[j].astype(F32)).astype(BF16)
            return carry

        lax.fori_loop(0, 4, one, 0)
        for copy in self.half_copies():
            copy.start()

    def pass_on(self):
        for copy in self.half_copies():
            copy.wait()
        held, half_in = self.held, self.half_in
        for chip, piece, i in (
            (self.plane.chip_y, self.upper, 0),
            (self.plane.chip_x, self.lower, 1),
        ):
            total = held[chip, piece].astype(F32) + half_in[i].astype(F32)
            held[chip, piece] = total.astype(BF16)
        for copy in self.full_copies():
            copy.start()

    def total(self):
        for copy in self.full_copies():
            copy.wait()
        total = self.held[self.plane.chip].astype(F32)
        return total + self.full_in[0].astype(F32) + self.full_in[1].astype(F32)


class PlaneGather:
    def __init__(self, plane, block, rows, send, recv):
        self.plane = plane
        self.block = block
        self.send = send
        self.recv = recv
        self.upper = pl.ds(0, rows // 2)
        self.lower = pl.ds(rows // 2, rows // 2)

    def same(self, ref, i, device):
        return remote(ref, ref, self.send(i), self.recv(i), device)

    def first(self):
        own = self.block(self.plane.f)
        return (
            self.same(own.at[self.upper], 0, self.plane.to_x),
            self.same(own.at[self.lower], 1, self.plane.to_y),
        )

    def second(self):
        plane = self.plane
        return (
            self.same(self.block(plane.f).at[self.upper], 2, plane.to_y),
            self.same(self.block(plane.fx).at[self.upper], 3, plane.to_y),
            self.same(self.block(plane.f).at[self.lower], 4, plane.to_x),
            self.same(self.block(plane.fy).at[self.lower], 5, plane.to_x),
        )

    def third(self):
        plane = self.plane
        owners = (plane.f, plane.fx, plane.fy, plane.fd)
        return [self.same(self.block(o), 6 + i, plane.to_c) for i, o in enumerate(owners)]

    def start(self):
        for copy in self.first():
            copy.start()

    def middle(self):
        for copy in self.first():
            copy.wait_recv()
        for copy in self.second():
            copy.start()

    def finish(self):
        for copy in self.second():
            copy.wait_recv()
        for copy in self.third():
            copy.start()

    def wait(self):
        for copy in self.third():
            copy.wait_recv()

    def settle(self):
        for copy in (*self.first(), *self.second(), *self.third()):
            copy.wait_send()


def attention_kernel(
    dp,
    fsdp,
    hidden,
    cot,
    weight_in,
    inner_in,
    outer_in,
    gain_attn,
    gain,
    turn,
    live,
    branch,
    qkv,
    unit,
    scale,
    normed,
    weight,
    attended,
    c_all,
    inner_out,
    outer_out,
    hid_v,
    normed_v,
    w_v,
    raw,
    stat,
    stat_in,
    att_v,
    cols_v,
    rows_v,
    inner_raw,
    inner_v,
    outer_raw,
    outer_v,
    local,
    w_send,
    w_recv,
    right_send,
    right_recv,
    left_send,
    left_recv,
    h_send,
    h_recv,
    t_send,
    t_recv,
    a_send,
    a_recv,
    b_send,
    b_recv,
    c_send,
    c_recv,
    z_send,
    z_recv,
    in_send,
    in_recv,
    out_send,
    out_recv,
):
    n = dp * fsdp
    z = lax.axis_index("dp")
    f = lax.axis_index("fsdp")
    me = z * fsdp + f
    plane = Plane(f)
    rows, width = hidden.shape
    seq, cols = cols_v.shape
    own_rows = weight_in.shape[1]
    slab = fsdp * own_rows
    scaling = HEAD_DIM ** (-0.5)
    greet_all(n, fsdp, me)

    def weight_rows(index):
        return pl.ds(pl.multiple_of(index * own_rows, own_rows), own_rows)

    def weight_copy(k):
        target = lax.rem(f + k, fsdp)
        return remote(
            weight_in.at[target],
            w_v.at[weight_rows(me)],
            w_send.at[k],
            w_recv.at[k],
            {"fsdp": target},
        )

    qkv_cols = pl.ds(0, 3 * cols)
    out_cols = pl.ds(3 * cols, cols)

    def slab_copy(part, p, near, far, send, recv):
        lanes = (qkv_cols, out_cols)[part]
        ref = w_v.at[pl.ds(pl.multiple_of(p * slab, slab), slab), lanes]
        return remote(ref, ref, send.at[part, near], recv.at[part, near], {"dp": far})

    def slab_start(part):
        @pl.when(z < dp - 1)
        def _():
            slab_copy(part, z, 1, z + 1, right_send, right_recv).start()

        @pl.when(z > 0)
        def _():
            slab_copy(part, z, 1, z - 1, left_send, left_recv).start()

    def slab_pass(part, d):
        @pl.when(z >= d)
        def _():
            slab_copy(part, z - d, d, 0, right_send, right_recv).wait_recv()

            @pl.when(z < dp - 1)
            def _():
                slab_copy(part, z - d, d + 1, z + 1, right_send, right_recv).start()

        @pl.when(z + d < dp)
        def _():
            slab_copy(part, z + d, d, 0, left_send, left_recv).wait_recv()

            @pl.when(z > 0)
            def _():
                slab_copy(part, z + d, d + 1, z - 1, left_send, left_recv).start()

    def slab_settle(part):
        @pl.when(z < dp - 1)
        def _():
            slab_copy(part, z, 1, z + 1, right_send, right_recv).wait_send()

        @pl.when(z > 0)
        def _():
            slab_copy(part, z, 1, z - 1, left_send, left_recv).wait_send()

        for d in range(1, dp):

            @pl.when((z >= d) & (z < dp - 1))
            def _(d=d):
                slab_copy(part, z - d, d + 1, z + 1, right_send, right_recv).wait_send()

            @pl.when((z + d < dp) & (z > 0))
            def _(d=d):
                slab_copy(part, z + d, d + 1, z - 1, left_send, left_recv).wait_send()

    experts = inner_v.shape[0]
    here = experts // fsdp
    ff = width // 2
    part = ff // dp

    def inner_block(target, half):
        lanes = pl.ds(pl.multiple_of(half * ff + target // fsdp * part, part), part)
        owned = pl.ds(lax.rem(target, fsdp) * here, here)
        return inner_v.at[owned, :, lanes], inner_out.at[me, pl.ds(half * here, here)]

    def inner_copies(k):
        target = spread(z, f, dp, fsdp, k)
        return [
            remote(
                *inner_block(target, half),
                in_send.at[k, half],
                in_recv.at[k, half],
                place(BOTH, fsdp, target),
            )
            for half in range(2)
        ]

    def outer_block(target):
        return outer_v.at[pl.ds(target * here, here)]

    def outer_copy(k):
        target = lax.rem(f + k, fsdp)
        return remote(
            outer_block(target), outer_out.at[f], out_send.at[k], out_recv.at[k], {"fsdp": target}
        )

    def cot_copy(i):
        return remote(
            cot,
            c_all.at[z, f],
            z_send.at[i],
            z_recv.at[i],
            {"dp": lax.rem(z + dp - i, dp)},
        )

    hidden_gather = PlaneGather(
        plane, lambda o: hid_v.at[o], rows, lambda i: h_send.at[i], lambda i: h_recv.at[i]
    )
    attended_gather = PlaneGather(
        plane, lambda o: att_v.at[o], seq, lambda i: a_send.at[i], lambda i: a_recv.at[i]
    )
    cot_gather = [
        PlaneGather(
            plane,
            lambda o, s=s: c_all.at[lax.rem(z + 1 + s, dp), o],
            rows,
            lambda i, s=s: c_send.at[s, i],
            lambda i, s=s: c_recv.at[s, i],
        )
        for s in range(dp)
    ]

    keeps = [
        pltpu.make_async_copy(hidden, hid_v.at[f], local.at[0]),
        pltpu.make_async_copy(weight_in.at[f], w_v.at[weight_rows(me)], local.at[1]),
        pltpu.make_async_copy(cot, c_all.at[z, f], local.at[2]),
        pltpu.make_async_copy(outer_in, outer_raw, local.at[3]),
        pltpu.make_async_copy(inner_in, inner_raw, local.at[4]),
    ]
    for copy in keeps:
        copy.start()
    for k in range(1, fsdp):
        weight_copy(k).start()
    for i in range(1, dp):
        cot_copy(i).start()
    keeps[0].wait()
    hidden_gather.start()
    keeps[1].wait()
    for k in range(1, fsdp):
        weight_copy(k).wait_recv()

    slab_start(0)
    hidden_gather.middle()
    keeps[2].wait()
    cot_gather[dp - 1].start()

    keeps[3].wait()
    outer_rows = outer_v.shape[1]

    def put_outer(i, tile, lanes, value):
        block = tile // outer_rows
        outer_v[pl.ds(i * block, block), :, lanes] = value.reshape(block, outer_rows, -1)

    reorder(lambda lanes: outer_raw[:, lanes], put_outer, outer_rows, experts)
    hidden_gather.finish()
    for k in range(1, fsdp):
        outer_copy(k).start()
    keeps[4].wait()

    def put_inner(i, tile, lanes, value):
        block = tile // own_rows
        inner_v[pl.ds(i * block, block), :, lanes] = value.reshape(block, own_rows, -1)

    reorder(lambda lanes: inner_raw[:, lanes], put_inner, own_rows, experts)
    owns = [
        pltpu.make_async_copy(outer_block(f), outer_out.at[f], local.at[3]),
        pltpu.make_async_copy(*inner_block(me, 0), local.at[4]),
        pltpu.make_async_copy(*inner_block(me, 1), local.at[5]),
    ]
    for copy in owns:
        copy.start()
    hidden_gather.wait()

    def norm_rows(i, carry):
        values = hid_v[i].astype(F32)
        values = values * lax.rsqrt(jnp.mean(values * values, axis=-1, keepdims=True) + EPS)
        r = pl.ds(pl.multiple_of(i * rows, rows), rows)
        normed_v[r, :] = (values * gain_attn[0:1, :]).astype(BF16)
        return carry

    lax.fori_loop(0, fsdp, norm_rows, 0)
    normed_store = pltpu.make_async_copy(normed_v, normed, local.at[0])
    normed_store.start()

    def cot_begin(s):
        cot_copy(s + 1).wait_recv()
        cot_gather[s].start()

    for d in range(1, dp):
        slab_pass(0, d)
        if d == 1:
            cot_gather[dp - 1].middle()
            cot_begin(0)
        elif d == 2:
            cot_gather[dp - 1].finish()
            cot_gather[0].middle()
            cot_begin(1)
    slab_start(1)
    for k in range(1, n):
        for copy in inner_copies(k):
            copy.start()

    tile = 256

    def project(i, carry):
        r = pl.ds(pl.multiple_of(i * tile, tile), tile)
        for j in range(3):
            col = pl.ds(j * cols, cols)
            value = dot(normed_v[r, :], w_v[:, col], ((1,), (0,)))
            if j < 2:
                raw[r, col] = value
            else:
                qkv[2, r, :] = value.astype(BF16)
        return carry

    lax.fori_loop(0, seq // tile, project, 0)
    row = lax.broadcasted_iota(jnp.int32, (8, 2 * cols), 0)
    lane_of = lax.broadcasted_iota(jnp.int32, (8, 2 * cols), 1)
    chooser = jnp.where(lane_of // cols == row, 1.0, 0.0).astype(F32)
    stat[...] = lax.dot_general(
        chooser,
        raw[...] * raw[...],
        (((1,), (1,)), ((), ())),
        precision=HIGH,
        preferred_element_type=F32,
    )

    def stat_copy(k):
        return remote(
            stat, stat_in.at[f], t_send.at[k], t_recv.at[k], {"fsdp": lax.rem(f + k, fsdp)}
        )

    for k in range(1, fsdp):
        stat_copy(k).start()
    stat_in[f] = stat[...]
    cot_gather[0].finish()
    cot_gather[1].middle()
    cot_begin(2)
    for k in range(1, fsdp):
        stat_copy(k).wait_recv()
    sums = stat_in[0]
    for i in range(1, fsdp):
        sums = sums + stat_in[i]
    corner = jnp.where(
        lax.broadcasted_iota(jnp.int32, (8, 128), 0) == lax.broadcasted_iota(jnp.int32, (8, 128), 1),
        1.0 / width,
        0.0,
    ).astype(F32)
    means = lax.dot_general(
        sums, corner, (((0,), (0,)), ((), ())), precision=HIGH, preferred_element_type=F32
    )
    slab_pass(1, 1)
    cot_gather[1].finish()
    cot_gather[2].middle()
    scale[...] = lax.rsqrt(means + EPS)
    for i in range(2):
        wide = pl.ds(i * cols, cols)
        unit[:, wide] = raw[:, wide] * scale[:, i : i + 1]
        for h in range(cols // HEAD_DIM):
            lane = pl.ds(i * cols + h * HEAD_DIM, HEAD_DIM)
            values = unit[:, lane] * gain[0:1, lane]
            values = values * turn[0] - pltpu.roll(values, HEAD_DIM // 2, 1) * turn[1]
            qkv[i, :, pl.ds(h * HEAD_DIM, HEAD_DIM)] = values.astype(BF16)

    def head(h, carry):
        lane = pl.ds(pl.multiple_of(h * HEAD_DIM, HEAD_DIM), HEAD_DIM)
        for t in range(seq // tile):
            r = pl.ds(t * tile, tile)
            extent = (t + 1) * tile
            upto = pl.ds(0, extent)
            scores = dot(qkv[0, r, lane], qkv[1, upto, lane], ((1,), (1,))) * scaling
            q_pos = t * tile + lax.broadcasted_iota(jnp.int32, (tile, extent), 0)
            k_pos = lax.broadcasted_iota(jnp.int32, (tile, extent), 1)
            allowed = (k_pos <= q_pos) & (live[0:1, 0:extent] > 0.0)
            masked = jnp.where(allowed, scores, -1e30)
            weights = jnp.exp(masked - jnp.max(masked, axis=-1, keepdims=True))
            weights = jnp.where(allowed, weights, 0.0)
            probs = weights / jnp.sum(weights, axis=-1, keepdims=True)
            att_v[f, r, lane] = dot(
                probs.astype(BF16), qkv[2, upto, lane], ((1,), (0,))
            ).astype(BF16)
        return carry

    lax.fori_loop(0, cols // HEAD_DIM, head, 0)
    attended_gather.start()
    slab_pass(1, 2)
    attended_gather.middle()
    cot_gather[2].finish()
    slab_pass(1, 3)
    attended_gather.finish()
    attended_gather.wait()
    attended_store = pltpu.make_async_copy(att_v, attended, local.at[2])
    attended_store.start()

    weight_store = pltpu.make_async_copy(w_v, weight, local.at[1])
    weight_store.start()


    def project_out(i, carry):
        r = pl.ds(pl.multiple_of(i * tile, tile), tile)
        total = dot(att_v[0, r, :], w_v[pl.ds(0, cols), out_cols], ((1,), (0,)))
        for j in range(1, fsdp):
            total += dot(att_v[j, r, :], w_v[pl.ds(j * cols, cols), out_cols], ((1,), (0,)))
        cols_v[r, :] = total.astype(BF16)
        return carry

    lax.fori_loop(0, seq // tile, project_out, 0)

    def branch_copy(k):
        target = lax.rem(f + k, fsdp)
        return remote(
            cols_v.at[pl.ds(pl.multiple_of(target * rows, rows), rows)],
            rows_v.at[f],
            b_send.at[k],
            b_recv.at[k],
            {"fsdp": target},
        )

    for k in range(1, fsdp):
        branch_copy(k).start()
    rows_v[f] = cols_v[pl.ds(pl.multiple_of(f * rows, rows), rows), :]
    for k in range(1, fsdp):
        branch_copy(k).wait()
    for i in range(fsdp):
        branch[:, pl.ds(i * cols, cols)] = rows_v[i]

    for s in range(dp):
        cot_gather[s].wait()
        cot_gather[s].settle()
    hidden_gather.settle()
    attended_gather.settle()
    for i in range(1, dp):
        cot_copy(i).wait_send()

    slab_settle(0)
    slab_settle(1)
    for k in range(1, fsdp):
        weight_copy(k).wait_send()
        stat_copy(k).wait_send()
        outer_copy(k).wait()
    for k in range(1, n):
        for copy in inner_copies(k):
            copy.wait()
    for copy in owns:
        copy.wait()
    normed_store.wait()
    weight_store.wait()
    attended_store.wait()


def attention_forward(
    hidden, cot, weight_in, inner_in, outer_in, gain_attn, gain, turn, live, ident
):
    dp = lax.axis_size("dp")
    fsdp = lax.axis_size("fsdp")
    n = dp * fsdp
    rows, width = hidden.shape
    seq = rows * fsdp
    cols = width // fsdp
    shape = jax.ShapeDtypeStruct
    dma = pltpu.SemaphoreType.DMA
    vmem = pltpu.VMEM
    anywhere = pl.BlockSpec(memory_space=pl.ANY)
    inside = pl.BlockSpec(memory_space=pltpu.VMEM)
    sems = [dma((fsdp,)), dma((fsdp,))] + [dma((2, dp + 1))] * 4
    for size in (10, fsdp, 10, fsdp):
        sems += [dma((size,)), dma((size,))]
    sems += [dma((dp, 10)), dma((dp, 10)), dma((dp,)), dma((dp,))]
    sems += [dma((n, 2)), dma((n, 2)), dma((fsdp,)), dma((fsdp,))]
    experts = inner_in.shape[1]
    out_rows = outer_in.shape[0]
    here = experts // fsdp
    return pl.pallas_call(
        functools.partial(attention_kernel, dp, fsdp),
        out_shape=(
            shape((rows, width), BF16),
            shape((3, seq, cols), BF16),
            shape((seq, 2 * cols), F32),
            shape((seq, 128), F32),
            shape((seq, width), BF16),
            shape((width, 4 * cols), BF16),
            shape((fsdp, seq, cols), BF16),
            shape((dp, fsdp, rows, width), BF16),
            shape((n, 2 * here, width // n, width // 2 // dp), BF16),
            shape((fsdp, here, out_rows, width), BF16),
        ),
        in_specs=[anywhere] * 5 + [inside] * 4,
        out_specs=(inside,) * 4 + (anywhere,) * 6,
        scratch_shapes=[
            vmem((fsdp, rows, width), BF16),
            vmem((seq, width), BF16),
            vmem((width, 4 * cols), BF16),
            vmem((seq, 2 * cols), F32),
            vmem((8, seq), F32),
            vmem((fsdp, 8, seq), F32),
            vmem((fsdp, seq, cols), BF16),
            vmem((seq, cols), BF16),
            vmem((fsdp, rows, cols), BF16),
            vmem((width // n * experts, width), BF16),
            vmem((experts, width // n, width), BF16),
            vmem((out_rows * experts, width), BF16),
            vmem((experts, out_rows, width), BF16),
            dma((6,)),
            *sems,
        ],
        compiler_params=pltpu.CompilerParams(
            collective_id=ident, has_side_effects=True, vmem_limit_bytes=63 * 1024 * 1024
        ),
    )(
        hidden,
        cot,
        weight_in,
        inner_in.reshape(-1, width),
        outer_in.reshape(-1, width),
        gain_attn,
        gain,
        turn,
        live,
    )


def attention_back_kernel(
    dp,
    fsdp,
    grad_rows,
    attended,
    weight,
    normed,
    qkv,
    unit,
    scale,
    gain,
    turn,
    live,
    grad_middle,
    hidden,
    gain_attn,
    terms,
    first_in,
    inner_in,
    outer_in,
    hidden_grad,
    terms_out,
    owned,
    inner_owned,
    outer_owned,
    inner_out,
    outer_out,
    att_v,
    w_v,
    normed_v,
    gcols,
    part1,
    held1,
    core1,
    half1,
    full1,
    part2,
    held2,
    core2,
    half2,
    full2,
    gatt,
    gval,
    gqk,
    gqkv,
    stat,
    stat_in,
    wgrad,
    z_in,
    term_v,
    term_in,
    local,
    v_send,
    v_recv,
    in_send,
    in_recv,
    out_send,
    out_recv,
    g_send,
    g_recv,
    s1_send,
    s1_recv,
    s2_send,
    s2_recv,
    t_send,
    t_recv,
    r_send,
    r_recv,
    l_send,
    l_recv,
    w_send,
    w_recv,
):
    n = dp * fsdp
    z = lax.axis_index("dp")
    f = lax.axis_index("fsdp")
    me = z * fsdp + f
    plane = Plane(f)
    rows, width = grad_rows.shape
    seq, cols = gcols.shape
    own_rows = width // n
    slab = fsdp * own_rows
    scaling = HEAD_DIM ** (-0.5)
    greet_all(n, fsdp, me)
    ff = width // 2
    ff_here = ff // dp

    inner_place = inner_out.at[f, :, pl.ds(pl.multiple_of(z * ff_here, ff_here), ff_here)]

    pair = outer_in.shape[1]
    outer_place = outer_out.at[f // 2, pl.ds(pl.multiple_of(lax.rem(f, 2) * pair, pair), pair)]

    loads = [
        pltpu.make_async_copy(attended, att_v, local.at[0]),
        pltpu.make_async_copy(weight, w_v, local.at[1]),
        pltpu.make_async_copy(normed, normed_v, local.at[2]),
        pltpu.make_async_copy(
            grad_rows.at[:, pl.ds(pl.multiple_of(f * cols, cols), cols)],
            gcols.at[pl.ds(pl.multiple_of(f * rows, rows), rows)],
            local.at[3],
        ),
    ]
    keeps = [
        pltpu.make_async_copy(inner_in.at[me], inner_place, local.at[4]),
        pltpu.make_async_copy(outer_in.at[f], outer_place, local.at[6]),
    ]
    for copy in loads:
        copy.start()

    def cols_copy(k):
        target = lax.rem(f + k, fsdp)
        return remote(
            grad_rows.at[:, pl.ds(pl.multiple_of(target * cols, cols), cols)],
            gcols.at[pl.ds(pl.multiple_of(f * rows, rows), rows)],
            g_send.at[k],
            g_recv.at[k],
            {"fsdp": target},
        )

    def inner_copy(k):
        target = spread(z, f, dp, fsdp, k)
        return remote(
            inner_in.at[target],
            inner_place,
            in_send.at[k],
            in_recv.at[k],
            place(BOTH, fsdp, target),
        )

    def outer_copy(k):
        target = lax.rem(f + k, fsdp)
        return remote(
            outer_in.at[target], outer_place, out_send.at[k], out_recv.at[k], {"fsdp": target}
        )

    def slab_rows(p):
        return pl.ds(pl.multiple_of(p * slab, slab), slab)

    def right_copy(part, d):
        lanes = parts[part]
        return remote(
            wgrad.at[slab_rows(z + d), lanes],
            z_in.at[z + d, :, lanes],
            r_send.at[part, d],
            r_recv.at[part, d - 1],
            {"dp": z + 1},
        )

    def left_copy(part, d):
        lanes = parts[part]
        return remote(
            wgrad.at[slab_rows(z - d), lanes],
            z_in.at[dp if d == 1 else z - d, :, lanes],
            l_send.at[part, d],
            l_recv.at[part, d - 1],
            {"dp": z - 1},
        )

    def arrived(part, slot, sem):
        lanes = parts[part]
        ref = z_in.at[slot, :, lanes]
        remote(ref, ref, sem, sem, plane.to_x).wait_recv()

    def pass_along(part, d):
        lanes = parts[part]

        def add(p):
            block = slab_rows(p)
            wgrad[block, lanes] = (
                wgrad[block, lanes].astype(F32) + z_in[p, :, lanes].astype(F32)
            ).astype(BF16)

        @pl.when(z + d < dp)
        def _():
            @pl.when(z > 0)
            def _():
                arrived(part, z + d, r_recv.at[part, d])
                add(z + d)

            right_copy(part, d).start()

        @pl.when(z >= d)
        def _():
            @pl.when(z < dp - 1)
            def _():
                arrived(part, z - d, l_recv.at[part, d])
                add(z - d)

            left_copy(part, d).start()

    qkv_cols = pl.ds(0, 3 * cols)
    out_cols = pl.ds(3 * cols, cols)
    parts = (pl.ds(0, 2 * cols), out_cols, pl.ds(2 * cols, cols))

    for k in range(1, fsdp):
        cols_copy(k).start()
    for k in range(1, n):
        inner_copy(k).start()
    for k in range(1, fsdp):
        outer_copy(k).start()
    for copy in keeps:
        copy.start()
    term_v[...] = terms[...]
    for copy in loads:
        copy.wait()
    for k in range(1, fsdp):
        cols_copy(k).wait_recv()

    def attended_back(i, carry):
        block = pl.ds(pl.multiple_of(i * cols, cols), cols)
        part1[i] = dot(gcols[...], w_v[block, out_cols], ((1,), (1,))).astype(BF16)
        return carry

    lax.fori_loop(0, fsdp, attended_back, 0)
    sum1 = PlaneSum(plane, part1, held1, core1, half1, full1, s1_send, s1_recv)
    sum1.start()

    def out_grads(i, carry):
        block = pl.ds(pl.multiple_of(i * cols, cols), cols)
        wgrad[block, out_cols] = dot(att_v[i], gcols[...], ((0,), (0,))).astype(BF16)
        return carry

    lax.fori_loop(0, fsdp // 2, out_grads, 0)
    sum1.add_core()
    lax.fori_loop(fsdp // 2, fsdp, out_grads, 0)
    sum1.pass_on()
    pass_along(1, 3)
    gqk[...] = jnp.zeros_like(gqk)
    gval[...] = jnp.zeros_like(gval)
    gatt[...] = sum1.total().astype(BF16)

    tile = 256

    def head(h, carry):
        lane = pl.ds(pl.multiple_of(h * HEAD_DIM, HEAD_DIM), HEAD_DIM)
        key_lane = pl.ds(pl.multiple_of(cols + h * HEAD_DIM, HEAD_DIM), HEAD_DIM)
        for t in range(seq // tile):
            r = pl.ds(t * tile, tile)
            extent = (t + 1) * tile
            upto = pl.ds(0, extent)
            query = qkv[0, r, lane]
            key = qkv[1, upto, lane]
            value = qkv[2, upto, lane]
            grad = gatt[r, lane]
            scores = dot(query, key, ((1,), (1,))) * scaling
            q_pos = t * tile + lax.broadcasted_iota(jnp.int32, (tile, extent), 0)
            k_pos = lax.broadcasted_iota(jnp.int32, (tile, extent), 1)
            allowed = (k_pos <= q_pos) & (live[0:1, 0:extent] > 0.0)
            masked = jnp.where(allowed, scores, -1e30)
            weights = jnp.exp(masked - jnp.max(masked, axis=-1, keepdims=True))
            weights = jnp.where(allowed, weights, 0.0)
            probs = weights / jnp.sum(weights, axis=-1, keepdims=True)
            grad_probs = dot(grad, value, ((1,), (1,)))
            mean = jnp.sum(probs * grad_probs, axis=-1, keepdims=True)
            grad_scores = (probs * (grad_probs - mean)).astype(BF16)
            gqk[r, lane] = dot(grad_scores, key, ((1,), (0,)))
            gqk[upto, key_lane] += dot(grad_scores, query, ((0,), (0,)))
            gval[upto, lane] += dot(probs.astype(BF16), grad, ((0,), (0,)))
        return carry

    lax.fori_loop(0, cols // HEAD_DIM, head, 0)

    def column_grads(part):
        lanes = parts[part]

        def one(i, carry):
            block = pl.ds(pl.multiple_of(i * 256, 256), 256)
            wgrad[block, lanes] = dot(normed_v[:, block], gqkv[:, lanes], ((0,), (0,))).astype(BF16)
            return carry

        lax.fori_loop(0, width // 256, one, 0)

    gqkv[:, parts[2]] = gval[...].astype(BF16)
    column_grads(2)
    pass_along(1, 2)
    pass_along(2, 3)

    heads_here = cols // HEAD_DIM
    for i in range(2):
        for h in range(heads_here):
            wide = pl.ds(i * cols + h * HEAD_DIM, HEAD_DIM)
            grad = gqk[:, wide] * scaling
            grad = grad * turn[0] + pltpu.roll(grad, HEAD_DIM // 2, 1) * turn[1]
            place_lanes = pl.ds(pl.multiple_of(f * cols + h * HEAD_DIM, HEAD_DIM), HEAD_DIM)
            term_v[1 + i : 2 + i, place_lanes] = jnp.sum(
                grad * unit[:, wide], axis=0, keepdims=True
            )
            gqk[:, wide] = grad * gain[0:1, wide]
    row = lax.broadcasted_iota(jnp.int32, (8, 2 * cols), 0)
    lane_of = lax.broadcasted_iota(jnp.int32, (8, 2 * cols), 1)
    chooser = jnp.where(lane_of // cols == row, 1.0, 0.0).astype(F32)
    stat[...] = lax.dot_general(
        chooser,
        gqk[...] * unit[...],
        (((1,), (1,)), ((), ())),
        precision=HIGH,
        preferred_element_type=F32,
    )

    def stat_copy(k):
        return remote(
            stat, stat_in.at[f], t_send.at[k], t_recv.at[k], {"fsdp": lax.rem(f + k, fsdp)}
        )

    for k in range(1, fsdp):
        stat_copy(k).start()
    stat_in[f] = stat[...]
    pass_along(1, 1)
    pass_along(2, 2)
    for k in range(1, fsdp):
        stat_copy(k).wait_recv()
    sums = stat_in[0]
    for i in range(1, fsdp):
        sums = sums + stat_in[i]
    corner = jnp.where(
        lax.broadcasted_iota(jnp.int32, (8, 128), 0) == lax.broadcasted_iota(jnp.int32, (8, 128), 1),
        1.0 / width,
        0.0,
    ).astype(F32)
    means = lax.dot_general(
        sums, corner, (((0,), (0,)), ((), ())), precision=HIGH, preferred_element_type=F32
    )
    for i in range(2):
        wide = pl.ds(i * cols, cols)
        grad = scale[:, i : i + 1] * (gqk[:, wide] - unit[:, wide] * means[:, i : i + 1])
        gqkv[:, wide] = grad.astype(BF16)

    step = 512

    def normed_back(i, carry):
        r = pl.ds(pl.multiple_of(i * rows, rows), rows)
        for c in range(width // step):
            col = pl.ds(c * step, step)
            part2[i, :, col] = dot(gqkv[r, :], w_v[col, qkv_cols], ((1,), (1,))).astype(BF16)
        return carry

    lax.fori_loop(0, fsdp, normed_back, 0)
    sum2 = PlaneSum(plane, part2, held2, core2, half2, full2, s2_send, s2_recv)
    sum2.start()

    column_grads(0)
    pass_along(0, 3)
    sum2.add_core()
    pass_along(2, 1)
    pass_along(0, 2)
    sum2.pass_on()

    grad = sum2.total()
    pass_along(0, 1)
    values = hidden[...].astype(F32)
    scale1 = lax.rsqrt(jnp.mean(values * values, axis=-1, keepdims=True) + EPS)
    values = values * scale1
    term_v[0:1, :] = jnp.sum(grad * values, axis=0, keepdims=True)
    grad = grad * gain_attn[0:1, :]
    grad = scale1 * (grad - values * jnp.mean(grad * values, axis=-1, keepdims=True))
    hidden_grad[...] = grad_middle[...] + grad

    def term_copy(k):
        target = lax.rem(me + k, n)
        lanes = pl.ds(pl.multiple_of(target // 2 * 128, 128), 128)
        return remote(
            term_v.at[:, lanes],
            term_in.at[me],
            v_send.at[k],
            v_recv.at[k],
            place(BOTH, fsdp, target),
        )

    for k in range(1, n):
        term_copy(k).start()
    term_in[me] = term_v[:, pl.ds(pl.multiple_of(me // 2 * 128, 128), 128)]

    for copy in keeps:
        copy.wait()
    for k in range(1, fsdp):
        outer_copy(k).wait()
    outer_load = pltpu.make_async_copy(outer_out, core2, local.at[0])
    outer_load.start()
    for k in range(1, n):
        inner_copy(k).wait()
    inner_loads = [
        pltpu.make_async_copy(first_in, part2.at[:, :, pl.ds(0, ff)], local.at[1]),
        pltpu.make_async_copy(inner_out, part2.at[:, :, pl.ds(ff, ff)], local.at[2]),
    ]
    for copy in inner_loads:
        copy.start()
    experts = fsdp * (inner_in.shape[1] // own_rows)
    outer_load.wait()
    outer_rows = core2.shape[0] * core2.shape[1]
    inner_rows = part2.shape[0] * part2.shape[1]

    def put_outer(i, tile, lanes, value):
        block = tile // rows
        held2[pl.ds(i * block, block), :, lanes] = value.reshape(block, rows, -1)

    reorder(
        lambda lanes: core2[:, :, lanes].reshape(outer_rows, -1),
        put_outer,
        experts,
        outer_rows // experts,
    )
    for copy in inner_loads:
        copy.wait()

    def put_inner(i, tile, lanes, value):
        normed_v[pl.ds(pl.multiple_of(i * tile, tile), tile), lanes] = value

    reorder(
        lambda lanes: part2[:, :, lanes].reshape(inner_rows, -1),
        put_inner,
        experts,
        inner_rows // experts,
    )
    stores = [
        pltpu.make_async_copy(held2, outer_owned, local.at[0]),
        pltpu.make_async_copy(normed_v, inner_owned, local.at[1]),
    ]
    for store in stores:
        store.start()

    @pl.when(z > 0)
    def _():
        for part in range(3):
            arrived(part, z, r_recv.at[part, 0])
        total = wgrad[slab_rows(z), :].astype(F32) + z_in[z].astype(F32)
        wgrad[slab_rows(z), :] = total.astype(BF16)

    @pl.when(z < dp - 1)
    def _():
        for part in range(3):
            arrived(part, dp, l_recv.at[part, 0])
        total = wgrad[slab_rows(z), :].astype(F32) + z_in[dp].astype(F32)
        wgrad[slab_rows(z), :] = total.astype(BF16)

    for part in range(3):
        for d in range(1, dp):

            @pl.when(z + d < dp)
            def _(part=part, d=d):
                right_copy(part, d).wait_send()

            @pl.when(z >= d)
            def _(part=part, d=d):
                left_copy(part, d).wait_send()

    def owner_rows(target):
        return wgrad.at[pl.ds(pl.multiple_of(z * slab + target * own_rows, own_rows), own_rows)]

    def owner_copy(k):
        target = lax.rem(f + k, fsdp)
        return remote(
            owner_rows(target), owned.at[f], w_send.at[k], w_recv.at[k], {"fsdp": target}
        )

    for k in range(1, fsdp):
        owner_copy(k).start()
    own_block = pl.multiple_of(z * slab + f * own_rows, own_rows)
    owned[f] = wgrad[pl.ds(own_block, own_rows), :]
    for k in range(1, fsdp):
        owner_copy(k).wait()
    for k in range(1, fsdp):
        cols_copy(k).wait_send()
        stat_copy(k).wait_send()
    for k in range(1, n):
        term_copy(k).wait()
    total = term_in[0]
    for i in range(1, n):
        total += term_in[i]
    terms_out[...] = total
    for store in stores:
        store.wait()


def attention_back(
    grad_rows,
    attended,
    weight,
    normed,
    qkv,
    unit,
    scale,
    gain,
    turn,
    live,
    grad_middle,
    hidden,
    gain_attn,
    terms,
    first_in,
    inner_in,
    outer_in,
    ident,
):
    dp = lax.axis_size("dp")
    fsdp = lax.axis_size("fsdp")
    n = dp * fsdp
    rows, width = grad_rows.shape
    seq = rows * fsdp
    cols = width // fsdp
    own_rows = width // n
    shape = jax.ShapeDtypeStruct
    dma = pltpu.SemaphoreType.DMA
    vmem = pltpu.VMEM
    anywhere = pl.BlockSpec(memory_space=pl.ANY)
    inside = pl.BlockSpec(memory_space=pltpu.VMEM)
    return pl.pallas_call(
        functools.partial(attention_back_kernel, dp, fsdp),
        out_shape=(
            shape((rows, width), F32),
            shape((terms.shape[0], 128), F32),
            shape((fsdp, own_rows, 4 * cols), BF16),
            shape((seq, width), BF16),
            shape((4, rows, width), BF16),
            shape((fsdp, rows, width // 2), BF16),
            shape((4, rows, width), BF16),
        ),
        in_specs=[anywhere] * 4 + [inside] * 10 + [anywhere] * 3,
        out_specs=(inside,) * 3 + (anywhere,) * 4,
        scratch_shapes=[
            vmem((fsdp, seq, cols), BF16),
            vmem((width, 4 * cols), BF16),
            vmem((seq, width), BF16),
            vmem((seq, cols), BF16),
            vmem((fsdp, seq, cols), BF16),
            vmem((4, seq, cols), BF16),
            vmem((4, seq, cols), BF16),
            vmem((2, seq // 2, cols), BF16),
            vmem((2, seq, cols), BF16),
            vmem((fsdp, rows, width), BF16),
            vmem((4, rows, width), BF16),
            vmem((4, rows, width), BF16),
            vmem((2, rows // 2, width), BF16),
            vmem((2, rows, width), BF16),
            vmem((seq, cols), BF16),
            vmem((seq, cols), F32),
            vmem((seq, 2 * cols), F32),
            vmem((seq, 3 * cols), BF16),
            vmem((8, seq), F32),
            vmem((fsdp, 8, seq), F32),
            vmem((width, 4 * cols), BF16),
            vmem((dp + 1, fsdp * own_rows, 4 * cols), BF16),
            vmem(terms.shape, F32),
            vmem((n, terms.shape[0], 128), F32),
            dma((7,)),
            dma((n,)),
            dma((n,)),
            dma((n,)),
            dma((n,)),
            dma((fsdp,)),
            dma((fsdp,)),
            dma((fsdp,)),
            dma((fsdp,)),
            dma((8,)),
            dma((8,)),
            dma((8,)),
            dma((8,)),
            dma((fsdp,)),
            dma((fsdp,)),
            dma((3, dp)),
            dma((3, dp)),
            dma((3, dp)),
            dma((3, dp)),
            dma((fsdp,)),
            dma((fsdp,)),
        ],
        compiler_params=pltpu.CompilerParams(
            collective_id=ident, has_side_effects=True, vmem_limit_bytes=63 * 1024 * 1024
        ),
    )(
        grad_rows,
        attended,
        weight,
        normed,
        qkv,
        unit,
        scale,
        gain,
        turn,
        live,
        grad_middle,
        hidden,
        gain_attn,
        terms,
        first_in,
        inner_in,
        outer_in,
    )


def expert_kernel(
    dp,
    fsdp,
    x_in,
    c_all,
    gates,
    inner_in,
    outer_in,
    sums,
    gate_sum,
    first_out,
    inner_out,
    outer_out,
    gathered,
    far,
    xv,
    cv,
    wi,
    wo,
    gi,
    go,
    ggu,
    act,
    gv,
    part,
    held,
    core_in,
    half_in,
    full_in,
    leaving,
    gates_in,
    grads_out,
    grads_in,
    local,
    g_send,
    g_recv,
    gg_send,
    gg_recv,
    f_send,
    f_recv,
    z_send,
    z_recv,
    a_send,
    a_recv,
    b_send,
    b_recv,
    k_send,
    k_recv,
    c_send,
    c_recv,
    s1_send,
    s1_recv,
    s2_send,
    s2_recv,
    o_send,
    o_recv,
    credit,
):
    rows, width = x_in.shape
    half = rows // 2
    z = lax.axis_index("dp")
    f = lax.axis_index("fsdp")
    core = lax.rem(f, 2)
    chip = f // 2
    xbit = lax.rem(chip, 2)
    ybit = chip // 2
    chip_x = ybit * 2 + (1 - xbit)
    chip_y = (1 - ybit) * 2 + xbit
    chip_d = (1 - ybit) * 2 + (1 - xbit)
    fx = chip_x * 2 + core
    fy = chip_y * 2 + core
    fd = chip_d * 2 + core
    fc = chip * 2 + (1 - core)
    to_x = {"fsdp": fx}
    to_y = {"fsdp": fy}
    to_c = {"fsdp": fc}
    upper = pl.ds(0, half)
    lower = pl.ds(half, half)

    def remote(src, dst, send, recv, device):
        return pltpu.make_async_remote_copy(
            src, dst, send, recv, device_id=device, device_id_type=MESH_ID
        )

    def plane_at(s):
        return lax.rem(z + 1 + s, dp)

    def far_copy(i):
        return remote(
            x_in,
            gathered.at[z, f],
            z_send.at[i],
            z_recv.at[i],
            {"dp": lax.rem(z + dp - i, dp)},
        )

    def gather_one(s):
        block = gathered.at[plane_at(s), f]
        return (
            remote(block.at[upper], block.at[upper], a_send.at[s, 0], a_recv.at[s, 0], to_x),
            remote(block.at[lower], block.at[lower], a_send.at[s, 1], a_recv.at[s, 1], to_y),
        )

    def gather_two(s):
        p = plane_at(s)
        copies = []
        for i, (owner, piece, device) in enumerate(
            ((f, upper, to_y), (fx, upper, to_y), (f, lower, to_x), (fy, lower, to_x))
        ):
            ref = gathered.at[p, owner, piece]
            copies.append(remote(ref, ref, b_send.at[s, i], b_recv.at[s, i], device))
        return copies

    def gather_core(s):
        p = plane_at(s)
        copies = []
        for i, owner in enumerate((f, fx, fy, fd)):
            ref = gathered.at[p, owner]
            copies.append(remote(ref, ref, k_send.at[s, i], k_recv.at[s, i], to_c))
        return copies

    def block_rows(owner):
        return pl.ds(pl.multiple_of(owner * rows, rows), rows)

    def core_copy(k, j):
        return remote(
            part.at[k, block_rows(j * 2 + 1 - core)],
            core_in.at[k, j],
            c_send.at[k, j],
            c_recv.at[k, j],
            to_c,
        )

    def half_copies(k):
        return (
            remote(
                held.at[k, chip_d, upper], half_in.at[k, 0], s1_send.at[k, 0], s1_recv.at[k, 0], to_x
            ),
            remote(
                held.at[k, chip_d, lower], half_in.at[k, 1], s1_send.at[k, 1], s1_recv.at[k, 1], to_y
            ),
        )

    def full_copies(k):
        return (
            remote(held.at[k, chip_x], full_in.at[k, 0], s2_send.at[k, 0], s2_recv.at[k, 0], to_x),
            remote(held.at[k, chip_y], full_in.at[k, 1], s2_send.at[k, 1], s2_recv.at[k, 1], to_y),
        )

    def out_copy(s, k):
        return remote(
            leaving.at[lax.rem(s, 2), k],
            far.at[k, z],
            o_send.at[s, k],
            o_recv.at[s, k],
            {"dp": plane_at(s)},
        )

    def add_core():
        def add_block(k, j):
            core_copy(k, j).wait()
            held[k, j] = (
                part[k, block_rows(j * 2 + core)].astype(F32) + core_in[k, j].astype(F32)
            ).astype(BF16)

        for k in range(2):
            add_block(k, chip_d)
            for copy in half_copies(k):
                copy.start()
        for k in range(2):
            for j in (chip_x, chip_y, chip):
                add_block(k, j)
        pl.semaphore_signal(credit, inc=1, device_id=to_c, device_id_type=MESH_ID)

    def pass_full():
        for k in range(2):
            for copy in half_copies(k):
                copy.wait()
            held[k, chip_y, upper] = (
                held[k, chip_y, upper].astype(F32) + half_in[k, 0].astype(F32)
            ).astype(BF16)
            held[k, chip_x, lower] = (
                held[k, chip_x, lower].astype(F32) + half_in[k, 1].astype(F32)
            ).astype(BF16)
            for copy in full_copies(k):
                copy.start()

    def total_here(k):
        for copy in full_copies(k):
            copy.wait()
        return held[k, chip].astype(F32) + full_in[k, 0].astype(F32) + full_in[k, 1].astype(F32)

    n = dp * fsdp
    me = z * fsdp + f
    greet_all(n, fsdp, me)

    def gate_copy(k):
        target = lax.rem(me + k, n)
        return remote(
            gates.at[target],
            gates_in.at[me],
            g_send.at[k],
            g_recv.at[k],
            place(BOTH, fsdp, target),
        )

    def gate_grad_copy(k):
        target = lax.rem(me + k, n)
        return remote(
            grads_out.at[target],
            grads_in.at[me],
            gg_send.at[k],
            gg_recv.at[k],
            place(BOTH, fsdp, target),
        )

    own_rows = wi.shape[2]
    first_lanes = pl.ds(pl.multiple_of(z * wi.shape[3], wi.shape[3]), wi.shape[3])

    def first_ref(e):
        return first_out.at[f, pl.ds(e * own_rows, own_rows), first_lanes]

    def first_copy(k, e):
        target = spread(z, f, dp, fsdp, k)
        return remote(
            wi.at[e, target],
            first_ref(e),
            f_send.at[k, e],
            f_recv.at[k, e],
            place(BOTH, fsdp, target),
        )

    far_copy(1).start()
    for k in range(1, n):
        gate_copy(k).start()
    loads = [pltpu.make_async_copy(x_in, gathered.at[z, f], local.at[0])]
    for q in range(4):
        loads.append(pltpu.make_async_copy(inner_in.at[:, q], wi.at[q], local.at[1 + q]))
    for e in range(2):
        loads.append(pltpu.make_async_copy(outer_in.at[:, e], wo.at[e], local.at[5 + e]))
    loads.append(pltpu.make_async_copy(gates.at[me], gates_in.at[me], local.at[7]))
    for load in loads:
        load.start()
    gi[...] = jnp.zeros_like(gi)
    go[...] = jnp.zeros_like(go)
    for load in loads:
        load.wait()

    def begin_gather(s):
        @pl.when(s < dp - 1)
        def _():
            far_copy(s + 1).wait_recv()

        for copy in gather_one(s):
            copy.start()

    def middle_gather(s):
        for copy in gather_one(s):
            copy.wait_recv()
        for copy in gather_two(s):
            copy.start()

    def end_gather(s):
        for copy in gather_two(s):
            copy.wait_recv()
        for copy in gather_core(s):
            copy.start()

    begin_gather(0)
    for i in range(2, dp):
        far_copy(i).start()
    middle_gather(0)
    end_gather(0)
    begin_gather(1)
    for k in range(1, n):
        gate_copy(k).wait()

    inner_rows = wi.shape[1] * wi.shape[2]
    ff_here = wo.shape[1] * wo.shape[2]
    tile = xv.shape[0] // 2

    def tile_step(t):
        r = pl.ds(pl.multiple_of(t * tile, tile), tile)
        x = xv[r, :]
        c = cv[r, :]
        for e in range(2):
            gate = dot(x, wi[e].reshape(inner_rows, ff_here), ((1,), (0,)))
            up = dot(x, wi[2 + e].reshape(inner_rows, ff_here), ((1,), (0,)))
            back = dot(c, wo[e].reshape(ff_here, width), ((1,), (1,)))
            sigmoid = 1.0 / (1.0 + jnp.exp(-gate))
            silu = gate * sigmoid
            active = (silu * up).astype(BF16).astype(F32)
            weight = gv[r, e : e + 1]
            gv[r, 8 + e : 9 + e] = jnp.sum(active * back, axis=-1, keepdims=True)
            act[e, r, :] = (weight * active).astype(BF16)
            back = weight * back
            ggu[e, r, :] = (back * up * sigmoid * (1.0 + gate * (1.0 - sigmoid))).astype(BF16)
            ggu[2 + e, r, :] = (back * silu).astype(BF16)
        step = 512
        for i in range(width // step):
            col = pl.ds(i * step, step)
            blocks = pl.ds(i * step // wi.shape[2], step // wi.shape[2])
            total = dot(act[0, r, :], wo[0, :, :, col].reshape(ff_here, step), ((1,), (0,)))
            total += dot(act[1, r, :], wo[1, :, :, col].reshape(ff_here, step), ((1,), (0,)))
            part[0, r, col] = total.astype(BF16)
            total = dot(ggu[0, r, :], wi[0, blocks].reshape(step, ff_here), ((1,), (1,)))
            for q in range(1, 4):
                total += dot(ggu[q, r, :], wi[q, blocks].reshape(step, ff_here), ((1,), (1,)))
            part[1, r, col] = total.astype(BF16)

    def weight_step():
        def inner_part(i, carry):
            col = pl.ds(pl.multiple_of(i * 256, 256), 256)
            xt = xv[:, col]
            for q in range(4):
                gi[q, col, :] += dot(xt, ggu[q], ((0,), (0,)))
            return carry

        lax.fori_loop(0, width // 256, inner_part, 0)

        def outer_part(i, carry):
            col = pl.ds(pl.multiple_of(i * 512, 512), 512)
            ct = cv[:, col]
            for e in range(2):
                go[e, :, col] += dot(act[e], ct, ((0,), (0,)))
            return carry

        lax.fori_loop(0, width // 512, outer_part, 0)

    def chunk(s, carry):
        p = plane_at(s)
        c_load = pltpu.make_async_copy(c_all.at[p], cv, local.at[1])
        c_load.start()

        def to_columns(j, carry):
            r = pl.ds(pl.multiple_of(j * rows, rows), rows)
            gv[r, :] = exact_dot(gates_in[p * fsdp + j], corner_of(8, 0, 1.0), ((0,), (0,)))
            return carry

        lax.fori_loop(0, fsdp, to_columns, 0)
        for copy in gather_core(s):
            copy.wait_recv()
        for j in range(8):
            pltpu.make_async_copy(
                gathered.at[p, j], xv.at[pl.ds(j * rows, rows)], local.at[3 + j]
            ).start()
        c_load.wait()
        for j in range(8):
            pltpu.make_async_copy(
                gathered.at[p, j], xv.at[pl.ds(j * rows, rows)], local.at[3 + j]
            ).wait()
        @pl.when(s < dp - 1)
        def _():
            middle_gather(s + 1)

        tile_step(0)

        @pl.when(s > 0)
        def _():
            pass_full()

        @pl.when(s < dp - 2)
        def _():
            begin_gather(s + 2)

        tile_step(1)

        @pl.when(s > 0)
        def _():
            pl.semaphore_wait(credit, 1)

        for k in range(2):
            for j in range(4):
                core_copy(k, j).start()
        def to_rows(j, carry):
            r = pl.ds(pl.multiple_of(j * rows, rows), rows)
            grads_out[p * fsdp + j] = exact_dot(corner_of(8, 8, 1.0), gv[r, :], ((1,), (1,)))
            return carry

        lax.fori_loop(0, fsdp, to_rows, 0)
        weight_step()

        @pl.when(s > 0)
        def _():
            @pl.when(s > 2)
            def _():
                for k in range(2):
                    out_copy(s - 3, k).wait_send()

            for k in range(2):
                leaving[lax.rem(s - 1, 2), k] = total_here(k).astype(BF16)
                out_copy(s - 1, k).start()

        add_core()

        @pl.when(s < dp - 1)
        def _():
            end_gather(s + 1)

        @pl.when(s == dp - 1)
        def _():
            for e in range(2):
                wi[e] = gi[e].astype(BF16).reshape(wi.shape[1:])
            for k in range(1, n):
                for e in range(2):
                    first_copy(k, e).start()

        return carry

    lax.fori_loop(0, dp, chunk, 0)

    pass_full()
    for k in range(1, n):
        gate_grad_copy(k).start()
    grads_in[me] = grads_out[me]
    for q in range(2, 4):
        wi[q] = gi[q].astype(BF16).reshape(wi.shape[1:])
    for e in range(2):
        wo[e] = go[e].astype(BF16).reshape(wo.shape[1:])
    stores = []
    for e in range(2):
        stores.append(pltpu.make_async_copy(wi.at[e, me], first_ref(e), local.at[e]))
        stores.append(pltpu.make_async_copy(wi.at[2 + e], inner_out.at[:, e], local.at[2 + e]))
    for e in range(2):
        stores.append(pltpu.make_async_copy(wo.at[e], outer_out.at[:, e], local.at[4 + e]))
    for store in stores:
        store.start()
    pl.semaphore_wait(credit, 1)
    for i in range(1, dp):
        for k in range(2):
            if i > dp - 3:
                out_copy(i - 1, k).wait_send()
            remote(
                held.at[k, chip],
                far.at[k, lax.rem(z + dp - i, dp)],
                o_send.at[i - 1, k],
                o_recv.at[i - 1, k],
                to_x,
            ).wait_recv()
    fetch = []
    for i in range(1, dp):
        for k in range(2):
            fetch.append(
                pltpu.make_async_copy(
                    far.at[k, lax.rem(z + i, dp)], core_in.at[k, i], local.at[6 + (i - 1) * 2 + k]
                )
            )
    for copy in fetch:
        copy.start()
    for copy in fetch:
        copy.wait()
    for k in range(2):
        total = total_here(k)
        for i in range(1, dp):
            total += core_in[k, i].astype(F32)
        sums[k] = total
    for k in range(1, n):
        gate_grad_copy(k).wait()
        for e in range(2):
            first_copy(k, e).wait()
    for j in range(fsdp):
        total = grads_in[j]
        for i in range(1, dp):
            total += grads_in[i * fsdp + j]
        gate_sum[j] = total
    for store in stores:
        store.wait()
    for i in range(1, dp):
        far_copy(i).wait_send()

    def settle(s, carry):
        for copy in (*gather_one(s), *gather_two(s), *gather_core(s)):
            copy.wait_send()
        return carry

    lax.fori_loop(0, dp, settle, 0)


def expert_pass(x_in, c_all, gates, inner_in, outer_in, ident):
    dp = lax.axis_size("dp")
    fsdp = lax.axis_size("fsdp")
    rows, width = x_in.shape
    n, four, own_rows, ff_here = inner_in.shape
    _, two, out_rows, _ = outer_in.shape
    chunk = fsdp * rows
    shape = jax.ShapeDtypeStruct
    dma = pltpu.SemaphoreType.DMA
    anywhere = pl.BlockSpec(memory_space=pl.ANY)
    got = pl.pallas_call(
        functools.partial(expert_kernel, dp, fsdp),
        out_shape=(
            shape((2, rows, width), F32),
            shape((fsdp, 8, 128), F32),
            shape((fsdp, 2 * own_rows, dp * ff_here), BF16),
            shape((n, 2, own_rows, ff_here), BF16),
            shape(outer_in.shape, BF16),
            shape((dp, fsdp, rows, width), BF16),
            shape((2, dp, rows, width), BF16),
        ),
        in_specs=[anywhere] * 5,
        out_specs=(pl.BlockSpec(memory_space=pltpu.VMEM),) * 2 + (anywhere,) * 5,
        scratch_shapes=[
            pltpu.VMEM((chunk, width), BF16),
            pltpu.VMEM((chunk, width), BF16),
            pltpu.VMEM((four, n, own_rows, ff_here), BF16),
            pltpu.VMEM((two, fsdp, out_rows, width), BF16),
            pltpu.VMEM((four, width, ff_here), F32),
            pltpu.VMEM((two, ff_here, width), F32),
            pltpu.VMEM((four, chunk, ff_here), BF16),
            pltpu.VMEM((two, chunk, ff_here), BF16),
            pltpu.VMEM((chunk, 128), F32),
            pltpu.VMEM((2, chunk, width), BF16),
            pltpu.VMEM((2, 4, rows, width), BF16),
            pltpu.VMEM((2, 4, rows, width), BF16),
            pltpu.VMEM((2, 2, rows // 2, width), BF16),
            pltpu.VMEM((2, 2, rows, width), BF16),
            pltpu.VMEM((2, 2, rows, width), BF16),
            pltpu.VMEM((n, 8, 128), F32),
            pltpu.VMEM((n, 8, 128), F32),
            pltpu.VMEM((n, 8, 128), F32),
            dma((12 + 2 * dp,)),
            dma((n,)),
            dma((n,)),
            dma((n,)),
            dma((n,)),
            dma((n, 2)),
            dma((n, 2)),
            dma((dp,)),
            dma((dp,)),
            dma((dp, 2)),
            dma((dp, 2)),
            dma((dp, 4)),
            dma((dp, 4)),
            dma((dp, 4)),
            dma((dp, 4)),
            dma((2, 4)),
            dma((2, 4)),
            dma((2, 2)),
            dma((2, 2)),
            dma((2, 2)),
            dma((2, 2)),
            dma((dp, 2)),
            dma((dp, 2)),
            pltpu.SemaphoreType.REGULAR,
        ],
        compiler_params=pltpu.CompilerParams(
            collective_id=ident, has_side_effects=True, vmem_limit_bytes=63 * 1024 * 1024
        ),
    )(x_in, c_all, gates, inner_in, outer_in)
    return got[:5]


def expert_pass_dense(normed2, grad_all, gates, inner_weight, outer_weight):
    n, parts, own_rows, ff_here = inner_weight.shape
    experts_here = parts // 2
    inner = experts_here * ff_here
    width = n * own_rows
    tokens = grad_all.shape[0]
    gates = gates[:, :, None]
    rows_all = lax.all_gather(normed2, BOTH, axis=0, tiled=True)
    inner_block = inner_weight.transpose(0, 2, 1, 3).reshape(width, 2 * inner)
    outer_shape = outer_weight.shape
    outer_block = outer_weight.transpose(1, 0, 2, 3).reshape(inner, width)
    gate_up = dot(rows_all, inner_block, ((1,), (0,)))
    gate = gate_up[:, :inner]
    up = gate_up[:, inner:]
    sigmoid = jax.nn.sigmoid(gate)
    silu = gate * sigmoid
    activation = (silu * up).astype(BF16).astype(F32)
    grad_act = dot(grad_all, outer_block, ((1,), (1,)))
    grad_gates = jnp.sum(
        (activation * grad_act).reshape(tokens, experts_here, ff_here), axis=-1
    )
    by_part = (tokens, experts_here, ff_here)
    activation = (activation.reshape(by_part) * gates).reshape(tokens, inner).astype(BF16)
    grad_act = (grad_act.reshape(by_part) * gates).reshape(tokens, inner)
    grad_gate_up = jnp.concatenate(
        [grad_act * up * sigmoid * (1.0 + gate * (1.0 - sigmoid)), grad_act * silu], axis=1
    ).astype(BF16)
    expert_sum = dot(activation, outer_block, ((1,), (0,))).astype(BF16)
    expert_sum = lax.psum_scatter(expert_sum, BOTH, scatter_dimension=0, tiled=True).astype(F32)
    if tokens > 8192:
        grad_gate_up, expert_sum = lax.optimization_barrier((grad_gate_up, expert_sum))
    grad_rows = dot(grad_gate_up, inner_block, ((1,), (1,))).astype(BF16)
    grad_rows = lax.psum_scatter(grad_rows, BOTH, scatter_dimension=0, tiled=True).astype(F32)
    inner_grad = dot(rows_all, grad_gate_up, ((0,), (0,))).astype(BF16)
    outer_grad = dot(activation, grad_all, ((0,), (0,))).astype(BF16)
    inner_grad = inner_grad.reshape(n, own_rows, parts, ff_here).transpose(0, 2, 1, 3)
    outer_grad = outer_grad.reshape(experts_here, outer_shape[0], outer_shape[2], width)
    return expert_sum, grad_rows, grad_gates, inner_grad, outer_grad.transpose(1, 0, 2, 3)


def body(
    hidden_in,
    lengths,
    routes,
    attn_gain,
    query_gain,
    key_gain,
    ffn_gain,
    qkv_weight,
    out_weight,
    router_weight,
    expert_in,
    expert_out,
    cotangent,
):
    rows, width = hidden_in.shape
    dp = lax.axis_size("dp")
    fsdp = lax.axis_size("fsdp")
    fused = fsdp == 8
    n = dp * fsdp
    experts = router_weight.shape[1]
    seq = rows * fsdp
    tokens = rows * n
    own_rows = width // n
    heads_here = HEADS // fsdp
    cols = heads_here * HEAD_DIM
    experts_here = experts // fsdp
    ff = expert_out.shape[0] * n
    ff_here = ff // dp
    z = lax.axis_index("dp")
    f = lax.axis_index("fsdp")
    valid = lengths[z]
    scaling = HEAD_DIM ** (-0.5)

    small = jnp.concatenate(
        [attn_gain, query_gain, key_gain, ffn_gain, router_weight.reshape(-1)]
    )
    small_rows = -(-small.size // 2048) * 16
    small = exchange(tiles_of(small, small_rows), BOTH, 0, False).reshape(n, -1)
    gains = small[:, : 4 * own_rows].reshape(n, 4, own_rows).transpose(1, 0, 2)
    gains = gains.reshape(4, width).astype(F32)
    router_full = small[:, 4 * own_rows : 4 * own_rows + own_rows * experts]
    router_full = router_full.reshape(width, experts)
    gain_attn, gain_query, gain_key, gain_ffn = gains[0], gains[1], gains[2], gains[3]

    attn_weight = jnp.concatenate(
        [
            qkv_weight.reshape(own_rows, 3, fsdp, cols),
            out_weight.reshape(own_rows, 1, fsdp, cols),
        ],
        axis=1,
    )
    attn_weight = attn_weight.transpose(2, 0, 1, 3).reshape(fsdp, own_rows, 4 * cols)
    live_mask = (f * rows + jnp.arange(rows, dtype=jnp.int32) < valid).astype(F32)[:, None]
    grad_total = cotangent.astype(F32) * live_mask

    here = f * cols
    qk_gain = jnp.stack(
        [
            lax.dynamic_slice(gain_query, (here,), (cols,)),
            lax.dynamic_slice(gain_key, (here,), (cols,)),
        ]
    )
    pos = jnp.arange(seq, dtype=jnp.int32)
    frequency = jnp.power(10000.0, -jnp.arange(HEAD_DIM // 2, dtype=F32) * 2.0 / HEAD_DIM)
    angles = pos.astype(F32)[:, None] * frequency[None, :]
    cosine = jnp.cos(angles)[:, None, None, :]
    sine = jnp.sin(angles)[:, None, None, :]

    if fused:
        gain_wide = jnp.broadcast_to(qk_gain.reshape(1, 2 * cols), (8, 2 * cols))
        turn = jnp.stack(
            [
                jnp.concatenate([cosine, cosine], axis=-1).reshape(seq, HEAD_DIM),
                jnp.concatenate([sine, -sine], axis=-1).reshape(seq, HEAD_DIM),
            ]
        )
        live_keys = jnp.broadcast_to((pos < valid).astype(F32)[None], (8, seq))
        (
            branch,
            qkv,
            qk_unit,
            qk_scale,
            normed_all,
            attn_weight,
            attended_all,
            grad_all,
            inner_weight,
            outer_weight,
        ) = attention_forward(
            hidden_in,
            grad_total.astype(BF16),
            attn_weight,
            expert_in,
            expert_out,
            jnp.broadcast_to(gain_attn[None], (8, width)),
            gain_wide,
            turn,
            live_keys,
            10,
        )
        branch = branch.astype(F32)
    else:
        attn_weight = lax.all_to_all(attn_weight, "fsdp", 0, 0, tiled=True)
        attn_weight = lax.all_gather(
            attn_weight.reshape(fsdp * own_rows, 4 * cols), "dp", axis=0, tiled=True
        )
        qkv_here = attn_weight[:, : 3 * cols]
        out_here = attn_weight[:, 3 * cols :]
        inner_weight = expert_in.reshape(own_rows, fsdp, experts_here, 2, dp, ff_here)
        inner_weight = inner_weight.transpose(4, 1, 3, 2, 0, 5)
        inner_weight = inner_weight.reshape(n, 2 * experts_here, own_rows, ff_here)
        outer_weight = expert_out.reshape(-1, fsdp, experts_here, width).transpose(1, 2, 0, 3)
        inner_weight = lax.all_to_all(inner_weight, BOTH, 0, 0, tiled=True)
        outer_weight = lax.all_to_all(outer_weight, "fsdp", 0, 0, tiled=True)
        hidden_all = lax.all_gather(hidden_in, "fsdp", axis=0, tiled=True).astype(F32)
        normed_all = (hidden_all * rms_scale(hidden_all) * gain_attn).astype(BF16)
        mixed = dot(normed_all, qkv_here, ((1,), (0,)))
        raw = mixed[:, : 2 * cols].reshape(seq, 2, cols)
        squares = plane_sum(jnp.sum(raw * raw, axis=-1), 1)
        qk_scale = lax.rsqrt(squares / width + EPS)[:, :, None]
        qk_unit = raw * qk_scale
        shape4 = (seq, 2, heads_here, HEAD_DIM)
        turned = rotate((qk_unit * qk_gain).reshape(shape4), cosine, sine, 1.0).astype(BF16)
        query = turned[:, 0]
        key = turned[:, 1]
        value = mixed[:, 2 * cols :].astype(BF16).reshape(seq, heads_here, HEAD_DIM)
        allowed = ((pos[None, :] <= pos[:, None]) & (pos[None, :] < valid))[None]
        scores = jnp.einsum("qhd,khd->hqk", query, key, preferred_element_type=F32) * scaling
        masked = jnp.where(allowed, scores, -1e30)
        weights = jnp.exp(masked - jnp.max(masked, axis=-1, keepdims=True))
        weights = jnp.where(allowed, weights, 0.0)
        probs = weights / jnp.sum(weights, axis=-1, keepdims=True)
        probs_low = probs.astype(BF16)
        attended = jnp.einsum("hqk,khd->qhd", probs_low, value, preferred_element_type=F32)
        attended = attended.reshape(seq, cols).astype(BF16)
        attended_all = lax.all_gather(attended, "fsdp", axis=0, tiled=False)
        branch = jnp.einsum(
            "fsc,fcn->sn",
            attended_all,
            out_here.reshape(fsdp, cols, cols),
            preferred_element_type=F32,
        )
        branch = exchange(branch.astype(BF16).reshape(fsdp, rows, cols), ("fsdp",), 2, True)
        branch = branch.transpose(1, 0, 2).reshape(rows, width).astype(F32)
        grad_all = lax.all_gather(grad_total.astype(BF16), BOTH, axis=0, tiled=True)

    hidden = hidden_in.astype(F32)
    scale1 = rms_scale(hidden)
    unit1 = hidden * scale1
    middle = hidden + branch
    scale2 = rms_scale(middle)
    unit2 = middle * scale2
    normed2 = (unit2 * gain_ffn).astype(BF16)
    logits = dot(normed2, router_full, ((1,), (0,)))
    router_probs = jax.nn.softmax(logits, axis=-1)
    chosen = jnp.sum(
        (routes[:, :, None] == jnp.arange(experts, dtype=jnp.int32)[None, None, :]).astype(F32),
        axis=1,
    )

    gates = (router_probs * chosen).reshape(rows, fsdp, experts_here).transpose(1, 2, 0)
    gates = jnp.broadcast_to(gates[None], (dp, fsdp, experts_here, rows))
    gates = gates.reshape(n, experts_here, rows)
    gates = jnp.pad(gates, ((0, 0), (0, 8 - experts_here), (0, 0)))
    if fused:
        sums, grad_gates, first_grad, inner_grad, outer_grad = expert_pass(
            normed2, grad_all.reshape(dp, seq, width), gates, inner_weight, outer_weight, 8
        )
        expert_sum = sums[0]
        grad_rows = sums[1]
        grad_gates = grad_gates[:, :experts_here]
    else:
        gates = exchange(gates, BOTH, 3, True)[:, :experts_here]
        gates = gates.transpose(0, 2, 1).reshape(tokens, experts_here)
        expert_sum, grad_rows, grad_gates, inner_grad, outer_grad = expert_pass_dense(
            normed2, grad_all, gates, inner_weight, outer_weight
        )
        grad_gates = grad_gates.reshape(n, rows, experts_here).transpose(0, 2, 1)
        grad_gates = jnp.pad(grad_gates, ((0, 0), (0, 8 - experts_here), (0, 0)))
        grad_gates = exchange(grad_gates, BOTH, 4, True)[:, :experts_here]
        grad_gates = jnp.sum(grad_gates.reshape(dp, fsdp, experts_here, rows), axis=0)
    grad_router_probs = grad_gates.reshape(experts, rows).transpose(1, 0) * chosen

    block_total = middle + expert_sum
    squares = jnp.stack(
        [
            jnp.sum(live_mask * block_total * block_total),
            jnp.sum(live_mask * branch * branch),
            jnp.sum(live_mask * expert_sum * expert_sum),
        ]
    )

    grad_logits = router_probs * (
        grad_router_probs - jnp.sum(router_probs * grad_router_probs, axis=-1, keepdims=True)
    )
    grad_logits = grad_logits.astype(BF16)
    grad_normed2 = grad_rows + dot(grad_logits, router_full, ((1,), (1,)))
    ffn_term = jnp.sum(grad_normed2 * unit2, axis=0)
    grad_middle = grad_total + norm_back(grad_normed2 * gain_ffn, unit2, scale2)

    if fused:
        terms = jnp.concatenate(
            [
                jnp.zeros((3, width), F32),
                ffn_term[None],
                jnp.broadcast_to(squares[:, None], (3, width)),
                jnp.zeros((1, width), F32),
                dot(grad_logits, normed2, ((0,), (0,))),
            ]
        )
        hidden_grad, terms, attn_grad, inner_grad, outer_grad, _, _ = attention_back(
            grad_middle.astype(BF16),
            attended_all,
            attn_weight,
            normed_all,
            qkv,
            qk_unit,
            qk_scale,
            gain_wide,
            turn,
            live_keys,
            grad_middle,
            hidden_in,
            jnp.broadcast_to(gain_attn[None], (8, width)),
            terms,
            first_grad,
            inner_grad.reshape(n, experts_here * own_rows, ff_here),
            outer_grad.reshape(fsdp, -1, width),
            9,
        )
        inner_grad = inner_grad.reshape(own_rows, experts, 2 * ff)
        outer_grad = outer_grad.reshape(-1, experts, width)
        terms = lax.dynamic_slice(terms, (0, lax.rem(f, 2) * own_rows), (terms.shape[0], own_rows))
        gain_grads = terms[:4]
        router_grad = terms[8:].transpose(1, 0)
        square_sums = terms[4:7, 0]
    else:
        grad_cols = grad_middle.astype(BF16).reshape(rows, fsdp, cols).transpose(1, 0, 2)
        grad_cols = exchange(grad_cols, ("fsdp",), 5, True).reshape(seq, cols)
        out_grad = jnp.einsum("fsc,sn->fcn", attended_all, grad_cols, preferred_element_type=F32)
        grad_attended = jnp.einsum(
            "sn,fcn->fsc", grad_cols, out_here.reshape(fsdp, cols, cols), preferred_element_type=F32
        )
        grad_attended = lax.psum_scatter(
            grad_attended.astype(BF16).reshape(fsdp * seq, cols), "fsdp", scatter_dimension=0, tiled=True
        )
        grad_attended = grad_attended.reshape(seq, heads_here, HEAD_DIM)
        grad_probs = jnp.einsum("qhd,khd->hqk", grad_attended, value, preferred_element_type=F32)
        grad_scores = probs * (grad_probs - jnp.sum(probs * grad_probs, axis=-1, keepdims=True))
        grad_scores = grad_scores.astype(BF16)
        grad_query = jnp.einsum("hqk,khd->qhd", grad_scores, key, preferred_element_type=F32)
        grad_key = jnp.einsum("hqk,qhd->khd", grad_scores, query, preferred_element_type=F32)
        grad_value = jnp.einsum("hqk,qhd->khd", probs_low, grad_attended, preferred_element_type=F32)
        grad_qk = rotate(jnp.stack([grad_query, grad_key], axis=1) * scaling, cosine, sine, -1.0)
        grad_qk = grad_qk.reshape(seq, 2, cols)
        qk_term = jnp.sum(grad_qk * qk_unit, axis=0)
        grad_qk = grad_qk * qk_gain
        inner_means = plane_sum(jnp.sum(grad_qk * qk_unit, axis=-1), 6)[:, :, None] / width
        grad_qk = qk_scale * (grad_qk - qk_unit * inner_means)
        grad_qkv = jnp.concatenate(
            [grad_qk.reshape(seq, 2 * cols), grad_value.reshape(seq, cols)], axis=1
        ).astype(BF16)
        qkv_grad = dot(normed_all, grad_qkv, ((0,), (0,)))
        grad_normed = dot(grad_qkv, qkv_here, ((1,), (1,))).astype(BF16)
        grad_normed = lax.psum_scatter(grad_normed, "fsdp", scatter_dimension=0, tiled=True).astype(F32)
        attn_grad = jnp.concatenate([qkv_grad, out_grad.reshape(width, cols)], axis=1).astype(BF16)
        attn_grad = lax.psum_scatter(attn_grad, "dp", scatter_dimension=0, tiled=True)
        attn_grad = attn_grad.reshape(fsdp, own_rows, 4 * cols)
        attn_grad = lax.all_to_all(attn_grad, "fsdp", 0, 0, tiled=True)
        inner_grad = lax.all_to_all(inner_grad, BOTH, 0, 0, tiled=True)
        outer_grad = lax.all_to_all(outer_grad, "fsdp", 0, 0, tiled=True)
        inner_grad = inner_grad.reshape(dp, fsdp, 2, experts_here, own_rows, ff_here)
        inner_grad = inner_grad.transpose(4, 1, 3, 2, 0, 5).reshape(own_rows, experts, 2 * ff)
        outer_grad = outer_grad.transpose(2, 0, 1, 3).reshape(-1, experts, width)
        attn_term = jnp.sum(grad_normed * unit1, axis=0)
        hidden_grad = grad_middle + norm_back(grad_normed * gain_attn, unit1, scale1)

        router_term = dot(normed2, grad_logits, ((0,), (0,)))
        qk_full = jnp.zeros((2, width), F32)
        qk_full = lax.dynamic_update_slice(qk_full, qk_term, (0, here))
        terms = jnp.concatenate([attn_term[None], qk_full, ffn_term[None]])
        terms = terms.reshape(4, n, own_rows).transpose(1, 0, 2).reshape(n, 4 * own_rows)
        terms = jnp.concatenate(
            [
                terms,
                router_term.reshape(n, own_rows * experts),
                jnp.broadcast_to(squares[None], (n, 3)),
            ],
            axis=1,
        )
        term_size = terms.shape[1]
        term_rows = -(-term_size // 1024) * 8
        terms = jnp.pad(terms, ((0, 0), (0, term_rows * 128 - term_size)))
        terms = exchange(terms.reshape(n, term_rows, 128), BOTH, 7, True)
        terms = jnp.sum(terms, axis=0).reshape(-1)
        gain_grads = terms[: 4 * own_rows].reshape(4, own_rows)
        router_grad = terms[4 * own_rows : 4 * own_rows + own_rows * experts]
        router_grad = router_grad.reshape(own_rows, experts)
        square_sums = terms[term_size - 3 : term_size]
    attn_grad = attn_grad.reshape(fsdp, own_rows, 4, cols).transpose(1, 2, 0, 3).astype(F32)
    attn_grad = attn_grad.reshape(own_rows, 4 * width)
    valid_cells = jnp.sum(lengths).astype(F32) * width
    stats = jnp.sqrt(square_sums / valid_cells)

    return (
        block_total.astype(BF16),
        hidden_grad,
        gain_grads[0],
        gain_grads[1],
        gain_grads[2],
        gain_grads[3],
        attn_grad[:, : 3 * width],
        attn_grad[:, 3 * width :],
        router_grad,
        inner_grad.astype(F32),
        outer_grad.astype(F32),
        stats,
    )


def solution(mesh):
    one = P(BOTH)
    two = P(BOTH, None)
    three = P(BOTH, None, None)
    in_specs = (two, P(), two, one, one, one, one, two, two, two, three, three, two)
    out_specs = (two, two, one, one, one, one, two, two, two, three, three, P())
    return jax.shard_map(body, mesh=mesh, in_specs=in_specs, out_specs=out_specs, check_vma=False)
```

```python
import functools

import jax
import jax.numpy as jnp
from jax import lax
from jax.experimental import pallas as pl
from jax.experimental.pallas import tpu as pltpu
from jax.sharding import PartitionSpec as P

HEADS = 16
HEAD_DIM = 128
EPS = 1e-05
BOTH = ("dp", "fsdp")
MESH_ID = pl.DeviceIdType.MESH
F32 = jnp.float32
BF16 = jnp.bfloat16


def rms_scale(values_in):
    return lax.rsqrt(jnp.mean(values_in * values_in, axis=-1, keepdims=True) + EPS)


def norm_back(grad_in, unit_rows, scaling):
    return scaling * (grad_in - unit_rows * jnp.mean(grad_in * unit_rows, axis=-1, keepdims=True))


def rotate(values_in, cosine, sine, direction):
    half_width = values_in.shape[-1] // 2
    first_half = values_in[..., :half_width]
    second_half = values_in[..., half_width:]
    return jnp.concatenate(
        [
            first_half * cosine - direction * second_half * sine,
            second_half * cosine + direction * first_half * sine,
        ],
        axis=-1,
    )


def place(axes, fsdp, index):
    if axes == BOTH:
        return {"dp": index // fsdp, "fsdp": lax.rem(index, fsdp)}
    return {axes[0]: index}


def exchange_kernel(axes, n, fsdp, spread, x, o, send, recv, own):
    if axes == BOTH:
        me = lax.axis_index("dp") * fsdp + lax.axis_index("fsdp")
    else:
        me = lax.axis_index(axes[0])
    barrier = pltpu.get_barrier_semaphore()
    for k in range(1, n):
        peer = place(axes, fsdp, lax.rem(me + k, n))
        pl.semaphore_signal(barrier, inc=1, device_id=peer, device_id_type=MESH_ID)
    pl.semaphore_wait(barrier, n - 1)
    local = pltpu.make_async_copy(x.at[me] if spread else x, o.at[me], own)
    local.start()
    copies = []
    for k in range(1, n):
        target = lax.rem(me + k, n)
        copy = pltpu.make_async_remote_copy(
            x.at[target] if spread else x,
            o.at[me],
            send.at[k],
            recv.at[k],
            device_id=place(axes, fsdp, target),
            device_id_type=MESH_ID,
        )
        copy.start()
        copies.append(copy)
    local.wait()
    for copy in copies:
        copy.wait()


def exchange(x, axes, ident, spread):
    fsdp = lax.axis_size("fsdp")
    n = lax.axis_size(axes)
    shape = x.shape if spread else (n,) + x.shape
    return pl.pallas_call(
        functools.partial(exchange_kernel, axes, n, fsdp, spread),
        out_shape=jax.ShapeDtypeStruct(shape, x.dtype),
        in_specs=[pl.BlockSpec(memory_space=pl.ANY)],
        out_specs=pl.BlockSpec(memory_space=pl.ANY),
        scratch_shapes=[
            pltpu.SemaphoreType.DMA((n,)),
            pltpu.SemaphoreType.DMA((n,)),
            pltpu.SemaphoreType.DMA,
        ],
        compiler_params=pltpu.CompilerParams(collective_id=ident, has_side_effects=True),
    )(x)


def tiles_of(x, rows):
    flat = x.reshape(-1)
    return jnp.pad(flat, (0, rows * 128 - flat.shape[0])).reshape(rows, 128)


def plane_sum(x, ident):
    rows = -(-x.size // 1024) * 8
    got = exchange(tiles_of(x, rows), ("fsdp",), ident, False)
    return jnp.sum(got, axis=0).reshape(-1)[: x.size].reshape(x.shape)


def dot(a, b, dims):
    return lax.dot_general(a, b, (dims, ((), ())), preferred_element_type=F32)


HIGH = lax.Precision.HIGHEST


def remote(src, dst, send, recv, device):
    return pltpu.make_async_remote_copy(
        src, dst, send, recv, device_id=device, device_id_type=MESH_ID
    )


def spread(z, f, dp, fsdp, k):
    step = k % dp
    step = (step + 1) // 2 if step % 2 else dp - step // 2
    return lax.rem(z + step, dp) * fsdp + lax.rem(f + k // dp, fsdp)


def greet_all(n, fsdp, me):
    barrier = pltpu.get_barrier_semaphore()
    for k in range(1, n):
        peer = place(BOTH, fsdp, lax.rem(me + k, n))
        pl.semaphore_signal(barrier, inc=1, device_id=peer, device_id_type=MESH_ID)
    pl.semaphore_wait(barrier, n - 1)


def reorder(get, put, outer, inner):
    total = outer * inner
    tile = 256
    step = 512

    def one(i, carry):
        row = i * tile + lax.broadcasted_iota(jnp.int32, (tile, total), 0)
        col = lax.broadcasted_iota(jnp.int32, (tile, total), 1)
        pick = jnp.where(lax.rem(row, outer) * inner + row // outer == col, 1.0, 0.0).astype(BF16)
        for c in range(2048 // step):
            lanes = pl.ds(c * step, step)
            put(i, tile, lanes, dot(pick, get(lanes), ((1,), (0,))).astype(BF16))
        return carry

    lax.fori_loop(0, total // tile, one, 0)


def corner_of(rows, shift, value):
    row = lax.broadcasted_iota(jnp.int32, (rows, 128), 0)
    lane = lax.broadcasted_iota(jnp.int32, (rows, 128), 1)
    return jnp.where(lane == row + shift, value, 0.0).astype(F32)


def exact_dot(a, b, dims):
    return lax.dot_general(
        a, b, (dims, ((), ())), precision=HIGH, preferred_element_type=F32
    )


class Plane:
    def __init__(self, f):
        self.f = f
        self.core = lax.rem(f, 2)
        self.chip = f // 2
        xbit = lax.rem(self.chip, 2)
        ybit = self.chip // 2
        self.chip_x = ybit * 2 + (1 - xbit)
        self.chip_y = (1 - ybit) * 2 + xbit
        self.chip_d = (1 - ybit) * 2 + (1 - xbit)
        self.fx = self.chip_x * 2 + self.core
        self.fy = self.chip_y * 2 + self.core
        self.fd = self.chip_d * 2 + self.core
        self.to_x = {"fsdp": self.fx}
        self.to_y = {"fsdp": self.fy}
        self.to_c = {"fsdp": self.chip * 2 + 1 - self.core}


class PlaneSum:
    def __init__(self, plane, part, held, core_in, half_in, full_in, send, recv):
        self.plane = plane
        self.part = part
        self.held = held
        self.core_in = core_in
        self.half_in = half_in
        self.full_in = full_in
        self.send = send
        self.recv = recv
        half = held.shape[1] // 2
        self.upper = pl.ds(0, half)
        self.lower = pl.ds(half, half)

    def core_copy(self, j):
        owner = j * 2 + 1 - self.plane.core
        return remote(
            self.part.at[owner],
            self.core_in.at[j],
            self.send.at[j],
            self.recv.at[j],
            self.plane.to_c,
        )

    def half_copies(self):
        block = self.held.at[self.plane.chip_d]
        send, recv, half_in = self.send, self.recv, self.half_in
        return (
            remote(block.at[self.upper], half_in.at[0], send.at[4], recv.at[4], self.plane.to_x),
            remote(block.at[self.lower], half_in.at[1], send.at[5], recv.at[5], self.plane.to_y),
        )

    def full_copies(self):
        held, full_in, send, recv = self.held, self.full_in, self.send, self.recv
        plane = self.plane
        return (
            remote(held.at[plane.chip_x], full_in.at[0], send.at[6], recv.at[6], plane.to_x),
            remote(held.at[plane.chip_y], full_in.at[1], send.at[7], recv.at[7], plane.to_y),
        )

    def start(self):
        for j in range(4):
            self.core_copy(j).start()

    def add_core(self):
        for j in range(4):
            self.core_copy(j).wait()

        def one(j, carry):
            own = self.part[j * 2 + self.plane.core].astype(F32)
            self.held[j] = (own + self.core_in[j].astype(F32)).astype(BF16)
            return carry

        lax.fori_loop(0, 4, one, 0)
        for copy in self.half_copies():
            copy.start()

    def pass_on(self):
        for copy in self.half_copies():
            copy.wait()
        held, half_in = self.held, self.half_in
        for chip, piece, i in (
            (self.plane.chip_y, self.upper, 0),
            (self.plane.chip_x, self.lower, 1),
        ):
            total = held[chip, piece].astype(F32) + half_in[i].astype(F32)
            held[chip, piece] = total.astype(BF16)
        for copy in self.full_copies():
            copy.start()

    def total(self):
        for copy in self.full_copies():
            copy.wait()
        total = self.held[self.plane.chip].astype(F32)
        return total + self.full_in[0].astype(F32) + self.full_in[1].astype(F32)


class PlaneGather:
    def __init__(self, plane, block, rows, send, recv):
        self.plane = plane
        self.block = block
        self.send = send
        self.recv = recv
        self.upper = pl.ds(0, rows // 2)
        self.lower = pl.ds(rows // 2, rows // 2)

    def same(self, ref, i, device):
        return remote(ref, ref, self.send(i), self.recv(i), device)

    def first(self):
        own = self.block(self.plane.f)
        return (
            self.same(own.at[self.upper], 0, self.plane.to_x),
            self.same(own.at[self.lower], 1, self.plane.to_y),
        )

    def second(self):
        plane = self.plane
        return (
            self.same(self.block(plane.f).at[self.upper], 2, plane.to_y),
            self.same(self.block(plane.fx).at[self.upper], 3, plane.to_y),
            self.same(self.block(plane.f).at[self.lower], 4, plane.to_x),
            self.same(self.block(plane.fy).at[self.lower], 5, plane.to_x),
        )

    def third(self):
        plane = self.plane
        owners = (plane.f, plane.fx, plane.fy, plane.fd)
        return [self.same(self.block(o), 6 + i, plane.to_c) for i, o in enumerate(owners)]

    def start(self):
        for copy in self.first():
            copy.start()

    def middle(self):
        for copy in self.first():
            copy.wait_recv()
        for copy in self.second():
            copy.start()

    def finish(self):
        for copy in self.second():
            copy.wait_recv()
        for copy in self.third():
            copy.start()

    def wait(self):
        for copy in self.third():
            copy.wait_recv()

    def settle(self):
        for copy in (*self.first(), *self.second(), *self.third()):
            copy.wait_send()


def attention_kernel(
    dp,
    fsdp,
    hidden,
    cot,
    weight_in,
    inner_in,
    outer_in,
    small,
    turn,
    live,
    gains,
    branch,
    qkv,
    unit,
    scale,
    normed,
    weight,
    attended,
    c_all,
    inner_out,
    outer_out,
    hid_v,
    small_in,
    normed_v,
    w_v,
    raw,
    stat,
    stat_in,
    att_v,
    cols_v,
    rows_v,
    inner_raw,
    inner_v,
    outer_raw,
    outer_v,
    local,
    m_send,
    m_recv,
    w_send,
    w_recv,
    right_send,
    right_recv,
    left_send,
    left_recv,
    h_send,
    h_recv,
    t_send,
    t_recv,
    a_send,
    a_recv,
    b_send,
    b_recv,
    c_send,
    c_recv,
    z_send,
    z_recv,
    in_send,
    in_recv,
    out_send,
    out_recv,
):
    n = dp * fsdp
    z = lax.axis_index("dp")
    f = lax.axis_index("fsdp")
    me = z * fsdp + f
    plane = Plane(f)
    rows, width = hidden.shape
    seq, cols = cols_v.shape
    own_rows = weight_in.shape[1]
    slab = fsdp * own_rows
    scaling = HEAD_DIM ** (-0.5)
    greet_all(n, fsdp, me)

    def weight_rows(index):
        return pl.ds(pl.multiple_of(index * own_rows, own_rows), own_rows)

    def weight_copy(k):
        target = lax.rem(f + k, fsdp)
        return remote(
            weight_in.at[target],
            w_v.at[weight_rows(me)],
            w_send.at[k],
            w_recv.at[k],
            {"fsdp": target},
        )

    qkv_cols = pl.ds(0, 3 * cols)
    out_cols = pl.ds(3 * cols, cols)

    def slab_copy(part, p, near, far, send, recv):
        lanes = (qkv_cols, out_cols)[part]
        ref = w_v.at[pl.ds(pl.multiple_of(p * slab, slab), slab), lanes]
        return remote(ref, ref, send.at[part, near], recv.at[part, near], {"dp": far})

    def slab_start(part):
        @pl.when(z < dp - 1)
        def _():
            slab_copy(part, z, 1, z + 1, right_send, right_recv).start()

        @pl.when(z > 0)
        def _():
            slab_copy(part, z, 1, z - 1, left_send, left_recv).start()

    def slab_pass(part, d):
        @pl.when(z >= d)
        def _():
            slab_copy(part, z - d, d, 0, right_send, right_recv).wait_recv()

            @pl.when(z < dp - 1)
            def _():
                slab_copy(part, z - d, d + 1, z + 1, right_send, right_recv).start()

        @pl.when(z + d < dp)
        def _():
            slab_copy(part, z + d, d, 0, left_send, left_recv).wait_recv()

            @pl.when(z > 0)
            def _():
                slab_copy(part, z + d, d + 1, z - 1, left_send, left_recv).start()

    def slab_settle(part):
        @pl.when(z < dp - 1)
        def _():
            slab_copy(part, z, 1, z + 1, right_send, right_recv).wait_send()

        @pl.when(z > 0)
        def _():
            slab_copy(part, z, 1, z - 1, left_send, left_recv).wait_send()

        for d in range(1, dp):

            @pl.when((z >= d) & (z < dp - 1))
            def _(d=d):
                slab_copy(part, z - d, d + 1, z + 1, right_send, right_recv).wait_send()

            @pl.when((z + d < dp) & (z > 0))
            def _(d=d):
                slab_copy(part, z + d, d + 1, z - 1, left_send, left_recv).wait_send()

    experts = inner_v.shape[0]
    here = experts // fsdp
    ff = width // 2
    part = ff // dp

    def inner_block(target, half):
        lanes = pl.ds(pl.multiple_of(half * ff + target // fsdp * part, part), part)
        owned = pl.ds(lax.rem(target, fsdp) * here, here)
        return inner_v.at[owned, :, lanes], inner_out.at[me, pl.ds(half * here, here)]

    def inner_copies(k):
        target = spread(z, f, dp, fsdp, k)
        return [
            remote(
                *inner_block(target, half),
                in_send.at[k, half],
                in_recv.at[k, half],
                place(BOTH, fsdp, target),
            )
            for half in range(2)
        ]

    def outer_block(target):
        return outer_v.at[pl.ds(target * here, here)]

    def outer_copy(k):
        target = lax.rem(f + k, fsdp)
        return remote(
            outer_block(target), outer_out.at[f], out_send.at[k], out_recv.at[k], {"fsdp": target}
        )

    def cot_copy(i):
        return remote(
            cot,
            c_all.at[z, f],
            z_send.at[i],
            z_recv.at[i],
            {"dp": lax.rem(z + dp - i, dp)},
        )

    hidden_gather = PlaneGather(
        plane, lambda o: hid_v.at[o], rows, lambda i: h_send.at[i], lambda i: h_recv.at[i]
    )
    attended_gather = PlaneGather(
        plane, lambda o: att_v.at[o], seq, lambda i: a_send.at[i], lambda i: a_recv.at[i]
    )
    cot_gather = [
        PlaneGather(
            plane,
            lambda o, s=s: c_all.at[lax.rem(z + 1 + s, dp), o],
            rows,
            lambda i, s=s: c_send.at[s, i],
            lambda i, s=s: c_recv.at[s, i],
        )
        for s in range(dp)
    ]

    keeps = [
        pltpu.make_async_copy(hidden, hid_v.at[f], local.at[0]),
        pltpu.make_async_copy(weight_in.at[f], w_v.at[weight_rows(me)], local.at[1]),
        pltpu.make_async_copy(cot, c_all.at[z, f], local.at[2]),
        pltpu.make_async_copy(outer_in, outer_raw, local.at[3]),
        pltpu.make_async_copy(inner_in, inner_raw, local.at[4]),
    ]
    for copy in keeps:
        copy.start()

    def small_copy(k):
        target = spread(z, f, dp, fsdp, k)
        return remote(
            small, small_in.at[me], m_send.at[k], m_recv.at[k], place(BOTH, fsdp, target)
        )

    for k in range(1, n):
        small_copy(k).start()
    small_in[me] = small[...]
    for k in range(1, fsdp):
        weight_copy(k).start()
    for i in range(1, dp):
        cot_copy(i).start()
    keeps[0].wait()
    hidden_gather.start()
    keeps[1].wait()
    for k in range(1, fsdp):
        weight_copy(k).wait_recv()

    slab_start(0)
    hidden_gather.middle()
    keeps[2].wait()
    cot_gather[dp - 1].start()

    keeps[3].wait()
    outer_rows = outer_v.shape[1]

    def put_outer(i, tile, lanes, value):
        block = tile // outer_rows
        outer_v[pl.ds(i * block, block), :, lanes] = value.reshape(block, outer_rows, -1)

    reorder(lambda lanes: outer_raw[:, lanes], put_outer, outer_rows, experts)
    hidden_gather.finish()
    for k in range(1, fsdp):
        outer_copy(k).start()
    keeps[4].wait()

    def put_inner(i, tile, lanes, value):
        block = tile // own_rows
        inner_v[pl.ds(i * block, block), :, lanes] = value.reshape(block, own_rows, -1)

    reorder(lambda lanes: inner_raw[:, lanes], put_inner, own_rows, experts)
    owns = [
        pltpu.make_async_copy(outer_block(f), outer_out.at[f], local.at[3]),
        pltpu.make_async_copy(*inner_block(me, 0), local.at[4]),
        pltpu.make_async_copy(*inner_block(me, 1), local.at[5]),
    ]
    for copy in owns:
        copy.start()
    hidden_gather.wait()
    for k in range(1, n):
        small_copy(k).wait()
    for c in range(n // 2):
        pair = small_in[2 * c].astype(F32) + small_in[2 * c + 1].astype(F32)
        gains[:, pl.ds(c * 128, 128)] = pair

    def norm_rows(i, carry):
        values = hid_v[i].astype(F32)
        values = values * lax.rsqrt(jnp.mean(values * values, axis=-1, keepdims=True) + EPS)
        r = pl.ds(pl.multiple_of(i * rows, rows), rows)
        normed_v[r, :] = (values * gains[0:1, :]).astype(BF16)
        return carry

    lax.fori_loop(0, fsdp, norm_rows, 0)
    normed_store = pltpu.make_async_copy(normed_v, normed, local.at[0])
    normed_store.start()

    def cot_begin(s):
        cot_copy(s + 1).wait_recv()
        cot_gather[s].start()

    for d in range(1, dp):
        slab_pass(0, d)
        if d == 1:
            cot_gather[dp - 1].middle()
            cot_begin(0)
        elif d == 2:
            cot_gather[dp - 1].finish()
            cot_gather[0].middle()
            cot_begin(1)
    slab_start(1)
    for k in range(1, n):
        for copy in inner_copies(k):
            copy.start()

    tile = 256

    def project(i, carry):
        r = pl.ds(pl.multiple_of(i * tile, tile), tile)
        for j in range(3):
            col = pl.ds(j * cols, cols)
            value = dot(normed_v[r, :], w_v[:, col], ((1,), (0,)))
            if j < 2:
                raw[r, col] = value
            else:
                qkv[2, r, :] = value.astype(BF16)
        return carry

    lax.fori_loop(0, seq // tile, project, 0)
    row = lax.broadcasted_iota(jnp.int32, (8, 2 * cols), 0)
    lane_of = lax.broadcasted_iota(jnp.int32, (8, 2 * cols), 1)
    chooser = jnp.where(lane_of // cols == row, 1.0, 0.0).astype(F32)
    stat[...] = lax.dot_general(
        chooser,
        raw[...] * raw[...],
        (((1,), (1,)), ((), ())),
        precision=HIGH,
        preferred_element_type=F32,
    )

    def stat_copy(k):
        return remote(
            stat, stat_in.at[f], t_send.at[k], t_recv.at[k], {"fsdp": lax.rem(f + k, fsdp)}
        )

    for k in range(1, fsdp):
        stat_copy(k).start()
    stat_in[f] = stat[...]
    cot_gather[0].finish()
    cot_gather[1].middle()
    cot_begin(2)
    for k in range(1, fsdp):
        stat_copy(k).wait_recv()
    sums = stat_in[0]
    for i in range(1, fsdp):
        sums = sums + stat_in[i]
    corner = jnp.where(
        lax.broadcasted_iota(jnp.int32, (8, 128), 0) == lax.broadcasted_iota(jnp.int32, (8, 128), 1),
        1.0 / width,
        0.0,
    ).astype(F32)
    means = lax.dot_general(
        sums, corner, (((0,), (0,)), ((), ())), precision=HIGH, preferred_element_type=F32
    )
    slab_pass(1, 1)
    cot_gather[1].finish()
    cot_gather[2].middle()
    scale[...] = lax.rsqrt(means + EPS)
    for i in range(2):
        wide = pl.ds(i * cols, cols)
        unit[:, wide] = raw[:, wide] * scale[:, i : i + 1]
        for h in range(cols // HEAD_DIM):
            lane = pl.ds(i * cols + h * HEAD_DIM, HEAD_DIM)
            own = pl.ds(pl.multiple_of(f * cols + h * HEAD_DIM, HEAD_DIM), HEAD_DIM)
            values = unit[:, lane] * gains[1 + i : 2 + i, own]
            values = values * turn[0] - pltpu.roll(values, HEAD_DIM // 2, 1) * turn[1]
            qkv[i, :, pl.ds(h * HEAD_DIM, HEAD_DIM)] = values.astype(BF16)

    def head(h, carry):
        lane = pl.ds(pl.multiple_of(h * HEAD_DIM, HEAD_DIM), HEAD_DIM)
        for t in range(seq // tile):
            r = pl.ds(t * tile, tile)
            extent = (t + 1) * tile
            upto = pl.ds(0, extent)
            scores = dot(qkv[0, r, lane], qkv[1, upto, lane], ((1,), (1,))) * scaling
            q_pos = t * tile + lax.broadcasted_iota(jnp.int32, (tile, extent), 0)
            k_pos = lax.broadcasted_iota(jnp.int32, (tile, extent), 1)
            allowed = (k_pos <= q_pos) & (live[0:1, 0:extent] > 0.0)
            masked = jnp.where(allowed, scores, -1e30)
            weights = jnp.exp(masked - jnp.max(masked, axis=-1, keepdims=True))
            weights = jnp.where(allowed, weights, 0.0)
            probs = weights / jnp.sum(weights, axis=-1, keepdims=True)
            att_v[f, r, lane] = dot(
                probs.astype(BF16), qkv[2, upto, lane], ((1,), (0,))
            ).astype(BF16)
        return carry

    lax.fori_loop(0, cols // HEAD_DIM, head, 0)
    attended_gather.start()
    slab_pass(1, 2)
    attended_gather.middle()
    cot_gather[2].finish()
    slab_pass(1, 3)
    attended_gather.finish()
    attended_gather.wait()
    attended_store = pltpu.make_async_copy(att_v, attended, local.at[2])
    attended_store.start()

    weight_store = pltpu.make_async_copy(w_v, weight, local.at[1])
    weight_store.start()


    def project_out(i, carry):
        r = pl.ds(pl.multiple_of(i * tile, tile), tile)
        total = dot(att_v[0, r, :], w_v[pl.ds(0, cols), out_cols], ((1,), (0,)))
        for j in range(1, fsdp):
            total += dot(att_v[j, r, :], w_v[pl.ds(j * cols, cols), out_cols], ((1,), (0,)))
        cols_v[r, :] = total.astype(BF16)
        return carry

    lax.fori_loop(0, seq // tile, project_out, 0)

    def branch_copy(k):
        target = lax.rem(f + k, fsdp)
        return remote(
            cols_v.at[pl.ds(pl.multiple_of(target * rows, rows), rows)],
            rows_v.at[f],
            b_send.at[k],
            b_recv.at[k],
            {"fsdp": target},
        )

    for k in range(1, fsdp):
        branch_copy(k).start()
    rows_v[f] = cols_v[pl.ds(pl.multiple_of(f * rows, rows), rows), :]
    for k in range(1, fsdp):
        branch_copy(k).wait()
    for i in range(fsdp):
        branch[:, pl.ds(i * cols, cols)] = rows_v[i]

    for s in range(dp):
        cot_gather[s].wait()
        cot_gather[s].settle()
    hidden_gather.settle()
    attended_gather.settle()
    for i in range(1, dp):
        cot_copy(i).wait_send()

    slab_settle(0)
    slab_settle(1)
    for k in range(1, fsdp):
        weight_copy(k).wait_send()
        stat_copy(k).wait_send()
        outer_copy(k).wait()
    for k in range(1, n):
        for copy in inner_copies(k):
            copy.wait()
    for copy in owns:
        copy.wait()
    normed_store.wait()
    weight_store.wait()
    attended_store.wait()


def attention_forward(
    hidden, cot, weight_in, inner_in, outer_in, small, turn, live, ident
):
    dp = lax.axis_size("dp")
    fsdp = lax.axis_size("fsdp")
    n = dp * fsdp
    rows, width = hidden.shape
    seq = rows * fsdp
    cols = width // fsdp
    shape = jax.ShapeDtypeStruct
    dma = pltpu.SemaphoreType.DMA
    vmem = pltpu.VMEM
    anywhere = pl.BlockSpec(memory_space=pl.ANY)
    inside = pl.BlockSpec(memory_space=pltpu.VMEM)
    sems = [dma((n,)), dma((n,)), dma((fsdp,)), dma((fsdp,))] + [dma((2, dp + 1))] * 4
    for size in (10, fsdp, 10, fsdp):
        sems += [dma((size,)), dma((size,))]
    sems += [dma((dp, 10)), dma((dp, 10)), dma((dp,)), dma((dp,))]
    sems += [dma((n, 2)), dma((n, 2)), dma((fsdp,)), dma((fsdp,))]
    experts = inner_in.shape[1]
    out_rows = outer_in.shape[0]
    here = experts // fsdp
    return pl.pallas_call(
        functools.partial(attention_kernel, dp, fsdp),
        out_shape=(
            shape((small.shape[0], width), F32),
            shape((rows, width), BF16),
            shape((3, seq, cols), BF16),
            shape((seq, 2 * cols), F32),
            shape((seq, 128), F32),
            shape((seq, width), BF16),
            shape((width, 4 * cols), BF16),
            shape((fsdp, seq, cols), BF16),
            shape((dp, fsdp, rows, width), BF16),
            shape((n, 2 * here, width // n, width // 2 // dp), BF16),
            shape((fsdp, here, out_rows, width), BF16),
        ),
        in_specs=[anywhere] * 5 + [inside] * 3,
        out_specs=(inside,) * 5 + (anywhere,) * 6,
        scratch_shapes=[
            vmem((fsdp, rows, width), BF16),
            vmem((n,) + small.shape, BF16),
            vmem((seq, width), BF16),
            vmem((width, 4 * cols), BF16),
            vmem((seq, 2 * cols), F32),
            vmem((8, seq), F32),
            vmem((fsdp, 8, seq), F32),
            vmem((fsdp, seq, cols), BF16),
            vmem((seq, cols), BF16),
            vmem((fsdp, rows, cols), BF16),
            vmem((width // n * experts, width), BF16),
            vmem((experts, width // n, width), BF16),
            vmem((out_rows * experts, width), BF16),
            vmem((experts, out_rows, width), BF16),
            dma((6,)),
            *sems,
        ],
        compiler_params=pltpu.CompilerParams(
            collective_id=ident, has_side_effects=True, vmem_limit_bytes=63 * 1024 * 1024
        ),
    )(
        hidden,
        cot,
        weight_in,
        inner_in.reshape(-1, width),
        outer_in.reshape(-1, width),
        small,
        turn,
        live,
    )


def attention_back_kernel(
    dp,
    fsdp,
    grad_rows,
    attended,
    weight,
    normed,
    qkv,
    unit,
    scale,
    gains,
    turn,
    live,
    grad_middle,
    hidden,
    terms,
    first_in,
    inner_in,
    outer_in,
    hidden_grad,
    terms_out,
    owned,
    inner_owned,
    outer_owned,
    inner_out,
    outer_out,
    att_v,
    w_v,
    normed_v,
    gcols,
    part1,
    held1,
    core1,
    half1,
    full1,
    part2,
    held2,
    core2,
    half2,
    full2,
    gatt,
    gval,
    gqk,
    gqkv,
    stat,
    stat_in,
    wgrad,
    z_in,
    term_v,
    term_in,
    local,
    v_send,
    v_recv,
    in_send,
    in_recv,
    out_send,
    out_recv,
    g_send,
    g_recv,
    s1_send,
    s1_recv,
    s2_send,
    s2_recv,
    t_send,
    t_recv,
    r_send,
    r_recv,
    l_send,
    l_recv,
    w_send,
    w_recv,
):
    n = dp * fsdp
    z = lax.axis_index("dp")
    f = lax.axis_index("fsdp")
    me = z * fsdp + f
    plane = Plane(f)
    rows, width = grad_rows.shape
    seq, cols = gcols.shape
    own_rows = width // n
    slab = fsdp * own_rows
    scaling = HEAD_DIM ** (-0.5)
    greet_all(n, fsdp, me)
    ff = width // 2
    ff_here = ff // dp

    inner_place = inner_out.at[f, :, pl.ds(pl.multiple_of(z * ff_here, ff_here), ff_here)]

    pair = outer_in.shape[1]
    outer_place = outer_out.at[f // 2, pl.ds(pl.multiple_of(lax.rem(f, 2) * pair, pair), pair)]

    loads = [
        pltpu.make_async_copy(attended, att_v, local.at[0]),
        pltpu.make_async_copy(weight, w_v, local.at[1]),
        pltpu.make_async_copy(normed, normed_v, local.at[2]),
        pltpu.make_async_copy(
            grad_rows.at[:, pl.ds(pl.multiple_of(f * cols, cols), cols)],
            gcols.at[pl.ds(pl.multiple_of(f * rows, rows), rows)],
            local.at[3],
        ),
    ]
    keeps = [
        pltpu.make_async_copy(inner_in.at[me], inner_place, local.at[4]),
        pltpu.make_async_copy(outer_in.at[f], outer_place, local.at[6]),
    ]
    for copy in loads:
        copy.start()

    def cols_copy(k):
        target = lax.rem(f + k, fsdp)
        return remote(
            grad_rows.at[:, pl.ds(pl.multiple_of(target * cols, cols), cols)],
            gcols.at[pl.ds(pl.multiple_of(f * rows, rows), rows)],
            g_send.at[k],
            g_recv.at[k],
            {"fsdp": target},
        )

    def inner_copy(k):
        target = spread(z, f, dp, fsdp, k)
        return remote(
            inner_in.at[target],
            inner_place,
            in_send.at[k],
            in_recv.at[k],
            place(BOTH, fsdp, target),
        )

    def outer_copy(k):
        target = lax.rem(f + k, fsdp)
        return remote(
            outer_in.at[target], outer_place, out_send.at[k], out_recv.at[k], {"fsdp": target}
        )

    def slab_rows(p):
        return pl.ds(pl.multiple_of(p * slab, slab), slab)

    def right_copy(part, d):
        lanes = parts[part]
        return remote(
            wgrad.at[slab_rows(z + d), lanes],
            z_in.at[z + d, :, lanes],
            r_send.at[part, d],
            r_recv.at[part, d - 1],
            {"dp": z + 1},
        )

    def left_copy(part, d):
        lanes = parts[part]
        return remote(
            wgrad.at[slab_rows(z - d), lanes],
            z_in.at[dp if d == 1 else z - d, :, lanes],
            l_send.at[part, d],
            l_recv.at[part, d - 1],
            {"dp": z - 1},
        )

    def arrived(part, slot, sem):
        lanes = parts[part]
        ref = z_in.at[slot, :, lanes]
        remote(ref, ref, sem, sem, plane.to_x).wait_recv()

    def pass_along(part, d):
        lanes = parts[part]

        def add(p):
            block = slab_rows(p)
            wgrad[block, lanes] = (
                wgrad[block, lanes].astype(F32) + z_in[p, :, lanes].astype(F32)
            ).astype(BF16)

        @pl.when(z + d < dp)
        def _():
            @pl.when(z > 0)
            def _():
                arrived(part, z + d, r_recv.at[part, d])
                add(z + d)

            right_copy(part, d).start()

        @pl.when(z >= d)
        def _():
            @pl.when(z < dp - 1)
            def _():
                arrived(part, z - d, l_recv.at[part, d])
                add(z - d)

            left_copy(part, d).start()

    qkv_cols = pl.ds(0, 3 * cols)
    out_cols = pl.ds(3 * cols, cols)
    parts = (pl.ds(0, 2 * cols), out_cols, pl.ds(2 * cols, cols))

    for k in range(1, fsdp):
        cols_copy(k).start()
    for k in range(1, n):
        inner_copy(k).start()
    for k in range(1, fsdp):
        outer_copy(k).start()
    for copy in keeps:
        copy.start()
    term_v[...] = terms[...]
    for copy in loads:
        copy.wait()
    for k in range(1, fsdp):
        cols_copy(k).wait_recv()

    def attended_back(i, carry):
        block = pl.ds(pl.multiple_of(i * cols, cols), cols)
        part1[i] = dot(gcols[...], w_v[block, out_cols], ((1,), (1,))).astype(BF16)
        return carry

    lax.fori_loop(0, fsdp, attended_back, 0)
    sum1 = PlaneSum(plane, part1, held1, core1, half1, full1, s1_send, s1_recv)
    sum1.start()

    def out_grads(i, carry):
        block = pl.ds(pl.multiple_of(i * cols, cols), cols)
        wgrad[block, out_cols] = dot(att_v[i], gcols[...], ((0,), (0,))).astype(BF16)
        return carry

    lax.fori_loop(0, fsdp // 2, out_grads, 0)
    sum1.add_core()
    lax.fori_loop(fsdp // 2, fsdp, out_grads, 0)
    sum1.pass_on()
    pass_along(1, 3)
    gqk[...] = jnp.zeros_like(gqk)
    gval[...] = jnp.zeros_like(gval)
    gatt[...] = sum1.total().astype(BF16)

    tile = 256

    def head(h, carry):
        lane = pl.ds(pl.multiple_of(h * HEAD_DIM, HEAD_DIM), HEAD_DIM)
        key_lane = pl.ds(pl.multiple_of(cols + h * HEAD_DIM, HEAD_DIM), HEAD_DIM)
        for t in range(seq // tile):
            r = pl.ds(t * tile, tile)
            extent = (t + 1) * tile
            upto = pl.ds(0, extent)
            query = qkv[0, r, lane]
            key = qkv[1, upto, lane]
            value = qkv[2, upto, lane]
            grad = gatt[r, lane]
            scores = dot(query, key, ((1,), (1,))) * scaling
            q_pos = t * tile + lax.broadcasted_iota(jnp.int32, (tile, extent), 0)
            k_pos = lax.broadcasted_iota(jnp.int32, (tile, extent), 1)
            allowed = (k_pos <= q_pos) & (live[0:1, 0:extent] > 0.0)
            masked = jnp.where(allowed, scores, -1e30)
            weights = jnp.exp(masked - jnp.max(masked, axis=-1, keepdims=True))
            weights = jnp.where(allowed, weights, 0.0)
            probs = weights / jnp.sum(weights, axis=-1, keepdims=True)
            grad_probs = dot(grad, value, ((1,), (1,)))
            mean = jnp.sum(probs * grad_probs, axis=-1, keepdims=True)
            grad_scores = (probs * (grad_probs - mean)).astype(BF16)
            gqk[r, lane] = dot(grad_scores, key, ((1,), (0,)))
            gqk[upto, key_lane] += dot(grad_scores, query, ((0,), (0,)))
            gval[upto, lane] += dot(probs.astype(BF16), grad, ((0,), (0,)))
        return carry

    lax.fori_loop(0, cols // HEAD_DIM, head, 0)

    def column_grads(part):
        lanes = parts[part]

        def one(i, carry):
            block = pl.ds(pl.multiple_of(i * 256, 256), 256)
            wgrad[block, lanes] = dot(normed_v[:, block], gqkv[:, lanes], ((0,), (0,))).astype(BF16)
            return carry

        lax.fori_loop(0, width // 256, one, 0)

    gqkv[:, parts[2]] = gval[...].astype(BF16)
    column_grads(2)
    pass_along(1, 2)
    pass_along(2, 3)

    heads_here = cols // HEAD_DIM
    for i in range(2):
        for h in range(heads_here):
            wide = pl.ds(i * cols + h * HEAD_DIM, HEAD_DIM)
            grad = gqk[:, wide] * scaling
            grad = grad * turn[0] + pltpu.roll(grad, HEAD_DIM // 2, 1) * turn[1]
            place_lanes = pl.ds(pl.multiple_of(f * cols + h * HEAD_DIM, HEAD_DIM), HEAD_DIM)
            term_v[1 + i : 2 + i, place_lanes] = jnp.sum(
                grad * unit[:, wide], axis=0, keepdims=True
            )
            gqk[:, wide] = grad * gains[1 + i : 2 + i, place_lanes]
    row = lax.broadcasted_iota(jnp.int32, (8, 2 * cols), 0)
    lane_of = lax.broadcasted_iota(jnp.int32, (8, 2 * cols), 1)
    chooser = jnp.where(lane_of // cols == row, 1.0, 0.0).astype(F32)
    stat[...] = lax.dot_general(
        chooser,
        gqk[...] * unit[...],
        (((1,), (1,)), ((), ())),
        precision=HIGH,
        preferred_element_type=F32,
    )

    def stat_copy(k):
        return remote(
            stat, stat_in.at[f], t_send.at[k], t_recv.at[k], {"fsdp": lax.rem(f + k, fsdp)}
        )

    for k in range(1, fsdp):
        stat_copy(k).start()
    stat_in[f] = stat[...]
    pass_along(1, 1)
    pass_along(2, 2)
    for k in range(1, fsdp):
        stat_copy(k).wait_recv()
    sums = stat_in[0]
    for i in range(1, fsdp):
        sums = sums + stat_in[i]
    corner = jnp.where(
        lax.broadcasted_iota(jnp.int32, (8, 128), 0) == lax.broadcasted_iota(jnp.int32, (8, 128), 1),
        1.0 / width,
        0.0,
    ).astype(F32)
    means = lax.dot_general(
        sums, corner, (((0,), (0,)), ((), ())), precision=HIGH, preferred_element_type=F32
    )
    for i in range(2):
        wide = pl.ds(i * cols, cols)
        grad = scale[:, i : i + 1] * (gqk[:, wide] - unit[:, wide] * means[:, i : i + 1])
        gqkv[:, wide] = grad.astype(BF16)

    step = 512

    def normed_back(i, carry):
        r = pl.ds(pl.multiple_of(i * rows, rows), rows)
        for c in range(width // step):
            col = pl.ds(c * step, step)
            part2[i, :, col] = dot(gqkv[r, :], w_v[col, qkv_cols], ((1,), (1,))).astype(BF16)
        return carry

    lax.fori_loop(0, fsdp, normed_back, 0)
    sum2 = PlaneSum(plane, part2, held2, core2, half2, full2, s2_send, s2_recv)
    sum2.start()

    column_grads(0)
    pass_along(0, 3)
    sum2.add_core()
    pass_along(2, 1)
    pass_along(0, 2)
    sum2.pass_on()

    grad = sum2.total()
    pass_along(0, 1)
    values = hidden[...].astype(F32)
    scale1 = lax.rsqrt(jnp.mean(values * values, axis=-1, keepdims=True) + EPS)
    values = values * scale1
    term_v[0:1, :] = jnp.sum(grad * values, axis=0, keepdims=True)
    grad = grad * gains[0:1, :]
    grad = scale1 * (grad - values * jnp.mean(grad * values, axis=-1, keepdims=True))
    hidden_grad[...] = grad_middle[...] + grad

    def term_copy(k):
        target = lax.rem(me + k, n)
        lanes = pl.ds(pl.multiple_of(target // 2 * 128, 128), 128)
        return remote(
            term_v.at[:, lanes],
            term_in.at[me],
            v_send.at[k],
            v_recv.at[k],
            place(BOTH, fsdp, target),
        )

    for k in range(1, n):
        term_copy(k).start()
    term_in[me] = term_v[:, pl.ds(pl.multiple_of(me // 2 * 128, 128), 128)]

    for copy in keeps:
        copy.wait()
    for k in range(1, fsdp):
        outer_copy(k).wait()
    outer_load = pltpu.make_async_copy(outer_out, core2, local.at[0])
    outer_load.start()
    for k in range(1, n):
        inner_copy(k).wait()
    inner_loads = [
        pltpu.make_async_copy(first_in, part2.at[:, :, pl.ds(0, ff)], local.at[1]),
        pltpu.make_async_copy(inner_out, part2.at[:, :, pl.ds(ff, ff)], local.at[2]),
    ]
    for copy in inner_loads:
        copy.start()
    experts = fsdp * (inner_in.shape[1] // own_rows)
    outer_load.wait()
    outer_rows = core2.shape[0] * core2.shape[1]
    inner_rows = part2.shape[0] * part2.shape[1]

    def put_outer(i, tile, lanes, value):
        block = tile // rows
        held2[pl.ds(i * block, block), :, lanes] = value.reshape(block, rows, -1)

    reorder(
        lambda lanes: core2[:, :, lanes].reshape(outer_rows, -1),
        put_outer,
        experts,
        outer_rows // experts,
    )
    for copy in inner_loads:
        copy.wait()

    def put_inner(i, tile, lanes, value):
        normed_v[pl.ds(pl.multiple_of(i * tile, tile), tile), lanes] = value

    reorder(
        lambda lanes: part2[:, :, lanes].reshape(inner_rows, -1),
        put_inner,
        experts,
        inner_rows // experts,
    )
    stores = [
        pltpu.make_async_copy(held2, outer_owned, local.at[0]),
        pltpu.make_async_copy(normed_v, inner_owned, local.at[1]),
    ]
    for store in stores:
        store.start()

    @pl.when(z > 0)
    def _():
        for part in range(3):
            arrived(part, z, r_recv.at[part, 0])
        total = wgrad[slab_rows(z), :].astype(F32) + z_in[z].astype(F32)
        wgrad[slab_rows(z), :] = total.astype(BF16)

    @pl.when(z < dp - 1)
    def _():
        for part in range(3):
            arrived(part, dp, l_recv.at[part, 0])
        total = wgrad[slab_rows(z), :].astype(F32) + z_in[dp].astype(F32)
        wgrad[slab_rows(z), :] = total.astype(BF16)

    for part in range(3):
        for d in range(1, dp):

            @pl.when(z + d < dp)
            def _(part=part, d=d):
                right_copy(part, d).wait_send()

            @pl.when(z >= d)
            def _(part=part, d=d):
                left_copy(part, d).wait_send()

    def owner_rows(target):
        return wgrad.at[pl.ds(pl.multiple_of(z * slab + target * own_rows, own_rows), own_rows)]

    def owner_copy(k):
        target = lax.rem(f + k, fsdp)
        return remote(
            owner_rows(target), owned.at[f], w_send.at[k], w_recv.at[k], {"fsdp": target}
        )

    for k in range(1, fsdp):
        owner_copy(k).start()
    own_block = pl.multiple_of(z * slab + f * own_rows, own_rows)
    owned[f] = wgrad[pl.ds(own_block, own_rows), :]
    for k in range(1, fsdp):
        owner_copy(k).wait()
    for k in range(1, fsdp):
        cols_copy(k).wait_send()
        stat_copy(k).wait_send()
    for k in range(1, n):
        term_copy(k).wait()
    total = term_in[0]
    for i in range(1, n):
        total += term_in[i]
    terms_out[...] = total
    for store in stores:
        store.wait()


def attention_back(
    grad_rows,
    attended,
    weight,
    normed,
    qkv,
    unit,
    scale,
    gains,
    turn,
    live,
    grad_middle,
    hidden,
    terms,
    first_in,
    inner_in,
    outer_in,
    ident,
):
    dp = lax.axis_size("dp")
    fsdp = lax.axis_size("fsdp")
    n = dp * fsdp
    rows, width = grad_rows.shape
    seq = rows * fsdp
    cols = width // fsdp
    own_rows = width // n
    shape = jax.ShapeDtypeStruct
    dma = pltpu.SemaphoreType.DMA
    vmem = pltpu.VMEM
    anywhere = pl.BlockSpec(memory_space=pl.ANY)
    inside = pl.BlockSpec(memory_space=pltpu.VMEM)
    return pl.pallas_call(
        functools.partial(attention_back_kernel, dp, fsdp),
        out_shape=(
            shape((rows, width), F32),
            shape((terms.shape[0], 128), F32),
            shape((fsdp, own_rows, 4 * cols), BF16),
            shape((seq, width), BF16),
            shape((4, rows, width), BF16),
            shape((fsdp, rows, width // 2), BF16),
            shape((4, rows, width), BF16),
        ),
        in_specs=[anywhere] * 4 + [inside] * 9 + [anywhere] * 3,
        out_specs=(inside,) * 3 + (anywhere,) * 4,
        scratch_shapes=[
            vmem((fsdp, seq, cols), BF16),
            vmem((width, 4 * cols), BF16),
            vmem((seq, width), BF16),
            vmem((seq, cols), BF16),
            vmem((fsdp, seq, cols), BF16),
            vmem((4, seq, cols), BF16),
            vmem((4, seq, cols), BF16),
            vmem((2, seq // 2, cols), BF16),
            vmem((2, seq, cols), BF16),
            vmem((fsdp, rows, width), BF16),
            vmem((4, rows, width), BF16),
            vmem((4, rows, width), BF16),
            vmem((2, rows // 2, width), BF16),
            vmem((2, rows, width), BF16),
            vmem((seq, cols), BF16),
            vmem((seq, cols), F32),
            vmem((seq, 2 * cols), F32),
            vmem((seq, 3 * cols), BF16),
            vmem((8, seq), F32),
            vmem((fsdp, 8, seq), F32),
            vmem((width, 4 * cols), BF16),
            vmem((dp + 1, fsdp * own_rows, 4 * cols), BF16),
            vmem(terms.shape, F32),
            vmem((n, terms.shape[0], 128), F32),
            dma((7,)),
            dma((n,)),
            dma((n,)),
            dma((n,)),
            dma((n,)),
            dma((fsdp,)),
            dma((fsdp,)),
            dma((fsdp,)),
            dma((fsdp,)),
            dma((8,)),
            dma((8,)),
            dma((8,)),
            dma((8,)),
            dma((fsdp,)),
            dma((fsdp,)),
            dma((3, dp)),
            dma((3, dp)),
            dma((3, dp)),
            dma((3, dp)),
            dma((fsdp,)),
            dma((fsdp,)),
        ],
        compiler_params=pltpu.CompilerParams(
            collective_id=ident, has_side_effects=True, vmem_limit_bytes=63 * 1024 * 1024
        ),
    )(
        grad_rows,
        attended,
        weight,
        normed,
        qkv,
        unit,
        scale,
        gains,
        turn,
        live,
        grad_middle,
        hidden,
        terms,
        first_in,
        inner_in,
        outer_in,
    )


def expert_kernel(
    dp,
    fsdp,
    x_in,
    c_all,
    gates,
    inner_in,
    outer_in,
    sums,
    gate_sum,
    first_out,
    inner_out,
    outer_out,
    gathered,
    far,
    xv,
    cv,
    wi,
    wo,
    gi,
    go,
    ggu,
    act,
    gv,
    part,
    held,
    core_in,
    half_in,
    full_in,
    leaving,
    gates_in,
    grads_out,
    grads_in,
    local,
    g_send,
    g_recv,
    gg_send,
    gg_recv,
    f_send,
    f_recv,
    z_send,
    z_recv,
    a_send,
    a_recv,
    b_send,
    b_recv,
    k_send,
    k_recv,
    c_send,
    c_recv,
    s1_send,
    s1_recv,
    s2_send,
    s2_recv,
    o_send,
    o_recv,
    credit,
):
    rows, width = x_in.shape
    half = rows // 2
    z = lax.axis_index("dp")
    f = lax.axis_index("fsdp")
    core = lax.rem(f, 2)
    chip = f // 2
    xbit = lax.rem(chip, 2)
    ybit = chip // 2
    chip_x = ybit * 2 + (1 - xbit)
    chip_y = (1 - ybit) * 2 + xbit
    chip_d = (1 - ybit) * 2 + (1 - xbit)
    fx = chip_x * 2 + core
    fy = chip_y * 2 + core
    fd = chip_d * 2 + core
    fc = chip * 2 + (1 - core)
    to_x = {"fsdp": fx}
    to_y = {"fsdp": fy}
    to_c = {"fsdp": fc}
    upper = pl.ds(0, half)
    lower = pl.ds(half, half)

    def remote(src, dst, send, recv, device):
        return pltpu.make_async_remote_copy(
            src, dst, send, recv, device_id=device, device_id_type=MESH_ID
        )

    def plane_at(s):
        return lax.rem(z + 1 + s, dp)

    def far_copy(i):
        return remote(
            x_in,
            gathered.at[z, f],
            z_send.at[i],
            z_recv.at[i],
            {"dp": lax.rem(z + dp - i, dp)},
        )

    def gather_one(s):
        block = gathered.at[plane_at(s), f]
        return (
            remote(block.at[upper], block.at[upper], a_send.at[s, 0], a_recv.at[s, 0], to_x),
            remote(block.at[lower], block.at[lower], a_send.at[s, 1], a_recv.at[s, 1], to_y),
        )

    def gather_two(s):
        p = plane_at(s)
        copies = []
        for i, (owner, piece, device) in enumerate(
            ((f, upper, to_y), (fx, upper, to_y), (f, lower, to_x), (fy, lower, to_x))
        ):
            ref = gathered.at[p, owner, piece]
            copies.append(remote(ref, ref, b_send.at[s, i], b_recv.at[s, i], device))
        return copies

    def gather_core(s):
        p = plane_at(s)
        copies = []
        for i, owner in enumerate((f, fx, fy, fd)):
            ref = gathered.at[p, owner]
            copies.append(remote(ref, ref, k_send.at[s, i], k_recv.at[s, i], to_c))
        return copies

    def block_rows(owner):
        return pl.ds(pl.multiple_of(owner * rows, rows), rows)

    def core_copy(k, j):
        return remote(
            part.at[k, block_rows(j * 2 + 1 - core)],
            core_in.at[k, j],
            c_send.at[k, j],
            c_recv.at[k, j],
            to_c,
        )

    def half_copies(k):
        return (
            remote(
                held.at[k, chip_d, upper], half_in.at[k, 0], s1_send.at[k, 0], s1_recv.at[k, 0], to_x
            ),
            remote(
                held.at[k, chip_d, lower], half_in.at[k, 1], s1_send.at[k, 1], s1_recv.at[k, 1], to_y
            ),
        )

    def full_copies(k):
        return (
            remote(held.at[k, chip_x], full_in.at[k, 0], s2_send.at[k, 0], s2_recv.at[k, 0], to_x),
            remote(held.at[k, chip_y], full_in.at[k, 1], s2_send.at[k, 1], s2_recv.at[k, 1], to_y),
        )

    def out_copy(s, k):
        return remote(
            leaving.at[lax.rem(s, 2), k],
            far.at[k, z],
            o_send.at[s, k],
            o_recv.at[s, k],
            {"dp": plane_at(s)},
        )

    def add_core():
        def add_block(k, j):
            core_copy(k, j).wait()
            held[k, j] = (
                part[k, block_rows(j * 2 + core)].astype(F32) + core_in[k, j].astype(F32)
            ).astype(BF16)

        for k in range(2):
            add_block(k, chip_d)
            for copy in half_copies(k):
                copy.start()
        for k in range(2):
            for j in (chip_x, chip_y, chip):
                add_block(k, j)
        pl.semaphore_signal(credit, inc=1, device_id=to_c, device_id_type=MESH_ID)

    def pass_full():
        for k in range(2):
            for copy in half_copies(k):
                copy.wait()
            held[k, chip_y, upper] = (
                held[k, chip_y, upper].astype(F32) + half_in[k, 0].astype(F32)
            ).astype(BF16)
            held[k, chip_x, lower] = (
                held[k, chip_x, lower].astype(F32) + half_in[k, 1].astype(F32)
            ).astype(BF16)
            for copy in full_copies(k):
                copy.start()

    def total_here(k):
        for copy in full_copies(k):
            copy.wait()
        return held[k, chip].astype(F32) + full_in[k, 0].astype(F32) + full_in[k, 1].astype(F32)

    n = dp * fsdp
    me = z * fsdp + f
    greet_all(n, fsdp, me)

    def gate_copy(k):
        target = lax.rem(me + k, n)
        return remote(
            gates.at[target],
            gates_in.at[me],
            g_send.at[k],
            g_recv.at[k],
            place(BOTH, fsdp, target),
        )

    def gate_grad_copy(k):
        target = lax.rem(me + k, n)
        return remote(
            grads_out.at[target],
            grads_in.at[me],
            gg_send.at[k],
            gg_recv.at[k],
            place(BOTH, fsdp, target),
        )

    own_rows = wi.shape[2]
    first_lanes = pl.ds(pl.multiple_of(z * wi.shape[3], wi.shape[3]), wi.shape[3])

    def first_ref(e):
        return first_out.at[f, pl.ds(e * own_rows, own_rows), first_lanes]

    def first_copy(k, e):
        target = spread(z, f, dp, fsdp, k)
        return remote(
            wi.at[e, target],
            first_ref(e),
            f_send.at[k, e],
            f_recv.at[k, e],
            place(BOTH, fsdp, target),
        )

    far_copy(1).start()
    for k in range(1, n):
        gate_copy(k).start()
    loads = [pltpu.make_async_copy(x_in, gathered.at[z, f], local.at[0])]
    for q in range(4):
        loads.append(pltpu.make_async_copy(inner_in.at[:, q], wi.at[q], local.at[1 + q]))
    for e in range(2):
        loads.append(pltpu.make_async_copy(outer_in.at[:, e], wo.at[e], local.at[5 + e]))
    loads.append(pltpu.make_async_copy(gates.at[me], gates_in.at[me], local.at[7]))
    for load in loads:
        load.start()
    gi[...] = jnp.zeros_like(gi)
    go[...] = jnp.zeros_like(go)
    for load in loads:
        load.wait()

    def begin_gather(s):
        @pl.when(s < dp - 1)
        def _():
            far_copy(s + 1).wait_recv()

        for copy in gather_one(s):
            copy.start()

    def middle_gather(s):
        for copy in gather_one(s):
            copy.wait_recv()
        for copy in gather_two(s):
            copy.start()

    def end_gather(s):
        for copy in gather_two(s):
            copy.wait_recv()
        for copy in gather_core(s):
            copy.start()

    begin_gather(0)
    for i in range(2, dp):
        far_copy(i).start()
    middle_gather(0)
    end_gather(0)
    begin_gather(1)
    for k in range(1, n):
        gate_copy(k).wait()

    inner_rows = wi.shape[1] * wi.shape[2]
    ff_here = wo.shape[1] * wo.shape[2]
    tile = xv.shape[0] // 2

    def tile_step(t):
        r = pl.ds(pl.multiple_of(t * tile, tile), tile)
        x = xv[r, :]
        c = cv[r, :]
        for e in range(2):
            gate = dot(x, wi[e].reshape(inner_rows, ff_here), ((1,), (0,)))
            up = dot(x, wi[2 + e].reshape(inner_rows, ff_here), ((1,), (0,)))
            back = dot(c, wo[e].reshape(ff_here, width), ((1,), (1,)))
            sigmoid = 1.0 / (1.0 + jnp.exp(-gate))
            silu = gate * sigmoid
            active = (silu * up).astype(BF16).astype(F32)
            weight = gv[r, e : e + 1]
            gv[r, 8 + e : 9 + e] = jnp.sum(active * back, axis=-1, keepdims=True)
            act[e, r, :] = (weight * active).astype(BF16)
            back = weight * back
            ggu[e, r, :] = (back * up * sigmoid * (1.0 + gate * (1.0 - sigmoid))).astype(BF16)
            ggu[2 + e, r, :] = (back * silu).astype(BF16)
        step = 512
        for i in range(width // step):
            col = pl.ds(i * step, step)
            blocks = pl.ds(i * step // wi.shape[2], step // wi.shape[2])
            total = dot(act[0, r, :], wo[0, :, :, col].reshape(ff_here, step), ((1,), (0,)))
            total += dot(act[1, r, :], wo[1, :, :, col].reshape(ff_here, step), ((1,), (0,)))
            part[0, r, col] = total.astype(BF16)
            total = dot(ggu[0, r, :], wi[0, blocks].reshape(step, ff_here), ((1,), (1,)))
            for q in range(1, 4):
                total += dot(ggu[q, r, :], wi[q, blocks].reshape(step, ff_here), ((1,), (1,)))
            part[1, r, col] = total.astype(BF16)

    def weight_step():
        def inner_part(i, carry):
            col = pl.ds(pl.multiple_of(i * 256, 256), 256)
            xt = xv[:, col]
            for q in range(4):
                gi[q, col, :] += dot(xt, ggu[q], ((0,), (0,)))
            return carry

        lax.fori_loop(0, width // 256, inner_part, 0)

        def outer_part(i, carry):
            col = pl.ds(pl.multiple_of(i * 512, 512), 512)
            ct = cv[:, col]
            for e in range(2):
                go[e, :, col] += dot(act[e], ct, ((0,), (0,)))
            return carry

        lax.fori_loop(0, width // 512, outer_part, 0)

    def chunk(s, carry):
        p = plane_at(s)
        c_load = pltpu.make_async_copy(c_all.at[p], cv, local.at[1])
        c_load.start()

        def to_columns(j, carry):
            r = pl.ds(pl.multiple_of(j * rows, rows), rows)
            gv[r, :] = exact_dot(gates_in[p * fsdp + j], corner_of(8, 0, 1.0), ((0,), (0,)))
            return carry

        lax.fori_loop(0, fsdp, to_columns, 0)
        for copy in gather_core(s):
            copy.wait_recv()
        for j in range(8):
            pltpu.make_async_copy(
                gathered.at[p, j], xv.at[pl.ds(j * rows, rows)], local.at[3 + j]
            ).start()
        c_load.wait()
        for j in range(8):
            pltpu.make_async_copy(
                gathered.at[p, j], xv.at[pl.ds(j * rows, rows)], local.at[3 + j]
            ).wait()
        @pl.when(s < dp - 1)
        def _():
            middle_gather(s + 1)

        tile_step(0)

        @pl.when(s > 0)
        def _():
            pass_full()

        @pl.when(s < dp - 2)
        def _():
            begin_gather(s + 2)

        tile_step(1)

        @pl.when(s > 0)
        def _():
            pl.semaphore_wait(credit, 1)

        for k in range(2):
            for j in range(4):
                core_copy(k, j).start()
        def to_rows(j, carry):
            r = pl.ds(pl.multiple_of(j * rows, rows), rows)
            grads_out[p * fsdp + j] = exact_dot(corner_of(8, 8, 1.0), gv[r, :], ((1,), (1,)))
            return carry

        lax.fori_loop(0, fsdp, to_rows, 0)
        weight_step()

        @pl.when(s > 0)
        def _():
            @pl.when(s > 2)
            def _():
                for k in range(2):
                    out_copy(s - 3, k).wait_send()

            for k in range(2):
                leaving[lax.rem(s - 1, 2), k] = total_here(k).astype(BF16)
                out_copy(s - 1, k).start()

        add_core()

        @pl.when(s < dp - 1)
        def _():
            end_gather(s + 1)

        @pl.when(s == dp - 1)
        def _():
            for e in range(2):
                wi[e] = gi[e].astype(BF16).reshape(wi.shape[1:])
            for k in range(1, n):
                for e in range(2):
                    first_copy(k, e).start()

        return carry

    lax.fori_loop(0, dp, chunk, 0)

    pass_full()
    for k in range(1, n):
        gate_grad_copy(k).start()
    grads_in[me] = grads_out[me]
    for q in range(2, 4):
        wi[q] = gi[q].astype(BF16).reshape(wi.shape[1:])
    for e in range(2):
        wo[e] = go[e].astype(BF16).reshape(wo.shape[1:])
    stores = []
    for e in range(2):
        stores.append(pltpu.make_async_copy(wi.at[e, me], first_ref(e), local.at[e]))
        stores.append(pltpu.make_async_copy(wi.at[2 + e], inner_out.at[:, e], local.at[2 + e]))
    for e in range(2):
        stores.append(pltpu.make_async_copy(wo.at[e], outer_out.at[:, e], local.at[4 + e]))
    for store in stores:
        store.start()
    pl.semaphore_wait(credit, 1)
    for i in range(1, dp):
        for k in range(2):
            if i > dp - 3:
                out_copy(i - 1, k).wait_send()
            remote(
                held.at[k, chip],
                far.at[k, lax.rem(z + dp - i, dp)],
                o_send.at[i - 1, k],
                o_recv.at[i - 1, k],
                to_x,
            ).wait_recv()
    fetch = []
    for i in range(1, dp):
        for k in range(2):
            fetch.append(
                pltpu.make_async_copy(
                    far.at[k, lax.rem(z + i, dp)], core_in.at[k, i], local.at[6 + (i - 1) * 2 + k]
                )
            )
    for copy in fetch:
        copy.start()
    for copy in fetch:
        copy.wait()
    for k in range(2):
        total = total_here(k)
        for i in range(1, dp):
            total += core_in[k, i].astype(F32)
        sums[k] = total
    for k in range(1, n):
        gate_grad_copy(k).wait()
        for e in range(2):
            first_copy(k, e).wait()
    for j in range(fsdp):
        total = grads_in[j]
        for i in range(1, dp):
            total += grads_in[i * fsdp + j]
        gate_sum[j] = total
    for store in stores:
        store.wait()
    for i in range(1, dp):
        far_copy(i).wait_send()

    def settle(s, carry):
        for copy in (*gather_one(s), *gather_two(s), *gather_core(s)):
            copy.wait_send()
        return carry

    lax.fori_loop(0, dp, settle, 0)


def expert_pass(x_in, c_all, gates, inner_in, outer_in, ident):
    dp = lax.axis_size("dp")
    fsdp = lax.axis_size("fsdp")
    rows, width = x_in.shape
    n, four, own_rows, ff_here = inner_in.shape
    _, two, out_rows, _ = outer_in.shape
    chunk = fsdp * rows
    shape = jax.ShapeDtypeStruct
    dma = pltpu.SemaphoreType.DMA
    anywhere = pl.BlockSpec(memory_space=pl.ANY)
    got = pl.pallas_call(
        functools.partial(expert_kernel, dp, fsdp),
        out_shape=(
            shape((2, rows, width), F32),
            shape((fsdp, 8, 128), F32),
            shape((fsdp, 2 * own_rows, dp * ff_here), BF16),
            shape((n, 2, own_rows, ff_here), BF16),
            shape(outer_in.shape, BF16),
            shape((dp, fsdp, rows, width), BF16),
            shape((2, dp, rows, width), BF16),
        ),
        in_specs=[anywhere] * 5,
        out_specs=(pl.BlockSpec(memory_space=pltpu.VMEM),) * 2 + (anywhere,) * 5,
        scratch_shapes=[
            pltpu.VMEM((chunk, width), BF16),
            pltpu.VMEM((chunk, width), BF16),
            pltpu.VMEM((four, n, own_rows, ff_here), BF16),
            pltpu.VMEM((two, fsdp, out_rows, width), BF16),
            pltpu.VMEM((four, width, ff_here), F32),
            pltpu.VMEM((two, ff_here, width), F32),
            pltpu.VMEM((four, chunk, ff_here), BF16),
            pltpu.VMEM((two, chunk, ff_here), BF16),
            pltpu.VMEM((chunk, 128), F32),
            pltpu.VMEM((2, chunk, width), BF16),
            pltpu.VMEM((2, 4, rows, width), BF16),
            pltpu.VMEM((2, 4, rows, width), BF16),
            pltpu.VMEM((2, 2, rows // 2, width), BF16),
            pltpu.VMEM((2, 2, rows, width), BF16),
            pltpu.VMEM((2, 2, rows, width), BF16),
            pltpu.VMEM((n, 8, 128), F32),
            pltpu.VMEM((n, 8, 128), F32),
            pltpu.VMEM((n, 8, 128), F32),
            dma((12 + 2 * dp,)),
            dma((n,)),
            dma((n,)),
            dma((n,)),
            dma((n,)),
            dma((n, 2)),
            dma((n, 2)),
            dma((dp,)),
            dma((dp,)),
            dma((dp, 2)),
            dma((dp, 2)),
            dma((dp, 4)),
            dma((dp, 4)),
            dma((dp, 4)),
            dma((dp, 4)),
            dma((2, 4)),
            dma((2, 4)),
            dma((2, 2)),
            dma((2, 2)),
            dma((2, 2)),
            dma((2, 2)),
            dma((dp, 2)),
            dma((dp, 2)),
            pltpu.SemaphoreType.REGULAR,
        ],
        compiler_params=pltpu.CompilerParams(
            collective_id=ident, has_side_effects=True, vmem_limit_bytes=63 * 1024 * 1024
        ),
    )(x_in, c_all, gates, inner_in, outer_in)
    return got[:5]


def expert_pass_dense(normed2, grad_all, gates, inner_weight, outer_weight):
    n, parts, own_rows, ff_here = inner_weight.shape
    experts_here = parts // 2
    inner = experts_here * ff_here
    width = n * own_rows
    tokens = grad_all.shape[0]
    gates = gates[:, :, None]
    rows_all = lax.all_gather(normed2, BOTH, axis=0, tiled=True)
    inner_block = inner_weight.transpose(0, 2, 1, 3).reshape(width, 2 * inner)
    outer_shape = outer_weight.shape
    outer_block = outer_weight.transpose(1, 0, 2, 3).reshape(inner, width)
    gate_up = dot(rows_all, inner_block, ((1,), (0,)))
    gate = gate_up[:, :inner]
    up = gate_up[:, inner:]
    sigmoid = jax.nn.sigmoid(gate)
    silu = gate * sigmoid
    activation = (silu * up).astype(BF16).astype(F32)
    grad_act = dot(grad_all, outer_block, ((1,), (1,)))
    grad_gates = jnp.sum(
        (activation * grad_act).reshape(tokens, experts_here, ff_here), axis=-1
    )
    by_part = (tokens, experts_here, ff_here)
    activation = (activation.reshape(by_part) * gates).reshape(tokens, inner).astype(BF16)
    grad_act = (grad_act.reshape(by_part) * gates).reshape(tokens, inner)
    grad_gate_up = jnp.concatenate(
        [grad_act * up * sigmoid * (1.0 + gate * (1.0 - sigmoid)), grad_act * silu], axis=1
    ).astype(BF16)
    expert_sum = dot(activation, outer_block, ((1,), (0,))).astype(BF16)
    expert_sum = lax.psum_scatter(expert_sum, BOTH, scatter_dimension=0, tiled=True).astype(F32)
    if tokens > 8192:
        grad_gate_up, expert_sum = lax.optimization_barrier((grad_gate_up, expert_sum))
    grad_rows = dot(grad_gate_up, inner_block, ((1,), (1,))).astype(BF16)
    grad_rows = lax.psum_scatter(grad_rows, BOTH, scatter_dimension=0, tiled=True).astype(F32)
    inner_grad = dot(rows_all, grad_gate_up, ((0,), (0,))).astype(BF16)
    outer_grad = dot(activation, grad_all, ((0,), (0,))).astype(BF16)
    inner_grad = inner_grad.reshape(n, own_rows, parts, ff_here).transpose(0, 2, 1, 3)
    outer_grad = outer_grad.reshape(experts_here, outer_shape[0], outer_shape[2], width)
    return expert_sum, grad_rows, grad_gates, inner_grad, outer_grad.transpose(1, 0, 2, 3)


def body(
    hidden_in,
    lengths,
    routes,
    attn_gain,
    query_gain,
    key_gain,
    ffn_gain,
    qkv_weight,
    out_weight,
    router_weight,
    expert_in,
    expert_out,
    cotangent,
):
    rows, width = hidden_in.shape
    dp = lax.axis_size("dp")
    fsdp = lax.axis_size("fsdp")
    fused = fsdp == 8
    n = dp * fsdp
    experts = router_weight.shape[1]
    seq = rows * fsdp
    tokens = rows * n
    own_rows = width // n
    heads_here = HEADS // fsdp
    cols = heads_here * HEAD_DIM
    experts_here = experts // fsdp
    ff = expert_out.shape[0] * n
    ff_here = ff // dp
    z = lax.axis_index("dp")
    f = lax.axis_index("fsdp")
    valid = lengths[z]
    scaling = HEAD_DIM ** (-0.5)

    if fused:
        small = jnp.stack([attn_gain, query_gain, key_gain, ffn_gain])
        blank = jnp.zeros((-(4 + experts) % 16, own_rows), BF16)
        small = jnp.concatenate([small, router_weight.transpose(1, 0), blank])
        odd = lax.rem(f, 2) == 1
        zero = jnp.zeros((), BF16)
        small = jnp.concatenate(
            [jnp.where(odd, zero, small), jnp.where(odd, small, zero)], axis=1
        )
    else:
        small = jnp.concatenate(
            [attn_gain, query_gain, key_gain, ffn_gain, router_weight.reshape(-1)]
        )
        small_rows = -(-small.size // 2048) * 16
        small = exchange(tiles_of(small, small_rows), BOTH, 0, False).reshape(n, -1)
        gains = small[:, : 4 * own_rows].reshape(n, 4, own_rows).transpose(1, 0, 2)
        gains = gains.reshape(4, width).astype(F32)
        router_full = small[:, 4 * own_rows : 4 * own_rows + own_rows * experts]
        router_full = router_full.reshape(width, experts)
        gain_attn, gain_query, gain_key, gain_ffn = gains[0], gains[1], gains[2], gains[3]

    attn_weight = jnp.concatenate(
        [
            qkv_weight.reshape(own_rows, 3, fsdp, cols),
            out_weight.reshape(own_rows, 1, fsdp, cols),
        ],
        axis=1,
    )
    attn_weight = attn_weight.transpose(2, 0, 1, 3).reshape(fsdp, own_rows, 4 * cols)
    live_mask = (f * rows + jnp.arange(rows, dtype=jnp.int32) < valid).astype(F32)[:, None]
    grad_total = cotangent.astype(F32) * live_mask

    here = f * cols
    pos = jnp.arange(seq, dtype=jnp.int32)
    frequency = jnp.power(10000.0, -jnp.arange(HEAD_DIM // 2, dtype=F32) * 2.0 / HEAD_DIM)
    angles = pos.astype(F32)[:, None] * frequency[None, :]
    cosine = jnp.cos(angles)[:, None, None, :]
    sine = jnp.sin(angles)[:, None, None, :]

    if fused:
        turn = jnp.stack(
            [
                jnp.concatenate([cosine, cosine], axis=-1).reshape(seq, HEAD_DIM),
                jnp.concatenate([sine, -sine], axis=-1).reshape(seq, HEAD_DIM),
            ]
        )
        live_keys = jnp.broadcast_to((pos < valid).astype(F32)[None], (8, seq))
        (
            gains,
            branch,
            qkv,
            qk_unit,
            qk_scale,
            normed_all,
            attn_weight,
            attended_all,
            grad_all,
            inner_weight,
            outer_weight,
        ) = attention_forward(
            hidden_in,
            grad_total.astype(BF16),
            attn_weight,
            expert_in,
            expert_out,
            small,
            turn,
            live_keys,
            10,
        )
        branch = branch.astype(F32)
        gain_ffn = gains[3]
        router_full = gains[4 : 4 + experts].transpose(1, 0).astype(BF16)
    else:
        qk_gain = jnp.stack(
            [
                lax.dynamic_slice(gain_query, (here,), (cols,)),
                lax.dynamic_slice(gain_key, (here,), (cols,)),
            ]
        )
        attn_weight = lax.all_to_all(attn_weight, "fsdp", 0, 0, tiled=True)
        attn_weight = lax.all_gather(
            attn_weight.reshape(fsdp * own_rows, 4 * cols), "dp", axis=0, tiled=True
        )
        qkv_here = attn_weight[:, : 3 * cols]
        out_here = attn_weight[:, 3 * cols :]
        inner_weight = expert_in.reshape(own_rows, fsdp, experts_here, 2, dp, ff_here)
        inner_weight = inner_weight.transpose(4, 1, 3, 2, 0, 5)
        inner_weight = inner_weight.reshape(n, 2 * experts_here, own_rows, ff_here)
        outer_weight = expert_out.reshape(-1, fsdp, experts_here, width).transpose(1, 2, 0, 3)
        inner_weight = lax.all_to_all(inner_weight, BOTH, 0, 0, tiled=True)
        outer_weight = lax.all_to_all(outer_weight, "fsdp", 0, 0, tiled=True)
        hidden_all = lax.all_gather(hidden_in, "fsdp", axis=0, tiled=True).astype(F32)
        normed_all = (hidden_all * rms_scale(hidden_all) * gain_attn).astype(BF16)
        mixed = dot(normed_all, qkv_here, ((1,), (0,)))
        raw = mixed[:, : 2 * cols].reshape(seq, 2, cols)
        squares = plane_sum(jnp.sum(raw * raw, axis=-1), 1)
        qk_scale = lax.rsqrt(squares / width + EPS)[:, :, None]
        qk_unit = raw * qk_scale
        shape4 = (seq, 2, heads_here, HEAD_DIM)
        turned = rotate((qk_unit * qk_gain).reshape(shape4), cosine, sine, 1.0).astype(BF16)
        query = turned[:, 0]
        key = turned[:, 1]
        value = mixed[:, 2 * cols :].astype(BF16).reshape(seq, heads_here, HEAD_DIM)
        allowed = ((pos[None, :] <= pos[:, None]) & (pos[None, :] < valid))[None]
        scores = jnp.einsum("qhd,khd->hqk", query, key, preferred_element_type=F32) * scaling
        masked = jnp.where(allowed, scores, -1e30)
        weights = jnp.exp(masked - jnp.max(masked, axis=-1, keepdims=True))
        weights = jnp.where(allowed, weights, 0.0)
        probs = weights / jnp.sum(weights, axis=-1, keepdims=True)
        probs_low = probs.astype(BF16)
        attended = jnp.einsum("hqk,khd->qhd", probs_low, value, preferred_element_type=F32)
        attended = attended.reshape(seq, cols).astype(BF16)
        attended_all = lax.all_gather(attended, "fsdp", axis=0, tiled=False)
        branch = jnp.einsum(
            "fsc,fcn->sn",
            attended_all,
            out_here.reshape(fsdp, cols, cols),
            preferred_element_type=F32,
        )
        branch = exchange(branch.astype(BF16).reshape(fsdp, rows, cols), ("fsdp",), 2, True)
        branch = branch.transpose(1, 0, 2).reshape(rows, width).astype(F32)
        grad_all = lax.all_gather(grad_total.astype(BF16), BOTH, axis=0, tiled=True)

    hidden = hidden_in.astype(F32)
    scale1 = rms_scale(hidden)
    unit1 = hidden * scale1
    middle = hidden + branch
    scale2 = rms_scale(middle)
    unit2 = middle * scale2
    normed2 = (unit2 * gain_ffn).astype(BF16)
    logits = dot(normed2, router_full, ((1,), (0,)))
    router_probs = jax.nn.softmax(logits, axis=-1)
    chosen = jnp.sum(
        (routes[:, :, None] == jnp.arange(experts, dtype=jnp.int32)[None, None, :]).astype(F32),
        axis=1,
    )

    gates = (router_probs * chosen).reshape(rows, fsdp, experts_here).transpose(1, 2, 0)
    gates = jnp.broadcast_to(gates[None], (dp, fsdp, experts_here, rows))
    gates = gates.reshape(n, experts_here, rows)
    gates = jnp.pad(gates, ((0, 0), (0, 8 - experts_here), (0, 0)))
    if fused:
        sums, grad_gates, first_grad, inner_grad, outer_grad = expert_pass(
            normed2, grad_all.reshape(dp, seq, width), gates, inner_weight, outer_weight, 8
        )
        expert_sum = sums[0]
        grad_rows = sums[1]
        grad_gates = grad_gates[:, :experts_here]
    else:
        gates = exchange(gates, BOTH, 3, True)[:, :experts_here]
        gates = gates.transpose(0, 2, 1).reshape(tokens, experts_here)
        expert_sum, grad_rows, grad_gates, inner_grad, outer_grad = expert_pass_dense(
            normed2, grad_all, gates, inner_weight, outer_weight
        )
        grad_gates = grad_gates.reshape(n, rows, experts_here).transpose(0, 2, 1)
        grad_gates = jnp.pad(grad_gates, ((0, 0), (0, 8 - experts_here), (0, 0)))
        grad_gates = exchange(grad_gates, BOTH, 4, True)[:, :experts_here]
        grad_gates = jnp.sum(grad_gates.reshape(dp, fsdp, experts_here, rows), axis=0)
    grad_router_probs = grad_gates.reshape(experts, rows).transpose(1, 0) * chosen

    block_total = middle + expert_sum
    squares = jnp.stack(
        [
            jnp.sum(live_mask * block_total * block_total),
            jnp.sum(live_mask * branch * branch),
            jnp.sum(live_mask * expert_sum * expert_sum),
        ]
    )

    grad_logits = router_probs * (
        grad_router_probs - jnp.sum(router_probs * grad_router_probs, axis=-1, keepdims=True)
    )
    grad_logits = grad_logits.astype(BF16)
    grad_normed2 = grad_rows + dot(grad_logits, router_full, ((1,), (1,)))
    ffn_term = jnp.sum(grad_normed2 * unit2, axis=0)
    grad_middle = grad_total + norm_back(grad_normed2 * gain_ffn, unit2, scale2)

    if fused:
        terms = jnp.concatenate(
            [
                jnp.zeros((3, width), F32),
                ffn_term[None],
                jnp.broadcast_to(squares[:, None], (3, width)),
                jnp.zeros((1, width), F32),
                dot(grad_logits, normed2, ((0,), (0,))),
            ]
        )
        hidden_grad, terms, attn_grad, inner_grad, outer_grad, _, _ = attention_back(
            grad_middle.astype(BF16),
            attended_all,
            attn_weight,
            normed_all,
            qkv,
            qk_unit,
            qk_scale,
            gains,
            turn,
            live_keys,
            grad_middle,
            hidden_in,
            terms,
            first_grad,
            inner_grad.reshape(n, experts_here * own_rows, ff_here),
            outer_grad.reshape(fsdp, -1, width),
            9,
        )
        inner_grad = inner_grad.reshape(own_rows, experts, 2 * ff)
        outer_grad = outer_grad.reshape(-1, experts, width)
        terms = lax.dynamic_slice(terms, (0, lax.rem(f, 2) * own_rows), (terms.shape[0], own_rows))
        gain_grads = terms[:4]
        router_grad = terms[8:].transpose(1, 0)
        square_sums = terms[4:7, 0]
    else:
        grad_cols = grad_middle.astype(BF16).reshape(rows, fsdp, cols).transpose(1, 0, 2)
        grad_cols = exchange(grad_cols, ("fsdp",), 5, True).reshape(seq, cols)
        out_grad = jnp.einsum("fsc,sn->fcn", attended_all, grad_cols, preferred_element_type=F32)
        grad_attended = jnp.einsum(
            "sn,fcn->fsc", grad_cols, out_here.reshape(fsdp, cols, cols), preferred_element_type=F32
        )
        grad_attended = lax.psum_scatter(
            grad_attended.astype(BF16).reshape(fsdp * seq, cols), "fsdp", scatter_dimension=0, tiled=True
        )
        grad_attended = grad_attended.reshape(seq, heads_here, HEAD_DIM)
        grad_probs = jnp.einsum("qhd,khd->hqk", grad_attended, value, preferred_element_type=F32)
        grad_scores = probs * (grad_probs - jnp.sum(probs * grad_probs, axis=-1, keepdims=True))
        grad_scores = grad_scores.astype(BF16)
        grad_query = jnp.einsum("hqk,khd->qhd", grad_scores, key, preferred_element_type=F32)
        grad_key = jnp.einsum("hqk,qhd->khd", grad_scores, query, preferred_element_type=F32)
        grad_value = jnp.einsum("hqk,qhd->khd", probs_low, grad_attended, preferred_element_type=F32)
        grad_qk = rotate(jnp.stack([grad_query, grad_key], axis=1) * scaling, cosine, sine, -1.0)
        grad_qk = grad_qk.reshape(seq, 2, cols)
        qk_term = jnp.sum(grad_qk * qk_unit, axis=0)
        grad_qk = grad_qk * qk_gain
        inner_means = plane_sum(jnp.sum(grad_qk * qk_unit, axis=-1), 6)[:, :, None] / width
        grad_qk = qk_scale * (grad_qk - qk_unit * inner_means)
        grad_qkv = jnp.concatenate(
            [grad_qk.reshape(seq, 2 * cols), grad_value.reshape(seq, cols)], axis=1
        ).astype(BF16)
        qkv_grad = dot(normed_all, grad_qkv, ((0,), (0,)))
        grad_normed = dot(grad_qkv, qkv_here, ((1,), (1,))).astype(BF16)
        grad_normed = lax.psum_scatter(grad_normed, "fsdp", scatter_dimension=0, tiled=True).astype(F32)
        attn_grad = jnp.concatenate([qkv_grad, out_grad.reshape(width, cols)], axis=1).astype(BF16)
        attn_grad = lax.psum_scatter(attn_grad, "dp", scatter_dimension=0, tiled=True)
        attn_grad = attn_grad.reshape(fsdp, own_rows, 4 * cols)
        attn_grad = lax.all_to_all(attn_grad, "fsdp", 0, 0, tiled=True)
        inner_grad = lax.all_to_all(inner_grad, BOTH, 0, 0, tiled=True)
        outer_grad = lax.all_to_all(outer_grad, "fsdp", 0, 0, tiled=True)
        inner_grad = inner_grad.reshape(dp, fsdp, 2, experts_here, own_rows, ff_here)
        inner_grad = inner_grad.transpose(4, 1, 3, 2, 0, 5).reshape(own_rows, experts, 2 * ff)
        outer_grad = outer_grad.transpose(2, 0, 1, 3).reshape(-1, experts, width)
        attn_term = jnp.sum(grad_normed * unit1, axis=0)
        hidden_grad = grad_middle + norm_back(grad_normed * gain_attn, unit1, scale1)

        router_term = dot(normed2, grad_logits, ((0,), (0,)))
        qk_full = jnp.zeros((2, width), F32)
        qk_full = lax.dynamic_update_slice(qk_full, qk_term, (0, here))
        terms = jnp.concatenate([attn_term[None], qk_full, ffn_term[None]])
        terms = terms.reshape(4, n, own_rows).transpose(1, 0, 2).reshape(n, 4 * own_rows)
        terms = jnp.concatenate(
            [
                terms,
                router_term.reshape(n, own_rows * experts),
                jnp.broadcast_to(squares[None], (n, 3)),
            ],
            axis=1,
        )
        term_size = terms.shape[1]
        term_rows = -(-term_size // 1024) * 8
        terms = jnp.pad(terms, ((0, 0), (0, term_rows * 128 - term_size)))
        terms = exchange(terms.reshape(n, term_rows, 128), BOTH, 7, True)
        terms = jnp.sum(terms, axis=0).reshape(-1)
        gain_grads = terms[: 4 * own_rows].reshape(4, own_rows)
        router_grad = terms[4 * own_rows : 4 * own_rows + own_rows * experts]
        router_grad = router_grad.reshape(own_rows, experts)
        square_sums = terms[term_size - 3 : term_size]
    attn_grad = attn_grad.reshape(fsdp, own_rows, 4, cols).transpose(1, 2, 0, 3).astype(F32)
    attn_grad = attn_grad.reshape(own_rows, 4 * width)
    valid_cells = jnp.sum(lengths).astype(F32) * width
    stats = jnp.sqrt(square_sums / valid_cells)

    return (
        block_total.astype(BF16),
        hidden_grad,
        gain_grads[0],
        gain_grads[1],
        gain_grads[2],
        gain_grads[3],
        attn_grad[:, : 3 * width],
        attn_grad[:, 3 * width :],
        router_grad,
        inner_grad.astype(F32),
        outer_grad.astype(F32),
        stats,
    )


def solution(mesh):
    one = P(BOTH)
    two = P(BOTH, None)
    three = P(BOTH, None, None)
    in_specs = (two, P(), two, one, one, one, one, two, two, two, three, three, two)
    out_specs = (two, two, one, one, one, one, two, two, two, three, three, P())
    return jax.shard_map(body, mesh=mesh, in_specs=in_specs, out_specs=out_specs, check_vma=False)
```

```python
import functools

import jax
import jax.numpy as jnp
import numpy as np
from jax import lax
from jax.experimental import pallas as pl
from jax.experimental.pallas import tpu as pltpu
from jax.sharding import PartitionSpec as P

HEADS = 16
HEAD_DIM = 128
EPS = 1e-05
BOTH = ("dp", "fsdp")
MESH_ID = pl.DeviceIdType.MESH
F32 = jnp.float32
BF16 = jnp.bfloat16


def rms_scale(values_in):
    return lax.rsqrt(jnp.mean(values_in * values_in, axis=-1, keepdims=True) + EPS)


def norm_back(grad_in, unit_rows, scaling):
    return scaling * (grad_in - unit_rows * jnp.mean(grad_in * unit_rows, axis=-1, keepdims=True))


def rotate(values_in, cosine, sine, direction):
    half_width = values_in.shape[-1] // 2
    first_half = values_in[..., :half_width]
    second_half = values_in[..., half_width:]
    return jnp.concatenate(
        [
            first_half * cosine - direction * second_half * sine,
            second_half * cosine + direction * first_half * sine,
        ],
        axis=-1,
    )


def turning(seq):
    steps = np.arange(HEAD_DIM // 2, dtype=np.float32) * np.float32(2.0) / np.float32(HEAD_DIM)
    frequency = np.power(np.float32(10000.0), -steps)
    angles = np.arange(seq, dtype=np.float32)[:, None] * frequency[None, :]
    cosine = np.cos(angles)
    sine = np.sin(angles)
    both = [np.concatenate([cosine, cosine], axis=1), np.concatenate([sine, -sine], axis=1)]
    return np.stack(both).astype(np.float32)


def place(axes, fsdp, index):
    if axes == BOTH:
        return {"dp": index // fsdp, "fsdp": lax.rem(index, fsdp)}
    return {axes[0]: index}


def exchange_kernel(axes, n, fsdp, spread, x, o, send, recv, own):
    if axes == BOTH:
        me = lax.axis_index("dp") * fsdp + lax.axis_index("fsdp")
    else:
        me = lax.axis_index(axes[0])
    barrier = pltpu.get_barrier_semaphore()
    for k in range(1, n):
        peer = place(axes, fsdp, lax.rem(me + k, n))
        pl.semaphore_signal(barrier, inc=1, device_id=peer, device_id_type=MESH_ID)
    pl.semaphore_wait(barrier, n - 1)
    local = pltpu.make_async_copy(x.at[me] if spread else x, o.at[me], own)
    local.start()
    copies = []
    for k in range(1, n):
        target = lax.rem(me + k, n)
        copy = pltpu.make_async_remote_copy(
            x.at[target] if spread else x,
            o.at[me],
            send.at[k],
            recv.at[k],
            device_id=place(axes, fsdp, target),
            device_id_type=MESH_ID,
        )
        copy.start()
        copies.append(copy)
    local.wait()
    for copy in copies:
        copy.wait()


def exchange(x, axes, ident, spread):
    fsdp = lax.axis_size("fsdp")
    n = lax.axis_size(axes)
    shape = x.shape if spread else (n,) + x.shape
    return pl.pallas_call(
        functools.partial(exchange_kernel, axes, n, fsdp, spread),
        out_shape=jax.ShapeDtypeStruct(shape, x.dtype),
        in_specs=[pl.BlockSpec(memory_space=pl.ANY)],
        out_specs=pl.BlockSpec(memory_space=pl.ANY),
        scratch_shapes=[
            pltpu.SemaphoreType.DMA((n,)),
            pltpu.SemaphoreType.DMA((n,)),
            pltpu.SemaphoreType.DMA,
        ],
        compiler_params=pltpu.CompilerParams(collective_id=ident, has_side_effects=True),
    )(x)


def tiles_of(x, rows):
    flat = x.reshape(-1)
    return jnp.pad(flat, (0, rows * 128 - flat.shape[0])).reshape(rows, 128)


def plane_sum(x, ident):
    rows = -(-x.size // 1024) * 8
    got = exchange(tiles_of(x, rows), ("fsdp",), ident, False)
    return jnp.sum(got, axis=0).reshape(-1)[: x.size].reshape(x.shape)


def dot(a, b, dims):
    return lax.dot_general(a, b, (dims, ((), ())), preferred_element_type=F32)


HIGH = lax.Precision.HIGHEST


def remote(src, dst, send, recv, device):
    return pltpu.make_async_remote_copy(
        src, dst, send, recv, device_id=device, device_id_type=MESH_ID
    )


def spread(z, f, dp, fsdp, k):
    step = k % dp
    step = (step + 1) // 2 if step % 2 else dp - step // 2
    return lax.rem(z + step, dp) * fsdp + lax.rem(f + k // dp, fsdp)


def greet_all(n, fsdp, me):
    barrier = pltpu.get_barrier_semaphore()
    for k in range(1, n):
        peer = place(BOTH, fsdp, lax.rem(me + k, n))
        pl.semaphore_signal(barrier, inc=1, device_id=peer, device_id_type=MESH_ID)
    pl.semaphore_wait(barrier, n - 1)


def reorder(get, put, outer, inner):
    total = outer * inner
    tile = 256
    step = 512

    def one(i, carry):
        row = i * tile + lax.broadcasted_iota(jnp.int32, (tile, total), 0)
        col = lax.broadcasted_iota(jnp.int32, (tile, total), 1)
        pick = jnp.where(lax.rem(row, outer) * inner + row // outer == col, 1.0, 0.0).astype(BF16)
        for c in range(2048 // step):
            lanes = pl.ds(c * step, step)
            put(i, tile, lanes, dot(pick, get(lanes), ((1,), (0,))).astype(BF16))
        return carry

    lax.fori_loop(0, total // tile, one, 0)


def corner_of(rows, shift, value):
    row = lax.broadcasted_iota(jnp.int32, (rows, 128), 0)
    lane = lax.broadcasted_iota(jnp.int32, (rows, 128), 1)
    return jnp.where(lane == row + shift, value, 0.0).astype(F32)


def exact_dot(a, b, dims):
    return lax.dot_general(
        a, b, (dims, ((), ())), precision=HIGH, preferred_element_type=F32
    )


class Plane:
    def __init__(self, f):
        self.f = f
        self.core = lax.rem(f, 2)
        self.chip = f // 2
        xbit = lax.rem(self.chip, 2)
        ybit = self.chip // 2
        self.chip_x = ybit * 2 + (1 - xbit)
        self.chip_y = (1 - ybit) * 2 + xbit
        self.chip_d = (1 - ybit) * 2 + (1 - xbit)
        self.fx = self.chip_x * 2 + self.core
        self.fy = self.chip_y * 2 + self.core
        self.fd = self.chip_d * 2 + self.core
        self.to_x = {"fsdp": self.fx}
        self.to_y = {"fsdp": self.fy}
        self.to_c = {"fsdp": self.chip * 2 + 1 - self.core}


class PlaneSum:
    def __init__(self, plane, part, held, core_in, half_in, full_in, send, recv):
        self.plane = plane
        self.part = part
        self.held = held
        self.core_in = core_in
        self.half_in = half_in
        self.full_in = full_in
        self.send = send
        self.recv = recv
        half = held.shape[1] // 2
        self.upper = pl.ds(0, half)
        self.lower = pl.ds(half, half)

    def core_copy(self, j):
        owner = j * 2 + 1 - self.plane.core
        return remote(
            self.part.at[owner],
            self.core_in.at[j],
            self.send.at[j],
            self.recv.at[j],
            self.plane.to_c,
        )

    def half_copies(self):
        block = self.held.at[self.plane.chip_d]
        send, recv, half_in = self.send, self.recv, self.half_in
        return (
            remote(block.at[self.upper], half_in.at[0], send.at[4], recv.at[4], self.plane.to_x),
            remote(block.at[self.lower], half_in.at[1], send.at[5], recv.at[5], self.plane.to_y),
        )

    def full_copies(self):
        held, full_in, send, recv = self.held, self.full_in, self.send, self.recv
        plane = self.plane
        return (
            remote(held.at[plane.chip_x], full_in.at[0], send.at[6], recv.at[6], plane.to_x),
            remote(held.at[plane.chip_y], full_in.at[1], send.at[7], recv.at[7], plane.to_y),
        )

    def start(self):
        for j in range(4):
            self.core_copy(j).start()

    def add_core(self):
        for j in range(4):
            self.core_copy(j).wait()

        def one(j, carry):
            own = self.part[j * 2 + self.plane.core].astype(F32)
            self.held[j] = (own + self.core_in[j].astype(F32)).astype(BF16)
            return carry

        lax.fori_loop(0, 4, one, 0)
        for copy in self.half_copies():
            copy.start()

    def pass_on(self):
        for copy in self.half_copies():
            copy.wait()
        held, half_in = self.held, self.half_in
        for chip, piece, i in (
            (self.plane.chip_y, self.upper, 0),
            (self.plane.chip_x, self.lower, 1),
        ):
            total = held[chip, piece].astype(F32) + half_in[i].astype(F32)
            held[chip, piece] = total.astype(BF16)
        for copy in self.full_copies():
            copy.start()

    def total(self):
        for copy in self.full_copies():
            copy.wait()
        total = self.held[self.plane.chip].astype(F32)
        return total + self.full_in[0].astype(F32) + self.full_in[1].astype(F32)


class PlaneGather:
    def __init__(self, plane, block, rows, send, recv):
        self.plane = plane
        self.block = block
        self.send = send
        self.recv = recv
        self.upper = pl.ds(0, rows // 2)
        self.lower = pl.ds(rows // 2, rows // 2)

    def same(self, ref, i, device):
        return remote(ref, ref, self.send(i), self.recv(i), device)

    def first(self):
        own = self.block(self.plane.f)
        return (
            self.same(own.at[self.upper], 0, self.plane.to_x),
            self.same(own.at[self.lower], 1, self.plane.to_y),
        )

    def second(self):
        plane = self.plane
        return (
            self.same(self.block(plane.f).at[self.upper], 2, plane.to_y),
            self.same(self.block(plane.fx).at[self.upper], 3, plane.to_y),
            self.same(self.block(plane.f).at[self.lower], 4, plane.to_x),
            self.same(self.block(plane.fy).at[self.lower], 5, plane.to_x),
        )

    def third(self):
        plane = self.plane
        owners = (plane.f, plane.fx, plane.fy, plane.fd)
        return [self.same(self.block(o), 6 + i, plane.to_c) for i, o in enumerate(owners)]

    def start(self):
        for copy in self.first():
            copy.start()

    def middle(self):
        for copy in self.first():
            copy.wait_recv()
        for copy in self.second():
            copy.start()

    def finish(self):
        for copy in self.second():
            copy.wait_recv()
        for copy in self.third():
            copy.start()

    def wait(self):
        for copy in self.third():
            copy.wait_recv()

    def settle(self):
        for copy in (*self.first(), *self.second(), *self.third()):
            copy.wait_send()


def attention_kernel(
    dp,
    fsdp,
    hidden,
    cot,
    weight_in,
    inner_in,
    outer_in,
    small,
    turn,
    live,
    gains,
    branch,
    qkv,
    unit,
    scale,
    normed,
    weight,
    attended,
    c_all,
    inner_out,
    outer_out,
    hid_v,
    small_in,
    normed_v,
    w_v,
    raw,
    stat,
    stat_in,
    att_v,
    cols_v,
    rows_v,
    inner_raw,
    inner_v,
    outer_raw,
    outer_v,
    local,
    m_send,
    m_recv,
    w_send,
    w_recv,
    right_send,
    right_recv,
    left_send,
    left_recv,
    h_send,
    h_recv,
    t_send,
    t_recv,
    a_send,
    a_recv,
    b_send,
    b_recv,
    c_send,
    c_recv,
    z_send,
    z_recv,
    in_send,
    in_recv,
    out_send,
    out_recv,
):
    n = dp * fsdp
    z = lax.axis_index("dp")
    f = lax.axis_index("fsdp")
    me = z * fsdp + f
    plane = Plane(f)
    rows, width = hidden.shape
    seq, cols = cols_v.shape
    own_rows = weight_in.shape[1]
    slab = fsdp * own_rows
    scaling = HEAD_DIM ** (-0.5)
    greet_all(n, fsdp, me)

    def weight_rows(index):
        return pl.ds(pl.multiple_of(index * own_rows, own_rows), own_rows)

    def weight_copy(k):
        target = lax.rem(f + k, fsdp)
        return remote(
            weight_in.at[target],
            w_v.at[weight_rows(me)],
            w_send.at[k],
            w_recv.at[k],
            {"fsdp": target},
        )

    qkv_cols = pl.ds(0, 3 * cols)
    out_cols = pl.ds(3 * cols, cols)

    def slab_copy(part, p, near, far, send, recv):
        lanes = (qkv_cols, out_cols)[part]
        ref = w_v.at[pl.ds(pl.multiple_of(p * slab, slab), slab), lanes]
        return remote(ref, ref, send.at[part, near], recv.at[part, near], {"dp": far})

    def slab_start(part):
        @pl.when(z < dp - 1)
        def _():
            slab_copy(part, z, 1, z + 1, right_send, right_recv).start()

        @pl.when(z > 0)
        def _():
            slab_copy(part, z, 1, z - 1, left_send, left_recv).start()

    def slab_pass(part, d):
        @pl.when(z >= d)
        def _():
            slab_copy(part, z - d, d, 0, right_send, right_recv).wait_recv()

            @pl.when(z < dp - 1)
            def _():
                slab_copy(part, z - d, d + 1, z + 1, right_send, right_recv).start()

        @pl.when(z + d < dp)
        def _():
            slab_copy(part, z + d, d, 0, left_send, left_recv).wait_recv()

            @pl.when(z > 0)
            def _():
                slab_copy(part, z + d, d + 1, z - 1, left_send, left_recv).start()

    def slab_settle(part):
        @pl.when(z < dp - 1)
        def _():
            slab_copy(part, z, 1, z + 1, right_send, right_recv).wait_send()

        @pl.when(z > 0)
        def _():
            slab_copy(part, z, 1, z - 1, left_send, left_recv).wait_send()

        for d in range(1, dp):

            @pl.when((z >= d) & (z < dp - 1))
            def _(d=d):
                slab_copy(part, z - d, d + 1, z + 1, right_send, right_recv).wait_send()

            @pl.when((z + d < dp) & (z > 0))
            def _(d=d):
                slab_copy(part, z + d, d + 1, z - 1, left_send, left_recv).wait_send()

    experts = inner_v.shape[0]
    here = experts // fsdp
    ff = width // 2
    part = ff // dp

    def inner_block(target, half):
        lanes = pl.ds(pl.multiple_of(half * ff + target // fsdp * part, part), part)
        owned = pl.ds(lax.rem(target, fsdp) * here, here)
        return inner_v.at[owned, :, lanes], inner_out.at[me, pl.ds(half * here, here)]

    def inner_copies(k):
        target = spread(z, f, dp, fsdp, k)
        return [
            remote(
                *inner_block(target, half),
                in_send.at[k, half],
                in_recv.at[k, half],
                place(BOTH, fsdp, target),
            )
            for half in range(2)
        ]

    def outer_block(target):
        return outer_v.at[pl.ds(target * here, here)]

    def outer_copy(k):
        target = lax.rem(f + k, fsdp)
        return remote(
            outer_block(target), outer_out.at[f], out_send.at[k], out_recv.at[k], {"fsdp": target}
        )

    def cot_copy(i):
        return remote(
            cot,
            c_all.at[z, f],
            z_send.at[i],
            z_recv.at[i],
            {"dp": lax.rem(z + dp - i, dp)},
        )

    hidden_gather = PlaneGather(
        plane, lambda o: hid_v.at[o], rows, lambda i: h_send.at[i], lambda i: h_recv.at[i]
    )
    attended_gather = PlaneGather(
        plane, lambda o: att_v.at[o], seq, lambda i: a_send.at[i], lambda i: a_recv.at[i]
    )
    cot_gather = [
        PlaneGather(
            plane,
            lambda o, s=s: c_all.at[lax.rem(z + 1 + s, dp), o],
            rows,
            lambda i, s=s: c_send.at[s, i],
            lambda i, s=s: c_recv.at[s, i],
        )
        for s in range(dp)
    ]

    keeps = [
        pltpu.make_async_copy(hidden, hid_v.at[f], local.at[0]),
        pltpu.make_async_copy(weight_in.at[f], w_v.at[weight_rows(me)], local.at[1]),
        pltpu.make_async_copy(cot, c_all.at[z, f], local.at[2]),
        pltpu.make_async_copy(outer_in, outer_raw, local.at[3]),
        pltpu.make_async_copy(inner_in, inner_raw, local.at[4]),
    ]
    for copy in keeps:
        copy.start()

    def small_copy(k):
        target = spread(z, f, dp, fsdp, k)
        return remote(
            small, small_in.at[me], m_send.at[k], m_recv.at[k], place(BOTH, fsdp, target)
        )

    for k in range(1, n):
        small_copy(k).start()
    small_in[me] = small[...]
    for k in range(1, fsdp):
        weight_copy(k).start()
    for i in range(1, dp):
        cot_copy(i).start()
    keeps[0].wait()
    hidden_gather.start()
    keeps[1].wait()
    for k in range(1, fsdp):
        weight_copy(k).wait_recv()

    slab_start(0)
    hidden_gather.middle()
    keeps[2].wait()
    cot_gather[dp - 1].start()

    keeps[3].wait()
    outer_rows = outer_v.shape[1]

    def put_outer(i, tile, lanes, value):
        block = tile // outer_rows
        outer_v[pl.ds(i * block, block), :, lanes] = value.reshape(block, outer_rows, -1)

    reorder(lambda lanes: outer_raw[:, lanes], put_outer, outer_rows, experts)
    hidden_gather.finish()
    for k in range(1, fsdp):
        outer_copy(k).start()
    keeps[4].wait()

    def put_inner(i, tile, lanes, value):
        block = tile // own_rows
        inner_v[pl.ds(i * block, block), :, lanes] = value.reshape(block, own_rows, -1)

    reorder(lambda lanes: inner_raw[:, lanes], put_inner, own_rows, experts)
    owns = [
        pltpu.make_async_copy(outer_block(f), outer_out.at[f], local.at[3]),
        pltpu.make_async_copy(*inner_block(me, 0), local.at[4]),
        pltpu.make_async_copy(*inner_block(me, 1), local.at[5]),
    ]
    for copy in owns:
        copy.start()
    hidden_gather.wait()
    for k in range(1, n):
        small_copy(k).wait()
    for c in range(n // 2):
        pair = small_in[2 * c].astype(F32) + small_in[2 * c + 1].astype(F32)
        gains[:, pl.ds(c * 128, 128)] = pair

    def norm_rows(i, carry):
        values = hid_v[i].astype(F32)
        values = values * lax.rsqrt(jnp.mean(values * values, axis=-1, keepdims=True) + EPS)
        r = pl.ds(pl.multiple_of(i * rows, rows), rows)
        normed_v[r, :] = (values * gains[0:1, :]).astype(BF16)
        return carry

    lax.fori_loop(0, fsdp, norm_rows, 0)
    normed_store = pltpu.make_async_copy(normed_v, normed, local.at[0])
    normed_store.start()

    def cot_begin(s):
        cot_copy(s + 1).wait_recv()
        cot_gather[s].start()

    for d in range(1, dp):
        slab_pass(0, d)
        if d == 1:
            cot_gather[dp - 1].middle()
            cot_begin(0)
        elif d == 2:
            cot_gather[dp - 1].finish()
            cot_gather[0].middle()
            cot_begin(1)
    slab_start(1)
    for k in range(1, n):
        for copy in inner_copies(k):
            copy.start()

    tile = 256

    def project(i, carry):
        r = pl.ds(pl.multiple_of(i * tile, tile), tile)
        for j in range(3):
            col = pl.ds(j * cols, cols)
            value = dot(normed_v[r, :], w_v[:, col], ((1,), (0,)))
            if j < 2:
                raw[r, col] = value
            else:
                qkv[2, r, :] = value.astype(BF16)
        return carry

    lax.fori_loop(0, seq // tile, project, 0)
    row = lax.broadcasted_iota(jnp.int32, (8, 2 * cols), 0)
    lane_of = lax.broadcasted_iota(jnp.int32, (8, 2 * cols), 1)
    chooser = jnp.where(lane_of // cols == row, 1.0, 0.0).astype(F32)
    stat[...] = lax.dot_general(
        chooser,
        raw[...] * raw[...],
        (((1,), (1,)), ((), ())),
        precision=HIGH,
        preferred_element_type=F32,
    )

    def stat_copy(k):
        return remote(
            stat, stat_in.at[f], t_send.at[k], t_recv.at[k], {"fsdp": lax.rem(f + k, fsdp)}
        )

    for k in range(1, fsdp):
        stat_copy(k).start()
    stat_in[f] = stat[...]
    cot_gather[0].finish()
    cot_gather[1].middle()
    cot_begin(2)
    for k in range(1, fsdp):
        stat_copy(k).wait_recv()
    sums = stat_in[0]
    for i in range(1, fsdp):
        sums = sums + stat_in[i]
    corner = jnp.where(
        lax.broadcasted_iota(jnp.int32, (8, 128), 0) == lax.broadcasted_iota(jnp.int32, (8, 128), 1),
        1.0 / width,
        0.0,
    ).astype(F32)
    means = lax.dot_general(
        sums, corner, (((0,), (0,)), ((), ())), precision=HIGH, preferred_element_type=F32
    )
    slab_pass(1, 1)
    cot_gather[1].finish()
    cot_gather[2].middle()
    scale[...] = lax.rsqrt(means + EPS)
    for i in range(2):
        wide = pl.ds(i * cols, cols)
        unit[:, wide] = raw[:, wide] * scale[:, i : i + 1]
        for h in range(cols // HEAD_DIM):
            lane = pl.ds(i * cols + h * HEAD_DIM, HEAD_DIM)
            own = pl.ds(pl.multiple_of(f * cols + h * HEAD_DIM, HEAD_DIM), HEAD_DIM)
            values = unit[:, lane] * gains[1 + i : 2 + i, own]
            values = values * turn[0] - pltpu.roll(values, HEAD_DIM // 2, 1) * turn[1]
            qkv[i, :, pl.ds(h * HEAD_DIM, HEAD_DIM)] = values.astype(BF16)

    def head(h, carry):
        lane = pl.ds(pl.multiple_of(h * HEAD_DIM, HEAD_DIM), HEAD_DIM)
        for t in range(seq // tile):
            r = pl.ds(t * tile, tile)
            extent = (t + 1) * tile
            upto = pl.ds(0, extent)
            scores = dot(qkv[0, r, lane], qkv[1, upto, lane], ((1,), (1,))) * scaling
            q_pos = t * tile + lax.broadcasted_iota(jnp.int32, (tile, extent), 0)
            k_pos = lax.broadcasted_iota(jnp.int32, (tile, extent), 1)
            allowed = (k_pos <= q_pos) & (live[0:1, 0:extent] > 0.0)
            masked = jnp.where(allowed, scores, -1e30)
            weights = jnp.exp(masked - jnp.max(masked, axis=-1, keepdims=True))
            weights = jnp.where(allowed, weights, 0.0)
            probs = weights / jnp.sum(weights, axis=-1, keepdims=True)
            att_v[f, r, lane] = dot(
                probs.astype(BF16), qkv[2, upto, lane], ((1,), (0,))
            ).astype(BF16)
        return carry

    lax.fori_loop(0, cols // HEAD_DIM, head, 0)
    attended_gather.start()
    slab_pass(1, 2)
    attended_gather.middle()
    cot_gather[2].finish()
    slab_pass(1, 3)
    attended_gather.finish()
    attended_gather.wait()
    attended_store = pltpu.make_async_copy(att_v, attended, local.at[2])
    attended_store.start()

    weight_store = pltpu.make_async_copy(w_v, weight, local.at[1])
    weight_store.start()


    def project_out(i, carry):
        r = pl.ds(pl.multiple_of(i * tile, tile), tile)
        total = dot(att_v[0, r, :], w_v[pl.ds(0, cols), out_cols], ((1,), (0,)))
        for j in range(1, fsdp):
            total += dot(att_v[j, r, :], w_v[pl.ds(j * cols, cols), out_cols], ((1,), (0,)))
        cols_v[r, :] = total.astype(BF16)
        return carry

    lax.fori_loop(0, seq // tile, project_out, 0)

    def branch_copy(k):
        target = lax.rem(f + k, fsdp)
        return remote(
            cols_v.at[pl.ds(pl.multiple_of(target * rows, rows), rows)],
            rows_v.at[f],
            b_send.at[k],
            b_recv.at[k],
            {"fsdp": target},
        )

    for k in range(1, fsdp):
        branch_copy(k).start()
    rows_v[f] = cols_v[pl.ds(pl.multiple_of(f * rows, rows), rows), :]
    for k in range(1, fsdp):
        branch_copy(k).wait()
    for i in range(fsdp):
        branch[:, pl.ds(i * cols, cols)] = rows_v[i]

    for s in range(dp):
        cot_gather[s].wait()
        cot_gather[s].settle()
    hidden_gather.settle()
    attended_gather.settle()
    for i in range(1, dp):
        cot_copy(i).wait_send()

    slab_settle(0)
    slab_settle(1)
    for k in range(1, fsdp):
        weight_copy(k).wait_send()
        stat_copy(k).wait_send()
        outer_copy(k).wait()
    for k in range(1, n):
        for copy in inner_copies(k):
            copy.wait()
    for copy in owns:
        copy.wait()
    normed_store.wait()
    weight_store.wait()
    attended_store.wait()


def attention_forward(
    hidden, cot, weight_in, inner_in, outer_in, small, turn, live, ident
):
    dp = lax.axis_size("dp")
    fsdp = lax.axis_size("fsdp")
    n = dp * fsdp
    rows, width = hidden.shape
    seq = rows * fsdp
    cols = width // fsdp
    shape = jax.ShapeDtypeStruct
    dma = pltpu.SemaphoreType.DMA
    vmem = pltpu.VMEM
    anywhere = pl.BlockSpec(memory_space=pl.ANY)
    inside = pl.BlockSpec(memory_space=pltpu.VMEM)
    sems = [dma((n,)), dma((n,)), dma((fsdp,)), dma((fsdp,))] + [dma((2, dp + 1))] * 4
    for size in (10, fsdp, 10, fsdp):
        sems += [dma((size,)), dma((size,))]
    sems += [dma((dp, 10)), dma((dp, 10)), dma((dp,)), dma((dp,))]
    sems += [dma((n, 2)), dma((n, 2)), dma((fsdp,)), dma((fsdp,))]
    experts = inner_in.shape[1]
    out_rows = outer_in.shape[0]
    here = experts // fsdp
    return pl.pallas_call(
        functools.partial(attention_kernel, dp, fsdp),
        out_shape=(
            shape((small.shape[0], width), F32),
            shape((rows, width), BF16),
            shape((3, seq, cols), BF16),
            shape((seq, 2 * cols), F32),
            shape((seq, 128), F32),
            shape((seq, width), BF16),
            shape((width, 4 * cols), BF16),
            shape((fsdp, seq, cols), BF16),
            shape((dp, fsdp, rows, width), BF16),
            shape((n, 2 * here, width // n, width // 2 // dp), BF16),
            shape((fsdp, here, out_rows, width), BF16),
        ),
        in_specs=[anywhere] * 5 + [inside] * 3,
        out_specs=(inside,) * 5 + (anywhere,) * 6,
        scratch_shapes=[
            vmem((fsdp, rows, width), BF16),
            vmem((n,) + small.shape, BF16),
            vmem((seq, width), BF16),
            vmem((width, 4 * cols), BF16),
            vmem((seq, 2 * cols), F32),
            vmem((8, seq), F32),
            vmem((fsdp, 8, seq), F32),
            vmem((fsdp, seq, cols), BF16),
            vmem((seq, cols), BF16),
            vmem((fsdp, rows, cols), BF16),
            vmem((width // n * experts, width), BF16),
            vmem((experts, width // n, width), BF16),
            vmem((out_rows * experts, width), BF16),
            vmem((experts, out_rows, width), BF16),
            dma((6,)),
            *sems,
        ],
        compiler_params=pltpu.CompilerParams(
            collective_id=ident, has_side_effects=True, vmem_limit_bytes=63 * 1024 * 1024
        ),
    )(
        hidden,
        cot,
        weight_in,
        inner_in.reshape(-1, width),
        outer_in.reshape(-1, width),
        small,
        turn,
        live,
    )


def attention_back_kernel(
    dp,
    fsdp,
    grad_rows,
    attended,
    weight,
    normed,
    qkv,
    unit,
    scale,
    gains,
    turn,
    live,
    grad_middle,
    hidden,
    terms,
    first_in,
    inner_in,
    outer_in,
    hidden_grad,
    terms_out,
    owned,
    inner_owned,
    outer_owned,
    inner_out,
    outer_out,
    att_v,
    w_v,
    normed_v,
    gcols,
    part1,
    held1,
    core1,
    half1,
    full1,
    part2,
    held2,
    core2,
    half2,
    full2,
    gatt,
    gval,
    gqk,
    gqkv,
    stat,
    stat_in,
    wgrad,
    z_in,
    term_v,
    term_in,
    local,
    v_send,
    v_recv,
    in_send,
    in_recv,
    out_send,
    out_recv,
    g_send,
    g_recv,
    s1_send,
    s1_recv,
    s2_send,
    s2_recv,
    t_send,
    t_recv,
    r_send,
    r_recv,
    l_send,
    l_recv,
    w_send,
    w_recv,
):
    n = dp * fsdp
    z = lax.axis_index("dp")
    f = lax.axis_index("fsdp")
    me = z * fsdp + f
    plane = Plane(f)
    rows, width = grad_rows.shape
    seq, cols = gcols.shape
    own_rows = width // n
    slab = fsdp * own_rows
    scaling = HEAD_DIM ** (-0.5)
    greet_all(n, fsdp, me)
    ff = width // 2
    ff_here = ff // dp

    inner_place = inner_out.at[f, :, pl.ds(pl.multiple_of(z * ff_here, ff_here), ff_here)]

    pair = outer_in.shape[1]
    outer_place = outer_out.at[f // 2, pl.ds(pl.multiple_of(lax.rem(f, 2) * pair, pair), pair)]

    loads = [
        pltpu.make_async_copy(attended, att_v, local.at[0]),
        pltpu.make_async_copy(weight, w_v, local.at[1]),
        pltpu.make_async_copy(normed, normed_v, local.at[2]),
        pltpu.make_async_copy(
            grad_rows.at[:, pl.ds(pl.multiple_of(f * cols, cols), cols)],
            gcols.at[pl.ds(pl.multiple_of(f * rows, rows), rows)],
            local.at[3],
        ),
    ]
    keeps = [
        pltpu.make_async_copy(inner_in.at[me], inner_place, local.at[4]),
        pltpu.make_async_copy(outer_in.at[f], outer_place, local.at[6]),
    ]
    for copy in loads:
        copy.start()

    def cols_copy(k):
        target = lax.rem(f + k, fsdp)
        return remote(
            grad_rows.at[:, pl.ds(pl.multiple_of(target * cols, cols), cols)],
            gcols.at[pl.ds(pl.multiple_of(f * rows, rows), rows)],
            g_send.at[k],
            g_recv.at[k],
            {"fsdp": target},
        )

    def inner_copy(k):
        target = spread(z, f, dp, fsdp, k)
        return remote(
            inner_in.at[target],
            inner_place,
            in_send.at[k],
            in_recv.at[k],
            place(BOTH, fsdp, target),
        )

    def outer_copy(k):
        target = lax.rem(f + k, fsdp)
        return remote(
            outer_in.at[target], outer_place, out_send.at[k], out_recv.at[k], {"fsdp": target}
        )

    def slab_rows(p):
        return pl.ds(pl.multiple_of(p * slab, slab), slab)

    def right_copy(part, d):
        lanes = parts[part]
        return remote(
            wgrad.at[slab_rows(z + d), lanes],
            z_in.at[z + d, :, lanes],
            r_send.at[part, d],
            r_recv.at[part, d - 1],
            {"dp": z + 1},
        )

    def left_copy(part, d):
        lanes = parts[part]
        return remote(
            wgrad.at[slab_rows(z - d), lanes],
            z_in.at[dp if d == 1 else z - d, :, lanes],
            l_send.at[part, d],
            l_recv.at[part, d - 1],
            {"dp": z - 1},
        )

    def arrived(part, slot, sem):
        lanes = parts[part]
        ref = z_in.at[slot, :, lanes]
        remote(ref, ref, sem, sem, plane.to_x).wait_recv()

    def pass_along(part, d):
        lanes = parts[part]

        def add(p):
            block = slab_rows(p)
            wgrad[block, lanes] = (
                wgrad[block, lanes].astype(F32) + z_in[p, :, lanes].astype(F32)
            ).astype(BF16)

        @pl.when(z + d < dp)
        def _():
            @pl.when(z > 0)
            def _():
                arrived(part, z + d, r_recv.at[part, d])
                add(z + d)

            right_copy(part, d).start()

        @pl.when(z >= d)
        def _():
            @pl.when(z < dp - 1)
            def _():
                arrived(part, z - d, l_recv.at[part, d])
                add(z - d)

            left_copy(part, d).start()

    qkv_cols = pl.ds(0, 3 * cols)
    out_cols = pl.ds(3 * cols, cols)
    parts = (pl.ds(0, 2 * cols), out_cols, pl.ds(2 * cols, cols))

    for k in range(1, fsdp):
        cols_copy(k).start()
    for k in range(1, n):
        inner_copy(k).start()
    for k in range(1, fsdp):
        outer_copy(k).start()
    for copy in keeps:
        copy.start()
    term_v[...] = terms[...]
    for copy in loads:
        copy.wait()
    for k in range(1, fsdp):
        cols_copy(k).wait_recv()

    def attended_back(i, carry):
        block = pl.ds(pl.multiple_of(i * cols, cols), cols)
        part1[i] = dot(gcols[...], w_v[block, out_cols], ((1,), (1,))).astype(BF16)
        return carry

    lax.fori_loop(0, fsdp, attended_back, 0)
    sum1 = PlaneSum(plane, part1, held1, core1, half1, full1, s1_send, s1_recv)
    sum1.start()

    def out_grads(i, carry):
        block = pl.ds(pl.multiple_of(i * cols, cols), cols)
        wgrad[block, out_cols] = dot(att_v[i], gcols[...], ((0,), (0,))).astype(BF16)
        return carry

    lax.fori_loop(0, fsdp // 2, out_grads, 0)
    sum1.add_core()
    lax.fori_loop(fsdp // 2, fsdp, out_grads, 0)
    sum1.pass_on()
    pass_along(1, 3)
    gqk[...] = jnp.zeros_like(gqk)
    gval[...] = jnp.zeros_like(gval)
    gatt[...] = sum1.total().astype(BF16)

    tile = 256

    def head(h, carry):
        lane = pl.ds(pl.multiple_of(h * HEAD_DIM, HEAD_DIM), HEAD_DIM)
        key_lane = pl.ds(pl.multiple_of(cols + h * HEAD_DIM, HEAD_DIM), HEAD_DIM)
        for t in range(seq // tile):
            r = pl.ds(t * tile, tile)
            extent = (t + 1) * tile
            upto = pl.ds(0, extent)
            query = qkv[0, r, lane]
            key = qkv[1, upto, lane]
            value = qkv[2, upto, lane]
            grad = gatt[r, lane]
            scores = dot(query, key, ((1,), (1,))) * scaling
            q_pos = t * tile + lax.broadcasted_iota(jnp.int32, (tile, extent), 0)
            k_pos = lax.broadcasted_iota(jnp.int32, (tile, extent), 1)
            allowed = (k_pos <= q_pos) & (live[0:1, 0:extent] > 0.0)
            masked = jnp.where(allowed, scores, -1e30)
            weights = jnp.exp(masked - jnp.max(masked, axis=-1, keepdims=True))
            weights = jnp.where(allowed, weights, 0.0)
            probs = weights / jnp.sum(weights, axis=-1, keepdims=True)
            grad_probs = dot(grad, value, ((1,), (1,)))
            mean = jnp.sum(probs * grad_probs, axis=-1, keepdims=True)
            grad_scores = (probs * (grad_probs - mean)).astype(BF16)
            gqk[r, lane] = dot(grad_scores, key, ((1,), (0,)))
            gqk[upto, key_lane] += dot(grad_scores, query, ((0,), (0,)))
            gval[upto, lane] += dot(probs.astype(BF16), grad, ((0,), (0,)))
        return carry

    lax.fori_loop(0, cols // HEAD_DIM, head, 0)

    def column_grads(part):
        lanes = parts[part]

        def one(i, carry):
            block = pl.ds(pl.multiple_of(i * 256, 256), 256)
            wgrad[block, lanes] = dot(normed_v[:, block], gqkv[:, lanes], ((0,), (0,))).astype(BF16)
            return carry

        lax.fori_loop(0, width // 256, one, 0)

    gqkv[:, parts[2]] = gval[...].astype(BF16)
    column_grads(2)
    pass_along(1, 2)
    pass_along(2, 3)

    heads_here = cols // HEAD_DIM
    for i in range(2):
        for h in range(heads_here):
            wide = pl.ds(i * cols + h * HEAD_DIM, HEAD_DIM)
            grad = gqk[:, wide] * scaling
            grad = grad * turn[0] + pltpu.roll(grad, HEAD_DIM // 2, 1) * turn[1]
            place_lanes = pl.ds(pl.multiple_of(f * cols + h * HEAD_DIM, HEAD_DIM), HEAD_DIM)
            term_v[1 + i : 2 + i, place_lanes] = jnp.sum(
                grad * unit[:, wide], axis=0, keepdims=True
            )
            gqk[:, wide] = grad * gains[1 + i : 2 + i, place_lanes]
    row = lax.broadcasted_iota(jnp.int32, (8, 2 * cols), 0)
    lane_of = lax.broadcasted_iota(jnp.int32, (8, 2 * cols), 1)
    chooser = jnp.where(lane_of // cols == row, 1.0, 0.0).astype(F32)
    stat[...] = lax.dot_general(
        chooser,
        gqk[...] * unit[...],
        (((1,), (1,)), ((), ())),
        precision=HIGH,
        preferred_element_type=F32,
    )

    def stat_copy(k):
        return remote(
            stat, stat_in.at[f], t_send.at[k], t_recv.at[k], {"fsdp": lax.rem(f + k, fsdp)}
        )

    for k in range(1, fsdp):
        stat_copy(k).start()
    stat_in[f] = stat[...]
    pass_along(1, 1)
    pass_along(2, 2)
    for k in range(1, fsdp):
        stat_copy(k).wait_recv()
    sums = stat_in[0]
    for i in range(1, fsdp):
        sums = sums + stat_in[i]
    corner = jnp.where(
        lax.broadcasted_iota(jnp.int32, (8, 128), 0) == lax.broadcasted_iota(jnp.int32, (8, 128), 1),
        1.0 / width,
        0.0,
    ).astype(F32)
    means = lax.dot_general(
        sums, corner, (((0,), (0,)), ((), ())), precision=HIGH, preferred_element_type=F32
    )
    for i in range(2):
        wide = pl.ds(i * cols, cols)
        grad = scale[:, i : i + 1] * (gqk[:, wide] - unit[:, wide] * means[:, i : i + 1])
        gqkv[:, wide] = grad.astype(BF16)

    step = 512

    def normed_back(i, carry):
        r = pl.ds(pl.multiple_of(i * rows, rows), rows)
        for c in range(width // step):
            col = pl.ds(c * step, step)
            part2[i, :, col] = dot(gqkv[r, :], w_v[col, qkv_cols], ((1,), (1,))).astype(BF16)
        return carry

    lax.fori_loop(0, fsdp, normed_back, 0)
    sum2 = PlaneSum(plane, part2, held2, core2, half2, full2, s2_send, s2_recv)
    sum2.start()

    column_grads(0)
    pass_along(0, 3)
    sum2.add_core()
    pass_along(2, 1)
    pass_along(0, 2)
    sum2.pass_on()

    grad = sum2.total()
    pass_along(0, 1)
    values = hidden[...].astype(F32)
    scale1 = lax.rsqrt(jnp.mean(values * values, axis=-1, keepdims=True) + EPS)
    values = values * scale1
    term_v[0:1, :] = jnp.sum(grad * values, axis=0, keepdims=True)
    grad = grad * gains[0:1, :]
    grad = scale1 * (grad - values * jnp.mean(grad * values, axis=-1, keepdims=True))
    hidden_grad[...] = grad_middle[...] + grad

    def term_copy(k):
        target = lax.rem(me + k, n)
        lanes = pl.ds(pl.multiple_of(target // 2 * 128, 128), 128)
        return remote(
            term_v.at[:, lanes],
            term_in.at[me],
            v_send.at[k],
            v_recv.at[k],
            place(BOTH, fsdp, target),
        )

    for k in range(1, n):
        term_copy(k).start()
    term_in[me] = term_v[:, pl.ds(pl.multiple_of(me // 2 * 128, 128), 128)]

    for copy in keeps:
        copy.wait()
    for k in range(1, fsdp):
        outer_copy(k).wait()
    outer_load = pltpu.make_async_copy(outer_out, core2, local.at[0])
    outer_load.start()
    for k in range(1, n):
        inner_copy(k).wait()
    inner_loads = [
        pltpu.make_async_copy(first_in, part2.at[:, :, pl.ds(0, ff)], local.at[1]),
        pltpu.make_async_copy(inner_out, part2.at[:, :, pl.ds(ff, ff)], local.at[2]),
    ]
    for copy in inner_loads:
        copy.start()
    experts = fsdp * (inner_in.shape[1] // own_rows)
    outer_load.wait()
    outer_rows = core2.shape[0] * core2.shape[1]
    inner_rows = part2.shape[0] * part2.shape[1]

    def put_outer(i, tile, lanes, value):
        block = tile // rows
        held2[pl.ds(i * block, block), :, lanes] = value.reshape(block, rows, -1)

    reorder(
        lambda lanes: core2[:, :, lanes].reshape(outer_rows, -1),
        put_outer,
        experts,
        outer_rows // experts,
    )
    for copy in inner_loads:
        copy.wait()

    def put_inner(i, tile, lanes, value):
        normed_v[pl.ds(pl.multiple_of(i * tile, tile), tile), lanes] = value

    reorder(
        lambda lanes: part2[:, :, lanes].reshape(inner_rows, -1),
        put_inner,
        experts,
        inner_rows // experts,
    )
    stores = [
        pltpu.make_async_copy(held2, outer_owned, local.at[0]),
        pltpu.make_async_copy(normed_v, inner_owned, local.at[1]),
    ]
    for store in stores:
        store.start()

    @pl.when(z > 0)
    def _():
        for part in range(3):
            arrived(part, z, r_recv.at[part, 0])
        total = wgrad[slab_rows(z), :].astype(F32) + z_in[z].astype(F32)
        wgrad[slab_rows(z), :] = total.astype(BF16)

    @pl.when(z < dp - 1)
    def _():
        for part in range(3):
            arrived(part, dp, l_recv.at[part, 0])
        total = wgrad[slab_rows(z), :].astype(F32) + z_in[dp].astype(F32)
        wgrad[slab_rows(z), :] = total.astype(BF16)

    for part in range(3):
        for d in range(1, dp):

            @pl.when(z + d < dp)
            def _(part=part, d=d):
                right_copy(part, d).wait_send()

            @pl.when(z >= d)
            def _(part=part, d=d):
                left_copy(part, d).wait_send()

    def owner_rows(target):
        return wgrad.at[pl.ds(pl.multiple_of(z * slab + target * own_rows, own_rows), own_rows)]

    def owner_copy(k):
        target = lax.rem(f + k, fsdp)
        return remote(
            owner_rows(target), owned.at[f], w_send.at[k], w_recv.at[k], {"fsdp": target}
        )

    for k in range(1, fsdp):
        owner_copy(k).start()
    own_block = pl.multiple_of(z * slab + f * own_rows, own_rows)
    owned[f] = wgrad[pl.ds(own_block, own_rows), :]
    for k in range(1, fsdp):
        owner_copy(k).wait()
    for k in range(1, fsdp):
        cols_copy(k).wait_send()
        stat_copy(k).wait_send()
    for k in range(1, n):
        term_copy(k).wait()
    total = term_in[0]
    for i in range(1, n):
        total += term_in[i]
    terms_out[...] = total
    for store in stores:
        store.wait()


def attention_back(
    grad_rows,
    attended,
    weight,
    normed,
    qkv,
    unit,
    scale,
    gains,
    turn,
    live,
    grad_middle,
    hidden,
    terms,
    first_in,
    inner_in,
    outer_in,
    ident,
):
    dp = lax.axis_size("dp")
    fsdp = lax.axis_size("fsdp")
    n = dp * fsdp
    rows, width = grad_rows.shape
    seq = rows * fsdp
    cols = width // fsdp
    own_rows = width // n
    shape = jax.ShapeDtypeStruct
    dma = pltpu.SemaphoreType.DMA
    vmem = pltpu.VMEM
    anywhere = pl.BlockSpec(memory_space=pl.ANY)
    inside = pl.BlockSpec(memory_space=pltpu.VMEM)
    return pl.pallas_call(
        functools.partial(attention_back_kernel, dp, fsdp),
        out_shape=(
            shape((rows, width), F32),
            shape((terms.shape[0], 128), F32),
            shape((fsdp, own_rows, 4 * cols), BF16),
            shape((seq, width), BF16),
            shape((4, rows, width), BF16),
            shape((fsdp, rows, width // 2), BF16),
            shape((4, rows, width), BF16),
        ),
        in_specs=[anywhere] * 4 + [inside] * 9 + [anywhere] * 3,
        out_specs=(inside,) * 3 + (anywhere,) * 4,
        scratch_shapes=[
            vmem((fsdp, seq, cols), BF16),
            vmem((width, 4 * cols), BF16),
            vmem((seq, width), BF16),
            vmem((seq, cols), BF16),
            vmem((fsdp, seq, cols), BF16),
            vmem((4, seq, cols), BF16),
            vmem((4, seq, cols), BF16),
            vmem((2, seq // 2, cols), BF16),
            vmem((2, seq, cols), BF16),
            vmem((fsdp, rows, width), BF16),
            vmem((4, rows, width), BF16),
            vmem((4, rows, width), BF16),
            vmem((2, rows // 2, width), BF16),
            vmem((2, rows, width), BF16),
            vmem((seq, cols), BF16),
            vmem((seq, cols), F32),
            vmem((seq, 2 * cols), F32),
            vmem((seq, 3 * cols), BF16),
            vmem((8, seq), F32),
            vmem((fsdp, 8, seq), F32),
            vmem((width, 4 * cols), BF16),
            vmem((dp + 1, fsdp * own_rows, 4 * cols), BF16),
            vmem(terms.shape, F32),
            vmem((n, terms.shape[0], 128), F32),
            dma((7,)),
            dma((n,)),
            dma((n,)),
            dma((n,)),
            dma((n,)),
            dma((fsdp,)),
            dma((fsdp,)),
            dma((fsdp,)),
            dma((fsdp,)),
            dma((8,)),
            dma((8,)),
            dma((8,)),
            dma((8,)),
            dma((fsdp,)),
            dma((fsdp,)),
            dma((3, dp)),
            dma((3, dp)),
            dma((3, dp)),
            dma((3, dp)),
            dma((fsdp,)),
            dma((fsdp,)),
        ],
        compiler_params=pltpu.CompilerParams(
            collective_id=ident, has_side_effects=True, vmem_limit_bytes=63 * 1024 * 1024
        ),
    )(
        grad_rows,
        attended,
        weight,
        normed,
        qkv,
        unit,
        scale,
        gains,
        turn,
        live,
        grad_middle,
        hidden,
        terms,
        first_in,
        inner_in,
        outer_in,
    )


def expert_kernel(
    dp,
    fsdp,
    x_in,
    c_all,
    gates,
    inner_in,
    outer_in,
    sums,
    gate_sum,
    first_out,
    inner_out,
    outer_out,
    gathered,
    far,
    xv,
    cv,
    wi,
    wo,
    gi,
    go,
    ggu,
    act,
    gv,
    part,
    held,
    core_in,
    half_in,
    full_in,
    leaving,
    gates_in,
    grads_out,
    grads_in,
    local,
    g_send,
    g_recv,
    gg_send,
    gg_recv,
    f_send,
    f_recv,
    z_send,
    z_recv,
    a_send,
    a_recv,
    b_send,
    b_recv,
    k_send,
    k_recv,
    c_send,
    c_recv,
    s1_send,
    s1_recv,
    s2_send,
    s2_recv,
    o_send,
    o_recv,
    credit,
):
    rows, width = x_in.shape
    half = rows // 2
    z = lax.axis_index("dp")
    f = lax.axis_index("fsdp")
    core = lax.rem(f, 2)
    chip = f // 2
    xbit = lax.rem(chip, 2)
    ybit = chip // 2
    chip_x = ybit * 2 + (1 - xbit)
    chip_y = (1 - ybit) * 2 + xbit
    chip_d = (1 - ybit) * 2 + (1 - xbit)
    fx = chip_x * 2 + core
    fy = chip_y * 2 + core
    fd = chip_d * 2 + core
    fc = chip * 2 + (1 - core)
    to_x = {"fsdp": fx}
    to_y = {"fsdp": fy}
    to_c = {"fsdp": fc}
    upper = pl.ds(0, half)
    lower = pl.ds(half, half)

    def remote(src, dst, send, recv, device):
        return pltpu.make_async_remote_copy(
            src, dst, send, recv, device_id=device, device_id_type=MESH_ID
        )

    def plane_at(s):
        return lax.rem(z + 1 + s, dp)

    def far_copy(i):
        return remote(
            x_in,
            gathered.at[z, f],
            z_send.at[i],
            z_recv.at[i],
            {"dp": lax.rem(z + dp - i, dp)},
        )

    def gather_one(s):
        block = gathered.at[plane_at(s), f]
        return (
            remote(block.at[upper], block.at[upper], a_send.at[s, 0], a_recv.at[s, 0], to_x),
            remote(block.at[lower], block.at[lower], a_send.at[s, 1], a_recv.at[s, 1], to_y),
        )

    def gather_two(s):
        p = plane_at(s)
        copies = []
        for i, (owner, piece, device) in enumerate(
            ((f, upper, to_y), (fx, upper, to_y), (f, lower, to_x), (fy, lower, to_x))
        ):
            ref = gathered.at[p, owner, piece]
            copies.append(remote(ref, ref, b_send.at[s, i], b_recv.at[s, i], device))
        return copies

    def gather_core(s):
        p = plane_at(s)
        copies = []
        for i, owner in enumerate((f, fx, fy, fd)):
            ref = gathered.at[p, owner]
            copies.append(remote(ref, ref, k_send.at[s, i], k_recv.at[s, i], to_c))
        return copies

    def block_rows(owner):
        return pl.ds(pl.multiple_of(owner * rows, rows), rows)

    def core_copy(k, j):
        return remote(
            part.at[k, block_rows(j * 2 + 1 - core)],
            core_in.at[k, j],
            c_send.at[k, j],
            c_recv.at[k, j],
            to_c,
        )

    def half_copies(k):
        return (
            remote(
                held.at[k, chip_d, upper], half_in.at[k, 0], s1_send.at[k, 0], s1_recv.at[k, 0], to_x
            ),
            remote(
                held.at[k, chip_d, lower], half_in.at[k, 1], s1_send.at[k, 1], s1_recv.at[k, 1], to_y
            ),
        )

    def full_copies(k):
        return (
            remote(held.at[k, chip_x], full_in.at[k, 0], s2_send.at[k, 0], s2_recv.at[k, 0], to_x),
            remote(held.at[k, chip_y], full_in.at[k, 1], s2_send.at[k, 1], s2_recv.at[k, 1], to_y),
        )

    def out_copy(s, k):
        return remote(
            leaving.at[lax.rem(s, 2), k],
            far.at[k, z],
            o_send.at[s, k],
            o_recv.at[s, k],
            {"dp": plane_at(s)},
        )

    def add_core():
        def add_block(k, j):
            core_copy(k, j).wait()
            held[k, j] = (
                part[k, block_rows(j * 2 + core)].astype(F32) + core_in[k, j].astype(F32)
            ).astype(BF16)

        for k in range(2):
            add_block(k, chip_d)
            for copy in half_copies(k):
                copy.start()
        for k in range(2):
            for j in (chip_x, chip_y, chip):
                add_block(k, j)
        pl.semaphore_signal(credit, inc=1, device_id=to_c, device_id_type=MESH_ID)

    def pass_full():
        for k in range(2):
            for copy in half_copies(k):
                copy.wait()
            held[k, chip_y, upper] = (
                held[k, chip_y, upper].astype(F32) + half_in[k, 0].astype(F32)
            ).astype(BF16)
            held[k, chip_x, lower] = (
                held[k, chip_x, lower].astype(F32) + half_in[k, 1].astype(F32)
            ).astype(BF16)
            for copy in full_copies(k):
                copy.start()

    def total_here(k):
        for copy in full_copies(k):
            copy.wait()
        return held[k, chip].astype(F32) + full_in[k, 0].astype(F32) + full_in[k, 1].astype(F32)

    n = dp * fsdp
    me = z * fsdp + f
    greet_all(n, fsdp, me)

    def gate_copy(k):
        target = lax.rem(me + k, n)
        return remote(
            gates.at[target],
            gates_in.at[me],
            g_send.at[k],
            g_recv.at[k],
            place(BOTH, fsdp, target),
        )

    def gate_grad_copy(k):
        target = lax.rem(me + k, n)
        return remote(
            grads_out.at[target],
            grads_in.at[me],
            gg_send.at[k],
            gg_recv.at[k],
            place(BOTH, fsdp, target),
        )

    own_rows = wi.shape[2]
    first_lanes = pl.ds(pl.multiple_of(z * wi.shape[3], wi.shape[3]), wi.shape[3])

    def first_ref(e):
        return first_out.at[f, pl.ds(e * own_rows, own_rows), first_lanes]

    def first_copy(k, e):
        target = spread(z, f, dp, fsdp, k)
        return remote(
            wi.at[e, target],
            first_ref(e),
            f_send.at[k, e],
            f_recv.at[k, e],
            place(BOTH, fsdp, target),
        )

    far_copy(1).start()
    for k in range(1, n):
        gate_copy(k).start()
    loads = [pltpu.make_async_copy(x_in, gathered.at[z, f], local.at[0])]
    for q in range(4):
        loads.append(pltpu.make_async_copy(inner_in.at[:, q], wi.at[q], local.at[1 + q]))
    for e in range(2):
        loads.append(pltpu.make_async_copy(outer_in.at[:, e], wo.at[e], local.at[5 + e]))
    loads.append(pltpu.make_async_copy(gates.at[me], gates_in.at[me], local.at[7]))
    for load in loads:
        load.start()
    gi[...] = jnp.zeros_like(gi)
    go[...] = jnp.zeros_like(go)
    for load in loads:
        load.wait()

    def begin_gather(s):
        @pl.when(s < dp - 1)
        def _():
            far_copy(s + 1).wait_recv()

        for copy in gather_one(s):
            copy.start()

    def middle_gather(s):
        for copy in gather_one(s):
            copy.wait_recv()
        for copy in gather_two(s):
            copy.start()

    def end_gather(s):
        for copy in gather_two(s):
            copy.wait_recv()
        for copy in gather_core(s):
            copy.start()

    begin_gather(0)
    for i in range(2, dp):
        far_copy(i).start()
    middle_gather(0)
    end_gather(0)
    begin_gather(1)
    for k in range(1, n):
        gate_copy(k).wait()

    inner_rows = wi.shape[1] * wi.shape[2]
    ff_here = wo.shape[1] * wo.shape[2]
    tile = xv.shape[0] // 2

    def tile_step(t):
        r = pl.ds(pl.multiple_of(t * tile, tile), tile)
        x = xv[r, :]
        c = cv[r, :]
        for e in range(2):
            gate = dot(x, wi[e].reshape(inner_rows, ff_here), ((1,), (0,)))
            up = dot(x, wi[2 + e].reshape(inner_rows, ff_here), ((1,), (0,)))
            back = dot(c, wo[e].reshape(ff_here, width), ((1,), (1,)))
            sigmoid = 1.0 / (1.0 + jnp.exp(-gate))
            silu = gate * sigmoid
            active = (silu * up).astype(BF16).astype(F32)
            weight = gv[r, e : e + 1]
            gv[r, 8 + e : 9 + e] = jnp.sum(active * back, axis=-1, keepdims=True)
            act[e, r, :] = (weight * active).astype(BF16)
            back = weight * back
            ggu[e, r, :] = (back * up * sigmoid * (1.0 + gate * (1.0 - sigmoid))).astype(BF16)
            ggu[2 + e, r, :] = (back * silu).astype(BF16)
        step = 512
        for i in range(width // step):
            col = pl.ds(i * step, step)
            blocks = pl.ds(i * step // wi.shape[2], step // wi.shape[2])
            total = dot(act[0, r, :], wo[0, :, :, col].reshape(ff_here, step), ((1,), (0,)))
            total += dot(act[1, r, :], wo[1, :, :, col].reshape(ff_here, step), ((1,), (0,)))
            part[0, r, col] = total.astype(BF16)
            total = dot(ggu[0, r, :], wi[0, blocks].reshape(step, ff_here), ((1,), (1,)))
            for q in range(1, 4):
                total += dot(ggu[q, r, :], wi[q, blocks].reshape(step, ff_here), ((1,), (1,)))
            part[1, r, col] = total.astype(BF16)

    def weight_step():
        def inner_part(i, carry):
            col = pl.ds(pl.multiple_of(i * 256, 256), 256)
            xt = xv[:, col]
            for q in range(4):
                gi[q, col, :] += dot(xt, ggu[q], ((0,), (0,)))
            return carry

        lax.fori_loop(0, width // 256, inner_part, 0)

        def outer_part(i, carry):
            col = pl.ds(pl.multiple_of(i * 512, 512), 512)
            ct = cv[:, col]
            for e in range(2):
                go[e, :, col] += dot(act[e], ct, ((0,), (0,)))
            return carry

        lax.fori_loop(0, width // 512, outer_part, 0)

    def chunk(s, carry):
        p = plane_at(s)
        c_load = pltpu.make_async_copy(c_all.at[p], cv, local.at[1])
        c_load.start()

        def to_columns(j, carry):
            r = pl.ds(pl.multiple_of(j * rows, rows), rows)
            gv[r, :] = exact_dot(gates_in[p * fsdp + j], corner_of(8, 0, 1.0), ((0,), (0,)))
            return carry

        lax.fori_loop(0, fsdp, to_columns, 0)
        for copy in gather_core(s):
            copy.wait_recv()
        for j in range(8):
            pltpu.make_async_copy(
                gathered.at[p, j], xv.at[pl.ds(j * rows, rows)], local.at[3 + j]
            ).start()
        c_load.wait()
        for j in range(8):
            pltpu.make_async_copy(
                gathered.at[p, j], xv.at[pl.ds(j * rows, rows)], local.at[3 + j]
            ).wait()
        @pl.when(s < dp - 1)
        def _():
            middle_gather(s + 1)

        tile_step(0)

        @pl.when(s > 0)
        def _():
            pass_full()

        @pl.when(s < dp - 2)
        def _():
            begin_gather(s + 2)

        tile_step(1)

        @pl.when(s > 0)
        def _():
            pl.semaphore_wait(credit, 1)

        for k in range(2):
            for j in range(4):
                core_copy(k, j).start()
        def to_rows(j, carry):
            r = pl.ds(pl.multiple_of(j * rows, rows), rows)
            grads_out[p * fsdp + j] = exact_dot(corner_of(8, 8, 1.0), gv[r, :], ((1,), (1,)))
            return carry

        lax.fori_loop(0, fsdp, to_rows, 0)
        weight_step()

        @pl.when(s > 0)
        def _():
            @pl.when(s > 2)
            def _():
                for k in range(2):
                    out_copy(s - 3, k).wait_send()

            for k in range(2):
                leaving[lax.rem(s - 1, 2), k] = total_here(k).astype(BF16)
                out_copy(s - 1, k).start()

        add_core()

        @pl.when(s < dp - 1)
        def _():
            end_gather(s + 1)

        @pl.when(s == dp - 1)
        def _():
            for e in range(2):
                wi[e] = gi[e].astype(BF16).reshape(wi.shape[1:])
            for k in range(1, n):
                for e in range(2):
                    first_copy(k, e).start()

        return carry

    lax.fori_loop(0, dp, chunk, 0)

    pass_full()
    for k in range(1, n):
        gate_grad_copy(k).start()
    grads_in[me] = grads_out[me]
    for q in range(2, 4):
        wi[q] = gi[q].astype(BF16).reshape(wi.shape[1:])
    for e in range(2):
        wo[e] = go[e].astype(BF16).reshape(wo.shape[1:])
    stores = []
    for e in range(2):
        stores.append(pltpu.make_async_copy(wi.at[e, me], first_ref(e), local.at[e]))
        stores.append(pltpu.make_async_copy(wi.at[2 + e], inner_out.at[:, e], local.at[2 + e]))
    for e in range(2):
        stores.append(pltpu.make_async_copy(wo.at[e], outer_out.at[:, e], local.at[4 + e]))
    for store in stores:
        store.start()
    pl.semaphore_wait(credit, 1)
    for i in range(1, dp):
        for k in range(2):
            if i > dp - 3:
                out_copy(i - 1, k).wait_send()
            remote(
                held.at[k, chip],
                far.at[k, lax.rem(z + dp - i, dp)],
                o_send.at[i - 1, k],
                o_recv.at[i - 1, k],
                to_x,
            ).wait_recv()
    fetch = []
    for i in range(1, dp):
        for k in range(2):
            fetch.append(
                pltpu.make_async_copy(
                    far.at[k, lax.rem(z + i, dp)], core_in.at[k, i], local.at[6 + (i - 1) * 2 + k]
                )
            )
    for copy in fetch:
        copy.start()
    for copy in fetch:
        copy.wait()
    for k in range(2):
        total = total_here(k)
        for i in range(1, dp):
            total += core_in[k, i].astype(F32)
        sums[k] = total
    for k in range(1, n):
        gate_grad_copy(k).wait()
        for e in range(2):
            first_copy(k, e).wait()
    for j in range(fsdp):
        total = grads_in[j]
        for i in range(1, dp):
            total += grads_in[i * fsdp + j]
        gate_sum[j] = total
    for store in stores:
        store.wait()
    for i in range(1, dp):
        far_copy(i).wait_send()

    def settle(s, carry):
        for copy in (*gather_one(s), *gather_two(s), *gather_core(s)):
            copy.wait_send()
        return carry

    lax.fori_loop(0, dp, settle, 0)


def expert_pass(x_in, c_all, gates, inner_in, outer_in, ident):
    dp = lax.axis_size("dp")
    fsdp = lax.axis_size("fsdp")
    rows, width = x_in.shape
    n, four, own_rows, ff_here = inner_in.shape
    _, two, out_rows, _ = outer_in.shape
    chunk = fsdp * rows
    shape = jax.ShapeDtypeStruct
    dma = pltpu.SemaphoreType.DMA
    anywhere = pl.BlockSpec(memory_space=pl.ANY)
    got = pl.pallas_call(
        functools.partial(expert_kernel, dp, fsdp),
        out_shape=(
            shape((2, rows, width), F32),
            shape((fsdp, 8, 128), F32),
            shape((fsdp, 2 * own_rows, dp * ff_here), BF16),
            shape((n, 2, own_rows, ff_here), BF16),
            shape(outer_in.shape, BF16),
            shape((dp, fsdp, rows, width), BF16),
            shape((2, dp, rows, width), BF16),
        ),
        in_specs=[anywhere] * 5,
        out_specs=(pl.BlockSpec(memory_space=pltpu.VMEM),) * 2 + (anywhere,) * 5,
        scratch_shapes=[
            pltpu.VMEM((chunk, width), BF16),
            pltpu.VMEM((chunk, width), BF16),
            pltpu.VMEM((four, n, own_rows, ff_here), BF16),
            pltpu.VMEM((two, fsdp, out_rows, width), BF16),
            pltpu.VMEM((four, width, ff_here), F32),
            pltpu.VMEM((two, ff_here, width), F32),
            pltpu.VMEM((four, chunk, ff_here), BF16),
            pltpu.VMEM((two, chunk, ff_here), BF16),
            pltpu.VMEM((chunk, 128), F32),
            pltpu.VMEM((2, chunk, width), BF16),
            pltpu.VMEM((2, 4, rows, width), BF16),
            pltpu.VMEM((2, 4, rows, width), BF16),
            pltpu.VMEM((2, 2, rows // 2, width), BF16),
            pltpu.VMEM((2, 2, rows, width), BF16),
            pltpu.VMEM((2, 2, rows, width), BF16),
            pltpu.VMEM((n, 8, 128), F32),
            pltpu.VMEM((n, 8, 128), F32),
            pltpu.VMEM((n, 8, 128), F32),
            dma((12 + 2 * dp,)),
            dma((n,)),
            dma((n,)),
            dma((n,)),
            dma((n,)),
            dma((n, 2)),
            dma((n, 2)),
            dma((dp,)),
            dma((dp,)),
            dma((dp, 2)),
            dma((dp, 2)),
            dma((dp, 4)),
            dma((dp, 4)),
            dma((dp, 4)),
            dma((dp, 4)),
            dma((2, 4)),
            dma((2, 4)),
            dma((2, 2)),
            dma((2, 2)),
            dma((2, 2)),
            dma((2, 2)),
            dma((dp, 2)),
            dma((dp, 2)),
            pltpu.SemaphoreType.REGULAR,
        ],
        compiler_params=pltpu.CompilerParams(
            collective_id=ident, has_side_effects=True, vmem_limit_bytes=63 * 1024 * 1024
        ),
    )(x_in, c_all, gates, inner_in, outer_in)
    return got[:5]


def expert_pass_dense(normed2, grad_all, gates, inner_weight, outer_weight):
    n, parts, own_rows, ff_here = inner_weight.shape
    experts_here = parts // 2
    inner = experts_here * ff_here
    width = n * own_rows
    tokens = grad_all.shape[0]
    gates = gates[:, :, None]
    rows_all = lax.all_gather(normed2, BOTH, axis=0, tiled=True)
    inner_block = inner_weight.transpose(0, 2, 1, 3).reshape(width, 2 * inner)
    outer_shape = outer_weight.shape
    outer_block = outer_weight.transpose(1, 0, 2, 3).reshape(inner, width)
    gate_up = dot(rows_all, inner_block, ((1,), (0,)))
    gate = gate_up[:, :inner]
    up = gate_up[:, inner:]
    sigmoid = jax.nn.sigmoid(gate)
    silu = gate * sigmoid
    activation = (silu * up).astype(BF16).astype(F32)
    grad_act = dot(grad_all, outer_block, ((1,), (1,)))
    grad_gates = jnp.sum(
        (activation * grad_act).reshape(tokens, experts_here, ff_here), axis=-1
    )
    by_part = (tokens, experts_here, ff_here)
    activation = (activation.reshape(by_part) * gates).reshape(tokens, inner).astype(BF16)
    grad_act = (grad_act.reshape(by_part) * gates).reshape(tokens, inner)
    grad_gate_up = jnp.concatenate(
        [grad_act * up * sigmoid * (1.0 + gate * (1.0 - sigmoid)), grad_act * silu], axis=1
    ).astype(BF16)
    expert_sum = dot(activation, outer_block, ((1,), (0,))).astype(BF16)
    expert_sum = lax.psum_scatter(expert_sum, BOTH, scatter_dimension=0, tiled=True).astype(F32)
    if tokens > 8192:
        grad_gate_up, expert_sum = lax.optimization_barrier((grad_gate_up, expert_sum))
    grad_rows = dot(grad_gate_up, inner_block, ((1,), (1,))).astype(BF16)
    grad_rows = lax.psum_scatter(grad_rows, BOTH, scatter_dimension=0, tiled=True).astype(F32)
    inner_grad = dot(rows_all, grad_gate_up, ((0,), (0,))).astype(BF16)
    outer_grad = dot(activation, grad_all, ((0,), (0,))).astype(BF16)
    inner_grad = inner_grad.reshape(n, own_rows, parts, ff_here).transpose(0, 2, 1, 3)
    outer_grad = outer_grad.reshape(experts_here, outer_shape[0], outer_shape[2], width)
    return expert_sum, grad_rows, grad_gates, inner_grad, outer_grad.transpose(1, 0, 2, 3)


def body(
    hidden_in,
    lengths,
    routes,
    attn_gain,
    query_gain,
    key_gain,
    ffn_gain,
    qkv_weight,
    out_weight,
    router_weight,
    expert_in,
    expert_out,
    cotangent,
):
    rows, width = hidden_in.shape
    dp = lax.axis_size("dp")
    fsdp = lax.axis_size("fsdp")
    fused = fsdp == 8
    n = dp * fsdp
    experts = router_weight.shape[1]
    seq = rows * fsdp
    tokens = rows * n
    own_rows = width // n
    heads_here = HEADS // fsdp
    cols = heads_here * HEAD_DIM
    experts_here = experts // fsdp
    ff = expert_out.shape[0] * n
    ff_here = ff // dp
    z = lax.axis_index("dp")
    f = lax.axis_index("fsdp")
    valid = lengths[z]
    scaling = HEAD_DIM ** (-0.5)

    if fused:
        small = jnp.stack([attn_gain, query_gain, key_gain, ffn_gain])
        blank = jnp.zeros((-(4 + experts) % 16, own_rows), BF16)
        small = jnp.concatenate([small, router_weight.transpose(1, 0), blank])
        odd = lax.rem(f, 2) == 1
        zero = jnp.zeros((), BF16)
        small = jnp.concatenate(
            [jnp.where(odd, zero, small), jnp.where(odd, small, zero)], axis=1
        )
    else:
        small = jnp.concatenate(
            [attn_gain, query_gain, key_gain, ffn_gain, router_weight.reshape(-1)]
        )
        small_rows = -(-small.size // 2048) * 16
        small = exchange(tiles_of(small, small_rows), BOTH, 0, False).reshape(n, -1)
        gains = small[:, : 4 * own_rows].reshape(n, 4, own_rows).transpose(1, 0, 2)
        gains = gains.reshape(4, width).astype(F32)
        router_full = small[:, 4 * own_rows : 4 * own_rows + own_rows * experts]
        router_full = router_full.reshape(width, experts)
        gain_attn, gain_query, gain_key, gain_ffn = gains[0], gains[1], gains[2], gains[3]

    attn_weight = jnp.concatenate(
        [
            qkv_weight.reshape(own_rows, 3, fsdp, cols),
            out_weight.reshape(own_rows, 1, fsdp, cols),
        ],
        axis=1,
    )
    attn_weight = attn_weight.transpose(2, 0, 1, 3).reshape(fsdp, own_rows, 4 * cols)
    live_mask = (f * rows + jnp.arange(rows, dtype=jnp.int32) < valid).astype(F32)[:, None]
    grad_total = cotangent.astype(F32) * live_mask

    here = f * cols
    pos = jnp.arange(seq, dtype=jnp.int32)
    frequency = jnp.power(10000.0, -jnp.arange(HEAD_DIM // 2, dtype=F32) * 2.0 / HEAD_DIM)
    angles = pos.astype(F32)[:, None] * frequency[None, :]
    cosine = jnp.cos(angles)[:, None, None, :]
    sine = jnp.sin(angles)[:, None, None, :]

    if fused:
        turn = jnp.asarray(turning(seq))
        live_keys = jnp.broadcast_to((pos < valid).astype(F32)[None], (8, seq))
        (
            gains,
            branch,
            qkv,
            qk_unit,
            qk_scale,
            normed_all,
            attn_weight,
            attended_all,
            grad_all,
            inner_weight,
            outer_weight,
        ) = attention_forward(
            hidden_in,
            grad_total.astype(BF16),
            attn_weight,
            expert_in,
            expert_out,
            small,
            turn,
            live_keys,
            10,
        )
        branch = branch.astype(F32)
        gain_ffn = gains[3]
        router_full = gains[4 : 4 + experts].transpose(1, 0).astype(BF16)
    else:
        qk_gain = jnp.stack(
            [
                lax.dynamic_slice(gain_query, (here,), (cols,)),
                lax.dynamic_slice(gain_key, (here,), (cols,)),
            ]
        )
        attn_weight = lax.all_to_all(attn_weight, "fsdp", 0, 0, tiled=True)
        attn_weight = lax.all_gather(
            attn_weight.reshape(fsdp * own_rows, 4 * cols), "dp", axis=0, tiled=True
        )
        qkv_here = attn_weight[:, : 3 * cols]
        out_here = attn_weight[:, 3 * cols :]
        inner_weight = expert_in.reshape(own_rows, fsdp, experts_here, 2, dp, ff_here)
        inner_weight = inner_weight.transpose(4, 1, 3, 2, 0, 5)
        inner_weight = inner_weight.reshape(n, 2 * experts_here, own_rows, ff_here)
        outer_weight = expert_out.reshape(-1, fsdp, experts_here, width).transpose(1, 2, 0, 3)
        inner_weight = lax.all_to_all(inner_weight, BOTH, 0, 0, tiled=True)
        outer_weight = lax.all_to_all(outer_weight, "fsdp", 0, 0, tiled=True)
        hidden_all = lax.all_gather(hidden_in, "fsdp", axis=0, tiled=True).astype(F32)
        normed_all = (hidden_all * rms_scale(hidden_all) * gain_attn).astype(BF16)
        mixed = dot(normed_all, qkv_here, ((1,), (0,)))
        raw = mixed[:, : 2 * cols].reshape(seq, 2, cols)
        squares = plane_sum(jnp.sum(raw * raw, axis=-1), 1)
        qk_scale = lax.rsqrt(squares / width + EPS)[:, :, None]
        qk_unit = raw * qk_scale
        shape4 = (seq, 2, heads_here, HEAD_DIM)
        turned = rotate((qk_unit * qk_gain).reshape(shape4), cosine, sine, 1.0).astype(BF16)
        query = turned[:, 0]
        key = turned[:, 1]
        value = mixed[:, 2 * cols :].astype(BF16).reshape(seq, heads_here, HEAD_DIM)
        allowed = ((pos[None, :] <= pos[:, None]) & (pos[None, :] < valid))[None]
        scores = jnp.einsum("qhd,khd->hqk", query, key, preferred_element_type=F32) * scaling
        masked = jnp.where(allowed, scores, -1e30)
        weights = jnp.exp(masked - jnp.max(masked, axis=-1, keepdims=True))
        weights = jnp.where(allowed, weights, 0.0)
        probs = weights / jnp.sum(weights, axis=-1, keepdims=True)
        probs_low = probs.astype(BF16)
        attended = jnp.einsum("hqk,khd->qhd", probs_low, value, preferred_element_type=F32)
        attended = attended.reshape(seq, cols).astype(BF16)
        attended_all = lax.all_gather(attended, "fsdp", axis=0, tiled=False)
        branch = jnp.einsum(
            "fsc,fcn->sn",
            attended_all,
            out_here.reshape(fsdp, cols, cols),
            preferred_element_type=F32,
        )
        branch = exchange(branch.astype(BF16).reshape(fsdp, rows, cols), ("fsdp",), 2, True)
        branch = branch.transpose(1, 0, 2).reshape(rows, width).astype(F32)
        grad_all = lax.all_gather(grad_total.astype(BF16), BOTH, axis=0, tiled=True)

    hidden = hidden_in.astype(F32)
    scale1 = rms_scale(hidden)
    unit1 = hidden * scale1
    middle = hidden + branch
    scale2 = rms_scale(middle)
    unit2 = middle * scale2
    normed2 = (unit2 * gain_ffn).astype(BF16)
    logits = dot(normed2, router_full, ((1,), (0,)))
    router_probs = jax.nn.softmax(logits, axis=-1)
    chosen = jnp.sum(
        (routes[:, :, None] == jnp.arange(experts, dtype=jnp.int32)[None, None, :]).astype(F32),
        axis=1,
    )

    gates = (router_probs * chosen).reshape(rows, fsdp, experts_here).transpose(1, 2, 0)
    gates = jnp.broadcast_to(gates[None], (dp, fsdp, experts_here, rows))
    gates = gates.reshape(n, experts_here, rows)
    gates = jnp.pad(gates, ((0, 0), (0, 8 - experts_here), (0, 0)))
    if fused:
        sums, grad_gates, first_grad, inner_grad, outer_grad = expert_pass(
            normed2, grad_all.reshape(dp, seq, width), gates, inner_weight, outer_weight, 8
        )
        expert_sum = sums[0]
        grad_rows = sums[1]
        grad_gates = grad_gates[:, :experts_here]
    else:
        gates = exchange(gates, BOTH, 3, True)[:, :experts_here]
        gates = gates.transpose(0, 2, 1).reshape(tokens, experts_here)
        expert_sum, grad_rows, grad_gates, inner_grad, outer_grad = expert_pass_dense(
            normed2, grad_all, gates, inner_weight, outer_weight
        )
        grad_gates = grad_gates.reshape(n, rows, experts_here).transpose(0, 2, 1)
        grad_gates = jnp.pad(grad_gates, ((0, 0), (0, 8 - experts_here), (0, 0)))
        grad_gates = exchange(grad_gates, BOTH, 4, True)[:, :experts_here]
        grad_gates = jnp.sum(grad_gates.reshape(dp, fsdp, experts_here, rows), axis=0)
    grad_router_probs = grad_gates.reshape(experts, rows).transpose(1, 0) * chosen

    block_total = middle + expert_sum
    squares = jnp.stack(
        [
            jnp.sum(live_mask * block_total * block_total),
            jnp.sum(live_mask * branch * branch),
            jnp.sum(live_mask * expert_sum * expert_sum),
        ]
    )

    grad_logits = router_probs * (
        grad_router_probs - jnp.sum(router_probs * grad_router_probs, axis=-1, keepdims=True)
    )
    grad_logits = grad_logits.astype(BF16)
    grad_normed2 = grad_rows + dot(grad_logits, router_full, ((1,), (1,)))
    ffn_term = jnp.sum(grad_normed2 * unit2, axis=0)
    grad_middle = grad_total + norm_back(grad_normed2 * gain_ffn, unit2, scale2)

    if fused:
        terms = jnp.concatenate(
            [
                jnp.zeros((3, width), F32),
                ffn_term[None],
                jnp.broadcast_to(squares[:, None], (3, width)),
                jnp.zeros((1, width), F32),
                dot(grad_logits, normed2, ((0,), (0,))),
            ]
        )
        hidden_grad, terms, attn_grad, inner_grad, outer_grad, _, _ = attention_back(
            grad_middle.astype(BF16),
            attended_all,
            attn_weight,
            normed_all,
            qkv,
            qk_unit,
            qk_scale,
            gains,
            turn,
            live_keys,
            grad_middle,
            hidden_in,
            terms,
            first_grad,
            inner_grad.reshape(n, experts_here * own_rows, ff_here),
            outer_grad.reshape(fsdp, -1, width),
            9,
        )
        inner_grad = inner_grad.reshape(own_rows, experts, 2 * ff)
        outer_grad = outer_grad.reshape(-1, experts, width)
        terms = lax.dynamic_slice(terms, (0, lax.rem(f, 2) * own_rows), (terms.shape[0], own_rows))
        gain_grads = terms[:4]
        router_grad = terms[8:].transpose(1, 0)
        square_sums = terms[4:7, 0]
    else:
        grad_cols = grad_middle.astype(BF16).reshape(rows, fsdp, cols).transpose(1, 0, 2)
        grad_cols = exchange(grad_cols, ("fsdp",), 5, True).reshape(seq, cols)
        out_grad = jnp.einsum("fsc,sn->fcn", attended_all, grad_cols, preferred_element_type=F32)
        grad_attended = jnp.einsum(
            "sn,fcn->fsc", grad_cols, out_here.reshape(fsdp, cols, cols), preferred_element_type=F32
        )
        grad_attended = lax.psum_scatter(
            grad_attended.astype(BF16).reshape(fsdp * seq, cols), "fsdp", scatter_dimension=0, tiled=True
        )
        grad_attended = grad_attended.reshape(seq, heads_here, HEAD_DIM)
        grad_probs = jnp.einsum("qhd,khd->hqk", grad_attended, value, preferred_element_type=F32)
        grad_scores = probs * (grad_probs - jnp.sum(probs * grad_probs, axis=-1, keepdims=True))
        grad_scores = grad_scores.astype(BF16)
        grad_query = jnp.einsum("hqk,khd->qhd", grad_scores, key, preferred_element_type=F32)
        grad_key = jnp.einsum("hqk,qhd->khd", grad_scores, query, preferred_element_type=F32)
        grad_value = jnp.einsum("hqk,qhd->khd", probs_low, grad_attended, preferred_element_type=F32)
        grad_qk = rotate(jnp.stack([grad_query, grad_key], axis=1) * scaling, cosine, sine, -1.0)
        grad_qk = grad_qk.reshape(seq, 2, cols)
        qk_term = jnp.sum(grad_qk * qk_unit, axis=0)
        grad_qk = grad_qk * qk_gain
        inner_means = plane_sum(jnp.sum(grad_qk * qk_unit, axis=-1), 6)[:, :, None] / width
        grad_qk = qk_scale * (grad_qk - qk_unit * inner_means)
        grad_qkv = jnp.concatenate(
            [grad_qk.reshape(seq, 2 * cols), grad_value.reshape(seq, cols)], axis=1
        ).astype(BF16)
        qkv_grad = dot(normed_all, grad_qkv, ((0,), (0,)))
        grad_normed = dot(grad_qkv, qkv_here, ((1,), (1,))).astype(BF16)
        grad_normed = lax.psum_scatter(grad_normed, "fsdp", scatter_dimension=0, tiled=True).astype(F32)
        attn_grad = jnp.concatenate([qkv_grad, out_grad.reshape(width, cols)], axis=1).astype(BF16)
        attn_grad = lax.psum_scatter(attn_grad, "dp", scatter_dimension=0, tiled=True)
        attn_grad = attn_grad.reshape(fsdp, own_rows, 4 * cols)
        attn_grad = lax.all_to_all(attn_grad, "fsdp", 0, 0, tiled=True)
        inner_grad = lax.all_to_all(inner_grad, BOTH, 0, 0, tiled=True)
        outer_grad = lax.all_to_all(outer_grad, "fsdp", 0, 0, tiled=True)
        inner_grad = inner_grad.reshape(dp, fsdp, 2, experts_here, own_rows, ff_here)
        inner_grad = inner_grad.transpose(4, 1, 3, 2, 0, 5).reshape(own_rows, experts, 2 * ff)
        outer_grad = outer_grad.transpose(2, 0, 1, 3).reshape(-1, experts, width)
        attn_term = jnp.sum(grad_normed * unit1, axis=0)
        hidden_grad = grad_middle + norm_back(grad_normed * gain_attn, unit1, scale1)

        router_term = dot(normed2, grad_logits, ((0,), (0,)))
        qk_full = jnp.zeros((2, width), F32)
        qk_full = lax.dynamic_update_slice(qk_full, qk_term, (0, here))
        terms = jnp.concatenate([attn_term[None], qk_full, ffn_term[None]])
        terms = terms.reshape(4, n, own_rows).transpose(1, 0, 2).reshape(n, 4 * own_rows)
        terms = jnp.concatenate(
            [
                terms,
                router_term.reshape(n, own_rows * experts),
                jnp.broadcast_to(squares[None], (n, 3)),
            ],
            axis=1,
        )
        term_size = terms.shape[1]
        term_rows = -(-term_size // 1024) * 8
        terms = jnp.pad(terms, ((0, 0), (0, term_rows * 128 - term_size)))
        terms = exchange(terms.reshape(n, term_rows, 128), BOTH, 7, True)
        terms = jnp.sum(terms, axis=0).reshape(-1)
        gain_grads = terms[: 4 * own_rows].reshape(4, own_rows)
        router_grad = terms[4 * own_rows : 4 * own_rows + own_rows * experts]
        router_grad = router_grad.reshape(own_rows, experts)
        square_sums = terms[term_size - 3 : term_size]
    attn_grad = attn_grad.reshape(fsdp, own_rows, 4, cols).transpose(1, 2, 0, 3).astype(F32)
    attn_grad = attn_grad.reshape(own_rows, 4 * width)
    valid_cells = jnp.sum(lengths).astype(F32) * width
    stats = jnp.sqrt(square_sums / valid_cells)

    return (
        block_total.astype(BF16),
        hidden_grad,
        gain_grads[0],
        gain_grads[1],
        gain_grads[2],
        gain_grads[3],
        attn_grad[:, : 3 * width],
        attn_grad[:, 3 * width :],
        router_grad,
        inner_grad.astype(F32),
        outer_grad.astype(F32),
        stats,
    )


def solution(mesh):
    one = P(BOTH)
    two = P(BOTH, None)
    three = P(BOTH, None, None)
    in_specs = (two, P(), two, one, one, one, one, two, two, two, three, three, two)
    out_specs = (two, two, one, one, one, one, two, two, two, three, three, P())
    return jax.shard_map(body, mesh=mesh, in_specs=in_specs, out_specs=out_specs, check_vma=False)
```
